32 devices in a mesh: box: 8 (over y, x, core), dir: 4 (over z).
Axes of the slice: x: 2, y: 2, z: 4, core: 2. Of those that a mesh axis runs over, the one named last changes fastest.
Arguments:
- currents: bfloat16 [512, 8, 128], P(('box', 'dir')), may hold values from -6 to 6
- positions: bfloat16 [512, 3, 128], P(('box', 'dir')), may hold values from -2 to 2
- radiation: bfloat16 [128, 256], replicated, may hold values from -0.5 to 0.5
- interp_index: int32 [512, 4], replicated, may hold values from 0 to 127
- interp_weight: float32 [512, 4], replicated, may hold values from -3 to 3
- child_phase: float32 [8, 512], replicated, may hold values from -3.140625 to 3.140625
- near_src: int32 [512, 27], P(('box', 'dir')), may hold values from 0 to 511, as said below
- trans_src: int32 [64, 32], P('box'), may hold values from 0 to 63, as said below
- trans_id: int32 [64, 32], P('box'), may hold values from 0 to 315
- trans_count: int32 [64], P('box'), may hold values from 16 to 32, as said below
- trans_table: float32 [316, 2, 512], replicated, may hold values from -0.009 to 0.009
Outputs:
- field: float32 [512, 8, 128], P(('box', 'dir'))
The draws below stay inside these ranges and needn't reach their ends.
Inputs may be any that keep to these rules, and one draw needn't show every extreme that they name: `near_src`: entry 0 of row i is i itself; every entry lies in the block of 16 boxes that holds i or in a block beside it. `trans_src`: every entry lies in the block of 8 parents that holds the row's parent or in a block beside it. Entries at and after trans_count are ignored; some parent in every block of 8 has 32.
All inputs are finite; a program needn't handle non-finite values.
Results may differ from the reference program's by a relative error of at most 0.0045.
Values may be sent and summed in bfloat16 or wider, within the bound.
No kernel may reach another device: no remote copies, remote signals or barrier semaphores. Data moves between devices by JAX's collectives and lax.ppermute only.
A program may use at most 64 MiB of HBM per device.

```python
import math
import jax
import jax.numpy as jnp
from jax import lax

BOX_DEV = 16
P_SIZE = 128
W = 8
K1 = 128
K = 512
STEN = 4
NN = 27
NT = 32
NTAB = 316
NBOX = 512
NPAR = 64
GROUP = 8


def window_sources(key, total, block, entries):
    index = jnp.arange(total, dtype=jnp.int32)
    group_idx = index // block
    lower = jnp.maximum(group_idx - 1, 0) * block
    upper = jnp.minimum(group_idx + 2, total // block) * block
    offsets = jax.random.randint(key, (total, entries), 0, 1 << 30, dtype=jnp.int32)
    return lower[:, None] + offsets % (upper - lower)[:, None]


def draw_positions(key, part):
    return jax.random.uniform(jax.random.fold_in(key, 41), (NBOX, 3, P_SIZE), jnp.float32, -2.0, 2.0).astype(jnp.bfloat16)


def draw_near_src(key, part):
    sources = window_sources(jax.random.fold_in(key, 11), NBOX, BOX_DEV, NN)
    return sources.at[:, 0].set(jnp.arange(NBOX, dtype=jnp.int32))


def draw_trans_src(key, part):
    return window_sources(jax.random.fold_in(key, 23), NPAR, GROUP, NT)


def draw_trans_count(key, part):
    counts = jax.random.randint(jax.random.fold_in(key, 31), (NPAR,), NT // 2, NT + 1, dtype=jnp.int32)
    index = jnp.arange(NPAR, dtype=jnp.int32)
    return jnp.where(index % GROUP == 0, NT, counts)


def set_ends(drawn, key, smallest, high):
    spot = [jax.random.randint(jax.random.fold_in(key, axis), (), 0, length) for axis, length in enumerate(drawn.shape)]
    longest = drawn.shape.index(max(drawn.shape))
    neighbour = spot[:longest] + [(spot[longest] + 1) % drawn.shape[longest]] + spot[longest + 1:]
    return drawn.at[tuple(spot)].set(smallest).at[tuple(neighbour)].set(high)


def block_levels(own_key, shape, cuts, least, largest):
    loudness, own = 1.0, jax.random.fold_in(own_key, 6)
    for axis_at, parts in cuts:
        heights = jnp.exp(jax.random.uniform(jax.random.fold_in(own, axis_at), (parts,), jnp.float32, least / len(cuts), largest / len(cuts)))
        loudness = loudness * jnp.repeat(heights, shape[axis_at] // parts).reshape([-1 if axis == axis_at else 1 for axis in range(len(shape))])
    return loudness


def centred(stream_key, shape, spread, most, split=(), kind=jnp.bfloat16):
    values = spread * jax.random.normal(stream_key, shape, jnp.float32)
    if split:
        values = values * block_levels(stream_key, shape, split, -0.22, 0.18)
    return jnp.clip(values, -most, most).astype(kind)


def setup_inputs(seed: int = 0) -> dict:
    key_list = jax.random.split(jax.random.key(seed), 12)
    currents = centred(key_list[0], (NBOX, W, P_SIZE), 1.0, 6.0, ((0, 32),))
    positions = draw_positions(jax.random.fold_in(key_list[11], 71), 0)
    radiation = centred(key_list[2], (P_SIZE, 2 * K1), P_SIZE ** -0.5, 0.5)
    interp_index = set_ends(jax.random.randint(key_list[3], (K, STEN), 0, K1), jax.random.fold_in(key_list[3], 1), 0, K1 - 1).astype(jnp.int32)
    interp_weight = centred(key_list[4], (K, STEN), 0.5, 3.0, (), jnp.float32)
    child_phase = jnp.clip(jax.random.uniform(key_list[5], (8, K), jnp.float32, -3.140625, 3.140625), -3.140625, 3.140625)
    near_src = draw_near_src(jax.random.fold_in(key_list[11], 71), 0)
    trans_src = draw_trans_src(jax.random.fold_in(key_list[11], 71), 0)
    trans_id = set_ends(jax.random.randint(key_list[8], (NPAR, NT), 0, NTAB), jax.random.fold_in(key_list[8], 1), 0, NTAB - 1).astype(jnp.int32)
    trans_count = draw_trans_count(jax.random.fold_in(key_list[11], 71), 0)
    trans_table = centred(key_list[10], (NTAB, 2, K), 0.0015, 0.009, (), jnp.float32)
    return dict(currents=currents, positions=positions, radiation=radiation, interp_index=interp_index, interp_weight=interp_weight, child_phase=child_phase, near_src=near_src, trans_src=trans_src, trans_id=trans_id, trans_count=trans_count, trans_table=trans_table)


def interp_matrix(interp_index, interp_weight, leaf_dirs):
    columns = jnp.arange(leaf_dirs, dtype=jnp.int32)
    matches = (interp_index[:, :, None] == columns[None, None, :]).astype(jnp.float32)
    return lax.optimization_barrier(jnp.sum(interp_weight[:, :, None] * matches, axis=1)).T

def near_tiles(own_pos, src_pos):
    entries = src_pos.shape[1]
    width = src_pos.shape[3]
    dist_sq = jnp.zeros((own_pos.shape[0], entries, width, width), jnp.float32)
    for axis_num in range(3):
        offset = own_pos[:, None, axis_num, :, None] - src_pos[:, :, axis_num, None, :]
        dist_sq = dist_sq + offset * offset
    distance = jnp.sqrt(dist_sq)
    factor = 1.0 / math.sqrt(entries * width)
    return (jnp.cos(4.0 * distance) / (distance + 0.5) * factor).astype(jnp.bfloat16)

def translate(window, sources, list_ids, counts, trans_tab):
    spectra = window[sources].astype(jnp.float32)
    coeff = trans_tab[list_ids]
    entries = jnp.arange(sources.shape[1], dtype=jnp.int32)
    live_mask = (entries[None, :] < counts[:, None]).astype(jnp.float32)
    coeff_re = coeff[:, :, 0, None, :] * live_mask[:, :, None, None]
    coeff_im = coeff[:, :, 1, None, :] * live_mask[:, :, None, None]
    real_part = lax.optimization_barrier(jnp.sum(coeff_re * spectra[:, :, 0] - coeff_im * spectra[:, :, 1], axis=1))
    imag_part = lax.optimization_barrier(jnp.sum(coeff_re * spectra[:, :, 1] + coeff_im * spectra[:, :, 0], axis=1))
    return jnp.stack([real_part, imag_part], axis=1)

def reference(currents, positions, radiation, interp_index, interp_weight, child_phase, near_src, trans_src, trans_id, trans_count, trans_table):

    def near_block(packed):
        box_ids, src_ids = packed
        own_pos = positions[box_ids].astype(jnp.float32)
        src_pos = positions[src_ids].astype(jnp.float32)
        src_x = currents[src_ids].astype(jnp.float32)
        tiles = near_tiles(own_pos, src_pos).astype(jnp.float32)
        return jnp.einsum('bemn,bewn->bwm', tiles, src_x)
    box_ids = jnp.arange(NBOX, dtype=jnp.int32).reshape(-1, 16)
    near_field = lax.map(near_block, (box_ids, near_src.reshape(-1, 16, NN))).reshape(NBOX, W, P_SIZE)
    imatrix = interp_matrix(interp_index, interp_weight, K1).astype(jnp.bfloat16)
    leaf = jnp.dot(currents.reshape(NBOX * W, P_SIZE), radiation, preferred_element_type=jnp.float32).astype(jnp.bfloat16)
    up_re = jnp.dot(leaf[:, :K1], imatrix, preferred_element_type=jnp.float32).reshape(NPAR, 8, W, K)
    up_im = jnp.dot(leaf[:, K1:], imatrix, preferred_element_type=jnp.float32).reshape(NPAR, 8, W, K)
    cos_phase = jnp.cos(child_phase)[None, :, None, :]
    sin_phase = jnp.sin(child_phase)[None, :, None, :]
    parent_re = lax.optimization_barrier(jnp.sum(cos_phase * up_re - sin_phase * up_im, axis=1))
    parent_im = lax.optimization_barrier(jnp.sum(sin_phase * up_re + cos_phase * up_im, axis=1))
    parent = lax.optimization_barrier(jnp.stack([parent_re, parent_im], axis=1).astype(jnp.bfloat16))

    def trans_block(packed):
        sources, list_ids, counts = packed
        return translate(parent, sources, list_ids, counts, trans_table)
    local_field = lax.map(trans_block, (trans_src.reshape(-1, GROUP, NT), trans_id.reshape(-1, GROUP, NT), trans_count.reshape(-1, GROUP)))
    local_field = lax.optimization_barrier(local_field.reshape(NPAR, 2, W, K).astype(jnp.bfloat16)).astype(jnp.float32)
    loc_re = local_field[:, 0][:, None]
    loc_im = local_field[:, 1][:, None]
    down_re = (cos_phase * loc_re + sin_phase * loc_im).reshape(NBOX * W, K).astype(jnp.bfloat16)
    down_im = (cos_phase * loc_im - sin_phase * loc_re).reshape(NBOX * W, K).astype(jnp.bfloat16)
    in_re = jnp.dot(down_re, imatrix.T, preferred_element_type=jnp.float32)
    in_im = jnp.dot(down_im, imatrix.T, preferred_element_type=jnp.float32)
    incoming = jnp.concatenate([in_re, in_im], axis=1).astype(jnp.bfloat16)
    far_field = lax.dot_general(incoming, radiation, (((1,), (1,)), ((), ())), preferred_element_type=jnp.float32)
    return near_field + far_field.reshape(NBOX, W, P_SIZE)
```

```python
import functools
import math

import jax
import jax.numpy as jnp
from jax import lax
from jax.experimental import pallas as pl
from jax.experimental.pallas import tpu as pltpu
from jax.sharding import PartitionSpec as P

F32 = jnp.float32
BF16 = jnp.bfloat16

WAVENUMBER = 4.0
OFFSET = 0.5
TURN = WAVENUMBER / (2.0 * math.pi)
C0, C1, C2, C3 = (4.551727469085273, -22.461833254303432, 18.47278585020764, -6.062355797782118)
LEAD = 0.21969679868984615
ROUNDER = 12582912.0
TILES = 8


def round_up(value, step):
    return -(-value // step) * step


def neighbours(x, axis):
    size = lax.axis_size(axis)
    up = [(i, i + 1) for i in range(size - 1)]
    down = [(j, i) for i, j in up]
    return lax.ppermute(x, axis, up), lax.ppermute(x, axis, down)


def split3(x):
    high = x.astype(BF16).astype(F32)
    rest = x - high
    mid = rest.astype(BF16).astype(F32)
    return high, mid, rest - mid


def nt_dot(a, b):
    return lax.dot_general(a, b, (((1,), (1,)), ((), ())), preferred_element_type=F32)


def nn_dot(a, b):
    return jnp.dot(a, b, preferred_element_type=F32)


def code_bits(boxes, entries):
    count_bits = entries.bit_length()
    source_bits = (3 * boxes - 1).bit_length()
    return source_bits + count_bits, count_bits


def build_pairs(near_src, base, length):
    boxes, entries = near_src.shape
    box_shift, source_shift = code_bits(boxes, entries)
    lanes = round_up(3 * boxes, 128)
    local = near_src - base
    lane = lax.broadcasted_iota(jnp.int32, (boxes, lanes), 1)
    count = jnp.zeros((boxes, lanes), jnp.int32)
    for e in range(entries):
        count = count + (local[:, e : e + 1] == lane).astype(jnp.int32)
    present = count > 0
    flags = present.astype(F32)
    row = lax.broadcasted_iota(jnp.int32, (lanes, lanes), 0)
    col = lax.broadcasted_iota(jnp.int32, (lanes, lanes), 1)
    rank = nn_dot(flags.astype(BF16), (row < col).astype(F32).astype(BF16))
    totals = jnp.sum(flags, axis=1, keepdims=True)
    box_row = lax.broadcasted_iota(jnp.int32, (boxes, boxes), 0)
    box_col = lax.broadcasted_iota(jnp.int32, (boxes, boxes), 1)
    before = (box_col < box_row).astype(F32).astype(BF16)
    offset = nn_dot(before, jnp.broadcast_to(totals, (boxes, lanes)).astype(BF16))
    place = jnp.where(present, rank + offset, -1.0)
    box = lax.broadcasted_iota(jnp.int32, (boxes, lanes), 0)
    code = ((box << box_shift) | (lane << source_shift) | count).astype(F32)
    place_t = place.T
    code_t = code.T
    rows = 3 * boxes
    slot = lax.broadcasted_iota(jnp.int32, (rows, length), 1).astype(F32)
    found = jnp.zeros((rows, length), F32)
    for i in range(boxes):
        hit = place_t[:rows, i : i + 1] == slot
        found = found + jnp.where(hit, code_t[:rows, i : i + 1], 0.0)
    pairs = jnp.sum(found, axis=0, keepdims=True)
    total = jnp.sum(totals, axis=0, keepdims=True)
    last = lax.broadcasted_iota(jnp.int32, (1, length), 1) == length - 1
    return jnp.where(last, total, pairs).astype(jnp.int32)


def outgoing_kernel(
    x_ref, rad_ref, idx_ref, wgt_ref, phase_ref, near_ref, parent_ref, imat_ref, cos_ref, sin_ref, pairs_ref
):
    leaf_dirs, parent_dirs = imat_ref.shape
    parents, rows, _ = parent_ref.shape
    waves = rows // 2
    boxes = near_ref.shape[0]
    base = (lax.axis_index(("box", "dir")) - 1) * boxes
    pairs_ref[...] = build_pairs(near_ref[...], base, pairs_ref.shape[1])
    column = lax.broadcasted_iota(jnp.int32, (leaf_dirs, parent_dirs), 0)
    imat = jnp.zeros((leaf_dirs, parent_dirs), F32)
    for s in range(idx_ref.shape[0]):
        imat = imat + jnp.where(idx_ref[s : s + 1, :] == column, wgt_ref[s : s + 1, :], 0.0)
    imat = imat.astype(BF16)
    imat_ref[...] = imat
    cos_phase = jnp.cos(phase_ref[...])
    sin_phase = jnp.sin(phase_ref[...])
    cos_ref[...] = cos_phase
    sin_ref[...] = sin_phase
    leaf = nn_dot(x_ref[...], rad_ref[...]).astype(BF16)
    up_re = nn_dot(leaf[:, :leaf_dirs], imat)
    up_im = nn_dot(leaf[:, leaf_dirs:], imat)
    for q in range(parents):
        re = jnp.zeros((waves, parent_dirs), F32)
        im = jnp.zeros((waves, parent_dirs), F32)
        for c in range(8):
            at = (q * 8 + c) * waves
            ure = up_re[at : at + waves]
            uim = up_im[at : at + waves]
            re = re + (cos_phase[c : c + 1] * ure - sin_phase[c : c + 1] * uim)
            im = im + (sin_phase[c : c + 1] * ure + cos_phase[c : c + 1] * uim)
        parent_ref[q] = jnp.concatenate([re, im], axis=0).astype(BF16)


def near_kernel(
    entries, pairs_ref, before_ref, own_ref, after_ref, out_ref, win_ref, src_ref, obs_ref, u0_ref, u1_ref, t0_ref, t1_ref
):
    boxes, rows, width = own_ref.shape
    waves = out_ref.shape[1]
    scale = TURN * TURN
    group = 128 // 16
    box_shift, source_shift = code_bits(boxes, entries)

    for part, ref in enumerate((before_ref, own_ref, after_ref)):
        win_ref[part * boxes : (part + 1) * boxes] = ref[...]
        pos = ref[...].astype(F32)[:, 8:16, :]
        norm = split3(scale * jnp.sum(pos * pos, axis=1, keepdims=True))
        at = lax.broadcasted_iota(jnp.int32, pos.shape, 1)
        first = jnp.where(at < 3, pos, 1.0)
        first = jnp.where(at == 3, norm[0], jnp.where(at == 4, norm[1], jnp.where(at == 5, norm[2], first)))
        second = jnp.where(at == 3, 1.0, pos + pltpu.roll(pos, 4, 1))
        feats = jnp.concatenate([first, second], axis=1).astype(BF16).reshape(boxes * 16, width)
        eye = lax.broadcasted_iota(jnp.int32, (width, width), 0) == lax.broadcasted_iota(
            jnp.int32, (width, width), 1
        )
        flipped = nt_dot(eye.astype(F32).astype(BF16), feats).astype(BF16)
        for j in range(boxes // group):
            src_ref[part * (boxes // group) + j] = flipped[:, j * 128 : (j + 1) * 128]
        if part == 1:
            cross = split3((-2.0 * scale) * pos)
            first = jnp.where(at < 3, cross[0], 1.0)
            first = jnp.where(at == 6, norm[0], jnp.where(at == 7, norm[1], first))
            second = jnp.where(at == 3, norm[2], cross[1] + pltpu.roll(cross[2], 4, 1))
            own = jnp.concatenate([first, second], axis=1).astype(BF16)
            pad = 128 - 16
            obs_ref[:, :pad, :] = jnp.zeros((boxes, pad, width), BF16)
            obs_ref[:, pad : pad + 16, :] = own
            obs_ref[:, pad + 16 :, :] = jnp.zeros((boxes, pad, width), BF16)

    out_ref[...] = jnp.zeros(out_ref.shape, F32)
    t1_ref[...] = jnp.zeros(t1_ref.shape, BF16)

    def decode(chunk, g):
        code = pairs_ref[0, chunk * TILES + g]
        i = code >> box_shift
        s = (code >> source_shift) & ((1 << (box_shift - source_shift)) - 1)
        return i, s, code & ((1 << source_shift) - 1)

    def distances(chunk, u_ref):
        for g in range(TILES):
            i, s, _ = decode(chunk, g)
            skip = pl.multiple_of((group - 1 - (s & (group - 1))) * 16, 16)
            u_ref[g] = nn_dot(src_ref[s >> 3], obs_ref[i, pl.ds(skip, 128), :])

    def tiles(u_ref, t_ref):
        for g in range(TILES):
            v = jnp.maximum(u_ref[g], 1e-12)
            q = v * lax.rsqrt(v)
            t = q - ((q + ROUNDER) - ROUNDER)
            z = t * t
            p = (((z + C3) * z + C2) * z + C1) * z + C0
            cosine = p * p - 0.5 / (LEAD * LEAD)
            t_ref[g] = (cosine * pl.reciprocal(q + OFFSET * TURN, approx=True)).astype(BF16)

    def products(chunk, t_ref):
        for g in range(TILES):
            i, s, count = decode(chunk, g)
            got = nn_dot(win_ref[s], t_ref[g])
            out_ref[i] += count.astype(F32) * got[:waves]

    total = pairs_ref[0, pairs_ref.shape[1] - 1]
    rounds = (total + (2 * TILES - 1)) // (2 * TILES)
    distances(0, u0_ref)

    def body(k, carry):
        distances(2 * k + 1, u1_ref)
        tiles(u0_ref, t0_ref)
        products(jnp.maximum(2 * k - 1, 0), t1_ref)
        distances(2 * k + 2, u0_ref)
        tiles(u1_ref, t1_ref)
        products(2 * k, t0_ref)
        return carry

    lax.fori_loop(0, rounds, body, 0)
    products(jnp.maximum(2 * rounds - 1, 0), t1_ref)
    factor = TURN / math.sqrt(entries * width) * 2.0 * LEAD * LEAD
    out_ref[...] = out_ref[...] * factor


def incoming_kernel(
    src_ref, id_ref, count_ref, before_ref, own_ref, after_ref, table_ref, cos_ref, sin_ref, imat_ref, rad_ref,
    near_ref, out_ref, down_re_ref, down_im_ref
):
    group, rows, parent_dirs = own_ref.shape
    waves = rows // 2
    parents = near_ref.shape[0] // 8
    row0 = lax.axis_index("dir") * parents
    base = lax.axis_index("box") * group
    window = (before_ref, own_ref, after_ref)
    cos_phase = cos_ref[...]
    sin_phase = sin_ref[...]
    for q in range(parents):
        row = row0 + q
        total = count_ref[row]

        def add_entry(e, sums, spectra_ref, row=row):
            re, im = sums
            spectrum = spectra_ref[src_ref[row, e] % group].astype(F32)
            coeff = table_ref[id_ref[row, e]]
            sre, sim = spectrum[:waves], spectrum[waves:]
            cre, cim = coeff[0:1], coeff[1:2]
            return re + (cre * sre - cim * sim), im + (cre * sim + cim * sre)

        def step(e, sums, row=row):
            part = src_ref[row, e] // group - (base // group - 1)
            return lax.switch(part, [lambda s, r=r: add_entry(e, s, r) for r in window], sums)

        zero = jnp.zeros((waves, parent_dirs), F32)
        re, im = lax.fori_loop(0, total, step, (zero, zero))
        re = re.astype(BF16).astype(F32)
        im = im.astype(BF16).astype(F32)
        for c in range(8):
            at = (q * 8 + c) * waves
            cos, sin = cos_phase[c : c + 1], sin_phase[c : c + 1]
            down_re_ref[at : at + waves] = cos * re + sin * im
            down_im_ref[at : at + waves] = cos * im - sin * re
    imat = imat_ref[...]
    in_re = nt_dot(down_re_ref[...].astype(BF16), imat)
    in_im = nt_dot(down_im_ref[...].astype(BF16), imat)
    incoming = jnp.concatenate([in_re, in_im], axis=1).astype(BF16)
    far = nt_dot(incoming, rad_ref[...])
    out_ref[...] = near_ref[...] + far.reshape(near_ref.shape)


def per_device(
    currents, positions, radiation, interp_index, interp_weight, child_phase, near_src, trans_src, trans_id,
    trans_count, trans_table
):
    boxes, waves, width = currents.shape
    entries = near_src.shape[1]
    leaf_dirs = radiation.shape[1] // 2
    parent_dirs = child_phase.shape[1]
    parents = boxes // 8
    vmem = pl.BlockSpec(memory_space=pltpu.VMEM)
    smem = pl.BlockSpec(memory_space=pltpu.SMEM)

    packet = jnp.concatenate([currents, positions, jnp.zeros((boxes, 16 - waves - 3, width), BF16)], axis=1)
    before, after = neighbours(packet, ("box", "dir"))

    length = round_up(boxes * entries + 3 * TILES + 1, 128)
    parent, imat, cos_phase, sin_phase, pairs = pl.pallas_call(
        outgoing_kernel,
        out_shape=(
            jax.ShapeDtypeStruct((parents, 2 * waves, parent_dirs), BF16),
            jax.ShapeDtypeStruct((leaf_dirs, parent_dirs), BF16),
            jax.ShapeDtypeStruct((8, parent_dirs), F32),
            jax.ShapeDtypeStruct((8, parent_dirs), F32),
            jax.ShapeDtypeStruct((1, length), jnp.int32),
        ),
        in_specs=[vmem] * 6,
        out_specs=(vmem,) * 5,
        compiler_params=pltpu.CompilerParams(vmem_limit_bytes=32 * 1024 * 1024),
        name="outgoing",
    )(currents.reshape(boxes * waves, width), radiation, interp_index.T, interp_weight.T, child_phase, near_src)

    own_group = lax.all_gather(parent, "dir", axis=0, tiled=True)
    group_before, group_after = neighbours(own_group, "box")

    near = pl.pallas_call(
        functools.partial(near_kernel, entries),
        out_shape=jax.ShapeDtypeStruct((boxes, waves, width), F32),
        in_specs=[smem, vmem, vmem, vmem],
        out_specs=vmem,
        scratch_shapes=[
            pltpu.VMEM((3 * boxes, 16, width), BF16),
            pltpu.VMEM((3 * boxes // 8, width, 128), BF16),
            pltpu.VMEM((boxes, 2 * (128 - 16) + 16, width), BF16),
            pltpu.VMEM((TILES, width, width), F32),
            pltpu.VMEM((TILES, width, width), F32),
            pltpu.VMEM((TILES, width, width), BF16),
            pltpu.VMEM((TILES, width, width), BF16),
        ],
        compiler_params=pltpu.CompilerParams(vmem_limit_bytes=32 * 1024 * 1024),
        name="near_field",
    )(pairs, before, packet, after)

    return pl.pallas_call(
        incoming_kernel,
        out_shape=jax.ShapeDtypeStruct((boxes, waves, width), F32),
        in_specs=[smem] * 3 + [vmem] * 9,
        out_specs=vmem,
        scratch_shapes=[
            pltpu.VMEM((boxes * waves, parent_dirs), F32),
            pltpu.VMEM((boxes * waves, parent_dirs), F32),
        ],
        compiler_params=pltpu.CompilerParams(vmem_limit_bytes=32 * 1024 * 1024),
        name="incoming",
    )(
        trans_src, trans_id, trans_count, group_before, own_group, group_after, trans_table, cos_phase, sin_phase,
        imat, radiation, near
    )


def solution(mesh):
    placed = (
        P(("box", "dir"), None, None),
        P(("box", "dir"), None, None),
        P(),
        P(),
        P(),
        P(),
        P(("box", "dir"), None),
        P("box", None),
        P("box", None),
        P("box"),
        P(),
    )
    return jax.shard_map(
        per_device,
        mesh=mesh,
        in_specs=placed,
        out_specs=P(("box", "dir"), None, None),
        check_vma=False,
    )
```

```python
import functools
import math

import jax
import jax.numpy as jnp
from jax import lax
from jax.experimental import pallas as pl
from jax.experimental.pallas import tpu as pltpu
from jax.sharding import PartitionSpec as P

F32 = jnp.float32
BF16 = jnp.bfloat16

WAVENUMBER = 4.0
OFFSET = 0.5
TURN = WAVENUMBER / (2.0 * math.pi)
C0, C1, C2, C3 = (4.551727469085273, -22.461833254303432, 18.47278585020764, -6.062355797782118)
LEAD = 0.21969679868984615
ROUNDER = 12582912.0
TILES = 8


def round_up(value, step):
    return -(-value // step) * step


def neighbours(x, axis):
    size = lax.axis_size(axis)
    up = [(i, i + 1) for i in range(size - 1)]
    down = [(j, i) for i, j in up]
    return lax.ppermute(x, axis, up), lax.ppermute(x, axis, down)


def split3(x):
    high = x.astype(BF16).astype(F32)
    rest = x - high
    mid = rest.astype(BF16).astype(F32)
    return high, mid, rest - mid


def nt_dot(a, b):
    return lax.dot_general(a, b, (((1,), (1,)), ((), ())), preferred_element_type=F32)


def nn_dot(a, b):
    return jnp.dot(a, b, preferred_element_type=F32)


def code_bits(boxes, entries):
    count_bits = entries.bit_length()
    source_bits = (3 * boxes - 1).bit_length()
    return source_bits + count_bits, count_bits


def build_pairs(near_src, base, length):
    boxes, entries = near_src.shape
    box_shift, source_shift = code_bits(boxes, entries)
    lanes = round_up(3 * boxes, 128)
    local = near_src - base
    lane = lax.broadcasted_iota(jnp.int32, (boxes, lanes), 1)
    count = jnp.zeros((boxes, lanes), jnp.int32)
    for e in range(entries):
        count = count + (local[:, e : e + 1] == lane).astype(jnp.int32)
    present = count > 0
    flags = present.astype(F32)
    row = lax.broadcasted_iota(jnp.int32, (lanes, lanes), 0)
    col = lax.broadcasted_iota(jnp.int32, (lanes, lanes), 1)
    rank = nn_dot(flags.astype(BF16), (row < col).astype(F32).astype(BF16))
    totals = jnp.sum(flags, axis=1, keepdims=True)
    box_row = lax.broadcasted_iota(jnp.int32, (boxes, boxes), 0)
    box_col = lax.broadcasted_iota(jnp.int32, (boxes, boxes), 1)
    before = (box_col < box_row).astype(F32).astype(BF16)
    offset = nn_dot(before, jnp.broadcast_to(totals, (boxes, lanes)).astype(BF16))
    place = jnp.where(present, rank + offset, -1.0)
    box = lax.broadcasted_iota(jnp.int32, (boxes, lanes), 0)
    code = ((box << box_shift) | (lane << source_shift) | count).astype(F32)
    place_t = place.T
    code_t = code.T
    rows = 3 * boxes
    slot = lax.broadcasted_iota(jnp.int32, (rows, length), 1).astype(F32)
    found = jnp.zeros((rows, length), F32)
    for i in range(boxes):
        hit = place_t[:rows, i : i + 1] == slot
        found = found + jnp.where(hit, code_t[:rows, i : i + 1], 0.0)
    pairs = jnp.sum(found, axis=0, keepdims=True)
    total = jnp.sum(totals, axis=0, keepdims=True)
    last = lax.broadcasted_iota(jnp.int32, (1, length), 1) == length - 1
    return jnp.where(last, total, pairs).astype(jnp.int32)


def fetch(copies, sems):
    started = [pltpu.make_async_copy(src, dst, sems.at[k]) for k, (src, dst) in enumerate(copies)]
    for copy in started:
        copy.start()
    for copy in started:
        copy.wait()


def outgoing_kernel(
    x_hbm, pos_hbm, rad_hbm, idx_hbm, wgt_hbm, phase_hbm, near_hbm, packet_ref, parent_hbm, imat_ref, cos_ref, sin_ref,
    pairs_ref, x_ref, pos_ref, rad_ref, idx_ref, wgt_ref, phase_ref, near_ref, parent_ref, sems
):
    fetch(
        (
            (x_hbm, x_ref),
            (pos_hbm, pos_ref),
            (rad_hbm, rad_ref),
            (idx_hbm, idx_ref),
            (wgt_hbm, wgt_ref),
            (phase_hbm, phase_ref),
            (near_hbm, near_ref),
        ),
        sems,
    )
    leaf_dirs, parent_dirs = imat_ref.shape
    parents, rows, _ = parent_ref.shape
    waves = rows // 2
    boxes, _, width = packet_ref.shape
    x = x_ref[...].astype(F32)
    planes = pos_ref[...].astype(F32)
    at = lax.broadcasted_iota(jnp.int32, (boxes, 16 - waves, width), 1)
    pos = jnp.zeros((boxes, 16 - waves, width), F32)
    for axis in range(3):
        pos = jnp.where(at == axis, planes[axis][:, None, :], pos)
    packet_ref[...] = jnp.concatenate([x, pos], axis=1).astype(BF16)
    column = lax.broadcasted_iota(jnp.int32, (leaf_dirs, parent_dirs), 0)
    imat = jnp.zeros((leaf_dirs, parent_dirs), F32)
    for s in range(idx_ref.shape[0]):
        imat = imat + jnp.where(idx_ref[s : s + 1, :] == column, wgt_ref[s : s + 1, :], 0.0)
    imat = imat.astype(BF16)
    imat_ref[...] = imat
    cos_phase = jnp.cos(phase_ref[...])
    sin_phase = jnp.sin(phase_ref[...])
    cos_ref[...] = cos_phase
    sin_ref[...] = sin_phase
    leaf = nn_dot(x.reshape(boxes * waves, width).astype(BF16), rad_ref[...]).astype(BF16)
    up_re = nn_dot(leaf[:, :leaf_dirs], imat)
    up_im = nn_dot(leaf[:, leaf_dirs:], imat)
    for q in range(parents):
        re = jnp.zeros((waves, parent_dirs), F32)
        im = jnp.zeros((waves, parent_dirs), F32)
        for c in range(8):
            at = (q * 8 + c) * waves
            ure = up_re[at : at + waves]
            uim = up_im[at : at + waves]
            re = re + (cos_phase[c : c + 1] * ure - sin_phase[c : c + 1] * uim)
            im = im + (sin_phase[c : c + 1] * ure + cos_phase[c : c + 1] * uim)
        parent_ref[q] = jnp.concatenate([re, im], axis=0).astype(BF16)
    send = pltpu.make_async_copy(parent_ref, parent_hbm, sems.at[0])
    send.start()
    base = (lax.axis_index(("box", "dir")) - 1) * boxes
    pairs_ref[...] = build_pairs(near_ref[...], base, pairs_ref.shape[1])
    send.wait()


def near_kernel(
    entries, pairs_ref, before_ref, own_ref, after_ref, out_ref, win_ref, src_ref, obs_ref, u0_ref, u1_ref, t0_ref, t1_ref
):
    boxes, rows, width = own_ref.shape
    waves = out_ref.shape[1]
    scale = TURN * TURN
    group = 128 // 16
    box_shift, source_shift = code_bits(boxes, entries)

    for part, ref in enumerate((before_ref, own_ref, after_ref)):
        win_ref[part * boxes : (part + 1) * boxes] = ref[...]
        pos = ref[...].astype(F32)[:, 8:16, :]
        norm = split3(scale * jnp.sum(pos * pos, axis=1, keepdims=True))
        at = lax.broadcasted_iota(jnp.int32, pos.shape, 1)
        first = jnp.where(at < 3, pos, 1.0)
        first = jnp.where(at == 3, norm[0], jnp.where(at == 4, norm[1], jnp.where(at == 5, norm[2], first)))
        second = jnp.where(at == 3, 1.0, pos + pltpu.roll(pos, 4, 1))
        feats = jnp.concatenate([first, second], axis=1).astype(BF16).reshape(boxes * 16, width)
        eye = lax.broadcasted_iota(jnp.int32, (width, width), 0) == lax.broadcasted_iota(
            jnp.int32, (width, width), 1
        )
        flipped = nt_dot(eye.astype(F32).astype(BF16), feats).astype(BF16)
        for j in range(boxes // group):
            src_ref[part * (boxes // group) + j] = flipped[:, j * 128 : (j + 1) * 128]
        if part == 1:
            cross = split3((-2.0 * scale) * pos)
            first = jnp.where(at < 3, cross[0], 1.0)
            first = jnp.where(at == 6, norm[0], jnp.where(at == 7, norm[1], first))
            second = jnp.where(at == 3, norm[2], cross[1] + pltpu.roll(cross[2], 4, 1))
            own = jnp.concatenate([first, second], axis=1).astype(BF16)
            pad = 128 - 16
            obs_ref[:, :pad, :] = jnp.zeros((boxes, pad, width), BF16)
            obs_ref[:, pad : pad + 16, :] = own
            obs_ref[:, pad + 16 :, :] = jnp.zeros((boxes, pad, width), BF16)

    out_ref[...] = jnp.zeros(out_ref.shape, F32)
    t1_ref[...] = jnp.zeros(t1_ref.shape, BF16)

    def decode(chunk, g):
        code = pairs_ref[0, chunk * TILES + g]
        i = code >> box_shift
        s = (code >> source_shift) & ((1 << (box_shift - source_shift)) - 1)
        return i, s, code & ((1 << source_shift) - 1)

    def distances(chunk, u_ref):
        for g in range(TILES):
            i, s, _ = decode(chunk, g)
            skip = pl.multiple_of((group - 1 - (s & (group - 1))) * 16, 16)
            u_ref[g] = nn_dot(src_ref[s >> 3], obs_ref[i, pl.ds(skip, 128), :])

    def tiles(u_ref, t_ref):
        for g in range(TILES):
            v = jnp.maximum(u_ref[g], 1e-12)
            q = v * lax.rsqrt(v)
            t = q - ((q + ROUNDER) - ROUNDER)
            z = t * t
            p = (((z + C3) * z + C2) * z + C1) * z + C0
            cosine = p * p - 0.5 / (LEAD * LEAD)
            t_ref[g] = (cosine * pl.reciprocal(q + OFFSET * TURN, approx=True)).astype(BF16)

    def products(chunk, t_ref):
        for g in range(TILES):
            i, s, count = decode(chunk, g)
            got = nn_dot(win_ref[s], t_ref[g])
            out_ref[i] += count.astype(F32) * got[:waves]

    total = pairs_ref[0, pairs_ref.shape[1] - 1]
    rounds = (total + (2 * TILES - 1)) // (2 * TILES)
    distances(0, u0_ref)

    def body(k, carry):
        distances(2 * k + 1, u1_ref)
        tiles(u0_ref, t0_ref)
        products(jnp.maximum(2 * k - 1, 0), t1_ref)
        distances(2 * k + 2, u0_ref)
        tiles(u1_ref, t1_ref)
        products(2 * k, t0_ref)
        return carry

    lax.fori_loop(0, rounds, body, 0)
    products(jnp.maximum(2 * rounds - 1, 0), t1_ref)
    factor = TURN / math.sqrt(entries * width) * 2.0 * LEAD * LEAD
    out_ref[...] = out_ref[...] * factor


def incoming_kernel(
    src_hbm, id_hbm, count_hbm, spectra_hbm, table_hbm, rad_hbm, cos_ref, sin_ref, imat_ref, near_ref, out_ref, src_ref,
    id_ref, count_ref, window_ref, table_ref, rad_ref, down_re_ref, down_im_ref, sems
):
    group = src_hbm.shape[0]
    window, rows, parent_dirs = window_ref.shape
    waves = rows // 2
    parents = near_ref.shape[0] // 8
    row0 = lax.axis_index("dir") * parents
    base = jnp.clip((lax.axis_index("box") - 1) * group, 0, spectra_hbm.shape[0] - window)
    fetch(
        (
            (src_hbm, src_ref),
            (id_hbm, id_ref),
            (count_hbm, count_ref),
            (spectra_hbm.at[pl.ds(base, window)], window_ref),
            (table_hbm, table_ref),
            (rad_hbm, rad_ref),
        ),
        sems,
    )
    cos_phase = cos_ref[...]
    sin_phase = sin_ref[...]
    for q in range(parents):
        row = row0 + q
        total = count_ref[row]
        re = jnp.zeros((waves, parent_dirs), F32)
        im = jnp.zeros((waves, parent_dirs), F32)
        for e in range(src_ref.shape[1]):
            spectrum = window_ref[jnp.clip(src_ref[row, e] - base, 0, window - 1)].astype(F32)
            coeff = table_ref[id_ref[row, e]] * (e < total).astype(F32)
            sre, sim = spectrum[:waves], spectrum[waves:]
            cre, cim = coeff[0:1], coeff[1:2]
            re = re + (cre * sre - cim * sim)
            im = im + (cre * sim + cim * sre)
        re = re.astype(BF16).astype(F32)
        im = im.astype(BF16).astype(F32)
        for c in range(8):
            at = (q * 8 + c) * waves
            cos, sin = cos_phase[c : c + 1], sin_phase[c : c + 1]
            down_re_ref[at : at + waves] = cos * re + sin * im
            down_im_ref[at : at + waves] = cos * im - sin * re
    imat = imat_ref[...]
    in_re = nt_dot(down_re_ref[...].astype(BF16), imat)
    in_im = nt_dot(down_im_ref[...].astype(BF16), imat)
    incoming = jnp.concatenate([in_re, in_im], axis=1).astype(BF16)
    far = nt_dot(incoming, rad_ref[...])
    out_ref[...] = near_ref[...] + far.reshape(near_ref.shape)


def per_device(
    currents, positions, radiation, interp_index, interp_weight, child_phase, near_src, trans_src, trans_id,
    trans_count, trans_table
):
    boxes, waves, width = currents.shape
    entries = near_src.shape[1]
    leaf_dirs = radiation.shape[1] // 2
    parent_dirs = child_phase.shape[1]
    parents = boxes // 8
    vmem = pl.BlockSpec(memory_space=pltpu.VMEM)
    smem = pl.BlockSpec(memory_space=pltpu.SMEM)
    hbm = pl.BlockSpec(memory_space=pltpu.HBM)

    length = round_up(boxes * entries + 3 * TILES + 1, 128)
    operands = (
        currents,
        positions.transpose(1, 0, 2),
        radiation,
        interp_index.T,
        interp_weight.T,
        child_phase,
        near_src,
    )
    packet, parent, imat, cos_phase, sin_phase, pairs = pl.pallas_call(
        outgoing_kernel,
        out_shape=(
            jax.ShapeDtypeStruct((boxes, 16, width), BF16),
            jax.ShapeDtypeStruct((parents, 2 * waves, parent_dirs), BF16),
            jax.ShapeDtypeStruct((leaf_dirs, parent_dirs), BF16),
            jax.ShapeDtypeStruct((8, parent_dirs), F32),
            jax.ShapeDtypeStruct((8, parent_dirs), F32),
            jax.ShapeDtypeStruct((1, length), jnp.int32),
        ),
        in_specs=[hbm] * len(operands),
        out_specs=(vmem, hbm, vmem, vmem, vmem, vmem),
        scratch_shapes=[pltpu.VMEM(x.shape, x.dtype) for x in operands]
        + [pltpu.VMEM((parents, 2 * waves, parent_dirs), BF16), pltpu.SemaphoreType.DMA((len(operands),))],
        compiler_params=pltpu.CompilerParams(vmem_limit_bytes=32 * 1024 * 1024),
        name="outgoing",
    )(*operands)

    before, after = neighbours(packet, ("box", "dir"))
    spectra = lax.all_gather(parent, ("box", "dir"), axis=0, tiled=True)

    near = pl.pallas_call(
        functools.partial(near_kernel, entries),
        out_shape=jax.ShapeDtypeStruct((boxes, waves, width), F32),
        in_specs=[smem, vmem, vmem, vmem],
        out_specs=vmem,
        scratch_shapes=[
            pltpu.VMEM((3 * boxes, 16, width), BF16),
            pltpu.VMEM((3 * boxes // 8, width, 128), BF16),
            pltpu.VMEM((boxes, 2 * (128 - 16) + 16, width), BF16),
            pltpu.VMEM((TILES, width, width), F32),
            pltpu.VMEM((TILES, width, width), F32),
            pltpu.VMEM((TILES, width, width), BF16),
            pltpu.VMEM((TILES, width, width), BF16),
        ],
        compiler_params=pltpu.CompilerParams(vmem_limit_bytes=32 * 1024 * 1024),
        name="near_field",
    )(pairs, before, packet, after)

    group = trans_src.shape[0]
    return pl.pallas_call(
        incoming_kernel,
        out_shape=jax.ShapeDtypeStruct((boxes, waves, width), F32),
        in_specs=[hbm] * 6 + [vmem] * 4,
        out_specs=vmem,
        scratch_shapes=[
            pltpu.SMEM(trans_src.shape, jnp.int32),
            pltpu.SMEM(trans_id.shape, jnp.int32),
            pltpu.SMEM(trans_count.shape, jnp.int32),
            pltpu.VMEM((3 * group, 2 * waves, parent_dirs), BF16),
            pltpu.VMEM(trans_table.shape, F32),
            pltpu.VMEM(radiation.shape, BF16),
            pltpu.VMEM((boxes * waves, parent_dirs), F32),
            pltpu.VMEM((boxes * waves, parent_dirs), F32),
            pltpu.SemaphoreType.DMA((6,)),
        ],
        compiler_params=pltpu.CompilerParams(vmem_limit_bytes=32 * 1024 * 1024),
        name="incoming",
    )(trans_src, trans_id, trans_count, spectra, trans_table, radiation, cos_phase, sin_phase, imat, near)


def solution(mesh):
    placed = (
        P(("box", "dir"), None, None),
        P(("box", "dir"), None, None),
        P(),
        P(),
        P(),
        P(),
        P(("box", "dir"), None),
        P("box", None),
        P("box", None),
        P("box"),
        P(),
    )
    return jax.shard_map(
        per_device,
        mesh=mesh,
        in_specs=placed,
        out_specs=P(("box", "dir"), None, None),
        check_vma=False,
    )
```

```python
import functools
import math

import jax
import jax.numpy as jnp
from jax import lax
from jax.experimental import pallas as pl
from jax.experimental.pallas import tpu as pltpu
from jax.sharding import PartitionSpec as P

F32 = jnp.float32
BF16 = jnp.bfloat16

WAVENUMBER = 4.0
OFFSET = 0.5
TURN = WAVENUMBER / (2.0 * math.pi)
C0, C1, C2, C3 = (4.551727469085273, -22.461833254303432, 18.47278585020764, -6.062355797782118)
LEAD = 0.21969679868984615
ROUNDER = 12582912.0
TILES = 8


def round_up(value, step):
    return -(-value // step) * step


def neighbours(x, axis):
    size = lax.axis_size(axis)
    up = [(i, i + 1) for i in range(size - 1)]
    down = [(j, i) for i, j in up]
    return lax.ppermute(x, axis, up), lax.ppermute(x, axis, down)


def split3(x):
    high = x.astype(BF16).astype(F32)
    rest = x - high
    mid = rest.astype(BF16).astype(F32)
    return high, mid, rest - mid


def nt_dot(a, b):
    return lax.dot_general(a, b, (((1,), (1,)), ((), ())), preferred_element_type=F32)


def nn_dot(a, b):
    return jnp.dot(a, b, preferred_element_type=F32)


def code_bits(boxes, entries):
    count_bits = entries.bit_length()
    source_bits = (3 * boxes - 1).bit_length()
    return source_bits + count_bits, count_bits


def build_pairs(near_src, base, length):
    boxes, entries = near_src.shape
    box_shift, source_shift = code_bits(boxes, entries)
    lanes = round_up(3 * boxes, 128)
    local = near_src - base
    local = jnp.where(local < 0, local + 3 * boxes, local)
    lane = lax.broadcasted_iota(jnp.int32, (boxes, lanes), 1)
    count = jnp.zeros((boxes, lanes), jnp.int32)
    for e in range(entries):
        count = count + (local[:, e : e + 1] == lane).astype(jnp.int32)
    row = lax.broadcasted_iota(jnp.int32, (lanes, lanes), 0)
    col = lax.broadcasted_iota(jnp.int32, (lanes, lanes), 1)
    ahead = (row < col).astype(F32).astype(BF16)
    box_row = lax.broadcasted_iota(jnp.int32, (boxes, boxes), 0)
    box_col = lax.broadcasted_iota(jnp.int32, (boxes, boxes), 1)
    above = (box_col < box_row).astype(F32).astype(BF16)

    def places(flags):
        rank = nn_dot(flags.astype(BF16), ahead)
        totals = jnp.sum(flags, axis=1, keepdims=True)
        offset = nn_dot(above, jnp.broadcast_to(totals, (boxes, lanes)).astype(BF16))
        return rank + offset, jnp.sum(totals, axis=0, keepdims=True)

    own = (count > 0) & (lane < boxes)
    other = (count > 0) & (lane >= boxes)
    own_place, own_total = places(own.astype(F32))
    other_place, other_total = places(other.astype(F32))
    place = jnp.where(own, own_place, jnp.where(other, float(length - 3) - other_place, -1.0))
    box = lax.broadcasted_iota(jnp.int32, (boxes, lanes), 0)
    code = ((box << box_shift) | (lane << source_shift) | count).astype(F32)
    place_t = place.T
    code_t = code.T
    rows = 3 * boxes
    slot = lax.broadcasted_iota(jnp.int32, (rows, length), 1).astype(F32)
    found = jnp.zeros((rows, length), F32)
    for i in range(boxes):
        hit = place_t[:rows, i : i + 1] == slot
        found = found + jnp.where(hit, code_t[:rows, i : i + 1], 0.0)
    pairs = jnp.sum(found, axis=0, keepdims=True)
    at = lax.broadcasted_iota(jnp.int32, (1, length), 1)
    pairs = jnp.where(at == length - 2, own_total, jnp.where(at == length - 1, other_total, pairs))
    return pairs.astype(jnp.int32)


def start_all(copies, sems):
    started = [pltpu.make_async_copy(src, dst, sems.at[k]) for k, (src, dst) in enumerate(copies)]
    for copy in started:
        copy.start()
    return started


def wait_all(started):
    for copy in started:
        copy.wait()


def outgoing_kernel(
    x_hbm, pos_hbm, rad_hbm, idx_hbm, wgt_hbm, phase_hbm, packet_ref, spectra_ref, imat_ref, cos_ref, sin_ref, rad_ref,
    x_ref, pos_ref, idx_ref, wgt_ref, phase_ref, sems
):
    wait_all(
        start_all(
            (
                (x_hbm, x_ref),
                (pos_hbm, pos_ref),
                (rad_hbm, rad_ref),
                (idx_hbm, idx_ref),
                (wgt_hbm, wgt_ref),
                (phase_hbm, phase_ref),
            ),
            sems,
        )
    )
    leaf_dirs, parent_dirs = imat_ref.shape
    boxes, waves, width = x_ref.shape
    chunks = parent_dirs // 128
    x = x_ref[...].astype(F32)
    planes = pos_ref[...].astype(F32)
    at = lax.broadcasted_iota(jnp.int32, (boxes, 16 - waves, width), 1)
    pos = jnp.zeros((boxes, 16 - waves, width), F32)
    for axis in range(3):
        pos = jnp.where(at == axis, planes[axis][:, None, :], pos)
    packet_ref[:boxes] = jnp.concatenate([x, pos], axis=1).astype(BF16)
    column = lax.broadcasted_iota(jnp.int32, (leaf_dirs, parent_dirs), 0)
    imat = jnp.zeros((leaf_dirs, parent_dirs), F32)
    for s in range(idx_ref.shape[0]):
        imat = imat + jnp.where(idx_ref[s : s + 1, :] == column, wgt_ref[s : s + 1, :], 0.0)
    imat = imat.astype(BF16)
    imat_ref[...] = imat
    cos_phase = jnp.cos(phase_ref[...])
    sin_phase = jnp.sin(phase_ref[...])
    cos_ref[...] = cos_phase
    sin_ref[...] = sin_phase
    leaf = nn_dot(x.reshape(boxes * waves, width).astype(BF16), rad_ref[...]).astype(BF16)
    up_re = nn_dot(leaf[:, :leaf_dirs], imat)
    up_im = nn_dot(leaf[:, leaf_dirs:], imat)
    for q in range(boxes // 8):
        re = jnp.zeros((waves, parent_dirs), F32)
        im = jnp.zeros((waves, parent_dirs), F32)
        for c in range(8):
            at = (q * 8 + c) * waves
            ure = up_re[at : at + waves]
            uim = up_im[at : at + waves]
            re = re + (cos_phase[c : c + 1] * ure - sin_phase[c : c + 1] * uim)
            im = im + (sin_phase[c : c + 1] * ure + cos_phase[c : c + 1] * uim)
        both = jnp.concatenate([re, im], axis=0).astype(BF16)
        for k in range(chunks):
            part = both[:, k * 128 : (k + 1) * 128]
            packet_ref[boxes + q * chunks + k] = part
            spectra_ref[q * chunks + k] = part


def group_kernel(own_ref, before_ref, after_ref, *refs):
    *turned_refs, _, group_ref = refs
    size = lax.axis_size("dir")
    rows = own_ref.shape[0]
    boxes = before_ref.shape[0] - rows
    here = lax.axis_index("dir")

    def place(which, value):
        group_ref[pl.ds(lax.rem(which + size, size) * rows, rows)] = value

    place(here - 1, before_ref[boxes:])
    place(here + 1, after_ref[boxes:])
    for turn, ref in zip(range(2, size - 1), turned_refs):
        place(here - turn, ref[...])
    if size > 2:

        @pl.when((here == 0) | (here == size - 1))
        def _():
            place(size - 1 - here, turned_refs[-1][...])

    place(here, own_ref[...])


def features(pos):
    scale = TURN * TURN
    norm = split3(scale * jnp.sum(pos * pos, axis=1, keepdims=True))
    at = lax.broadcasted_iota(jnp.int32, pos.shape, 1)
    first = jnp.where(at < 3, pos, 1.0)
    first = jnp.where(at == 3, norm[0], jnp.where(at == 4, norm[1], jnp.where(at == 5, norm[2], first)))
    second = jnp.where(at == 3, 1.0, pos + pltpu.roll(pos, 4, 1))
    source = jnp.concatenate([first, second], axis=1).astype(BF16)
    cross = split3((-2.0 * scale) * pos)
    first = jnp.where(at < 3, cross[0], 1.0)
    first = jnp.where(at == 6, norm[0], jnp.where(at == 7, norm[1], first))
    second = jnp.where(at == 3, norm[2], cross[1] + pltpu.roll(cross[2], 4, 1))
    return source, jnp.concatenate([first, second], axis=1).astype(BF16)


def turn_sources(source, src_ref, start):
    boxes, rows, width = source.shape
    eye = lax.broadcasted_iota(jnp.int32, (width, width), 0) == lax.broadcasted_iota(jnp.int32, (width, width), 1)
    turned = nt_dot(eye.astype(F32).astype(BF16), source.reshape(boxes * rows, width)).astype(BF16)
    for j in range(boxes * rows // 128):
        src_ref[start + j] = turned[:, j * 128 : (j + 1) * 128]


def near_sum(entries, total, pair_at, src_ref, win_ref, obs_ref, out_ref, scratch):
    u0_ref, u1_ref, t0_ref, t1_ref = scratch
    boxes, waves, width = out_ref.shape
    per_row = 128 // 16
    box_shift, source_shift = code_bits(boxes, entries)
    t1_ref[...] = jnp.zeros(t1_ref.shape, BF16)

    def decode(chunk, g):
        code = pair_at(chunk * TILES + g)
        i = code >> box_shift
        s = (code >> source_shift) & ((1 << (box_shift - source_shift)) - 1)
        return i, s, code & ((1 << source_shift) - 1)

    def distances(chunk, u_ref):
        for g in range(TILES):
            i, s, _ = decode(chunk, g)
            skip = pl.multiple_of((per_row - 1 - (s & (per_row - 1))) * 16, 16)
            u_ref[g] = nn_dot(src_ref[s >> 3], obs_ref[i, pl.ds(skip, 128), :])

    def tiles(u_ref, t_ref):
        for g in range(TILES):
            for at in range(0, width, 32):
                v = jnp.maximum(u_ref[g, at : at + 32], 1e-12)
                q = v * lax.rsqrt(v)
                t = q - ((q + ROUNDER) - ROUNDER)
                z = t * t
                p = (((z + C3) * z + C2) * z + C1) * z + C0
                cosine = p * p - 0.5 / (LEAD * LEAD)
                t_ref[g, at : at + 32] = (cosine * pl.reciprocal(q + OFFSET * TURN, approx=True)).astype(BF16)

    def products(chunk, t_ref):
        for g in range(TILES):
            i, s, count = decode(chunk, g)
            got = nn_dot(win_ref[s], t_ref[g])
            out_ref[i] += count.astype(F32) * got[:waves]

    rounds = (total + (2 * TILES - 1)) // (2 * TILES)
    distances(0, u0_ref)

    def body(k, carry):
        distances(2 * k + 1, u1_ref)
        tiles(u0_ref, t0_ref)
        products(jnp.maximum(2 * k - 1, 0), t1_ref)
        distances(2 * k + 2, u0_ref)
        tiles(u1_ref, t1_ref)
        products(2 * k, t0_ref)
        return carry

    lax.fori_loop(0, rounds, body, 0)
    products(jnp.maximum(2 * rounds - 1, 0), t1_ref)


def own_near_kernel(
    own_ref, near_hbm, src_hbm, id_hbm, count_hbm, table_hbm, out_ref, pairs_ref, obs_ref, gain_ref, near_ref, list_ref,
    trans_src_ref, trans_id_ref, trans_count_ref, rows_ref, src_ref, *scratch
):
    *scratch, sems = scratch
    boxes, waves, width = out_ref.shape
    entries = near_ref.shape[1]
    length = pairs_ref.shape[1]
    parents, window = gain_ref.shape[:2]
    listed = src_hbm.shape[1]
    near_copy, *list_copies = start_all(
        (
            (near_hbm, near_ref),
            (src_hbm, trans_src_ref),
            (id_hbm, trans_id_ref),
            (count_hbm, trans_count_ref),
        ),
        sems,
    )
    out_ref[...] = jnp.zeros(out_ref.shape, F32)
    gain_ref[...] = jnp.zeros(gain_ref.shape, F32)
    source, observer = features(own_ref[:boxes].astype(F32)[:, 8:16, :])
    turn_sources(source, src_ref, 0)
    pad = 128 - 16
    obs_ref[:, :pad, :] = jnp.zeros((boxes, pad, width), BF16)
    obs_ref[:, pad : pad + 16, :] = observer
    obs_ref[:, pad + 16 :, :] = jnp.zeros((boxes, pad, width), BF16)
    near_copy.wait()
    base = lax.axis_index(("box", "dir")) * boxes
    pairs_ref[...] = build_pairs(near_ref[...], base, length)
    send_list = pltpu.make_async_copy(pairs_ref, list_ref, sems.at[0])
    send_list.start()
    wait_all(list_copies)
    row0 = lax.axis_index("dir") * parents
    for q in range(parents):
        for e in range(listed):
            pltpu.make_async_copy(
                table_hbm.at[trans_id_ref[row0 + q, e]], rows_ref.at[q * listed + e], sems.at[1]
            ).start()
    send_list.wait()
    near_sum(entries, list_ref[0, length - 2], lambda k: list_ref[0, k], src_ref, own_ref, obs_ref, out_ref, scratch)
    pltpu.make_async_copy(rows_ref, rows_ref, sems.at[1]).wait()
    first = (lax.axis_index("box") - 1) * (window // 3)
    for q in range(parents):
        for e in range(listed):
            live = (e < trans_count_ref[row0 + q]).astype(F32)
            s = jnp.clip(trans_src_ref[row0 + q, e] - first, 0, window - 1)
            gain_ref[q, s] += rows_ref[q * listed + e] * live


def rest_near_kernel(
    entries, pairs_ref, own_ref, before_ref, after_ref, obs_ref, sum_ref, out_ref, win_ref, src_ref, *scratch
):
    boxes, waves, width = out_ref.shape
    length = pairs_ref.shape[1]
    for part, ref in ((2, before_ref), (1, after_ref)):
        win_ref[part * boxes : (part + 1) * boxes] = ref[:boxes]
        source, _ = features(ref[:boxes].astype(F32)[:, 8:16, :])
        turn_sources(source, src_ref, part * (boxes * 16 // 128))
    win_ref[0] = own_ref[0]
    src_ref[0] = jnp.zeros(src_ref.shape[1:], BF16)
    out_ref[...] = sum_ref[...]
    near_sum(
        entries,
        pairs_ref[0, length - 1],
        lambda k: pairs_ref[0, length - 3 - k],
        src_ref,
        win_ref,
        obs_ref,
        out_ref,
        scratch,
    )


def incoming_kernel(
    entries, before_ref, own_ref, after_ref, gain_ref, cos_ref, sin_ref, imat_ref, rad_ref, near_ref, out_ref, down_re_ref,
    down_im_ref
):
    parents, window, _, parent_dirs = gain_ref.shape
    boxes, waves, width = near_ref.shape
    chunks = parent_dirs // 128
    group = window // 3
    cos_phase = cos_ref[...]
    sin_phase = sin_ref[...]
    sums = tuple(jnp.zeros((waves, 128), F32) for _ in range(parents * chunks * 2))
    for part, ref in enumerate((before_ref, own_ref, after_ref)):

        def add_source(s, sums, part=part, ref=ref):
            sums = list(sums)
            gains = [gain_ref[q, part * group + s] for q in range(parents)]
            for k in range(chunks):
                spectrum = ref[s * chunks + k].astype(F32)
                sre, sim = spectrum[:waves], spectrum[waves:]
                for q in range(parents):
                    gre = gains[q][0:1, k * 128 : (k + 1) * 128]
                    gim = gains[q][1:2, k * 128 : (k + 1) * 128]
                    at = (q * chunks + k) * 2
                    sums[at] = sums[at] + (gre * sre - gim * sim)
                    sums[at + 1] = sums[at + 1] + (gre * sim + gim * sre)
            return tuple(sums)

        sums = lax.fori_loop(0, group, add_source, sums, unroll=8)
    for q in range(parents):
        for k in range(chunks):
            at = (q * chunks + k) * 2
            re = sums[at].astype(BF16).astype(F32)
            im = sums[at + 1].astype(BF16).astype(F32)
            lanes = slice(k * 128, (k + 1) * 128)
            for c in range(8):
                cos, sin = cos_phase[c : c + 1, lanes], sin_phase[c : c + 1, lanes]
                rows = slice((q * 8 + c) * waves, (q * 8 + c + 1) * waves)
                down_re_ref[rows, lanes] = cos * re + sin * im
                down_im_ref[rows, lanes] = cos * im - sin * re
    imat = imat_ref[...]
    in_re = nt_dot(down_re_ref[...].astype(BF16), imat)
    in_im = nt_dot(down_im_ref[...].astype(BF16), imat)
    incoming = jnp.concatenate([in_re, in_im], axis=1).astype(BF16)
    far = nt_dot(incoming, rad_ref[...])
    factor = TURN / math.sqrt(entries * width) * 2.0 * LEAD * LEAD
    out_ref[...] = near_ref[...] * factor + far.reshape(near_ref.shape)


def per_device(
    currents, positions, radiation, interp_index, interp_weight, child_phase, near_src, trans_src, trans_id,
    trans_count, trans_table
):
    boxes, waves, width = currents.shape
    entries = near_src.shape[1]
    leaf_dirs = radiation.shape[1] // 2
    parent_dirs = child_phase.shape[1]
    parents = boxes // 8
    spectra_rows = parents * parent_dirs // 128
    size = lax.axis_size("dir")
    vmem = pl.BlockSpec(memory_space=pltpu.VMEM)
    smem = pl.BlockSpec(memory_space=pltpu.SMEM)
    hbm = pl.BlockSpec(memory_space=pltpu.HBM)
    params = pltpu.CompilerParams(vmem_limit_bytes=32 * 1024 * 1024)

    def in_hbm(x):
        return pltpu.with_memory_space_constraint(x, pltpu.HBM)

    def shaped(shape, dtype):
        return jax.ShapeDtypeStruct(shape, dtype)

    operands = (currents, positions.transpose(1, 0, 2), radiation, interp_index.T, interp_weight.T, child_phase)
    packet, spectra, imat, cos_phase, sin_phase, rad = pl.pallas_call(
        outgoing_kernel,
        out_shape=(
            shaped((boxes + spectra_rows, 16, width), BF16),
            shaped((spectra_rows, 2 * waves, 128), BF16),
            shaped((leaf_dirs, parent_dirs), BF16),
            shaped((8, parent_dirs), F32),
            shaped((8, parent_dirs), F32),
            shaped(radiation.shape, BF16),
        ),
        in_specs=[hbm] * len(operands),
        out_specs=(vmem,) * 6,
        scratch_shapes=[pltpu.VMEM(x.shape, x.dtype) for x in operands if x is not radiation]
        + [pltpu.SemaphoreType.DMA((len(operands),))],
        compiler_params=params,
        name="outgoing",
    )(*[in_hbm(x) for x in operands])

    before, after = neighbours(packet, ("box", "dir"))
    turned = [
        lax.ppermute(spectra, "dir", [(i, (i + turn) % size) for i in range(size)]) for turn in range(2, size - 1)
    ]
    if size > 2:
        turned.append(lax.ppermute(spectra, "dir", [(0, size - 1), (size - 1, 0)]))

    length = round_up(boxes * entries + 6 * TILES + 2, 128)
    window = 3 * trans_src.shape[0]
    near_scratch = [
        pltpu.VMEM((TILES, width, width), F32),
        pltpu.VMEM((TILES, width, width), F32),
        pltpu.VMEM((TILES, width, width), BF16),
        pltpu.VMEM((TILES, width, width), BF16),
    ]
    own_sum, pairs, observers, gains = pl.pallas_call(
        own_near_kernel,
        out_shape=(
            shaped((boxes, waves, width), F32),
            shaped((1, length), jnp.int32),
            shaped((boxes, 2 * (128 - 16) + 16, width), BF16),
            shaped((parents, window, 2, parent_dirs), F32),
        ),
        in_specs=[vmem] + [hbm] * 5,
        out_specs=(vmem,) * 4,
        scratch_shapes=[
            pltpu.VMEM(near_src.shape, jnp.int32),
            pltpu.SMEM((1, length), jnp.int32),
            pltpu.SMEM(trans_src.shape, jnp.int32),
            pltpu.SMEM(trans_id.shape, jnp.int32),
            pltpu.SMEM(trans_count.shape, jnp.int32),
            pltpu.VMEM((parents * trans_src.shape[1], 2, parent_dirs), F32),
            pltpu.VMEM((boxes * 16 // 128, width, 128), BF16),
        ]
        + near_scratch
        + [pltpu.SemaphoreType.DMA((4,))],
        compiler_params=params,
        name="own_near",
    )(packet, *[in_hbm(x) for x in (near_src, trans_src, trans_id, trans_count, trans_table)])

    group = pl.pallas_call(
        group_kernel,
        out_shape=shaped((size * spectra_rows, 2 * waves, 128), BF16),
        in_specs=[vmem] * (4 + len(turned)),
        out_specs=vmem,
        compiler_params=params,
        name="group",
    )(spectra, before, after, *turned, pairs)
    group_before, group_after = neighbours(group, "box")

    near = pl.pallas_call(
        functools.partial(rest_near_kernel, entries),
        out_shape=shaped((boxes, waves, width), F32),
        in_specs=[smem] + [vmem] * 5,
        out_specs=vmem,
        scratch_shapes=[
            pltpu.VMEM((3 * boxes, 16, width), BF16),
            pltpu.VMEM((3 * boxes * 16 // 128, width, 128), BF16),
        ]
        + near_scratch,
        compiler_params=params,
        name="rest_near",
    )(pairs, packet, before, after, observers, own_sum)

    return pl.pallas_call(
        functools.partial(incoming_kernel, entries),
        out_shape=shaped((boxes, waves, width), F32),
        in_specs=[vmem] * 9,
        out_specs=vmem,
        scratch_shapes=[
            pltpu.VMEM((boxes * waves, parent_dirs), F32),
            pltpu.VMEM((boxes * waves, parent_dirs), F32),
        ],
        compiler_params=params,
        name="incoming",
    )(group_before, group, group_after, gains, cos_phase, sin_phase, imat, rad, near)


def solution(mesh):
    placed = (
        P(("box", "dir"), None, None),
        P(("box", "dir"), None, None),
        P(),
        P(),
        P(),
        P(),
        P(("box", "dir"), None),
        P("box", None),
        P("box", None),
        P("box"),
        P(),
    )
    return jax.shard_map(
        per_device,
        mesh=mesh,
        in_specs=placed,
        out_specs=P(("box", "dir"), None, None),
        check_vma=False,
    )
```

```python
import functools
import math

import jax
import jax.numpy as jnp
from jax import lax
from jax.experimental import pallas as pl
from jax.experimental.pallas import tpu as pltpu
from jax.sharding import PartitionSpec as P

F32 = jnp.float32
BF16 = jnp.bfloat16

WAVENUMBER = 4.0
OFFSET = 0.5
TURN = WAVENUMBER / (2.0 * math.pi)
C0, C1, C2, C3 = (4.551727469085273, -22.461833254303432, 18.47278585020764, -6.062355797782118)
LEAD = 0.21969679868984615
ROUNDER = 12582912.0
TILES = 8


def round_up(value, step):
    return -(-value // step) * step


def neighbours(x, axis):
    size = lax.axis_size(axis)
    up = [(i, i + 1) for i in range(size - 1)]
    down = [(j, i) for i, j in up]
    return lax.ppermute(x, axis, up), lax.ppermute(x, axis, down)


def split3(x):
    high = x.astype(BF16).astype(F32)
    rest = x - high
    mid = rest.astype(BF16).astype(F32)
    return high, mid, rest - mid


def nt_dot(a, b):
    return lax.dot_general(a, b, (((1,), (1,)), ((), ())), preferred_element_type=F32)


def nn_dot(a, b):
    return jnp.dot(a, b, preferred_element_type=F32)


def code_bits(boxes, entries):
    count_bits = entries.bit_length()
    source_bits = (3 * boxes - 1).bit_length()
    return source_bits + count_bits, count_bits


def build_pairs(near_src, base, length):
    boxes, entries = near_src.shape
    box_shift, source_shift = code_bits(boxes, entries)
    lanes = round_up(3 * boxes, 128)
    local = near_src - base
    local = jnp.where(local < 0, local + 3 * boxes, local)
    lane = lax.broadcasted_iota(jnp.int32, (boxes, lanes), 1)
    count = jnp.zeros((boxes, lanes), jnp.int32)
    for e in range(entries):
        count = count + (local[:, e : e + 1] == lane).astype(jnp.int32)
    row = lax.broadcasted_iota(jnp.int32, (lanes, lanes), 0)
    col = lax.broadcasted_iota(jnp.int32, (lanes, lanes), 1)
    ahead = (row < col).astype(F32).astype(BF16)
    box_row = lax.broadcasted_iota(jnp.int32, (boxes, boxes), 0)
    box_col = lax.broadcasted_iota(jnp.int32, (boxes, boxes), 1)
    above = (box_col < box_row).astype(F32).astype(BF16)

    def places(flags):
        rank = nn_dot(flags.astype(BF16), ahead)
        totals = jnp.sum(flags, axis=1, keepdims=True)
        offset = nn_dot(above, jnp.broadcast_to(totals, (boxes, lanes)).astype(BF16))
        return rank + offset, jnp.sum(totals, axis=0, keepdims=True)

    own = (count > 0) & (lane < boxes)
    other = (count > 0) & (lane >= boxes)
    own_place, own_total = places(own.astype(F32))
    other_place, other_total = places(other.astype(F32))
    place = jnp.where(own, own_place, jnp.where(other, float(length - 3) - other_place, -1.0))
    box = lax.broadcasted_iota(jnp.int32, (boxes, lanes), 0)
    code = ((box << box_shift) | (lane << source_shift) | count).astype(F32)
    place_t = place.T
    code_t = code.T
    rows = 3 * boxes
    slot = lax.broadcasted_iota(jnp.int32, (rows, length), 1).astype(F32)
    found = jnp.zeros((rows, length), F32)
    for i in range(boxes):
        hit = place_t[:rows, i : i + 1] == slot
        found = found + jnp.where(hit, code_t[:rows, i : i + 1], 0.0)
    pairs = jnp.sum(found, axis=0, keepdims=True)
    at = lax.broadcasted_iota(jnp.int32, (1, length), 1)
    pairs = jnp.where(at == length - 2, own_total, jnp.where(at == length - 1, other_total, pairs))
    return pairs.astype(jnp.int32)


def start_all(copies, sems):
    started = [pltpu.make_async_copy(src, dst, sems.at[k]) for k, (src, dst) in enumerate(copies)]
    for copy in started:
        copy.start()
    return started


def wait_all(started):
    for copy in started:
        copy.wait()


def outgoing_kernel(
    x_hbm, pos_hbm, rad_hbm, idx_hbm, wgt_hbm, phase_hbm, packet_ref, spectra_ref, imat_ref, cos_ref, sin_ref, rad_ref,
    x_ref, pos_ref, idx_ref, wgt_ref, phase_ref, sems
):
    wait_all(
        start_all(
            (
                (x_hbm, x_ref),
                (pos_hbm, pos_ref),
                (rad_hbm, rad_ref),
                (idx_hbm, idx_ref),
                (wgt_hbm, wgt_ref),
                (phase_hbm, phase_ref),
            ),
            sems,
        )
    )
    leaf_dirs, parent_dirs = imat_ref.shape
    boxes, waves, width = x_ref.shape
    chunks = parent_dirs // 128
    x = x_ref[...].astype(F32)
    planes = pos_ref[...].astype(F32)
    at = lax.broadcasted_iota(jnp.int32, (boxes, 16 - waves, width), 1)
    pos = jnp.zeros((boxes, 16 - waves, width), F32)
    for axis in range(3):
        pos = jnp.where(at == axis, planes[axis][:, None, :], pos)
    packet_ref[:boxes] = jnp.concatenate([x, pos], axis=1).astype(BF16)
    column = lax.broadcasted_iota(jnp.int32, (leaf_dirs, parent_dirs), 0)
    imat = jnp.zeros((leaf_dirs, parent_dirs), F32)
    for s in range(idx_ref.shape[0]):
        imat = imat + jnp.where(idx_ref[s : s + 1, :] == column, wgt_ref[s : s + 1, :], 0.0)
    imat = imat.astype(BF16)
    imat_ref[...] = imat
    cos_phase = jnp.cos(phase_ref[...])
    sin_phase = jnp.sin(phase_ref[...])
    cos_ref[...] = cos_phase
    sin_ref[...] = sin_phase
    leaf = nn_dot(x.reshape(boxes * waves, width).astype(BF16), rad_ref[...]).astype(BF16)
    up_re = nn_dot(leaf[:, :leaf_dirs], imat)
    up_im = nn_dot(leaf[:, leaf_dirs:], imat)
    for q in range(boxes // 8):
        re = jnp.zeros((waves, parent_dirs), F32)
        im = jnp.zeros((waves, parent_dirs), F32)
        for c in range(8):
            at = (q * 8 + c) * waves
            ure = up_re[at : at + waves]
            uim = up_im[at : at + waves]
            re = re + (cos_phase[c : c + 1] * ure - sin_phase[c : c + 1] * uim)
            im = im + (sin_phase[c : c + 1] * ure + cos_phase[c : c + 1] * uim)
        both = jnp.concatenate([re, im], axis=0).astype(BF16)
        for k in range(chunks):
            part = both[:, k * 128 : (k + 1) * 128]
            packet_ref[boxes + q * chunks + k] = part
            spectra_ref[q * chunks + k] = part


def group_kernel(own_ref, before_ref, after_ref, *refs):
    *turned_refs, _, group_ref = refs
    size = lax.axis_size("dir")
    rows = own_ref.shape[0]
    boxes = before_ref.shape[0] - rows
    here = lax.axis_index("dir")

    def place(which, value):
        group_ref[pl.ds(lax.rem(which + size, size) * rows, rows)] = value

    place(here - 1, before_ref[boxes:])
    place(here + 1, after_ref[boxes:])
    for turn, ref in zip(range(2, size - 1), turned_refs):
        place(here - turn, ref[...])
    if size > 2:

        @pl.when((here == 0) | (here == size - 1))
        def _():
            place(size - 1 - here, turned_refs[-1][...])

    place(here, own_ref[...])


def features(pos):
    scale = TURN * TURN
    norm = split3(scale * jnp.sum(pos * pos, axis=1, keepdims=True))
    at = lax.broadcasted_iota(jnp.int32, pos.shape, 1)
    first = jnp.where(at < 3, pos, 1.0)
    first = jnp.where(at == 3, norm[0], jnp.where(at == 4, norm[1], jnp.where(at == 5, norm[2], first)))
    second = jnp.where(at == 3, 1.0, pos + pltpu.roll(pos, 4, 1))
    source = jnp.concatenate([first, second], axis=1).astype(BF16)
    cross = split3((-2.0 * scale) * pos)
    first = jnp.where(at < 3, cross[0], 1.0)
    first = jnp.where(at == 6, norm[0], jnp.where(at == 7, norm[1], first))
    second = jnp.where(at == 3, norm[2], cross[1] + pltpu.roll(cross[2], 4, 1))
    return source, jnp.concatenate([first, second], axis=1).astype(BF16)


def turn_sources(source, src_ref, start):
    boxes, rows, width = source.shape
    eye = lax.broadcasted_iota(jnp.int32, (width, width), 0) == lax.broadcasted_iota(jnp.int32, (width, width), 1)
    turned = nt_dot(eye.astype(F32).astype(BF16), source.reshape(boxes * rows, width)).astype(BF16)
    for j in range(boxes * rows // 128):
        src_ref[start + j] = turned[:, j * 128 : (j + 1) * 128]


def near_sum(entries, total, pair_at, src_ref, win_ref, obs_ref, out_ref, scratch):
    u0_ref, u1_ref, t0_ref, t1_ref = scratch
    boxes, waves, width = out_ref.shape
    per_row = 128 // 16
    box_shift, source_shift = code_bits(boxes, entries)
    t1_ref[...] = jnp.zeros(t1_ref.shape, BF16)

    def decode(chunk, g):
        code = pair_at(chunk * TILES + g)
        i = code >> box_shift
        s = (code >> source_shift) & ((1 << (box_shift - source_shift)) - 1)
        return i, s, code & ((1 << source_shift) - 1)

    def distances(chunk, g, u_ref):
        i, s, _ = decode(chunk, g)
        skip = pl.multiple_of((per_row - 1 - (s & (per_row - 1))) * 16, 16)
        u_ref[g] = nn_dot(src_ref[s >> 3], obs_ref[i, pl.ds(skip, 128), :])

    def tile(g, u_ref, t_ref):
        for at in range(0, width, 32):
            v = jnp.maximum(u_ref[g, at : at + 32], 1e-12)
            q = v * lax.rsqrt(v)
            t = q - ((q + ROUNDER) - ROUNDER)
            z = t * t
            p = (((z + C3) * z + C2) * z + C1) * z + C0
            cosine = p * p - 0.5 / (LEAD * LEAD)
            t_ref[g, at : at + 32] = (cosine * pl.reciprocal(q + OFFSET * TURN, approx=True)).astype(BF16)

    def product(chunk, g, t_ref):
        i, s, count = decode(chunk, g)
        got = nn_dot(win_ref[s], t_ref[g])
        out_ref[i] += count.astype(F32) * got[:waves]

    def stages(chunk, u_ref, next_u_ref, t_ref, last_t_ref):
        for g in range(TILES):
            distances(chunk + 1, g, next_u_ref)
            product(jnp.maximum(chunk - 1, 0), g, last_t_ref)
            tile(g, u_ref, t_ref)

    rounds = (total + (2 * TILES - 1)) // (2 * TILES)
    for g in range(TILES):
        distances(0, g, u0_ref)

    def body(k, carry):
        stages(2 * k, u0_ref, u1_ref, t0_ref, t1_ref)
        stages(2 * k + 1, u1_ref, u0_ref, t1_ref, t0_ref)
        return carry

    lax.fori_loop(0, rounds, body, 0)
    for g in range(TILES):
        product(jnp.maximum(2 * rounds - 1, 0), g, t1_ref)


def own_near_kernel(
    own_ref, near_hbm, src_hbm, id_hbm, count_hbm, table_hbm, out_ref, pairs_ref, obs_ref, gain_ref, near_ref, list_ref,
    trans_src_ref, trans_id_ref, trans_count_ref, rows_ref, src_ref, *scratch
):
    *scratch, sems = scratch
    boxes, waves, width = out_ref.shape
    entries = near_ref.shape[1]
    length = pairs_ref.shape[1]
    parents, window = gain_ref.shape[:2]
    listed = src_hbm.shape[1]
    near_copy, *list_copies = start_all(
        (
            (near_hbm, near_ref),
            (src_hbm, trans_src_ref),
            (id_hbm, trans_id_ref),
            (count_hbm, trans_count_ref),
        ),
        sems,
    )
    out_ref[...] = jnp.zeros(out_ref.shape, F32)
    gain_ref[...] = jnp.zeros(gain_ref.shape, F32)
    source, observer = features(own_ref[:boxes].astype(F32)[:, 8:16, :])
    turn_sources(source, src_ref, 0)
    pad = 128 - 16
    obs_ref[:, :pad, :] = jnp.zeros((boxes, pad, width), BF16)
    obs_ref[:, pad : pad + 16, :] = observer
    obs_ref[:, pad + 16 :, :] = jnp.zeros((boxes, pad, width), BF16)
    near_copy.wait()
    base = lax.axis_index(("box", "dir")) * boxes
    pairs_ref[...] = build_pairs(near_ref[...], base, length)
    send_list = pltpu.make_async_copy(pairs_ref, list_ref, sems.at[0])
    send_list.start()
    wait_all(list_copies)
    row0 = lax.axis_index("dir") * parents
    for q in range(parents):
        for e in range(listed):
            pltpu.make_async_copy(
                table_hbm.at[trans_id_ref[row0 + q, e]], rows_ref.at[q * listed + e], sems.at[1]
            ).start()
    send_list.wait()
    near_sum(entries, list_ref[0, length - 2], lambda k: list_ref[0, k], src_ref, own_ref, obs_ref, out_ref, scratch)
    pltpu.make_async_copy(rows_ref, rows_ref, sems.at[1]).wait()
    first = (lax.axis_index("box") - 1) * (window // 3)
    for q in range(parents):
        for e in range(listed):
            live = (e < trans_count_ref[row0 + q]).astype(F32)
            s = jnp.clip(trans_src_ref[row0 + q, e] - first, 0, window - 1)
            gain_ref[q, s] += rows_ref[q * listed + e] * live


def rest_near_kernel(
    entries, pairs_ref, own_ref, before_ref, after_ref, obs_ref, sum_ref, out_ref, win_ref, src_ref, *scratch
):
    boxes, waves, width = out_ref.shape
    length = pairs_ref.shape[1]
    for part, ref in ((2, before_ref), (1, after_ref)):
        win_ref[part * boxes : (part + 1) * boxes] = ref[:boxes]
        source, _ = features(ref[:boxes].astype(F32)[:, 8:16, :])
        turn_sources(source, src_ref, part * (boxes * 16 // 128))
    win_ref[0] = own_ref[0]
    src_ref[0] = jnp.zeros(src_ref.shape[1:], BF16)
    out_ref[...] = sum_ref[...]
    near_sum(
        entries,
        pairs_ref[0, length - 1],
        lambda k: pairs_ref[0, length - 3 - k],
        src_ref,
        win_ref,
        obs_ref,
        out_ref,
        scratch,
    )


def incoming_kernel(
    entries, before_ref, own_ref, after_ref, gain_ref, cos_ref, sin_ref, imat_ref, rad_ref, near_ref, out_ref, down_re_ref,
    down_im_ref
):
    parents, window, _, parent_dirs = gain_ref.shape
    boxes, waves, width = near_ref.shape
    chunks = parent_dirs // 128
    group = window // 3
    cos_phase = cos_ref[...]
    sin_phase = sin_ref[...]
    sums = tuple(jnp.zeros((waves, 128), F32) for _ in range(parents * chunks * 2))
    for part, ref in enumerate((before_ref, own_ref, after_ref)):

        def add_source(s, sums, part=part, ref=ref):
            sums = list(sums)
            gains = [gain_ref[q, part * group + s] for q in range(parents)]
            for k in range(chunks):
                spectrum = ref[s * chunks + k].astype(F32)
                sre, sim = spectrum[:waves], spectrum[waves:]
                for q in range(parents):
                    gre = gains[q][0:1, k * 128 : (k + 1) * 128]
                    gim = gains[q][1:2, k * 128 : (k + 1) * 128]
                    at = (q * chunks + k) * 2
                    sums[at] = sums[at] + (gre * sre - gim * sim)
                    sums[at + 1] = sums[at + 1] + (gre * sim + gim * sre)
            return tuple(sums)

        sums = lax.fori_loop(0, group, add_source, sums, unroll=8)
    for q in range(parents):
        for k in range(chunks):
            at = (q * chunks + k) * 2
            re = sums[at].astype(BF16).astype(F32)
            im = sums[at + 1].astype(BF16).astype(F32)
            lanes = slice(k * 128, (k + 1) * 128)
            for c in range(8):
                cos, sin = cos_phase[c : c + 1, lanes], sin_phase[c : c + 1, lanes]
                rows = slice((q * 8 + c) * waves, (q * 8 + c + 1) * waves)
                down_re_ref[rows, lanes] = cos * re + sin * im
                down_im_ref[rows, lanes] = cos * im - sin * re
    imat = imat_ref[...]
    in_re = nt_dot(down_re_ref[...].astype(BF16), imat)
    in_im = nt_dot(down_im_ref[...].astype(BF16), imat)
    incoming = jnp.concatenate([in_re, in_im], axis=1).astype(BF16)
    far = nt_dot(incoming, rad_ref[...])
    factor = TURN / math.sqrt(entries * width) * 2.0 * LEAD * LEAD
    out_ref[...] = near_ref[...] * factor + far.reshape(near_ref.shape)


def per_device(
    currents, positions, radiation, interp_index, interp_weight, child_phase, near_src, trans_src, trans_id,
    trans_count, trans_table
):
    boxes, waves, width = currents.shape
    entries = near_src.shape[1]
    leaf_dirs = radiation.shape[1] // 2
    parent_dirs = child_phase.shape[1]
    parents = boxes // 8
    spectra_rows = parents * parent_dirs // 128
    size = lax.axis_size("dir")
    vmem = pl.BlockSpec(memory_space=pltpu.VMEM)
    smem = pl.BlockSpec(memory_space=pltpu.SMEM)
    hbm = pl.BlockSpec(memory_space=pltpu.HBM)
    params = pltpu.CompilerParams(vmem_limit_bytes=32 * 1024 * 1024)

    def in_hbm(x):
        return pltpu.with_memory_space_constraint(x, pltpu.HBM)

    def shaped(shape, dtype):
        return jax.ShapeDtypeStruct(shape, dtype)

    operands = (currents, positions.transpose(1, 0, 2), radiation, interp_index.T, interp_weight.T, child_phase)
    packet, spectra, imat, cos_phase, sin_phase, rad = pl.pallas_call(
        outgoing_kernel,
        out_shape=(
            shaped((boxes + spectra_rows, 16, width), BF16),
            shaped((spectra_rows, 2 * waves, 128), BF16),
            shaped((leaf_dirs, parent_dirs), BF16),
            shaped((8, parent_dirs), F32),
            shaped((8, parent_dirs), F32),
            shaped(radiation.shape, BF16),
        ),
        in_specs=[hbm] * len(operands),
        out_specs=(vmem,) * 6,
        scratch_shapes=[pltpu.VMEM(x.shape, x.dtype) for x in operands if x is not radiation]
        + [pltpu.SemaphoreType.DMA((len(operands),))],
        compiler_params=params,
        name="outgoing",
    )(*[in_hbm(x) for x in operands])

    before, after = neighbours(packet, ("box", "dir"))
    turned = [
        lax.ppermute(spectra, "dir", [(i, (i + turn) % size) for i in range(size)]) for turn in range(2, size - 1)
    ]
    if size > 2:
        turned.append(lax.ppermute(spectra, "dir", [(0, size - 1), (size - 1, 0)]))

    length = round_up(boxes * entries + 6 * TILES + 2, 128)
    window = 3 * trans_src.shape[0]
    near_scratch = [
        pltpu.VMEM((TILES, width, width), F32),
        pltpu.VMEM((TILES, width, width), F32),
        pltpu.VMEM((TILES, width, width), BF16),
        pltpu.VMEM((TILES, width, width), BF16),
    ]
    own_sum, pairs, observers, gains = pl.pallas_call(
        own_near_kernel,
        out_shape=(
            shaped((boxes, waves, width), F32),
            shaped((1, length), jnp.int32),
            shaped((boxes, 2 * (128 - 16) + 16, width), BF16),
            shaped((parents, window, 2, parent_dirs), F32),
        ),
        in_specs=[vmem] + [hbm] * 5,
        out_specs=(vmem,) * 4,
        scratch_shapes=[
            pltpu.VMEM(near_src.shape, jnp.int32),
            pltpu.SMEM((1, length), jnp.int32),
            pltpu.SMEM(trans_src.shape, jnp.int32),
            pltpu.SMEM(trans_id.shape, jnp.int32),
            pltpu.SMEM(trans_count.shape, jnp.int32),
            pltpu.VMEM((parents * trans_src.shape[1], 2, parent_dirs), F32),
            pltpu.VMEM((boxes * 16 // 128, width, 128), BF16),
        ]
        + near_scratch
        + [pltpu.SemaphoreType.DMA((4,))],
        compiler_params=params,
        name="own_near",
    )(packet, *[in_hbm(x) for x in (near_src, trans_src, trans_id, trans_count, trans_table)])

    group = pl.pallas_call(
        group_kernel,
        out_shape=shaped((size * spectra_rows, 2 * waves, 128), BF16),
        in_specs=[vmem] * (4 + len(turned)),
        out_specs=vmem,
        compiler_params=params,
        name="group",
    )(spectra, before, after, *turned, pairs)
    group_before, group_after = neighbours(group, "box")

    near = pl.pallas_call(
        functools.partial(rest_near_kernel, entries),
        out_shape=shaped((boxes, waves, width), F32),
        in_specs=[smem] + [vmem] * 5,
        out_specs=vmem,
        scratch_shapes=[
            pltpu.VMEM((3 * boxes, 16, width), BF16),
            pltpu.VMEM((3 * boxes * 16 // 128, width, 128), BF16),
        ]
        + near_scratch,
        compiler_params=params,
        name="rest_near",
    )(pairs, packet, before, after, observers, own_sum)

    return pl.pallas_call(
        functools.partial(incoming_kernel, entries),
        out_shape=shaped((boxes, waves, width), F32),
        in_specs=[vmem] * 9,
        out_specs=vmem,
        scratch_shapes=[
            pltpu.VMEM((boxes * waves, parent_dirs), F32),
            pltpu.VMEM((boxes * waves, parent_dirs), F32),
        ],
        compiler_params=params,
        name="incoming",
    )(group_before, group, group_after, gains, cos_phase, sin_phase, imat, rad, near)


def solution(mesh):
    placed = (
        P(("box", "dir"), None, None),
        P(("box", "dir"), None, None),
        P(),
        P(),
        P(),
        P(),
        P(("box", "dir"), None),
        P("box", None),
        P("box", None),
        P("box"),
        P(),
    )
    return jax.shard_map(
        per_device,
        mesh=mesh,
        in_specs=placed,
        out_specs=P(("box", "dir"), None, None),
        check_vma=False,
    )
```

```python
import functools
import math

import jax
import jax.numpy as jnp
from jax import lax
from jax.experimental import pallas as pl
from jax.experimental.pallas import tpu as pltpu
from jax.sharding import PartitionSpec as P

F32 = jnp.float32
BF16 = jnp.bfloat16

WAVENUMBER = 4.0
OFFSET = 0.5
TURN = WAVENUMBER / (2.0 * math.pi)
C0, C1, C2, C3 = (4.551727469085273, -22.461833254303432, 18.47278585020764, -6.062355797782118)
LEAD = 0.21969679868984615
ROUNDER = 12582912.0
TILES = 8


def round_up(value, step):
    return -(-value // step) * step


def neighbours(x, axis):
    size = lax.axis_size(axis)
    up = [(i, i + 1) for i in range(size - 1)]
    down = [(j, i) for i, j in up]
    return lax.ppermute(x, axis, up), lax.ppermute(x, axis, down)


def split3(x):
    high = x.astype(BF16).astype(F32)
    rest = x - high
    mid = rest.astype(BF16).astype(F32)
    return high, mid, rest - mid


def nt_dot(a, b):
    return lax.dot_general(a, b, (((1,), (1,)), ((), ())), preferred_element_type=F32)


def nn_dot(a, b):
    return jnp.dot(a, b, preferred_element_type=F32)


def code_bits(boxes, entries):
    count_bits = entries.bit_length()
    source_bits = (3 * boxes - 1).bit_length()
    return source_bits + count_bits, count_bits


def build_pairs(near_src, base, length):
    boxes, entries = near_src.shape
    box_shift, source_shift = code_bits(boxes, entries)
    lanes = round_up(3 * boxes, 128)
    local = near_src - base
    local = jnp.where(local < 0, local + 3 * boxes, local)
    lane = lax.broadcasted_iota(jnp.int32, (boxes, lanes), 1)
    count = jnp.zeros((boxes, lanes), jnp.int32)
    for e in range(entries):
        count = count + (local[:, e : e + 1] == lane).astype(jnp.int32)
    row = lax.broadcasted_iota(jnp.int32, (lanes, lanes), 0)
    col = lax.broadcasted_iota(jnp.int32, (lanes, lanes), 1)
    ahead = (row < col).astype(F32).astype(BF16)
    box_row = lax.broadcasted_iota(jnp.int32, (boxes, boxes), 0)
    box_col = lax.broadcasted_iota(jnp.int32, (boxes, boxes), 1)
    above = (box_col < box_row).astype(F32).astype(BF16)

    def places(flags):
        rank = nn_dot(flags.astype(BF16), ahead)
        totals = jnp.sum(flags, axis=1, keepdims=True)
        offset = nn_dot(above, jnp.broadcast_to(totals, (boxes, lanes)).astype(BF16))
        return rank + offset, jnp.sum(totals, axis=0, keepdims=True)

    own = (count > 0) & (lane < boxes)
    other = (count > 0) & (lane >= boxes)
    own_place, own_total = places(own.astype(F32))
    other_place, other_total = places(other.astype(F32))
    place = jnp.where(own, own_place, jnp.where(other, float(length - 3) - other_place, -1.0))
    box = lax.broadcasted_iota(jnp.int32, (boxes, lanes), 0)
    code = ((box << box_shift) | (lane << source_shift) | count).astype(F32)
    place_t = place.T
    code_t = code.T
    rows = 3 * boxes
    slot = lax.broadcasted_iota(jnp.int32, (rows, length), 1).astype(F32)
    found = jnp.zeros((rows, length), F32)
    for i in range(boxes):
        hit = place_t[:rows, i : i + 1] == slot
        found = found + jnp.where(hit, code_t[:rows, i : i + 1], 0.0)
    pairs = jnp.sum(found, axis=0, keepdims=True)
    at = lax.broadcasted_iota(jnp.int32, (1, length), 1)
    pairs = jnp.where(at == length - 2, own_total, jnp.where(at == length - 1, other_total, pairs))
    return pairs.astype(jnp.int32)


def start_all(copies, sems):
    started = [pltpu.make_async_copy(src, dst, sems.at[k]) for k, (src, dst) in enumerate(copies)]
    for copy in started:
        copy.start()
    return started


def wait_all(started):
    for copy in started:
        copy.wait()


def outgoing_kernel(
    x_hbm, pos_hbm, rad_hbm, idx_hbm, wgt_hbm, phase_hbm, packet_ref, spectra_ref, imat_ref, cos_ref, sin_ref, rad_ref,
    x_ref, pos_ref, idx_ref, wgt_ref, phase_ref, sems
):
    wait_all(
        start_all(
            (
                (x_hbm, x_ref),
                (pos_hbm, pos_ref),
                (rad_hbm, rad_ref),
                (idx_hbm, idx_ref),
                (wgt_hbm, wgt_ref),
                (phase_hbm, phase_ref),
            ),
            sems,
        )
    )
    leaf_dirs, parent_dirs = imat_ref.shape
    boxes, waves, width = x_ref.shape
    chunks = parent_dirs // 128
    x = x_ref[...].astype(F32)
    planes = pos_ref[...].astype(F32)
    at = lax.broadcasted_iota(jnp.int32, (boxes, 16 - waves, width), 1)
    pos = jnp.zeros((boxes, 16 - waves, width), F32)
    for axis in range(3):
        pos = jnp.where(at == axis, planes[axis][:, None, :], pos)
    packet_ref[:boxes] = jnp.concatenate([x, pos], axis=1).astype(BF16)
    column = lax.broadcasted_iota(jnp.int32, (leaf_dirs, parent_dirs), 0)
    imat = jnp.zeros((leaf_dirs, parent_dirs), F32)
    for s in range(idx_ref.shape[0]):
        imat = imat + jnp.where(idx_ref[s : s + 1, :] == column, wgt_ref[s : s + 1, :], 0.0)
    imat = imat.astype(BF16)
    imat_ref[...] = imat
    cos_phase = jnp.cos(phase_ref[...])
    sin_phase = jnp.sin(phase_ref[...])
    cos_ref[...] = cos_phase
    sin_ref[...] = sin_phase
    leaf = nn_dot(x.reshape(boxes * waves, width).astype(BF16), rad_ref[...]).astype(BF16)
    up_re = nn_dot(leaf[:, :leaf_dirs], imat)
    up_im = nn_dot(leaf[:, leaf_dirs:], imat)
    for q in range(boxes // 8):
        re = jnp.zeros((waves, parent_dirs), F32)
        im = jnp.zeros((waves, parent_dirs), F32)
        for c in range(8):
            at = (q * 8 + c) * waves
            ure = up_re[at : at + waves]
            uim = up_im[at : at + waves]
            re = re + (cos_phase[c : c + 1] * ure - sin_phase[c : c + 1] * uim)
            im = im + (sin_phase[c : c + 1] * ure + cos_phase[c : c + 1] * uim)
        both = jnp.concatenate([re, im], axis=0).astype(BF16)
        for k in range(chunks):
            part = both[:, k * 128 : (k + 1) * 128]
            packet_ref[boxes + q * chunks + k] = part
            spectra_ref[q * chunks + k] = part


def group_kernel(own_ref, before_ref, after_ref, *refs):
    *turned_refs, _, group_ref = refs
    size = lax.axis_size("dir")
    rows = own_ref.shape[0]
    boxes = before_ref.shape[0] - rows
    here = lax.axis_index("dir")

    def place(which, value):
        group_ref[pl.ds(lax.rem(which + size, size) * rows, rows)] = value

    place(here - 1, before_ref[boxes:])
    place(here + 1, after_ref[boxes:])
    for turn, ref in zip(range(2, size - 1), turned_refs):
        place(here - turn, ref[...])
    if size > 2:

        @pl.when((here == 0) | (here == size - 1))
        def _():
            place(size - 1 - here, turned_refs[-1][...])

    place(here, own_ref[...])


def features(pos):
    scale = TURN * TURN
    norm = split3(scale * jnp.sum(pos * pos, axis=1, keepdims=True))
    at = lax.broadcasted_iota(jnp.int32, pos.shape, 1)
    first = jnp.where(at < 3, pos, 1.0)
    first = jnp.where(at == 3, norm[0], jnp.where(at == 4, norm[1], jnp.where(at == 5, norm[2], first)))
    second = jnp.where(at == 3, 1.0, pos + pltpu.roll(pos, 4, 1))
    source = jnp.concatenate([first, second], axis=1).astype(BF16)
    cross = split3((-2.0 * scale) * pos)
    first = jnp.where(at < 3, cross[0], 1.0)
    first = jnp.where(at == 6, norm[0], jnp.where(at == 7, norm[1], first))
    second = jnp.where(at == 3, norm[2], cross[1] + pltpu.roll(cross[2], 4, 1))
    return source, jnp.concatenate([first, second], axis=1).astype(BF16)


def turn_sources(source, src_ref, start):
    boxes, rows, width = source.shape
    eye = lax.broadcasted_iota(jnp.int32, (width, width), 0) == lax.broadcasted_iota(jnp.int32, (width, width), 1)
    turned = nt_dot(eye.astype(F32).astype(BF16), source.reshape(boxes * rows, width)).astype(BF16)
    for j in range(boxes * rows // 128):
        src_ref[start + j] = turned[:, j * 128 : (j + 1) * 128]


def inverse(d):
    low, high = d[:16], d[16:]
    pair = low * high
    over = pl.reciprocal(pair[:8] * pair[8:], approx=True)
    over_pair = jnp.concatenate([over * pair[8:], over * pair[:8]], axis=0)
    return jnp.concatenate([over_pair * high, over_pair * low], axis=0)


def near_sum(entries, total, pair_at, src_ref, win_ref, obs_ref, out_ref, scratch):
    u0_ref, u1_ref, t0_ref, t1_ref = scratch
    boxes, waves, width = out_ref.shape
    per_row = 128 // 16
    box_shift, source_shift = code_bits(boxes, entries)
    t1_ref[...] = jnp.zeros(t1_ref.shape, BF16)

    def decode(chunk, g):
        code = pair_at(chunk * TILES + g)
        i = code >> box_shift
        s = (code >> source_shift) & ((1 << (box_shift - source_shift)) - 1)
        return i, s, code & ((1 << source_shift) - 1)

    def distances(chunk, g, u_ref):
        i, s, _ = decode(chunk, g)
        skip = pl.multiple_of((per_row - 1 - (s & (per_row - 1))) * 16, 16)
        u_ref[g] = nn_dot(src_ref[s >> 3], obs_ref[i, pl.ds(skip, 128), :])

    def tile(g, u_ref, t_ref):
        for at in range(0, width, 32):
            v = jnp.maximum(u_ref[g, at : at + 32], 1e-12)
            q = v * lax.rsqrt(v)
            t = q - ((q + ROUNDER) - ROUNDER)
            z = t * t
            p = (((z + C3) * z + C2) * z + C1) * z + C0
            cosine = p * p - 0.5 / (LEAD * LEAD)
            t_ref[g, at : at + 32] = (cosine * inverse(q + OFFSET * TURN)).astype(BF16)

    def product(chunk, g, t_ref):
        i, s, count = decode(chunk, g)
        got = nn_dot(win_ref[s], t_ref[g])
        out_ref[i] += count.astype(F32) * got[:waves]

    def stages(chunk, u_ref, next_u_ref, t_ref, last_t_ref):
        for g in range(TILES):
            distances(chunk + 1, g, next_u_ref)
            product(jnp.maximum(chunk - 1, 0), g, last_t_ref)
            tile(g, u_ref, t_ref)

    rounds = (total + (2 * TILES - 1)) // (2 * TILES)
    for g in range(TILES):
        distances(0, g, u0_ref)

    def body(k, carry):
        stages(2 * k, u0_ref, u1_ref, t0_ref, t1_ref)
        stages(2 * k + 1, u1_ref, u0_ref, t1_ref, t0_ref)
        return carry

    lax.fori_loop(0, rounds, body, 0)
    for g in range(TILES):
        product(jnp.maximum(2 * rounds - 1, 0), g, t1_ref)


def own_near_kernel(
    own_ref, near_hbm, src_hbm, id_hbm, count_hbm, table_hbm, out_ref, pairs_ref, obs_ref, gain_ref, near_ref, list_ref,
    trans_src_ref, trans_id_ref, trans_count_ref, rows_ref, src_ref, *scratch
):
    *scratch, sems = scratch
    boxes, waves, width = out_ref.shape
    entries = near_ref.shape[1]
    length = pairs_ref.shape[1]
    parents, window = gain_ref.shape[:2]
    listed = src_hbm.shape[1]
    near_copy, *list_copies = start_all(
        (
            (near_hbm, near_ref),
            (src_hbm, trans_src_ref),
            (id_hbm, trans_id_ref),
            (count_hbm, trans_count_ref),
        ),
        sems,
    )
    out_ref[...] = jnp.zeros(out_ref.shape, F32)
    gain_ref[...] = jnp.zeros(gain_ref.shape, F32)
    source, observer = features(own_ref[:boxes].astype(F32)[:, 8:16, :])
    turn_sources(source, src_ref, 0)
    pad = 128 - 16
    obs_ref[:, :pad, :] = jnp.zeros((boxes, pad, width), BF16)
    obs_ref[:, pad : pad + 16, :] = observer
    obs_ref[:, pad + 16 :, :] = jnp.zeros((boxes, pad, width), BF16)
    near_copy.wait()
    base = lax.axis_index(("box", "dir")) * boxes
    pairs_ref[...] = build_pairs(near_ref[...], base, length)
    send_list = pltpu.make_async_copy(pairs_ref, list_ref, sems.at[0])
    send_list.start()
    wait_all(list_copies)
    row0 = lax.axis_index("dir") * parents
    for q in range(parents):
        for e in range(listed):
            pltpu.make_async_copy(
                table_hbm.at[trans_id_ref[row0 + q, e]], rows_ref.at[q * listed + e], sems.at[1]
            ).start()
    send_list.wait()
    near_sum(entries, list_ref[0, length - 2], lambda k: list_ref[0, k], src_ref, own_ref, obs_ref, out_ref, scratch)
    pltpu.make_async_copy(rows_ref, rows_ref, sems.at[1]).wait()
    first = (lax.axis_index("box") - 1) * (window // 3)
    for q in range(parents):
        for e in range(listed):
            live = (e < trans_count_ref[row0 + q]).astype(F32)
            s = jnp.clip(trans_src_ref[row0 + q, e] - first, 0, window - 1)
            gain_ref[q, s] += rows_ref[q * listed + e] * live


def rest_near_kernel(
    entries, pairs_ref, own_ref, before_ref, after_ref, obs_ref, sum_ref, out_ref, win_ref, src_ref, *scratch
):
    boxes, waves, width = out_ref.shape
    length = pairs_ref.shape[1]
    for part, ref in ((2, before_ref), (1, after_ref)):
        win_ref[part * boxes : (part + 1) * boxes] = ref[:boxes]
        source, _ = features(ref[:boxes].astype(F32)[:, 8:16, :])
        turn_sources(source, src_ref, part * (boxes * 16 // 128))
    win_ref[0] = own_ref[0]
    src_ref[0] = jnp.zeros(src_ref.shape[1:], BF16)
    out_ref[...] = sum_ref[...]
    near_sum(
        entries,
        pairs_ref[0, length - 1],
        lambda k: pairs_ref[0, length - 3 - k],
        src_ref,
        win_ref,
        obs_ref,
        out_ref,
        scratch,
    )


def incoming_kernel(
    entries, before_ref, own_ref, after_ref, gain_ref, cos_ref, sin_ref, imat_ref, rad_ref, near_ref, out_ref, down_re_ref,
    down_im_ref
):
    parents, window, _, parent_dirs = gain_ref.shape
    boxes, waves, width = near_ref.shape
    chunks = parent_dirs // 128
    group = window // 3
    cos_phase = cos_ref[...]
    sin_phase = sin_ref[...]
    sums = tuple(jnp.zeros((waves, 128), F32) for _ in range(parents * chunks * 2))
    for part, ref in enumerate((before_ref, own_ref, after_ref)):

        def add_source(s, sums, part=part, ref=ref):
            sums = list(sums)
            gains = [gain_ref[q, part * group + s] for q in range(parents)]
            for k in range(chunks):
                spectrum = ref[s * chunks + k].astype(F32)
                sre, sim = spectrum[:waves], spectrum[waves:]
                for q in range(parents):
                    gre = gains[q][0:1, k * 128 : (k + 1) * 128]
                    gim = gains[q][1:2, k * 128 : (k + 1) * 128]
                    at = (q * chunks + k) * 2
                    sums[at] = sums[at] + (gre * sre - gim * sim)
                    sums[at + 1] = sums[at + 1] + (gre * sim + gim * sre)
            return tuple(sums)

        sums = lax.fori_loop(0, group, add_source, sums, unroll=8)
    for q in range(parents):
        for k in range(chunks):
            at = (q * chunks + k) * 2
            re = sums[at].astype(BF16).astype(F32)
            im = sums[at + 1].astype(BF16).astype(F32)
            lanes = slice(k * 128, (k + 1) * 128)
            for c in range(8):
                cos, sin = cos_phase[c : c + 1, lanes], sin_phase[c : c + 1, lanes]
                rows = slice((q * 8 + c) * waves, (q * 8 + c + 1) * waves)
                down_re_ref[rows, lanes] = cos * re + sin * im
                down_im_ref[rows, lanes] = cos * im - sin * re
    imat = imat_ref[...]
    in_re = nt_dot(down_re_ref[...].astype(BF16), imat)
    in_im = nt_dot(down_im_ref[...].astype(BF16), imat)
    incoming = jnp.concatenate([in_re, in_im], axis=1).astype(BF16)
    far = nt_dot(incoming, rad_ref[...])
    factor = TURN / math.sqrt(entries * width) * 2.0 * LEAD * LEAD
    out_ref[...] = near_ref[...] * factor + far.reshape(near_ref.shape)


def per_device(
    currents, positions, radiation, interp_index, interp_weight, child_phase, near_src, trans_src, trans_id,
    trans_count, trans_table
):
    boxes, waves, width = currents.shape
    entries = near_src.shape[1]
    leaf_dirs = radiation.shape[1] // 2
    parent_dirs = child_phase.shape[1]
    parents = boxes // 8
    spectra_rows = parents * parent_dirs // 128
    size = lax.axis_size("dir")
    vmem = pl.BlockSpec(memory_space=pltpu.VMEM)
    smem = pl.BlockSpec(memory_space=pltpu.SMEM)
    hbm = pl.BlockSpec(memory_space=pltpu.HBM)
    params = pltpu.CompilerParams(vmem_limit_bytes=32 * 1024 * 1024)

    def in_hbm(x):
        return pltpu.with_memory_space_constraint(x, pltpu.HBM)

    def shaped(shape, dtype):
        return jax.ShapeDtypeStruct(shape, dtype)

    operands = (currents, positions.transpose(1, 0, 2), radiation, interp_index.T, interp_weight.T, child_phase)
    packet, spectra, imat, cos_phase, sin_phase, rad = pl.pallas_call(
        outgoing_kernel,
        out_shape=(
            shaped((boxes + spectra_rows, 16, width), BF16),
            shaped((spectra_rows, 2 * waves, 128), BF16),
            shaped((leaf_dirs, parent_dirs), BF16),
            shaped((8, parent_dirs), F32),
            shaped((8, parent_dirs), F32),
            shaped(radiation.shape, BF16),
        ),
        in_specs=[hbm] * len(operands),
        out_specs=(vmem,) * 6,
        scratch_shapes=[pltpu.VMEM(x.shape, x.dtype) for x in operands if x is not radiation]
        + [pltpu.SemaphoreType.DMA((len(operands),))],
        compiler_params=params,
        name="outgoing",
    )(*[in_hbm(x) for x in operands])

    before, after = neighbours(packet, ("box", "dir"))
    turned = [
        lax.ppermute(spectra, "dir", [(i, (i + turn) % size) for i in range(size)]) for turn in range(2, size - 1)
    ]
    if size > 2:
        turned.append(lax.ppermute(spectra, "dir", [(0, size - 1), (size - 1, 0)]))

    length = round_up(boxes * entries + 6 * TILES + 2, 128)
    window = 3 * trans_src.shape[0]
    near_scratch = [
        pltpu.VMEM((TILES, width, width), F32),
        pltpu.VMEM((TILES, width, width), F32),
        pltpu.VMEM((TILES, width, width), BF16),
        pltpu.VMEM((TILES, width, width), BF16),
    ]
    own_sum, pairs, observers, gains = pl.pallas_call(
        own_near_kernel,
        out_shape=(
            shaped((boxes, waves, width), F32),
            shaped((1, length), jnp.int32),
            shaped((boxes, 2 * (128 - 16) + 16, width), BF16),
            shaped((parents, window, 2, parent_dirs), F32),
        ),
        in_specs=[vmem] + [hbm] * 5,
        out_specs=(vmem,) * 4,
        scratch_shapes=[
            pltpu.VMEM(near_src.shape, jnp.int32),
            pltpu.SMEM((1, length), jnp.int32),
            pltpu.SMEM(trans_src.shape, jnp.int32),
            pltpu.SMEM(trans_id.shape, jnp.int32),
            pltpu.SMEM(trans_count.shape, jnp.int32),
            pltpu.VMEM((parents * trans_src.shape[1], 2, parent_dirs), F32),
            pltpu.VMEM((boxes * 16 // 128, width, 128), BF16),
        ]
        + near_scratch
        + [pltpu.SemaphoreType.DMA((4,))],
        compiler_params=params,
        name="own_near",
    )(packet, *[in_hbm(x) for x in (near_src, trans_src, trans_id, trans_count, trans_table)])

    group = pl.pallas_call(
        group_kernel,
        out_shape=shaped((size * spectra_rows, 2 * waves, 128), BF16),
        in_specs=[vmem] * (4 + len(turned)),
        out_specs=vmem,
        compiler_params=params,
        name="group",
    )(spectra, before, after, *turned, pairs)
    group_before, group_after = neighbours(group, "box")

    near = pl.pallas_call(
        functools.partial(rest_near_kernel, entries),
        out_shape=shaped((boxes, waves, width), F32),
        in_specs=[smem] + [vmem] * 5,
        out_specs=vmem,
        scratch_shapes=[
            pltpu.VMEM((3 * boxes, 16, width), BF16),
            pltpu.VMEM((3 * boxes * 16 // 128, width, 128), BF16),
        ]
        + near_scratch,
        compiler_params=params,
        name="rest_near",
    )(pairs, packet, before, after, observers, own_sum)

    return pl.pallas_call(
        functools.partial(incoming_kernel, entries),
        out_shape=shaped((boxes, waves, width), F32),
        in_specs=[vmem] * 9,
        out_specs=vmem,
        scratch_shapes=[
            pltpu.VMEM((boxes * waves, parent_dirs), F32),
            pltpu.VMEM((boxes * waves, parent_dirs), F32),
        ],
        compiler_params=params,
        name="incoming",
    )(group_before, group, group_after, gains, cos_phase, sin_phase, imat, rad, near)


def solution(mesh):
    placed = (
        P(("box", "dir"), None, None),
        P(("box", "dir"), None, None),
        P(),
        P(),
        P(),
        P(),
        P(("box", "dir"), None),
        P("box", None),
        P("box", None),
        P("box"),
        P(),
    )
    return jax.shard_map(
        per_device,
        mesh=mesh,
        in_specs=placed,
        out_specs=P(("box", "dir"), None, None),
        check_vma=False,
    )
```

```python
import functools
import math

import jax
import jax.numpy as jnp
from jax import lax
from jax.experimental import pallas as pl
from jax.experimental.pallas import tpu as pltpu
from jax.sharding import PartitionSpec as P

F32 = jnp.float32
BF16 = jnp.bfloat16

WAVENUMBER = 4.0
OFFSET = 0.5
TURN = WAVENUMBER / (2.0 * math.pi)
C0, C1, C2, C3 = (4.551727469085273, -22.461833254303432, 18.47278585020764, -6.062355797782118)
LEAD = 0.21969679868984615
ROUNDER = 12582912.0
ITEMS = 4


def round_up(value, step):
    return -(-value // step) * step


def neighbours(x, axis):
    size = lax.axis_size(axis)
    up = [(i, i + 1) for i in range(size - 1)]
    down = [(j, i) for i, j in up]
    return lax.ppermute(x, axis, up), lax.ppermute(x, axis, down)


def split3(x):
    high = x.astype(BF16).astype(F32)
    rest = x - high
    mid = rest.astype(BF16).astype(F32)
    return high, mid, rest - mid


def nt_dot(a, b):
    return lax.dot_general(a, b, (((1,), (1,)), ((), ())), preferred_element_type=F32)


def nn_dot(a, b):
    return jnp.dot(a, b, preferred_element_type=F32)


def code_shifts(boxes, entries):
    count_bits = entries.bit_length()
    box_bits = (boxes - 1).bit_length()
    return count_bits, count_bits + box_bits, 2 * count_bits + box_bits, 2 * (count_bits + box_bits)


def list_items(near_src, base, length):
    boxes, entries = near_src.shape
    first_box, second_count, second_box, source = code_shifts(boxes, entries)
    lanes = round_up(3 * boxes, 128)
    local = near_src - base
    local = jnp.where(local < 0, local + 3 * boxes, local)
    lane = lax.broadcasted_iota(jnp.int32, (boxes, lanes), 1)
    box = lax.broadcasted_iota(jnp.int32, (boxes, lanes), 0)
    count = jnp.zeros((boxes, lanes), jnp.int32)
    for e in range(entries):
        count = count + (local[:, e : e + 1] == lane).astype(jnp.int32)
    present = count > 0
    flags = present.astype(F32)
    box_row = lax.broadcasted_iota(jnp.int32, (boxes, boxes), 0)
    box_col = lax.broadcasted_iota(jnp.int32, (boxes, boxes), 1)
    rank = nn_dot((box_col < box_row).astype(F32).astype(BF16), flags.astype(BF16)).astype(jnp.int32)
    items = (jnp.sum(flags, axis=0, keepdims=True).astype(jnp.int32) + 1) >> 1
    own = lax.broadcasted_iota(jnp.int32, (1, lanes), 1) < boxes
    own_items = jnp.where(own, items, 0).astype(F32)
    other_items = jnp.where(own, 0, items).astype(F32)
    row = lax.broadcasted_iota(jnp.int32, (lanes, lanes), 0)
    col = lax.broadcasted_iota(jnp.int32, (lanes, lanes), 1)
    ahead = (row < col).astype(F32).astype(BF16)
    both = jnp.concatenate([own_items, other_items, jnp.zeros((6, lanes), F32)], axis=0).astype(BF16)
    offset = nn_dot(both, ahead).astype(jnp.int32)
    half = rank >> 1
    place = jnp.where(lane < boxes, offset[0:1] + half, (length - 3) - (offset[1:2] + half))
    place = jnp.where(present, place, -1)
    code = jnp.where(
        (rank & 1) == 0,
        (lane << source) | (box << first_box) | count,
        (box << second_box) | (count << second_count),
    )
    place_t = place.T
    code_t = code.T
    rows = 3 * boxes
    slot = lax.broadcasted_iota(jnp.int32, (rows, length), 1)
    found = jnp.zeros((rows, length), jnp.int32)
    for i in range(boxes):
        hit = place_t[:rows, i : i + 1] == slot
        found = found + jnp.where(hit, code_t[:rows, i : i + 1], 0)
    listed = jnp.sum(found, axis=0, keepdims=True)
    own_total = jnp.sum(own_items, axis=1, keepdims=True).astype(jnp.int32)
    other_total = jnp.sum(other_items, axis=1, keepdims=True).astype(jnp.int32)
    at = lax.broadcasted_iota(jnp.int32, (1, length), 1)
    return jnp.where(at == length - 2, own_total, jnp.where(at == length - 1, other_total, listed))


def start_all(copies, sems):
    started = [pltpu.make_async_copy(src, dst, sems.at[k]) for k, (src, dst) in enumerate(copies)]
    for copy in started:
        copy.start()
    return started


def wait_all(started):
    for copy in started:
        copy.wait()


def outgoing_kernel(
    x_hbm, pos_hbm, rad_hbm, idx_hbm, wgt_hbm, phase_hbm, packet_ref, spectra_ref, imat_ref, cos_ref, sin_ref, rad_ref,
    x_ref, pos_ref, idx_ref, wgt_ref, phase_ref, sems
):
    wait_all(
        start_all(
            (
                (x_hbm, x_ref),
                (pos_hbm, pos_ref),
                (rad_hbm, rad_ref),
                (idx_hbm, idx_ref),
                (wgt_hbm, wgt_ref),
                (phase_hbm, phase_ref),
            ),
            sems,
        )
    )
    leaf_dirs, parent_dirs = imat_ref.shape
    boxes, waves, width = x_ref.shape
    chunks = parent_dirs // 128
    x = x_ref[...].astype(F32)
    planes = pos_ref[...].astype(F32)
    at = lax.broadcasted_iota(jnp.int32, (boxes, 16 - waves, width), 1)
    pos = jnp.zeros((boxes, 16 - waves, width), F32)
    for axis in range(3):
        pos = jnp.where(at == axis, planes[axis][:, None, :], pos)
    packet_ref[:boxes] = jnp.concatenate([x, pos], axis=1).astype(BF16)
    column = lax.broadcasted_iota(jnp.int32, (leaf_dirs, parent_dirs), 0)
    imat = jnp.zeros((leaf_dirs, parent_dirs), F32)
    for s in range(idx_ref.shape[0]):
        imat = imat + jnp.where(idx_ref[s : s + 1, :] == column, wgt_ref[s : s + 1, :], 0.0)
    imat = imat.astype(BF16)
    imat_ref[...] = imat
    cos_phase = jnp.cos(phase_ref[...])
    sin_phase = jnp.sin(phase_ref[...])
    cos_ref[...] = cos_phase
    sin_ref[...] = sin_phase
    leaf = nn_dot(x.reshape(boxes * waves, width).astype(BF16), rad_ref[...]).astype(BF16)
    up_re = nn_dot(leaf[:, :leaf_dirs], imat)
    up_im = nn_dot(leaf[:, leaf_dirs:], imat)
    for q in range(boxes // 8):
        re = jnp.zeros((waves, parent_dirs), F32)
        im = jnp.zeros((waves, parent_dirs), F32)
        for c in range(8):
            at = (q * 8 + c) * waves
            ure = up_re[at : at + waves]
            uim = up_im[at : at + waves]
            re = re + (cos_phase[c : c + 1] * ure - sin_phase[c : c + 1] * uim)
            im = im + (sin_phase[c : c + 1] * ure + cos_phase[c : c + 1] * uim)
        both = jnp.concatenate([re, im], axis=0).astype(BF16)
        for k in range(chunks):
            part = both[:, k * 128 : (k + 1) * 128]
            packet_ref[boxes + q * chunks + k] = part
            spectra_ref[q * chunks + k] = part


def group_kernel(own_ref, before_ref, after_ref, *refs):
    *turned_refs, _, group_ref = refs
    size = lax.axis_size("dir")
    rows = own_ref.shape[0]
    boxes = before_ref.shape[0] - rows
    here = lax.axis_index("dir")

    def place(which, value):
        group_ref[pl.ds(lax.rem(which + size, size) * rows, rows)] = value

    place(here - 1, before_ref[boxes:])
    place(here + 1, after_ref[boxes:])
    for turn, ref in zip(range(2, size - 1), turned_refs):
        place(here - turn, ref[...])
    if size > 2:

        @pl.when((here == 0) | (here == size - 1))
        def _():
            place(size - 1 - here, turned_refs[-1][...])

    place(here, own_ref[...])


def features(pos):
    scale = TURN * TURN
    norm = split3(scale * jnp.sum(pos * pos, axis=1, keepdims=True))
    at = lax.broadcasted_iota(jnp.int32, pos.shape, 1)
    first = jnp.where(at < 3, pos, 1.0)
    first = jnp.where(at == 3, norm[0], jnp.where(at == 4, norm[1], jnp.where(at == 5, norm[2], first)))
    second = jnp.where(at == 3, 1.0, pos + pltpu.roll(pos, 4, 1))
    source = jnp.concatenate([first, second], axis=1).astype(BF16)
    cross = split3((-2.0 * scale) * pos)
    first = jnp.where(at < 3, cross[0], 1.0)
    first = jnp.where(at == 6, norm[0], jnp.where(at == 7, norm[1], first))
    second = jnp.where(at == 3, norm[2], cross[1] + pltpu.roll(cross[2], 4, 1))
    return source, jnp.concatenate([first, second], axis=1).astype(BF16)


def turn_sources(source, src_ref, start):
    boxes, rows, width = source.shape
    eye = lax.broadcasted_iota(jnp.int32, (width, width), 0) == lax.broadcasted_iota(jnp.int32, (width, width), 1)
    turned = nt_dot(eye.astype(F32).astype(BF16), source.reshape(boxes * rows, width))
    for b in range(boxes):
        at = b * rows
        lanes = turned[:, at // 128 * 128 : at // 128 * 128 + 128]
        if at % 128:
            lanes = pltpu.roll(lanes, 128 - at % 128, 1)
        src_ref[start + b] = lanes.astype(BF16)


def near_sum(entries, total, item_at, src_ref, win_ref, obs_ref, out_ref, scratch):
    u0_ref, u1_ref, t0_ref, t1_ref = scratch
    boxes, waves, width = out_ref.shape
    first_box, second_count, second_box, source = code_shifts(boxes, entries)
    t1_ref[...] = jnp.zeros(t1_ref.shape, BF16)

    def field(code, low, high):
        return (code >> low) & ((1 << (high - low)) - 1)

    def distances(chunk, g, u_ref):
        code = item_at(chunk * ITEMS + g)
        observers = [obs_ref[field(code, first_box, second_count)], obs_ref[field(code, second_box, source)]]
        u_ref[g] = nn_dot(src_ref[code >> source][:, :16], jnp.concatenate(observers, axis=1))

    def tile(g, u_ref, t_ref):
        for at in range(0, width, 16):
            v = jnp.maximum(u_ref[g, at : at + 16], 1e-12)
            q = v * lax.rsqrt(v)
            t = q - ((q + ROUNDER) - ROUNDER)
            z = t * t
            p = (((z + C3) * z + C2) * z + C1) * z + C0
            cosine = p * p - 0.5 / (LEAD * LEAD)
            t_ref[g, at : at + 16] = (cosine * pltpu.reciprocal(q + OFFSET * TURN, approx=True)).astype(BF16)

    def product(chunk, g, t_ref):
        code = item_at(chunk * ITEMS + g)
        got = nn_dot(win_ref[code >> source], t_ref[g])
        out_ref[field(code, first_box, second_count)] += field(code, 0, first_box).astype(F32) * got[:waves, :width]
        out_ref[field(code, second_box, source)] += field(code, second_count, second_box).astype(F32) * got[:waves, width:]

    def stages(chunk, u_ref, next_u_ref, t_ref, last_t_ref):
        for g in range(ITEMS):
            distances(chunk + 1, g, next_u_ref)
            product(jnp.maximum(chunk - 1, 0), g, last_t_ref)
            tile(g, u_ref, t_ref)

    rounds = (total + (2 * ITEMS - 1)) // (2 * ITEMS)
    for g in range(ITEMS):
        distances(0, g, u0_ref)

    def body(k, carry):
        stages(2 * k, u0_ref, u1_ref, t0_ref, t1_ref)
        stages(2 * k + 1, u1_ref, u0_ref, t1_ref, t0_ref)
        return carry

    lax.fori_loop(0, rounds, body, 0)
    for g in range(ITEMS):
        product(jnp.maximum(2 * rounds - 1, 0), g, t1_ref)


def own_near_kernel(
    own_ref, near_hbm, src_hbm, id_hbm, count_hbm, table_hbm, out_ref, items_ref, obs_ref, gain_ref, near_ref, list_ref,
    trans_src_ref, trans_id_ref, trans_count_ref, rows_ref, src_ref, *scratch
):
    *scratch, sems = scratch
    boxes, waves, width = out_ref.shape
    entries = near_ref.shape[1]
    length = items_ref.shape[1]
    parents, window = gain_ref.shape[:2]
    listed = src_hbm.shape[1]
    near_copy, *list_copies = start_all(
        (
            (near_hbm, near_ref),
            (src_hbm, trans_src_ref),
            (id_hbm, trans_id_ref),
            (count_hbm, trans_count_ref),
        ),
        sems,
    )
    out_ref[...] = jnp.zeros(out_ref.shape, F32)
    gain_ref[...] = jnp.zeros(gain_ref.shape, F32)
    source, observer = features(own_ref[:boxes].astype(F32)[:, 8:16, :])
    turn_sources(source, src_ref, 0)
    obs_ref[...] = observer
    near_copy.wait()
    base = lax.axis_index(("box", "dir")) * boxes
    items_ref[...] = list_items(near_ref[...], base, length)
    send_list = pltpu.make_async_copy(items_ref, list_ref, sems.at[0])
    send_list.start()
    wait_all(list_copies)
    row0 = lax.axis_index("dir") * parents
    for q in range(parents):
        for e in range(listed):
            pltpu.make_async_copy(
                table_hbm.at[trans_id_ref[row0 + q, e]], rows_ref.at[q * listed + e], sems.at[1]
            ).start()
    send_list.wait()
    near_sum(entries, list_ref[0, length - 2], lambda k: list_ref[0, k], src_ref, own_ref, obs_ref, out_ref, scratch)
    pltpu.make_async_copy(rows_ref, rows_ref, sems.at[1]).wait()
    first = (lax.axis_index("box") - 1) * (window // 3)
    for q in range(parents):
        for e in range(listed):
            live = (e < trans_count_ref[row0 + q]).astype(F32)
            s = jnp.clip(trans_src_ref[row0 + q, e] - first, 0, window - 1)
            gain_ref[q, s] += rows_ref[q * listed + e] * live


def rest_near_kernel(
    entries, items_ref, own_ref, before_ref, after_ref, obs_ref, sum_ref, out_ref, win_ref, src_ref, *scratch
):
    boxes, waves, width = out_ref.shape
    length = items_ref.shape[1]
    for part, ref in ((2, before_ref), (1, after_ref)):
        win_ref[part * boxes : (part + 1) * boxes] = ref[:boxes]
        source, _ = features(ref[:boxes].astype(F32)[:, 8:16, :])
        turn_sources(source, src_ref, part * boxes)
    win_ref[0] = own_ref[0]
    src_ref[0] = jnp.zeros(src_ref.shape[1:], BF16)
    out_ref[...] = sum_ref[...]
    near_sum(
        entries,
        items_ref[0, length - 1],
        lambda k: items_ref[0, length - 3 - k],
        src_ref,
        win_ref,
        obs_ref,
        out_ref,
        scratch,
    )


def incoming_kernel(
    entries, before_ref, own_ref, after_ref, gain_ref, cos_ref, sin_ref, imat_ref, rad_ref, near_ref, out_ref, down_re_ref,
    down_im_ref
):
    parents, window, _, parent_dirs = gain_ref.shape
    boxes, waves, width = near_ref.shape
    chunks = parent_dirs // 128
    group = window // 3
    cos_phase = cos_ref[...]
    sin_phase = sin_ref[...]
    sums = tuple(jnp.zeros((waves, 128), F32) for _ in range(parents * chunks * 2))
    for part, ref in enumerate((before_ref, own_ref, after_ref)):

        def add_source(s, sums, part=part, ref=ref):
            sums = list(sums)
            gains = [gain_ref[q, part * group + s] for q in range(parents)]
            for k in range(chunks):
                spectrum = ref[s * chunks + k].astype(F32)
                sre, sim = spectrum[:waves], spectrum[waves:]
                for q in range(parents):
                    gre = gains[q][0:1, k * 128 : (k + 1) * 128]
                    gim = gains[q][1:2, k * 128 : (k + 1) * 128]
                    at = (q * chunks + k) * 2
                    sums[at] = sums[at] + (gre * sre - gim * sim)
                    sums[at + 1] = sums[at + 1] + (gre * sim + gim * sre)
            return tuple(sums)

        sums = lax.fori_loop(0, group, add_source, sums, unroll=8)
    for q in range(parents):
        for k in range(chunks):
            at = (q * chunks + k) * 2
            re = sums[at].astype(BF16).astype(F32)
            im = sums[at + 1].astype(BF16).astype(F32)
            lanes = slice(k * 128, (k + 1) * 128)
            for c in range(8):
                cos, sin = cos_phase[c : c + 1, lanes], sin_phase[c : c + 1, lanes]
                rows = slice((q * 8 + c) * waves, (q * 8 + c + 1) * waves)
                down_re_ref[rows, lanes] = cos * re + sin * im
                down_im_ref[rows, lanes] = cos * im - sin * re
    imat = imat_ref[...]
    in_re = nt_dot(down_re_ref[...].astype(BF16), imat)
    in_im = nt_dot(down_im_ref[...].astype(BF16), imat)
    incoming = jnp.concatenate([in_re, in_im], axis=1).astype(BF16)
    far = nt_dot(incoming, rad_ref[...])
    factor = TURN / math.sqrt(entries * width) * 2.0 * LEAD * LEAD
    out_ref[...] = near_ref[...] * factor + far.reshape(near_ref.shape)


def per_device(
    currents, positions, radiation, interp_index, interp_weight, child_phase, near_src, trans_src, trans_id,
    trans_count, trans_table
):
    boxes, waves, width = currents.shape
    entries = near_src.shape[1]
    leaf_dirs = radiation.shape[1] // 2
    parent_dirs = child_phase.shape[1]
    parents = boxes // 8
    spectra_rows = parents * parent_dirs // 128
    size = lax.axis_size("dir")
    vmem = pl.BlockSpec(memory_space=pltpu.VMEM)
    smem = pl.BlockSpec(memory_space=pltpu.SMEM)
    hbm = pl.BlockSpec(memory_space=pltpu.HBM)
    params = pltpu.CompilerParams(vmem_limit_bytes=32 * 1024 * 1024)

    def in_hbm(x):
        return pltpu.with_memory_space_constraint(x, pltpu.HBM)

    def shaped(shape, dtype):
        return jax.ShapeDtypeStruct(shape, dtype)

    operands = (currents, positions.transpose(1, 0, 2), radiation, interp_index.T, interp_weight.T, child_phase)
    packet, spectra, imat, cos_phase, sin_phase, rad = pl.pallas_call(
        outgoing_kernel,
        out_shape=(
            shaped((boxes + spectra_rows, 16, width), BF16),
            shaped((spectra_rows, 2 * waves, 128), BF16),
            shaped((leaf_dirs, parent_dirs), BF16),
            shaped((8, parent_dirs), F32),
            shaped((8, parent_dirs), F32),
            shaped(radiation.shape, BF16),
        ),
        in_specs=[hbm] * len(operands),
        out_specs=(vmem,) * 6,
        scratch_shapes=[pltpu.VMEM(x.shape, x.dtype) for x in operands if x is not radiation]
        + [pltpu.SemaphoreType.DMA((len(operands),))],
        compiler_params=params,
        name="outgoing",
    )(*[in_hbm(x) for x in operands])

    before, after = neighbours(packet, ("box", "dir"))
    turned = [
        lax.ppermute(spectra, "dir", [(i, (i + turn) % size) for i in range(size)]) for turn in range(2, size - 1)
    ]
    if size > 2:
        turned.append(lax.ppermute(spectra, "dir", [(0, size - 1), (size - 1, 0)]))

    length = round_up((boxes * entries + 3 * boxes) // 2 + 6 * ITEMS + 2, 128)
    window = 3 * trans_src.shape[0]
    near_scratch = [
        pltpu.VMEM((ITEMS, width, 2 * width), F32),
        pltpu.VMEM((ITEMS, width, 2 * width), F32),
        pltpu.VMEM((ITEMS, width, 2 * width), BF16),
        pltpu.VMEM((ITEMS, width, 2 * width), BF16),
    ]
    own_sum, items, observers, gains = pl.pallas_call(
        own_near_kernel,
        out_shape=(
            shaped((boxes, waves, width), F32),
            shaped((1, length), jnp.int32),
            shaped((boxes, 16, width), BF16),
            shaped((parents, window, 2, parent_dirs), F32),
        ),
        in_specs=[vmem] + [hbm] * 5,
        out_specs=(vmem,) * 4,
        scratch_shapes=[
            pltpu.VMEM(near_src.shape, jnp.int32),
            pltpu.SMEM((1, length), jnp.int32),
            pltpu.SMEM(trans_src.shape, jnp.int32),
            pltpu.SMEM(trans_id.shape, jnp.int32),
            pltpu.SMEM(trans_count.shape, jnp.int32),
            pltpu.VMEM((parents * trans_src.shape[1], 2, parent_dirs), F32),
            pltpu.VMEM((boxes, width, 128), BF16),
        ]
        + near_scratch
        + [pltpu.SemaphoreType.DMA((4,))],
        compiler_params=params,
        name="own_near",
    )(packet, *[in_hbm(x) for x in (near_src, trans_src, trans_id, trans_count, trans_table)])

    group = pl.pallas_call(
        group_kernel,
        out_shape=shaped((size * spectra_rows, 2 * waves, 128), BF16),
        in_specs=[vmem] * (4 + len(turned)),
        out_specs=vmem,
        compiler_params=params,
        name="group",
    )(spectra, before, after, *turned, items)
    group_before, group_after = neighbours(group, "box")

    near = pl.pallas_call(
        functools.partial(rest_near_kernel, entries),
        out_shape=shaped((boxes, waves, width), F32),
        in_specs=[smem] + [vmem] * 5,
        out_specs=vmem,
        scratch_shapes=[
            pltpu.VMEM((3 * boxes, 16, width), BF16),
            pltpu.VMEM((3 * boxes, width, 128), BF16),
        ]
        + near_scratch,
        compiler_params=params,
        name="rest_near",
    )(items, packet, before, after, observers, own_sum)

    return pl.pallas_call(
        functools.partial(incoming_kernel, entries),
        out_shape=shaped((boxes, waves, width), F32),
        in_specs=[vmem] * 9,
        out_specs=vmem,
        scratch_shapes=[
            pltpu.VMEM((boxes * waves, parent_dirs), F32),
            pltpu.VMEM((boxes * waves, parent_dirs), F32),
        ],
        compiler_params=params,
        name="incoming",
    )(group_before, group, group_after, gains, cos_phase, sin_phase, imat, rad, near)


def solution(mesh):
    placed = (
        P(("box", "dir"), None, None),
        P(("box", "dir"), None, None),
        P(),
        P(),
        P(),
        P(),
        P(("box", "dir"), None),
        P("box", None),
        P("box", None),
        P("box"),
        P(),
    )
    return jax.shard_map(
        per_device,
        mesh=mesh,
        in_specs=placed,
        out_specs=P(("box", "dir"), None, None),
        check_vma=False,
    )
```

```python
import functools
import math

import jax
import jax.numpy as jnp
from jax import lax
from jax.experimental import pallas as pl
from jax.experimental.pallas import tpu as pltpu
from jax.sharding import PartitionSpec as P

F32 = jnp.float32
BF16 = jnp.bfloat16

WAVENUMBER = 4.0
OFFSET = 0.5
TURN = WAVENUMBER / (2.0 * math.pi)
C0, C1, C2, C3 = (4.551727469085273, -22.461833254303432, 18.47278585020764, -6.062355797782118)
LEAD = 0.21969679868984615
ROUNDER = 12582912.0
ITEMS = 4
ROWS = 32


def round_up(value, step):
    return -(-value // step) * step


def neighbours(x, axis):
    size = lax.axis_size(axis)
    up = [(i, i + 1) for i in range(size - 1)]
    down = [(j, i) for i, j in up]
    return lax.ppermute(x, axis, up), lax.ppermute(x, axis, down)


def split3(x):
    high = x.astype(BF16).astype(F32)
    rest = x - high
    mid = rest.astype(BF16).astype(F32)
    return high, mid, rest - mid


def nt_dot(a, b):
    return lax.dot_general(a, b, (((1,), (1,)), ((), ())), preferred_element_type=F32)


def nn_dot(a, b):
    return jnp.dot(a, b, preferred_element_type=F32)


def code_shifts(boxes, entries):
    count_bits = entries.bit_length()
    box_bits = (boxes - 1).bit_length()
    return count_bits, count_bits + box_bits, 2 * count_bits + box_bits, 2 * (count_bits + box_bits)


def list_items(near_src, base, length):
    boxes, entries = near_src.shape
    first_box, second_count, second_box, source = code_shifts(boxes, entries)
    lanes = round_up(3 * boxes, 128)
    local = near_src - base
    local = jnp.where(local < 0, local + 3 * boxes, local)
    lane = lax.broadcasted_iota(jnp.int32, (boxes, lanes), 1)
    box = lax.broadcasted_iota(jnp.int32, (boxes, lanes), 0)
    count = jnp.zeros((boxes, lanes), jnp.int32)
    for e in range(entries):
        count = count + (local[:, e : e + 1] == lane).astype(jnp.int32)
    present = count > 0
    flags = present.astype(F32)
    box_row = lax.broadcasted_iota(jnp.int32, (boxes, boxes), 0)
    box_col = lax.broadcasted_iota(jnp.int32, (boxes, boxes), 1)
    rank = nn_dot((box_col < box_row).astype(F32).astype(BF16), flags.astype(BF16)).astype(jnp.int32)
    items = (jnp.sum(flags, axis=0, keepdims=True).astype(jnp.int32) + 1) >> 1
    own = lax.broadcasted_iota(jnp.int32, (1, lanes), 1) < boxes
    own_items = jnp.where(own, items, 0).astype(F32)
    other_items = jnp.where(own, 0, items).astype(F32)
    row = lax.broadcasted_iota(jnp.int32, (lanes, lanes), 0)
    col = lax.broadcasted_iota(jnp.int32, (lanes, lanes), 1)
    ahead = (row < col).astype(F32).astype(BF16)
    both = jnp.concatenate([own_items, other_items, jnp.zeros((6, lanes), F32)], axis=0).astype(BF16)
    offset = nn_dot(both, ahead).astype(jnp.int32)
    half = rank >> 1
    place = jnp.where(lane < boxes, offset[0:1] + half, (length - 3) - (offset[1:2] + half))
    place = jnp.where(present, place, -1)
    code = jnp.where(
        (rank & 1) == 0,
        (lane << source) | (box << first_box) | count,
        (box << second_box) | (count << second_count),
    )
    place_t = place.T
    code_t = code.T
    rows = 3 * boxes
    slot = lax.broadcasted_iota(jnp.int32, (rows, length), 1)
    found = jnp.zeros((rows, length), jnp.int32)
    for i in range(boxes):
        hit = place_t[:rows, i : i + 1] == slot
        found = found + jnp.where(hit, code_t[:rows, i : i + 1], 0)
    listed = jnp.sum(found, axis=0, keepdims=True)
    own_total = jnp.sum(own_items, axis=1, keepdims=True).astype(jnp.int32)
    other_total = jnp.sum(other_items, axis=1, keepdims=True).astype(jnp.int32)
    at = lax.broadcasted_iota(jnp.int32, (1, length), 1)
    return jnp.where(at == length - 2, own_total, jnp.where(at == length - 1, other_total, listed))


def start_all(copies, sems):
    started = [pltpu.make_async_copy(src, dst, sems.at[k]) for k, (src, dst) in enumerate(copies)]
    for copy in started:
        copy.start()
    return started


def wait_all(started):
    for copy in started:
        copy.wait()


def outgoing_kernel(
    x_hbm, pos_hbm, rad_hbm, idx_hbm, wgt_hbm, phase_hbm, packet_ref, spectra_ref, imat_ref, cos_ref, sin_ref, rad_ref,
    x_ref, pos_ref, idx_ref, wgt_ref, phase_ref, sems
):
    wait_all(
        start_all(
            (
                (x_hbm, x_ref),
                (pos_hbm, pos_ref),
                (rad_hbm, rad_ref),
                (idx_hbm, idx_ref),
                (wgt_hbm, wgt_ref),
                (phase_hbm, phase_ref),
            ),
            sems,
        )
    )
    leaf_dirs, parent_dirs = imat_ref.shape
    boxes, waves, width = x_ref.shape
    chunks = parent_dirs // 128
    x = x_ref[...].astype(F32)
    planes = pos_ref[...].astype(F32)
    at = lax.broadcasted_iota(jnp.int32, (boxes, 16 - waves, width), 1)
    pos = jnp.zeros((boxes, 16 - waves, width), F32)
    for axis in range(3):
        pos = jnp.where(at == axis, planes[axis][:, None, :], pos)
    packet_ref[:boxes] = jnp.concatenate([x, pos], axis=1).astype(BF16)
    column = lax.broadcasted_iota(jnp.int32, (leaf_dirs, parent_dirs), 0)
    imat = jnp.zeros((leaf_dirs, parent_dirs), F32)
    for s in range(idx_ref.shape[0]):
        imat = imat + jnp.where(idx_ref[s : s + 1, :] == column, wgt_ref[s : s + 1, :], 0.0)
    imat = imat.astype(BF16)
    imat_ref[...] = imat
    cos_phase = jnp.cos(phase_ref[...])
    sin_phase = jnp.sin(phase_ref[...])
    cos_ref[...] = cos_phase
    sin_ref[...] = sin_phase
    leaf = nn_dot(x.reshape(boxes * waves, width).astype(BF16), rad_ref[...]).astype(BF16)
    up_re = nn_dot(leaf[:, :leaf_dirs], imat)
    up_im = nn_dot(leaf[:, leaf_dirs:], imat)
    for q in range(boxes // 8):
        re = jnp.zeros((waves, parent_dirs), F32)
        im = jnp.zeros((waves, parent_dirs), F32)
        for c in range(8):
            at = (q * 8 + c) * waves
            ure = up_re[at : at + waves]
            uim = up_im[at : at + waves]
            re = re + (cos_phase[c : c + 1] * ure - sin_phase[c : c + 1] * uim)
            im = im + (sin_phase[c : c + 1] * ure + cos_phase[c : c + 1] * uim)
        both = jnp.concatenate([re, im], axis=0).astype(BF16)
        for k in range(chunks):
            part = both[:, k * 128 : (k + 1) * 128]
            packet_ref[boxes + q * chunks + k] = part
            spectra_ref[q * chunks + k] = part


def group_kernel(own_ref, before_ref, after_ref, *refs):
    *turned_refs, _, group_ref = refs
    size = lax.axis_size("dir")
    rows = own_ref.shape[0]
    boxes = before_ref.shape[0] - rows
    here = lax.axis_index("dir")

    def place(which, value):
        group_ref[pl.ds(lax.rem(which + size, size) * rows, rows)] = value

    place(here - 1, before_ref[boxes:])
    place(here + 1, after_ref[boxes:])
    for turn, ref in zip(range(2, size - 1), turned_refs):
        place(here - turn, ref[...])
    if size > 2:

        @pl.when((here == 0) | (here == size - 1))
        def _():
            place(size - 1 - here, turned_refs[-1][...])

    place(here, own_ref[...])


def features(pos):
    scale = TURN * TURN
    norm = split3(scale * jnp.sum(pos * pos, axis=1, keepdims=True))
    at = lax.broadcasted_iota(jnp.int32, pos.shape, 1)
    first = jnp.where(at < 3, pos, 1.0)
    first = jnp.where(at == 3, norm[0], jnp.where(at == 4, norm[1], jnp.where(at == 5, norm[2], first)))
    second = jnp.where(at == 3, 1.0, pos + pltpu.roll(pos, 4, 1))
    source = jnp.concatenate([first, second], axis=1).astype(BF16)
    cross = split3((-2.0 * scale) * pos)
    first = jnp.where(at < 3, cross[0], 1.0)
    first = jnp.where(at == 6, norm[0], jnp.where(at == 7, norm[1], first))
    second = jnp.where(at == 3, norm[2], cross[1] + pltpu.roll(cross[2], 4, 1))
    return source, jnp.concatenate([first, second], axis=1).astype(BF16)


def turn_sources(source, src_ref, start):
    boxes, rows, width = source.shape
    eye = lax.broadcasted_iota(jnp.int32, (width, width), 0) == lax.broadcasted_iota(jnp.int32, (width, width), 1)
    turned = nt_dot(eye.astype(F32).astype(BF16), source.reshape(boxes * rows, width))
    for b in range(boxes):
        at = b * rows
        lanes = turned[:, at // 128 * 128 : at // 128 * 128 + 128]
        if at % 128:
            lanes = pltpu.roll(lanes, 128 - at % 128, 1)
        src_ref[start + b] = lanes.astype(BF16)


def near_sum(entries, total, item_at, src_ref, win_ref, obs_ref, out_ref, scratch):
    u0_ref, u1_ref, t0_ref, t1_ref = scratch
    boxes, waves, width = out_ref.shape
    first_box, second_count, second_box, source = code_shifts(boxes, entries)
    t1_ref[...] = jnp.zeros(t1_ref.shape, BF16)

    def field(code, low, high):
        return (code >> low) & ((1 << (high - low)) - 1)

    def distances(chunk, g, u_ref):
        code = item_at(chunk * ITEMS + g)
        observers = [obs_ref[field(code, first_box, second_count)], obs_ref[field(code, second_box, source)]]
        u_ref[g] = nn_dot(src_ref[code >> source][:, :16], jnp.concatenate(observers, axis=1))

    def tile(g, u_ref, t_ref):
        for at in range(0, width, ROWS):
            v = jnp.maximum(u_ref[g, at : at + ROWS], 1e-12)
            q = v * lax.rsqrt(v)
            t = q - ((q + ROUNDER) - ROUNDER)
            z = t * t
            p = (((z + C3) * z + C2) * z + C1) * z + C0
            cosine = p * p - 0.5 / (LEAD * LEAD)
            t_ref[g, at : at + ROWS] = (cosine * pltpu.reciprocal(q + OFFSET * TURN, approx=True)).astype(BF16)

    def product(chunk, g, t_ref):
        code = item_at(chunk * ITEMS + g)
        got = nn_dot(win_ref[code >> source], t_ref[g])
        out_ref[field(code, first_box, second_count)] += field(code, 0, first_box).astype(F32) * got[:waves, :width]
        out_ref[field(code, second_box, source)] += field(code, second_count, second_box).astype(F32) * got[:waves, width:]

    def stages(chunk, u_ref, next_u_ref, t_ref, last_t_ref):
        for g in range(ITEMS):
            distances(chunk + 1, g, next_u_ref)
            product(jnp.maximum(chunk - 1, 0), g, last_t_ref)
            tile(g, u_ref, t_ref)

    rounds = (total + (2 * ITEMS - 1)) // (2 * ITEMS)
    for g in range(ITEMS):
        distances(0, g, u0_ref)

    def body(k, carry):
        stages(2 * k, u0_ref, u1_ref, t0_ref, t1_ref)
        stages(2 * k + 1, u1_ref, u0_ref, t1_ref, t0_ref)
        return carry

    lax.fori_loop(0, rounds, body, 0)
    for g in range(ITEMS):
        product(jnp.maximum(2 * rounds - 1, 0), g, t1_ref)


def own_near_kernel(
    own_ref, near_hbm, src_hbm, id_hbm, count_hbm, table_hbm, out_ref, items_ref, obs_ref, gain_ref, near_ref, list_ref,
    trans_src_ref, trans_id_ref, trans_count_ref, rows_ref, src_ref, *scratch
):
    *scratch, sems = scratch
    boxes, waves, width = out_ref.shape
    entries = near_ref.shape[1]
    length = items_ref.shape[1]
    parents, window = gain_ref.shape[:2]
    listed = src_hbm.shape[1]
    near_copy, *list_copies = start_all(
        (
            (near_hbm, near_ref),
            (src_hbm, trans_src_ref),
            (id_hbm, trans_id_ref),
            (count_hbm, trans_count_ref),
        ),
        sems,
    )
    out_ref[...] = jnp.zeros(out_ref.shape, F32)
    gain_ref[...] = jnp.zeros(gain_ref.shape, F32)
    source, observer = features(own_ref[:boxes].astype(F32)[:, 8:16, :])
    turn_sources(source, src_ref, 0)
    obs_ref[...] = observer
    near_copy.wait()
    base = lax.axis_index(("box", "dir")) * boxes
    items_ref[...] = list_items(near_ref[...], base, length)
    send_list = pltpu.make_async_copy(items_ref, list_ref, sems.at[0])
    send_list.start()
    wait_all(list_copies)
    row0 = lax.axis_index("dir") * parents
    for q in range(parents):
        for e in range(listed):
            pltpu.make_async_copy(
                table_hbm.at[trans_id_ref[row0 + q, e]], rows_ref.at[q * listed + e], sems.at[1]
            ).start()
    send_list.wait()
    near_sum(entries, list_ref[0, length - 2], lambda k: list_ref[0, k], src_ref, own_ref, obs_ref, out_ref, scratch)
    pltpu.make_async_copy(rows_ref, rows_ref, sems.at[1]).wait()
    first = (lax.axis_index("box") - 1) * (window // 3)
    for q in range(parents):
        for e in range(listed):
            live = (e < trans_count_ref[row0 + q]).astype(F32)
            s = jnp.clip(trans_src_ref[row0 + q, e] - first, 0, window - 1)
            gain_ref[q, s] += rows_ref[q * listed + e] * live


def rest_near_kernel(
    entries, items_ref, own_ref, before_ref, after_ref, obs_ref, sum_ref, out_ref, win_ref, src_ref, *scratch
):
    boxes, waves, width = out_ref.shape
    length = items_ref.shape[1]
    for part, ref in ((2, before_ref), (1, after_ref)):
        win_ref[part * boxes : (part + 1) * boxes] = ref[:boxes]
        source, _ = features(ref[:boxes].astype(F32)[:, 8:16, :])
        turn_sources(source, src_ref, part * boxes)
    win_ref[0] = own_ref[0]
    src_ref[0] = jnp.zeros(src_ref.shape[1:], BF16)
    out_ref[...] = sum_ref[...]
    near_sum(
        entries,
        items_ref[0, length - 1],
        lambda k: items_ref[0, length - 3 - k],
        src_ref,
        win_ref,
        obs_ref,
        out_ref,
        scratch,
    )


def incoming_kernel(
    entries, before_ref, own_ref, after_ref, gain_ref, cos_ref, sin_ref, imat_ref, rad_ref, near_ref, out_ref, down_re_ref,
    down_im_ref
):
    parents, window, _, parent_dirs = gain_ref.shape
    boxes, waves, width = near_ref.shape
    chunks = parent_dirs // 128
    group = window // 3
    cos_phase = cos_ref[...]
    sin_phase = sin_ref[...]
    sums = tuple(jnp.zeros((waves, 128), F32) for _ in range(parents * chunks * 2))
    for part, ref in enumerate((before_ref, own_ref, after_ref)):

        def add_source(s, sums, part=part, ref=ref):
            sums = list(sums)
            gains = [gain_ref[q, part * group + s] for q in range(parents)]
            for k in range(chunks):
                spectrum = ref[s * chunks + k].astype(F32)
                sre, sim = spectrum[:waves], spectrum[waves:]
                for q in range(parents):
                    gre = gains[q][0:1, k * 128 : (k + 1) * 128]
                    gim = gains[q][1:2, k * 128 : (k + 1) * 128]
                    at = (q * chunks + k) * 2
                    sums[at] = sums[at] + (gre * sre - gim * sim)
                    sums[at + 1] = sums[at + 1] + (gre * sim + gim * sre)
            return tuple(sums)

        sums = lax.fori_loop(0, group, add_source, sums, unroll=8)
    for q in range(parents):
        for k in range(chunks):
            at = (q * chunks + k) * 2
            re = sums[at].astype(BF16).astype(F32)
            im = sums[at + 1].astype(BF16).astype(F32)
            lanes = slice(k * 128, (k + 1) * 128)
            for c in range(8):
                cos, sin = cos_phase[c : c + 1, lanes], sin_phase[c : c + 1, lanes]
                rows = slice((q * 8 + c) * waves, (q * 8 + c + 1) * waves)
                down_re_ref[rows, lanes] = cos * re + sin * im
                down_im_ref[rows, lanes] = cos * im - sin * re
    imat = imat_ref[...]
    in_re = nt_dot(down_re_ref[...].astype(BF16), imat)
    in_im = nt_dot(down_im_ref[...].astype(BF16), imat)
    incoming = jnp.concatenate([in_re, in_im], axis=1).astype(BF16)
    far = nt_dot(incoming, rad_ref[...])
    factor = TURN / math.sqrt(entries * width) * 2.0 * LEAD * LEAD
    out_ref[...] = near_ref[...] * factor + far.reshape(near_ref.shape)


def per_device(
    currents, positions, radiation, interp_index, interp_weight, child_phase, near_src, trans_src, trans_id,
    trans_count, trans_table
):
    boxes, waves, width = currents.shape
    entries = near_src.shape[1]
    leaf_dirs = radiation.shape[1] // 2
    parent_dirs = child_phase.shape[1]
    parents = boxes // 8
    spectra_rows = parents * parent_dirs // 128
    size = lax.axis_size("dir")
    vmem = pl.BlockSpec(memory_space=pltpu.VMEM)
    smem = pl.BlockSpec(memory_space=pltpu.SMEM)
    hbm = pl.BlockSpec(memory_space=pltpu.HBM)
    params = pltpu.CompilerParams(vmem_limit_bytes=32 * 1024 * 1024)

    def in_hbm(x):
        return pltpu.with_memory_space_constraint(x, pltpu.HBM)

    def shaped(shape, dtype):
        return jax.ShapeDtypeStruct(shape, dtype)

    operands = (currents, positions.transpose(1, 0, 2), radiation, interp_index.T, interp_weight.T, child_phase)
    packet, spectra, imat, cos_phase, sin_phase, rad = pl.pallas_call(
        outgoing_kernel,
        out_shape=(
            shaped((boxes + spectra_rows, 16, width), BF16),
            shaped((spectra_rows, 2 * waves, 128), BF16),
            shaped((leaf_dirs, parent_dirs), BF16),
            shaped((8, parent_dirs), F32),
            shaped((8, parent_dirs), F32),
            shaped(radiation.shape, BF16),
        ),
        in_specs=[hbm] * len(operands),
        out_specs=(vmem,) * 6,
        scratch_shapes=[pltpu.VMEM(x.shape, x.dtype) for x in operands if x is not radiation]
        + [pltpu.SemaphoreType.DMA((len(operands),))],
        compiler_params=params,
        name="outgoing",
    )(*[in_hbm(x) for x in operands])

    before, after = neighbours(packet, ("box", "dir"))
    turned = [
        lax.ppermute(spectra, "dir", [(i, (i + turn) % size) for i in range(size)]) for turn in range(2, size - 1)
    ]
    if size > 2:
        turned.append(lax.ppermute(spectra, "dir", [(0, size - 1), (size - 1, 0)]))

    length = round_up((boxes * entries + 3 * boxes) // 2 + 6 * ITEMS + 2, 128)
    window = 3 * trans_src.shape[0]
    near_scratch = [
        pltpu.VMEM((ITEMS, width, 2 * width), F32),
        pltpu.VMEM((ITEMS, width, 2 * width), F32),
        pltpu.VMEM((ITEMS, width, 2 * width), BF16),
        pltpu.VMEM((ITEMS, width, 2 * width), BF16),
    ]
    own_sum, items, observers, gains = pl.pallas_call(
        own_near_kernel,
        out_shape=(
            shaped((boxes, waves, width), F32),
            shaped((1, length), jnp.int32),
            shaped((boxes, 16, width), BF16),
            shaped((parents, window, 2, parent_dirs), F32),
        ),
        in_specs=[vmem] + [hbm] * 5,
        out_specs=(vmem,) * 4,
        scratch_shapes=[
            pltpu.VMEM(near_src.shape, jnp.int32),
            pltpu.SMEM((1, length), jnp.int32),
            pltpu.SMEM(trans_src.shape, jnp.int32),
            pltpu.SMEM(trans_id.shape, jnp.int32),
            pltpu.SMEM(trans_count.shape, jnp.int32),
            pltpu.VMEM((parents * trans_src.shape[1], 2, parent_dirs), F32),
            pltpu.VMEM((boxes, width, 128), BF16),
        ]
        + near_scratch
        + [pltpu.SemaphoreType.DMA((4,))],
        compiler_params=params,
        name="own_near",
    )(packet, *[in_hbm(x) for x in (near_src, trans_src, trans_id, trans_count, trans_table)])

    group = pl.pallas_call(
        group_kernel,
        out_shape=shaped((size * spectra_rows, 2 * waves, 128), BF16),
        in_specs=[vmem] * (4 + len(turned)),
        out_specs=vmem,
        compiler_params=params,
        name="group",
    )(spectra, before, after, *turned, items)
    group_before, group_after = neighbours(group, "box")

    near = pl.pallas_call(
        functools.partial(rest_near_kernel, entries),
        out_shape=shaped((boxes, waves, width), F32),
        in_specs=[smem] + [vmem] * 5,
        out_specs=vmem,
        scratch_shapes=[
            pltpu.VMEM((3 * boxes, 16, width), BF16),
            pltpu.VMEM((3 * boxes, width, 128), BF16),
        ]
        + near_scratch,
        compiler_params=params,
        name="rest_near",
    )(items, packet, before, after, observers, own_sum)

    return pl.pallas_call(
        functools.partial(incoming_kernel, entries),
        out_shape=shaped((boxes, waves, width), F32),
        in_specs=[vmem] * 9,
        out_specs=vmem,
        scratch_shapes=[
            pltpu.VMEM((boxes * waves, parent_dirs), F32),
            pltpu.VMEM((boxes * waves, parent_dirs), F32),
        ],
        compiler_params=params,
        name="incoming",
    )(group_before, group, group_after, gains, cos_phase, sin_phase, imat, rad, near)


def solution(mesh):
    placed = (
        P(("box", "dir"), None, None),
        P(("box", "dir"), None, None),
        P(),
        P(),
        P(),
        P(),
        P(("box", "dir"), None),
        P("box", None),
        P("box", None),
        P("box"),
        P(),
    )
    return jax.shard_map(
        per_device,
        mesh=mesh,
        in_specs=placed,
        out_specs=P(("box", "dir"), None, None),
        check_vma=False,
    )
```

```python
import functools
import math

import jax
import jax.numpy as jnp
from jax import lax
from jax.experimental import pallas as pl
from jax.experimental.pallas import tpu as pltpu
from jax.sharding import PartitionSpec as P

F32 = jnp.float32
BF16 = jnp.bfloat16

WAVENUMBER = 4.0
OFFSET = 0.5
TURN = WAVENUMBER / (2.0 * math.pi)
S0, S1, S2 = (-0.08849679958812066, 0.5822236432316782, -1.1456733260321648)
LEAD = -70.99877392901621
ROUNDER = 12582912.0
ITEMS = 4
ROWS = 32
OWN_MOST = 4


def round_up(value, step):
    return -(-value // step) * step


def neighbours(x, axis):
    size = lax.axis_size(axis)
    up = [(i, i + 1) for i in range(size - 1)]
    down = [(j, i) for i, j in up]
    return lax.ppermute(x, axis, up), lax.ppermute(x, axis, down)


def split3(x):
    high = x.astype(BF16).astype(F32)
    rest = x - high
    mid = rest.astype(BF16).astype(F32)
    return high, mid, rest - mid


def nt_dot(a, b):
    return lax.dot_general(a, b, (((1,), (1,)), ((), ())), preferred_element_type=F32)


def nn_dot(a, b):
    return jnp.dot(a, b, preferred_element_type=F32)


def code_shifts(boxes, entries):
    count_bits = entries.bit_length()
    box_bits = (boxes - 1).bit_length()
    return count_bits, count_bits + box_bits, 2 * count_bits + box_bits, 2 * (count_bits + box_bits)


def list_items(near_src, base, length, most):
    boxes, entries = near_src.shape
    first_box, second_count, second_box, source = code_shifts(boxes, entries)
    lanes = round_up(3 * boxes, 128)
    local = near_src - base
    local = jnp.where(local < 0, local + 3 * boxes, local)
    lane = lax.broadcasted_iota(jnp.int32, (boxes, lanes), 1)
    box = lax.broadcasted_iota(jnp.int32, (boxes, lanes), 0)
    count = jnp.zeros((boxes, lanes), jnp.int32)
    for e in range(entries):
        count = count + (local[:, e : e + 1] == lane).astype(jnp.int32)
    present = count > 0
    flags = present.astype(F32)
    box_row = lax.broadcasted_iota(jnp.int32, (boxes, boxes), 0)
    box_col = lax.broadcasted_iota(jnp.int32, (boxes, boxes), 1)
    rank = nn_dot((box_col < box_row).astype(F32).astype(BF16), flags.astype(BF16)).astype(jnp.int32)
    items = (jnp.sum(flags, axis=0, keepdims=True).astype(jnp.int32) + 1) >> 1
    own = lax.broadcasted_iota(jnp.int32, (1, lanes), 1) < boxes
    own_items = jnp.where(own, items, 0).astype(F32)
    other_items = jnp.where(own, 0, items).astype(F32)
    row = lax.broadcasted_iota(jnp.int32, (lanes, lanes), 0)
    col = lax.broadcasted_iota(jnp.int32, (lanes, lanes), 1)
    ahead = (row < col).astype(F32).astype(BF16)
    both = jnp.concatenate([own_items, other_items, jnp.zeros((6, lanes), F32)], axis=0).astype(BF16)
    offset = nn_dot(both, ahead).astype(jnp.int32)
    own_total = jnp.sum(own_items, axis=1, keepdims=True).astype(jnp.int32)
    other_total = jnp.sum(other_items, axis=1, keepdims=True).astype(jnp.int32)
    own_place = offset[0:1] + (rank >> 1)
    other_place = jnp.where(lane < boxes, other_total + own_place - most, offset[1:2] + (rank >> 1))
    place = jnp.where((lane < boxes) & (own_place < most), own_place, (length - 3) - other_place)
    place = jnp.where(present, place, -1)
    code = jnp.where(
        (rank & 1) == 0,
        (lane << source) | (box << first_box) | count,
        (box << second_box) | (count << second_count),
    )
    place_t = place.T
    code_t = code.T
    rows = 3 * boxes
    slot = lax.broadcasted_iota(jnp.int32, (rows, length), 1)
    found = jnp.zeros((rows, length), jnp.int32)
    for i in range(boxes):
        hit = place_t[:rows, i : i + 1] == slot
        found = found + jnp.where(hit, code_t[:rows, i : i + 1], 0)
    listed = jnp.sum(found, axis=0, keepdims=True)
    other_total = other_total + jnp.maximum(own_total - most, 0)
    own_total = jnp.minimum(own_total, most)
    at = lax.broadcasted_iota(jnp.int32, (1, length), 1)
    return jnp.where(at == length - 2, own_total, jnp.where(at == length - 1, other_total, listed))


def start_all(copies, sems):
    started = [pltpu.make_async_copy(src, dst, sems.at[k]) for k, (src, dst) in enumerate(copies)]
    for copy in started:
        copy.start()
    return started


def wait_all(started):
    for copy in started:
        copy.wait()


def outgoing_kernel(
    x_hbm, pos_hbm, rad_hbm, idx_hbm, wgt_hbm, phase_hbm, packet_ref, spectra_ref, imat_ref, cos_ref, sin_ref, rad_ref,
    x_ref, pos_ref, idx_ref, wgt_ref, phase_ref, sems
):
    wait_all(
        start_all(
            (
                (x_hbm, x_ref),
                (pos_hbm, pos_ref),
                (rad_hbm, rad_ref),
                (idx_hbm, idx_ref),
                (wgt_hbm, wgt_ref),
                (phase_hbm, phase_ref),
            ),
            sems,
        )
    )
    leaf_dirs, parent_dirs = imat_ref.shape
    boxes, waves, width = x_ref.shape
    chunks = parent_dirs // 128
    x = x_ref[...].astype(F32)
    planes = pos_ref[...].astype(F32)
    at = lax.broadcasted_iota(jnp.int32, (boxes, 16 - waves, width), 1)
    pos = jnp.zeros((boxes, 16 - waves, width), F32)
    for axis in range(3):
        pos = jnp.where(at == axis, planes[axis][:, None, :], pos)
    packet_ref[:boxes] = jnp.concatenate([x, pos], axis=1).astype(BF16)
    column = lax.broadcasted_iota(jnp.int32, (leaf_dirs, parent_dirs), 0)
    imat = jnp.zeros((leaf_dirs, parent_dirs), F32)
    for s in range(idx_ref.shape[0]):
        imat = imat + jnp.where(idx_ref[s : s + 1, :] == column, wgt_ref[s : s + 1, :], 0.0)
    imat = imat.astype(BF16)
    imat_ref[...] = imat
    cos_phase = jnp.cos(phase_ref[...])
    sin_phase = jnp.sin(phase_ref[...])
    cos_ref[...] = cos_phase
    sin_ref[...] = sin_phase
    leaf = nn_dot(x.reshape(boxes * waves, width).astype(BF16), rad_ref[...]).astype(BF16)
    up_re = nn_dot(leaf[:, :leaf_dirs], imat)
    up_im = nn_dot(leaf[:, leaf_dirs:], imat)
    for q in range(boxes // 8):
        re = jnp.zeros((waves, parent_dirs), F32)
        im = jnp.zeros((waves, parent_dirs), F32)
        for c in range(8):
            at = (q * 8 + c) * waves
            ure = up_re[at : at + waves]
            uim = up_im[at : at + waves]
            re = re + (cos_phase[c : c + 1] * ure - sin_phase[c : c + 1] * uim)
            im = im + (sin_phase[c : c + 1] * ure + cos_phase[c : c + 1] * uim)
        both = jnp.concatenate([re, im], axis=0).astype(BF16)
        for k in range(chunks):
            part = both[:, k * 128 : (k + 1) * 128]
            packet_ref[boxes + q * chunks + k] = part
            spectra_ref[q * chunks + k] = part


def group_kernel(own_ref, before_ref, after_ref, *refs):
    *turned_refs, _, group_ref = refs
    size = lax.axis_size("dir")
    rows = own_ref.shape[0]
    boxes = before_ref.shape[0] - rows
    here = lax.axis_index("dir")

    def place(which, value):
        group_ref[pl.ds(lax.rem(which + size, size) * rows, rows)] = value

    place(here - 1, before_ref[boxes:])
    place(here + 1, after_ref[boxes:])
    for turn, ref in zip(range(2, size - 1), turned_refs):
        place(here - turn, ref[...])
    if size > 2:

        @pl.when((here == 0) | (here == size - 1))
        def _():
            place(size - 1 - here, turned_refs[-1][...])

    place(here, own_ref[...])


def features(pos):
    scale = TURN * TURN
    norm = split3(scale * jnp.sum(pos * pos, axis=1, keepdims=True))
    at = lax.broadcasted_iota(jnp.int32, pos.shape, 1)
    first = jnp.where(at < 3, pos, 1.0)
    first = jnp.where(at == 3, norm[0], jnp.where(at == 4, norm[1], jnp.where(at == 5, norm[2], first)))
    second = jnp.where(at == 3, 1.0, pos + pltpu.roll(pos, 4, 1))
    source = jnp.concatenate([first, second], axis=1).astype(BF16)
    cross = split3((-2.0 * scale) * pos)
    first = jnp.where(at < 3, cross[0], 1.0)
    first = jnp.where(at == 6, norm[0], jnp.where(at == 7, norm[1], first))
    second = jnp.where(at == 3, norm[2], cross[1] + pltpu.roll(cross[2], 4, 1))
    return source, jnp.concatenate([first, second], axis=1).astype(BF16)


def turn_sources(source, src_ref, start):
    boxes, rows, width = source.shape
    eye = lax.broadcasted_iota(jnp.int32, (width, width), 0) == lax.broadcasted_iota(jnp.int32, (width, width), 1)
    turned = nt_dot(eye.astype(F32).astype(BF16), source.reshape(boxes * rows, width))
    for b in range(boxes):
        at = b * rows
        lanes = turned[:, at // 128 * 128 : at // 128 * 128 + 128]
        if at % 128:
            lanes = pltpu.roll(lanes, 128 - at % 128, 1)
        src_ref[start + b] = lanes.astype(BF16)


def near_sum(entries, total, item_at, src_ref, win_ref, obs_ref, out_ref, scratch):
    u0_ref, u1_ref, t0_ref, t1_ref = scratch
    boxes, waves, width = out_ref.shape
    first_box, second_count, second_box, source = code_shifts(boxes, entries)
    t1_ref[...] = jnp.zeros(t1_ref.shape, BF16)

    def field(code, low, high):
        return (code >> low) & ((1 << (high - low)) - 1)

    def distances(chunk, g, u_ref):
        code = item_at(chunk * ITEMS + g)
        observers = [obs_ref[field(code, first_box, second_count)], obs_ref[field(code, second_box, source)]]
        u_ref[g] = nn_dot(src_ref[code >> source][:, :16], jnp.concatenate(observers, axis=1))

    def tile(g, u_ref, t_ref):
        for at in range(0, width, ROWS):
            v = jnp.maximum(u_ref[g, at : at + ROWS], 1e-12)
            q = v * lax.rsqrt(v)
            t = q - ((q + ROUNDER) - ROUNDER)
            x = 0.25 - jnp.abs(t)
            z = x * x
            cosine = x * (((z + S2) * z + S1) * z + S0)
            t_ref[g, at : at + ROWS] = (cosine * pltpu.reciprocal(q + OFFSET * TURN, approx=True)).astype(BF16)

    def product(chunk, g, t_ref):
        code = item_at(chunk * ITEMS + g)
        got = nn_dot(win_ref[code >> source], t_ref[g])
        out_ref[field(code, first_box, second_count)] += field(code, 0, first_box).astype(F32) * got[:waves, :width]
        out_ref[field(code, second_box, source)] += field(code, second_count, second_box).astype(F32) * got[:waves, width:]

    def stages(chunk, u_ref, next_u_ref, t_ref, last_t_ref):
        for g in range(ITEMS):
            distances(chunk + 1, g, next_u_ref)
            product(jnp.maximum(chunk - 1, 0), g, last_t_ref)
            tile(g, u_ref, t_ref)

    rounds = (total + (2 * ITEMS - 1)) // (2 * ITEMS)
    for g in range(ITEMS):
        distances(0, g, u0_ref)

    def body(k, carry):
        stages(2 * k, u0_ref, u1_ref, t0_ref, t1_ref)
        stages(2 * k + 1, u1_ref, u0_ref, t1_ref, t0_ref)
        return carry

    lax.fori_loop(0, rounds, body, 0)
    for g in range(ITEMS):
        product(jnp.maximum(2 * rounds - 1, 0), g, t1_ref)


def own_near_kernel(
    own_ref, near_hbm, src_hbm, id_hbm, count_hbm, table_hbm, out_ref, items_ref, obs_ref, src_ref, gain_ref, near_ref,
    list_ref, trans_src_ref, trans_id_ref, trans_count_ref, rows_ref, *scratch
):
    *scratch, sems = scratch
    boxes, waves, width = out_ref.shape
    entries = near_ref.shape[1]
    length = items_ref.shape[1]
    parents, window = gain_ref.shape[:2]
    listed = src_hbm.shape[1]
    near_copy, *list_copies = start_all(
        (
            (near_hbm, near_ref),
            (src_hbm, trans_src_ref),
            (id_hbm, trans_id_ref),
            (count_hbm, trans_count_ref),
        ),
        sems,
    )
    out_ref[...] = jnp.zeros(out_ref.shape, F32)
    gain_ref[...] = jnp.zeros(gain_ref.shape, F32)
    source, observer = features(own_ref[:boxes].astype(F32)[:, 8:16, :])
    turn_sources(source, src_ref, 0)
    obs_ref[...] = observer
    near_copy.wait()
    base = lax.axis_index(("box", "dir")) * boxes
    items_ref[...] = list_items(near_ref[...], base, length, OWN_MOST * boxes)
    send_list = pltpu.make_async_copy(items_ref, list_ref, sems.at[0])
    send_list.start()
    wait_all(list_copies)
    row0 = lax.axis_index("dir") * parents
    for q in range(parents):
        for e in range(listed):
            pltpu.make_async_copy(
                table_hbm.at[trans_id_ref[row0 + q, e]], rows_ref.at[q * listed + e], sems.at[1]
            ).start()
    send_list.wait()
    near_sum(entries, list_ref[0, length - 2], lambda k: list_ref[0, k], src_ref, own_ref, obs_ref, out_ref, scratch)
    pltpu.make_async_copy(rows_ref, rows_ref, sems.at[1]).wait()
    first = (lax.axis_index("box") - 1) * (window // 3)
    for q in range(parents):
        for e in range(listed):
            live = (e < trans_count_ref[row0 + q]).astype(F32)
            s = jnp.clip(trans_src_ref[row0 + q, e] - first, 0, window - 1)
            gain_ref[q, s] += rows_ref[q * listed + e] * live


def rest_near_kernel(
    entries, items_ref, own_ref, before_ref, after_ref, obs_ref, own_src_ref, sum_ref, out_ref, win_ref, src_ref, *scratch
):
    boxes, waves, width = out_ref.shape
    length = items_ref.shape[1]
    for part, ref in ((2, before_ref), (1, after_ref)):
        win_ref[part * boxes : (part + 1) * boxes] = ref[:boxes]
        source, _ = features(ref[:boxes].astype(F32)[:, 8:16, :])
        turn_sources(source, src_ref, part * boxes)
    win_ref[:boxes] = own_ref[:boxes]
    src_ref[:boxes] = own_src_ref[...]
    out_ref[...] = sum_ref[...]
    near_sum(
        entries,
        items_ref[0, length - 1],
        lambda k: items_ref[0, length - 3 - k],
        src_ref,
        win_ref,
        obs_ref,
        out_ref,
        scratch,
    )


def incoming_kernel(
    entries, before_ref, own_ref, after_ref, gain_ref, cos_ref, sin_ref, imat_ref, rad_ref, near_ref, out_ref, down_re_ref,
    down_im_ref
):
    parents, window, _, parent_dirs = gain_ref.shape
    boxes, waves, width = near_ref.shape
    chunks = parent_dirs // 128
    group = window // 3
    cos_phase = cos_ref[...]
    sin_phase = sin_ref[...]
    sums = tuple(jnp.zeros((waves, 128), F32) for _ in range(parents * chunks * 2))
    for part, ref in enumerate((before_ref, own_ref, after_ref)):

        def add_source(s, sums, part=part, ref=ref):
            sums = list(sums)
            gains = [gain_ref[q, part * group + s] for q in range(parents)]
            for k in range(chunks):
                spectrum = ref[s * chunks + k].astype(F32)
                sre, sim = spectrum[:waves], spectrum[waves:]
                for q in range(parents):
                    gre = gains[q][0:1, k * 128 : (k + 1) * 128]
                    gim = gains[q][1:2, k * 128 : (k + 1) * 128]
                    at = (q * chunks + k) * 2
                    sums[at] = sums[at] + (gre * sre - gim * sim)
                    sums[at + 1] = sums[at + 1] + (gre * sim + gim * sre)
            return tuple(sums)

        sums = lax.fori_loop(0, group, add_source, sums, unroll=8)
    for q in range(parents):
        for k in range(chunks):
            at = (q * chunks + k) * 2
            re = sums[at].astype(BF16).astype(F32)
            im = sums[at + 1].astype(BF16).astype(F32)
            lanes = slice(k * 128, (k + 1) * 128)
            for c in range(8):
                cos, sin = cos_phase[c : c + 1, lanes], sin_phase[c : c + 1, lanes]
                rows = slice((q * 8 + c) * waves, (q * 8 + c + 1) * waves)
                down_re_ref[rows, lanes] = cos * re + sin * im
                down_im_ref[rows, lanes] = cos * im - sin * re
    imat = imat_ref[...]
    in_re = nt_dot(down_re_ref[...].astype(BF16), imat)
    in_im = nt_dot(down_im_ref[...].astype(BF16), imat)
    incoming = jnp.concatenate([in_re, in_im], axis=1).astype(BF16)
    far = nt_dot(incoming, rad_ref[...])
    factor = TURN * LEAD / math.sqrt(entries * width)
    out_ref[...] = near_ref[...] * factor + far.reshape(near_ref.shape)


def per_device(
    currents, positions, radiation, interp_index, interp_weight, child_phase, near_src, trans_src, trans_id,
    trans_count, trans_table
):
    boxes, waves, width = currents.shape
    entries = near_src.shape[1]
    leaf_dirs = radiation.shape[1] // 2
    parent_dirs = child_phase.shape[1]
    parents = boxes // 8
    spectra_rows = parents * parent_dirs // 128
    size = lax.axis_size("dir")
    vmem = pl.BlockSpec(memory_space=pltpu.VMEM)
    smem = pl.BlockSpec(memory_space=pltpu.SMEM)
    hbm = pl.BlockSpec(memory_space=pltpu.HBM)
    params = pltpu.CompilerParams(vmem_limit_bytes=32 * 1024 * 1024)

    def in_hbm(x):
        return pltpu.with_memory_space_constraint(x, pltpu.HBM)

    def shaped(shape, dtype):
        return jax.ShapeDtypeStruct(shape, dtype)

    operands = (currents, positions.transpose(1, 0, 2), radiation, interp_index.T, interp_weight.T, child_phase)
    packet, spectra, imat, cos_phase, sin_phase, rad = pl.pallas_call(
        outgoing_kernel,
        out_shape=(
            shaped((boxes + spectra_rows, 16, width), BF16),
            shaped((spectra_rows, 2 * waves, 128), BF16),
            shaped((leaf_dirs, parent_dirs), BF16),
            shaped((8, parent_dirs), F32),
            shaped((8, parent_dirs), F32),
            shaped(radiation.shape, BF16),
        ),
        in_specs=[hbm] * len(operands),
        out_specs=(vmem,) * 6,
        scratch_shapes=[pltpu.VMEM(x.shape, x.dtype) for x in operands if x is not radiation]
        + [pltpu.SemaphoreType.DMA((len(operands),))],
        compiler_params=params,
        name="outgoing",
    )(*[in_hbm(x) for x in operands])

    before, after = neighbours(packet, ("box", "dir"))
    turned = [
        lax.ppermute(spectra, "dir", [(i, (i + turn) % size) for i in range(size)]) for turn in range(2, size - 1)
    ]
    if size > 2:
        turned.append(lax.ppermute(spectra, "dir", [(0, size - 1), (size - 1, 0)]))

    length = round_up((boxes * entries + 3 * boxes) // 2 + 6 * ITEMS + 2, 128)
    window = 3 * trans_src.shape[0]
    near_scratch = [
        pltpu.VMEM((ITEMS, width, 2 * width), F32),
        pltpu.VMEM((ITEMS, width, 2 * width), F32),
        pltpu.VMEM((ITEMS, width, 2 * width), BF16),
        pltpu.VMEM((ITEMS, width, 2 * width), BF16),
    ]
    own_sum, items, observers, sources, gains = pl.pallas_call(
        own_near_kernel,
        out_shape=(
            shaped((boxes, waves, width), F32),
            shaped((1, length), jnp.int32),
            shaped((boxes, 16, width), BF16),
            shaped((boxes, width, 128), BF16),
            shaped((parents, window, 2, parent_dirs), F32),
        ),
        in_specs=[vmem] + [hbm] * 5,
        out_specs=(vmem,) * 5,
        scratch_shapes=[
            pltpu.VMEM(near_src.shape, jnp.int32),
            pltpu.SMEM((1, length), jnp.int32),
            pltpu.SMEM(trans_src.shape, jnp.int32),
            pltpu.SMEM(trans_id.shape, jnp.int32),
            pltpu.SMEM(trans_count.shape, jnp.int32),
            pltpu.VMEM((parents * trans_src.shape[1], 2, parent_dirs), F32),
        ]
        + near_scratch
        + [pltpu.SemaphoreType.DMA((4,))],
        compiler_params=params,
        name="own_near",
    )(packet, *[in_hbm(x) for x in (near_src, trans_src, trans_id, trans_count, trans_table)])

    group = pl.pallas_call(
        group_kernel,
        out_shape=shaped((size * spectra_rows, 2 * waves, 128), BF16),
        in_specs=[vmem] * (4 + len(turned)),
        out_specs=vmem,
        compiler_params=params,
        name="group",
    )(spectra, before, after, *turned, items)
    group_before, group_after = neighbours(group, "box")

    near = pl.pallas_call(
        functools.partial(rest_near_kernel, entries),
        out_shape=shaped((boxes, waves, width), F32),
        in_specs=[smem] + [vmem] * 6,
        out_specs=vmem,
        scratch_shapes=[
            pltpu.VMEM((3 * boxes, 16, width), BF16),
            pltpu.VMEM((3 * boxes, width, 128), BF16),
        ]
        + near_scratch,
        compiler_params=params,
        name="rest_near",
    )(items, packet, before, after, observers, sources, own_sum)

    return pl.pallas_call(
        functools.partial(incoming_kernel, entries),
        out_shape=shaped((boxes, waves, width), F32),
        in_specs=[vmem] * 9,
        out_specs=vmem,
        scratch_shapes=[
            pltpu.VMEM((boxes * waves, parent_dirs), F32),
            pltpu.VMEM((boxes * waves, parent_dirs), F32),
        ],
        compiler_params=params,
        name="incoming",
    )(group_before, group, group_after, gains, cos_phase, sin_phase, imat, rad, near)


def solution(mesh):
    placed = (
        P(("box", "dir"), None, None),
        P(("box", "dir"), None, None),
        P(),
        P(),
        P(),
        P(),
        P(("box", "dir"), None),
        P("box", None),
        P("box", None),
        P("box"),
        P(),
    )
    return jax.shard_map(
        per_device,
        mesh=mesh,
        in_specs=placed,
        out_specs=P(("box", "dir"), None, None),
        check_vma=False,
    )
```

```python
import functools
import math

import jax
import jax.numpy as jnp
from jax import lax
from jax.experimental import pallas as pl
from jax.experimental.pallas import tpu as pltpu
from jax.sharding import PartitionSpec as P

F32 = jnp.float32
BF16 = jnp.bfloat16

WAVENUMBER = 4.0
OFFSET = 0.5
TURN = WAVENUMBER / (2.0 * math.pi)
S0, S1, S2 = (-0.08849679958812066, 0.5822236432316782, -1.1456733260321648)
LEAD = -70.99877392901621
ROUNDER = 12582912.0
ITEMS = 4
ROWS = 32
OWN_MOST = 4


def round_up(value, step):
    return -(-value // step) * step


def swapped(x, axis, pairs):
    return lax.ppermute(x, axis, [way for i, j in pairs for way in ((i, j), (j, i))])


def split3(x):
    high = x.astype(BF16).astype(F32)
    rest = x - high
    mid = rest.astype(BF16).astype(F32)
    return high, mid, rest - mid


def nt_dot(a, b):
    return lax.dot_general(a, b, (((1,), (1,)), ((), ())), preferred_element_type=F32)


def nn_dot(a, b):
    return jnp.dot(a, b, preferred_element_type=F32)


def code_shifts(boxes, entries):
    count_bits = entries.bit_length()
    box_bits = (boxes - 1).bit_length()
    return count_bits, count_bits + box_bits, 2 * count_bits + box_bits, 2 * (count_bits + box_bits)


def list_places(boxes, entries):
    gap = 6 * ITEMS
    most = OWN_MOST * boxes
    cross = most + gap
    end = cross + boxes * ((boxes + 1) // 2) + gap + (boxes * entries + 3 * boxes) // 2 + gap + 3
    return most, cross, round_up(end, 128)


def list_items(near_src, block, here, size):
    boxes, entries = near_src.shape
    most, cross_start, length = list_places(boxes, entries)
    first_box, second_count, second_box, source = code_shifts(boxes, entries)
    lanes = round_up(3 * boxes, 128)
    odd = (here & 1) == 1
    edge = (here == 0) | (here == size - 1)
    local = near_src - block * boxes
    below = local + jnp.where(odd, 2 * boxes, 3 * boxes)
    above = local + jnp.where(odd, boxes, 0)
    local = jnp.where(local < 0, below, jnp.where(local >= boxes, above, local))
    lane = lax.broadcasted_iota(jnp.int32, (boxes, lanes), 1)
    box = lax.broadcasted_iota(jnp.int32, (boxes, lanes), 0)
    count = jnp.zeros((boxes, lanes), jnp.int32)
    for e in range(entries):
        count = count + (local[:, e : e + 1] == lane).astype(jnp.int32)
    present = count > 0
    flags = present.astype(F32)
    box_row = lax.broadcasted_iota(jnp.int32, (boxes, boxes), 0)
    box_col = lax.broadcasted_iota(jnp.int32, (boxes, boxes), 1)
    rank = nn_dot((box_col < box_row).astype(F32).astype(BF16), flags.astype(BF16)).astype(jnp.int32)
    items = (jnp.sum(flags, axis=0, keepdims=True).astype(jnp.int32) + 1) >> 1
    from_own = lane < boxes
    from_cross = (lane >= 2 * boxes) & edge
    own_items = jnp.where(from_own[:1], items, 0).astype(F32)
    cross_items = jnp.where(from_cross[:1], items, 0).astype(F32)
    other_items = jnp.where(from_own[:1] | from_cross[:1], 0, items).astype(F32)
    row = lax.broadcasted_iota(jnp.int32, (lanes, lanes), 0)
    col = lax.broadcasted_iota(jnp.int32, (lanes, lanes), 1)
    ahead = (row < col).astype(F32).astype(BF16)
    lists = jnp.concatenate([own_items, other_items, cross_items, jnp.zeros((5, lanes), F32)], axis=0)
    offset = nn_dot(lists.astype(BF16), ahead).astype(jnp.int32)
    own_total = jnp.sum(own_items, axis=1, keepdims=True).astype(jnp.int32)
    other_total = jnp.sum(other_items, axis=1, keepdims=True).astype(jnp.int32)
    cross_total = jnp.sum(cross_items, axis=1, keepdims=True).astype(jnp.int32)
    half = rank >> 1
    own_place = offset[0:1] + half
    other_place = jnp.where(from_own, other_total + own_place - most, offset[1:2] + half)
    place = jnp.where(from_own & (own_place < most), own_place, (length - 4) - other_place)
    place = jnp.where(from_cross, cross_start + offset[2:3] + half, place)
    place = jnp.where(present, place, -1)
    code = jnp.where(
        (rank & 1) == 0,
        (lane << source) | (box << first_box) | count,
        (box << second_box) | (count << second_count),
    )
    place_t = place.T
    code_t = code.T
    rows = 3 * boxes
    slot = lax.broadcasted_iota(jnp.int32, (rows, length), 1)
    found = jnp.zeros((rows, length), jnp.int32)
    for i in range(boxes):
        hit = place_t[:rows, i : i + 1] == slot
        found = found + jnp.where(hit, code_t[:rows, i : i + 1], 0)
    listed = jnp.sum(found, axis=0, keepdims=True)
    other_total = other_total + jnp.maximum(own_total - most, 0)
    own_total = jnp.minimum(own_total, most)
    at = lax.broadcasted_iota(jnp.int32, (1, length), 1)
    listed = jnp.where(at == length - 3, own_total, listed)
    return jnp.where(at == length - 2, other_total, jnp.where(at == length - 1, cross_total, listed))


def start_all(copies, sems):
    started = [pltpu.make_async_copy(src, dst, sems.at[k]) for k, (src, dst) in enumerate(copies)]
    for copy in started:
        copy.start()
    return started


def wait_all(started):
    for copy in started:
        copy.wait()


def outgoing_kernel(
    x_hbm, pos_hbm, rad_hbm, idx_hbm, wgt_hbm, phase_hbm, packet_ref, spectra_ref, imat_ref, cos_ref, sin_ref, rad_ref,
    x_ref, pos_ref, idx_ref, wgt_ref, phase_ref, sems
):
    wait_all(
        start_all(
            (
                (x_hbm, x_ref),
                (pos_hbm, pos_ref),
                (rad_hbm, rad_ref),
                (idx_hbm, idx_ref),
                (wgt_hbm, wgt_ref),
                (phase_hbm, phase_ref),
            ),
            sems,
        )
    )
    leaf_dirs, parent_dirs = imat_ref.shape
    boxes, waves, width = x_ref.shape
    chunks = parent_dirs // 128
    x = x_ref[...].astype(F32)
    planes = pos_ref[...].astype(F32)
    at = lax.broadcasted_iota(jnp.int32, (boxes, 16 - waves, width), 1)
    pos = jnp.zeros((boxes, 16 - waves, width), F32)
    for axis in range(3):
        pos = jnp.where(at == axis, planes[axis][:, None, :], pos)
    packet_ref[:boxes] = jnp.concatenate([x, pos], axis=1).astype(BF16)
    column = lax.broadcasted_iota(jnp.int32, (leaf_dirs, parent_dirs), 0)
    imat = jnp.zeros((leaf_dirs, parent_dirs), F32)
    for s in range(idx_ref.shape[0]):
        imat = imat + jnp.where(idx_ref[s : s + 1, :] == column, wgt_ref[s : s + 1, :], 0.0)
    imat = imat.astype(BF16)
    imat_ref[...] = imat
    cos_phase = jnp.cos(phase_ref[...])
    sin_phase = jnp.sin(phase_ref[...])
    cos_ref[...] = cos_phase
    sin_ref[...] = sin_phase
    leaf = nn_dot(x.reshape(boxes * waves, width).astype(BF16), rad_ref[...]).astype(BF16)
    up_re = nn_dot(leaf[:, :leaf_dirs], imat)
    up_im = nn_dot(leaf[:, leaf_dirs:], imat)
    for q in range(boxes // 8):
        re = jnp.zeros((waves, parent_dirs), F32)
        im = jnp.zeros((waves, parent_dirs), F32)
        for c in range(8):
            at = (q * 8 + c) * waves
            ure = up_re[at : at + waves]
            uim = up_im[at : at + waves]
            re = re + (cos_phase[c : c + 1] * ure - sin_phase[c : c + 1] * uim)
            im = im + (sin_phase[c : c + 1] * ure + cos_phase[c : c + 1] * uim)
        both = jnp.concatenate([re, im], axis=0).astype(BF16)
        for k in range(chunks):
            part = both[:, k * 128 : (k + 1) * 128]
            packet_ref[boxes + q * chunks + k] = part
            spectra_ref[q * chunks + k] = part


def carries_packet(step):
    return step & (step + 1) == 0


def group_kernel(own_ref, *refs):
    *step_refs, _, group_ref = refs
    size = lax.axis_size("dir")
    rows = own_ref.shape[0]
    here = lax.axis_index("dir")
    group_ref[pl.ds(here * rows, rows)] = own_ref[...]
    for step, ref in enumerate(step_refs, 1):
        group_ref[pl.ds((here ^ step) * rows, rows)] = ref[ref.shape[0] - rows :]
    group_ref[size * rows :] = step_refs[-1][: step_refs[-1].shape[0] - rows]


def features(pos):
    scale = TURN * TURN
    norm = split3(scale * jnp.sum(pos * pos, axis=1, keepdims=True))
    at = lax.broadcasted_iota(jnp.int32, pos.shape, 1)
    first = jnp.where(at < 3, pos, 1.0)
    first = jnp.where(at == 3, norm[0], jnp.where(at == 4, norm[1], jnp.where(at == 5, norm[2], first)))
    second = jnp.where(at == 3, 1.0, pos + pltpu.roll(pos, 4, 1))
    source = jnp.concatenate([first, second], axis=1).astype(BF16)
    cross = split3((-2.0 * scale) * pos)
    first = jnp.where(at < 3, cross[0], 1.0)
    first = jnp.where(at == 6, norm[0], jnp.where(at == 7, norm[1], first))
    second = jnp.where(at == 3, norm[2], cross[1] + pltpu.roll(cross[2], 4, 1))
    return source, jnp.concatenate([first, second], axis=1).astype(BF16)


def turn_sources(source, src_ref, start):
    boxes, rows, width = source.shape
    eye = lax.broadcasted_iota(jnp.int32, (width, width), 0) == lax.broadcasted_iota(jnp.int32, (width, width), 1)
    turned = nt_dot(eye.astype(F32).astype(BF16), source.reshape(boxes * rows, width))
    for b in range(boxes):
        at = b * rows
        lanes = turned[:, at // 128 * 128 : at // 128 * 128 + 128]
        if at % 128:
            lanes = pltpu.roll(lanes, 128 - at % 128, 1)
        src_ref[start + b] = lanes.astype(BF16)


def near_sum(entries, total, item_at, first_source, src_ref, win_ref, obs_ref, out_ref, scratch):
    u0_ref, u1_ref, t0_ref, t1_ref = scratch
    boxes, waves, width = out_ref.shape
    first_box, second_count, second_box, source = code_shifts(boxes, entries)
    t1_ref[...] = jnp.zeros(t1_ref.shape, BF16)

    def field(code, low, high):
        return (code >> low) & ((1 << (high - low)) - 1)

    def source_at(code):
        return jnp.maximum((code >> source) - first_source, 0) if first_source else code >> source

    def distances(chunk, g, u_ref):
        code = item_at(chunk * ITEMS + g)
        observers = [obs_ref[field(code, first_box, second_count)], obs_ref[field(code, second_box, source)]]
        u_ref[g] = nn_dot(src_ref[source_at(code)][:, :16], jnp.concatenate(observers, axis=1))

    def tile(g, u_ref, t_ref):
        for at in range(0, width, ROWS):
            v = jnp.maximum(u_ref[g, at : at + ROWS], 1e-12)
            q = v * lax.rsqrt(v)
            t = q - ((q + ROUNDER) - ROUNDER)
            x = 0.25 - jnp.abs(t)
            z = x * x
            cosine = x * (((z + S2) * z + S1) * z + S0)
            t_ref[g, at : at + ROWS] = (cosine * pltpu.reciprocal(q + OFFSET * TURN, approx=True)).astype(BF16)

    def product(chunk, g, t_ref):
        code = item_at(chunk * ITEMS + g)
        got = nn_dot(win_ref[source_at(code)], t_ref[g])
        out_ref[field(code, first_box, second_count)] += field(code, 0, first_box).astype(F32) * got[:waves, :width]
        out_ref[field(code, second_box, source)] += field(code, second_count, second_box).astype(F32) * got[:waves, width:]

    def stages(chunk, u_ref, next_u_ref, t_ref, last_t_ref):
        for g in range(ITEMS):
            distances(chunk + 1, g, next_u_ref)
            product(jnp.maximum(chunk - 1, 0), g, last_t_ref)
            tile(g, u_ref, t_ref)

    rounds = (total + (2 * ITEMS - 1)) // (2 * ITEMS)
    for g in range(ITEMS):
        distances(0, g, u0_ref)

    def body(k, carry):
        stages(2 * k, u0_ref, u1_ref, t0_ref, t1_ref)
        stages(2 * k + 1, u1_ref, u0_ref, t1_ref, t0_ref)
        return carry

    lax.fori_loop(0, rounds, body, 0)
    for g in range(ITEMS):
        product(jnp.maximum(2 * rounds - 1, 0), g, t1_ref)


def own_near_kernel(
    own_ref, near_hbm, src_hbm, id_hbm, count_hbm, table_hbm, out_ref, items_ref, obs_ref, src_ref, gain_ref, near_ref,
    list_ref, trans_src_ref, trans_id_ref, trans_count_ref, rows_ref, *scratch
):
    *scratch, sems = scratch
    boxes, waves, width = out_ref.shape
    entries = near_ref.shape[1]
    length = items_ref.shape[1]
    parents, window = gain_ref.shape[:2]
    listed = src_hbm.shape[1]
    near_copy, *list_copies = start_all(
        (
            (near_hbm, near_ref),
            (src_hbm, trans_src_ref),
            (id_hbm, trans_id_ref),
            (count_hbm, trans_count_ref),
        ),
        sems,
    )
    out_ref[...] = jnp.zeros(out_ref.shape, F32)
    gain_ref[...] = jnp.zeros(gain_ref.shape, F32)
    source, observer = features(own_ref[:boxes].astype(F32)[:, 8:16, :])
    turn_sources(source, src_ref, 0)
    obs_ref[...] = observer
    near_copy.wait()
    block = lax.axis_index(("box", "dir"))
    items_ref[...] = list_items(near_ref[...], block, lax.axis_index("dir"), lax.axis_size("dir"))
    send_list = pltpu.make_async_copy(items_ref, list_ref, sems.at[0])
    send_list.start()
    wait_all(list_copies)
    row0 = lax.axis_index("dir") * parents
    for q in range(parents):
        for e in range(listed):
            pltpu.make_async_copy(
                table_hbm.at[trans_id_ref[row0 + q, e]], rows_ref.at[q * listed + e], sems.at[1]
            ).start()
    send_list.wait()
    near_sum(entries, list_ref[0, length - 3], lambda k: list_ref[0, k], 0, src_ref, own_ref, obs_ref, out_ref, scratch)
    pltpu.make_async_copy(rows_ref, rows_ref, sems.at[1]).wait()
    first = (lax.axis_index("box") - 1) * (window // 3)
    for q in range(parents):
        for e in range(listed):
            live = (e < trans_count_ref[row0 + q]).astype(F32)
            s = jnp.clip(trans_src_ref[row0 + q, e] - first, 0, window - 1)
            gain_ref[q, s] += rows_ref[q * listed + e] * live


def group_near_kernel(entries, items_ref, own_ref, *refs):
    *step_refs, obs_ref, own_src_ref, sum_ref, out_ref, win_ref, src_ref, u0_ref, u1_ref, t0_ref, t1_ref = refs
    boxes, waves, width = out_ref.shape
    length = items_ref.shape[1]
    here = lax.axis_index("dir")
    other_side = jnp.where((here & 1) == 0, here - 1, here + 1)

    def take(ref, part):
        win_ref[part * boxes : (part + 1) * boxes] = ref[:boxes]
        source, _ = features(ref[:boxes].astype(F32)[:, 8:16, :])
        turn_sources(source, src_ref, part * boxes)

    win_ref[:boxes] = own_ref[:boxes]
    src_ref[:boxes] = own_src_ref[...]
    take(step_refs[0], 1)
    for k, ref in enumerate(step_refs[1:], 2):
        pl.when((here ^ ((1 << k) - 1)) == other_side)(functools.partial(take, ref, 2))
    out_ref[...] = sum_ref[...]
    near_sum(
        entries,
        items_ref[0, length - 2],
        lambda k: items_ref[0, length - 4 - k],
        0,
        src_ref,
        win_ref,
        obs_ref,
        out_ref,
        (u0_ref, u1_ref, t0_ref, t1_ref),
    )


def incoming_kernel(
    entries, items_ref, even_ref, own_ref, odd_ref, gain_ref, cos_ref, sin_ref, imat_ref, rad_ref, obs_ref, near_ref, out_ref,
    sum_ref, win_ref, src_ref, down_re_ref, down_im_ref, *scratch
):
    parents, window, _, parent_dirs = gain_ref.shape
    boxes, waves, width = near_ref.shape
    chunks = parent_dirs // 128
    group = window // 3
    cross_start = list_places(boxes, entries)[1]
    cross_total = items_ref[0, items_ref.shape[1] - 1]
    odd_box = lax.axis_index("box") & 1
    sum_ref[...] = near_ref[...]

    @pl.when(cross_total > 0)
    def _():
        first = jnp.where(lax.axis_index("dir") == 0, 1, 0)

        @pl.when(first == odd_box)
        def _():
            win_ref[...] = even_ref[even_ref.shape[0] - boxes :]

        @pl.when(first != odd_box)
        def _():
            win_ref[...] = odd_ref[odd_ref.shape[0] - boxes :]

        source, _ = features(win_ref[...].astype(F32)[:, 8:16, :])
        turn_sources(source, src_ref, 0)
        near_sum(
            entries,
            cross_total,
            lambda k: items_ref[0, cross_start + k],
            2 * boxes,
            src_ref,
            win_ref,
            obs_ref,
            sum_ref,
            scratch,
        )

    cos_phase = cos_ref[...]
    sin_phase = sin_ref[...]
    sums = tuple(jnp.zeros((waves, 128), F32) for _ in range(parents * chunks * 2))
    for part, ref in ((2 - 2 * odd_box, even_ref), (1, own_ref), (2 * odd_box, odd_ref)):

        def add_source(s, sums, part=part, ref=ref):
            sums = list(sums)
            gains = [gain_ref[q, part * group + s] for q in range(parents)]
            for k in range(chunks):
                spectrum = ref[s * chunks + k].astype(F32)
                sre, sim = spectrum[:waves], spectrum[waves:]
                for q in range(parents):
                    gre = gains[q][0:1, k * 128 : (k + 1) * 128]
                    gim = gains[q][1:2, k * 128 : (k + 1) * 128]
                    at = (q * chunks + k) * 2
                    sums[at] = sums[at] + (gre * sre - gim * sim)
                    sums[at + 1] = sums[at + 1] + (gre * sim + gim * sre)
            return tuple(sums)

        sums = lax.fori_loop(0, group, add_source, sums, unroll=8)
    for q in range(parents):
        for k in range(chunks):
            at = (q * chunks + k) * 2
            re = sums[at].astype(BF16).astype(F32)
            im = sums[at + 1].astype(BF16).astype(F32)
            lanes = slice(k * 128, (k + 1) * 128)
            for c in range(8):
                cos, sin = cos_phase[c : c + 1, lanes], sin_phase[c : c + 1, lanes]
                rows = slice((q * 8 + c) * waves, (q * 8 + c + 1) * waves)
                down_re_ref[rows, lanes] = cos * re + sin * im
                down_im_ref[rows, lanes] = cos * im - sin * re
    imat = imat_ref[...]
    in_re = nt_dot(down_re_ref[...].astype(BF16), imat)
    in_im = nt_dot(down_im_ref[...].astype(BF16), imat)
    incoming = jnp.concatenate([in_re, in_im], axis=1).astype(BF16)
    far = nt_dot(incoming, rad_ref[...])
    factor = TURN * LEAD / math.sqrt(entries * width)
    out_ref[...] = sum_ref[...] * factor + far.reshape(near_ref.shape)


def per_device(
    currents, positions, radiation, interp_index, interp_weight, child_phase, near_src, trans_src, trans_id,
    trans_count, trans_table
):
    boxes, waves, width = currents.shape
    entries = near_src.shape[1]
    leaf_dirs = radiation.shape[1] // 2
    parent_dirs = child_phase.shape[1]
    parents = boxes // 8
    spectra_rows = parents * parent_dirs // 128
    size = lax.axis_size("dir")
    vmem = pl.BlockSpec(memory_space=pltpu.VMEM)
    smem = pl.BlockSpec(memory_space=pltpu.SMEM)
    hbm = pl.BlockSpec(memory_space=pltpu.HBM)
    params = pltpu.CompilerParams(vmem_limit_bytes=32 * 1024 * 1024)

    def in_hbm(x):
        return pltpu.with_memory_space_constraint(x, pltpu.HBM)

    def shaped(shape, dtype):
        return jax.ShapeDtypeStruct(shape, dtype)

    operands = (currents, positions.transpose(1, 0, 2), radiation, interp_index.T, interp_weight.T, child_phase)
    packet, spectra, imat, cos_phase, sin_phase, rad = pl.pallas_call(
        outgoing_kernel,
        out_shape=(
            shaped((boxes + spectra_rows, 16, width), BF16),
            shaped((spectra_rows, 2 * waves, 128), BF16),
            shaped((leaf_dirs, parent_dirs), BF16),
            shaped((8, parent_dirs), F32),
            shaped((8, parent_dirs), F32),
            shaped(radiation.shape, BF16),
        ),
        in_specs=[hbm] * len(operands),
        out_specs=(vmem,) * 6,
        scratch_shapes=[pltpu.VMEM(x.shape, x.dtype) for x in operands if x is not radiation]
        + [pltpu.SemaphoreType.DMA((len(operands),))],
        compiler_params=params,
        name="outgoing",
    )(*[in_hbm(x) for x in operands])

    steps = []
    for step in range(1, size):
        pairs = [(i, i ^ step) for i in range(size) if i < i ^ step]
        steps.append(swapped(packet if carries_packet(step) else spectra, "dir", pairs))

    length = list_places(boxes, entries)[2]
    window = 3 * trans_src.shape[0]
    near_scratch = [
        pltpu.VMEM((ITEMS, width, 2 * width), F32),
        pltpu.VMEM((ITEMS, width, 2 * width), F32),
        pltpu.VMEM((ITEMS, width, 2 * width), BF16),
        pltpu.VMEM((ITEMS, width, 2 * width), BF16),
    ]
    own_sum, items, observers, sources, gains = pl.pallas_call(
        own_near_kernel,
        out_shape=(
            shaped((boxes, waves, width), F32),
            shaped((1, length), jnp.int32),
            shaped((boxes, 16, width), BF16),
            shaped((boxes, width, 128), BF16),
            shaped((parents, window, 2, parent_dirs), F32),
        ),
        in_specs=[vmem] + [hbm] * 5,
        out_specs=(vmem,) * 5,
        scratch_shapes=[
            pltpu.VMEM(near_src.shape, jnp.int32),
            pltpu.SMEM((1, length), jnp.int32),
            pltpu.SMEM(trans_src.shape, jnp.int32),
            pltpu.SMEM(trans_id.shape, jnp.int32),
            pltpu.SMEM(trans_count.shape, jnp.int32),
            pltpu.VMEM((parents * trans_src.shape[1], 2, parent_dirs), F32),
        ]
        + near_scratch
        + [pltpu.SemaphoreType.DMA((4,))],
        compiler_params=params,
        name="own_near",
    )(packet, *[in_hbm(x) for x in (near_src, trans_src, trans_id, trans_count, trans_table)])

    group = pl.pallas_call(
        group_kernel,
        out_shape=shaped((size * spectra_rows + boxes, 2 * waves, 128), BF16),
        in_specs=[vmem] * (2 + len(steps)),
        out_specs=vmem,
        compiler_params=params,
        name="group",
    )(spectra, *steps, items)
    groups = lax.axis_size("box")
    group_even = swapped(group, "box", [(i, i + 1) for i in range(0, groups - 1, 2)])
    group_odd = swapped(group, "box", [(i, i + 1) for i in range(1, groups - 1, 2)])

    packets = [x for step, x in enumerate(steps, 1) if carries_packet(step)]
    near = pl.pallas_call(
        functools.partial(group_near_kernel, entries),
        out_shape=shaped((boxes, waves, width), F32),
        in_specs=[smem] + [vmem] * (4 + len(packets)),
        out_specs=vmem,
        scratch_shapes=[
            pltpu.VMEM((3 * boxes, 16, width), BF16),
            pltpu.VMEM((3 * boxes, width, 128), BF16),
        ]
        + near_scratch,
        compiler_params=params,
        name="group_near",
    )(items, packet, *packets, observers, sources, own_sum)

    return pl.pallas_call(
        functools.partial(incoming_kernel, entries),
        out_shape=shaped((boxes, waves, width), F32),
        in_specs=[smem] + [vmem] * 10,
        out_specs=vmem,
        scratch_shapes=[
            pltpu.VMEM((boxes, waves, width), F32),
            pltpu.VMEM((boxes, 16, width), BF16),
            pltpu.VMEM((boxes, width, 128), BF16),
            pltpu.VMEM((boxes * waves, parent_dirs), F32),
            pltpu.VMEM((boxes * waves, parent_dirs), F32),
        ]
        + near_scratch,
        compiler_params=params,
        name="incoming",
    )(items, group_even, group, group_odd, gains, cos_phase, sin_phase, imat, rad, observers, near)


def solution(mesh):
    placed = (
        P(("box", "dir"), None, None),
        P(("box", "dir"), None, None),
        P(),
        P(),
        P(),
        P(),
        P(("box", "dir"), None),
        P("box", None),
        P("box", None),
        P("box"),
        P(),
    )
    return jax.shard_map(
        per_device,
        mesh=mesh,
        in_specs=placed,
        out_specs=P(("box", "dir"), None, None),
        check_vma=False,
    )
```

```python
import functools
import math

import jax
import jax.numpy as jnp
from jax import lax
from jax.experimental import pallas as pl
from jax.experimental.pallas import tpu as pltpu
from jax.sharding import PartitionSpec as P

F32 = jnp.float32
BF16 = jnp.bfloat16

WAVENUMBER = 4.0
OFFSET = 0.5
TURN = WAVENUMBER / (2.0 * math.pi)
S0, S1, S2 = (-0.08849679958812066, 0.5822236432316782, -1.1456733260321648)
LEAD = -70.99877392901621
ITEMS = 4
ROWS = 32
OWN_MOST = 4


def round_up(value, step):
    return -(-value // step) * step


def swapped(x, axis, pairs):
    return lax.ppermute(x, axis, [way for i, j in pairs for way in ((i, j), (j, i))])


def split3(x):
    high = x.astype(BF16).astype(F32)
    rest = x - high
    mid = rest.astype(BF16).astype(F32)
    return high, mid, rest - mid


def nt_dot(a, b):
    return lax.dot_general(a, b, (((1,), (1,)), ((), ())), preferred_element_type=F32)


def nn_dot(a, b):
    return jnp.dot(a, b, preferred_element_type=F32)


def code_shifts(boxes, entries):
    count_bits = entries.bit_length()
    box_bits = (boxes - 1).bit_length()
    return count_bits, count_bits + box_bits, 2 * count_bits + box_bits, 2 * (count_bits + box_bits)


def list_places(boxes, entries):
    gap = 6 * ITEMS
    most = OWN_MOST * boxes
    cross = most + gap
    end = cross + boxes * ((boxes + 1) // 2) + gap + (boxes * entries + 3 * boxes) // 2 + gap + 3
    return most, cross, round_up(end, 128)


def list_items(near_src, block, here, size):
    boxes, entries = near_src.shape
    most, cross_start, length = list_places(boxes, entries)
    first_box, second_count, second_box, source = code_shifts(boxes, entries)
    lanes = round_up(3 * boxes, 128)
    odd = (here & 1) == 1
    edge = (here == 0) | (here == size - 1)
    local = near_src - block * boxes
    below = local + jnp.where(odd, 2 * boxes, 3 * boxes)
    above = local + jnp.where(odd, boxes, 0)
    local = jnp.where(local < 0, below, jnp.where(local >= boxes, above, local))
    lane = lax.broadcasted_iota(jnp.int32, (boxes, lanes), 1)
    box = lax.broadcasted_iota(jnp.int32, (boxes, lanes), 0)
    count = jnp.zeros((boxes, lanes), jnp.int32)
    for e in range(entries):
        count = count + (local[:, e : e + 1] == lane).astype(jnp.int32)
    present = count > 0
    flags = present.astype(F32)
    box_row = lax.broadcasted_iota(jnp.int32, (boxes, boxes), 0)
    box_col = lax.broadcasted_iota(jnp.int32, (boxes, boxes), 1)
    rank = nn_dot((box_col < box_row).astype(F32).astype(BF16), flags.astype(BF16)).astype(jnp.int32)
    items = (jnp.sum(flags, axis=0, keepdims=True).astype(jnp.int32) + 1) >> 1
    from_own = lane < boxes
    from_cross = (lane >= 2 * boxes) & edge
    own_items = jnp.where(from_own[:1], items, 0).astype(F32)
    cross_items = jnp.where(from_cross[:1], items, 0).astype(F32)
    other_items = jnp.where(from_own[:1] | from_cross[:1], 0, items).astype(F32)
    row = lax.broadcasted_iota(jnp.int32, (lanes, lanes), 0)
    col = lax.broadcasted_iota(jnp.int32, (lanes, lanes), 1)
    ahead = (row < col).astype(F32).astype(BF16)
    lists = jnp.concatenate([own_items, other_items, cross_items, jnp.zeros((5, lanes), F32)], axis=0)
    offset = nn_dot(lists.astype(BF16), ahead).astype(jnp.int32)
    own_total = jnp.sum(own_items, axis=1, keepdims=True).astype(jnp.int32)
    other_total = jnp.sum(other_items, axis=1, keepdims=True).astype(jnp.int32)
    cross_total = jnp.sum(cross_items, axis=1, keepdims=True).astype(jnp.int32)
    half = rank >> 1
    own_place = offset[0:1] + half
    other_place = jnp.where(from_own, other_total + own_place - most, offset[1:2] + half)
    place = jnp.where(from_own & (own_place < most), own_place, (length - 4) - other_place)
    place = jnp.where(from_cross, cross_start + offset[2:3] + half, place)
    place = jnp.where(present, place, -1)
    code = jnp.where(
        (rank & 1) == 0,
        (lane << source) | (box << first_box) | count,
        (box << second_box) | (count << second_count),
    )
    place_t = place.T
    code_t = code.T
    rows = 3 * boxes
    slot = lax.broadcasted_iota(jnp.int32, (rows, length), 1)
    found = jnp.zeros((rows, length), jnp.int32)
    for i in range(boxes):
        hit = place_t[:rows, i : i + 1] == slot
        found = found + jnp.where(hit, code_t[:rows, i : i + 1], 0)
    listed = jnp.sum(found, axis=0, keepdims=True)
    other_total = other_total + jnp.maximum(own_total - most, 0)
    own_total = jnp.minimum(own_total, most)
    at = lax.broadcasted_iota(jnp.int32, (1, length), 1)
    listed = jnp.where(at == length - 3, own_total, listed)
    return jnp.where(at == length - 2, other_total, jnp.where(at == length - 1, cross_total, listed))


def start_all(copies, sems):
    started = [pltpu.make_async_copy(src, dst, sems.at[k]) for k, (src, dst) in enumerate(copies)]
    for copy in started:
        copy.start()
    return started


def wait_all(started):
    for copy in started:
        copy.wait()


def outgoing_kernel(
    x_hbm, pos_hbm, rad_hbm, idx_hbm, wgt_hbm, phase_hbm, packet_ref, spectra_ref, imat_ref, cos_ref, sin_ref, rad_ref,
    x_ref, pos_ref, idx_ref, wgt_ref, phase_ref, sems
):
    wait_all(
        start_all(
            (
                (x_hbm, x_ref),
                (pos_hbm, pos_ref),
                (rad_hbm, rad_ref),
                (idx_hbm, idx_ref),
                (wgt_hbm, wgt_ref),
                (phase_hbm, phase_ref),
            ),
            sems,
        )
    )
    leaf_dirs, parent_dirs = imat_ref.shape
    boxes, waves, width = x_ref.shape
    chunks = parent_dirs // 128
    x = x_ref[...].astype(F32)
    planes = pos_ref[...].astype(F32)
    at = lax.broadcasted_iota(jnp.int32, (boxes, 16 - waves, width), 1)
    pos = jnp.zeros((boxes, 16 - waves, width), F32)
    for axis in range(3):
        pos = jnp.where(at == axis, planes[axis][:, None, :], pos)
    packet_ref[:boxes] = jnp.concatenate([x, pos], axis=1).astype(BF16)
    column = lax.broadcasted_iota(jnp.int32, (leaf_dirs, parent_dirs), 0)
    imat = jnp.zeros((leaf_dirs, parent_dirs), F32)
    for s in range(idx_ref.shape[0]):
        imat = imat + jnp.where(idx_ref[s : s + 1, :] == column, wgt_ref[s : s + 1, :], 0.0)
    imat = imat.astype(BF16)
    imat_ref[...] = imat
    cos_phase = jnp.cos(phase_ref[...])
    sin_phase = jnp.sin(phase_ref[...])
    cos_ref[...] = cos_phase
    sin_ref[...] = sin_phase
    leaf = nn_dot(x.reshape(boxes * waves, width).astype(BF16), rad_ref[...]).astype(BF16)
    up_re = nn_dot(leaf[:, :leaf_dirs], imat)
    up_im = nn_dot(leaf[:, leaf_dirs:], imat)
    for q in range(boxes // 8):
        re = jnp.zeros((waves, parent_dirs), F32)
        im = jnp.zeros((waves, parent_dirs), F32)
        for c in range(8):
            at = (q * 8 + c) * waves
            ure = up_re[at : at + waves]
            uim = up_im[at : at + waves]
            re = re + (cos_phase[c : c + 1] * ure - sin_phase[c : c + 1] * uim)
            im = im + (sin_phase[c : c + 1] * ure + cos_phase[c : c + 1] * uim)
        both = jnp.concatenate([re, im], axis=0).astype(BF16)
        for k in range(chunks):
            part = both[:, k * 128 : (k + 1) * 128]
            packet_ref[boxes + q * chunks + k] = part
            spectra_ref[q * chunks + k] = part


def carries_packet(step):
    return step & (step + 1) == 0


def group_kernel(own_ref, *refs):
    *step_refs, _, group_ref = refs
    size = lax.axis_size("dir")
    rows = own_ref.shape[0]
    here = lax.axis_index("dir")
    group_ref[pl.ds(here * rows, rows)] = own_ref[...]
    for step, ref in enumerate(step_refs, 1):
        group_ref[pl.ds((here ^ step) * rows, rows)] = ref[ref.shape[0] - rows :]
    group_ref[size * rows :] = step_refs[-1][: step_refs[-1].shape[0] - rows]


def features(pos):
    scale = TURN * TURN
    norm = split3(scale * jnp.sum(pos * pos, axis=1, keepdims=True))
    at = lax.broadcasted_iota(jnp.int32, pos.shape, 1)
    first = jnp.where(at < 3, pos, 1.0)
    first = jnp.where(at == 3, norm[0], jnp.where(at == 4, norm[1], jnp.where(at == 5, norm[2], first)))
    second = jnp.where(at == 3, 1.0, pos + pltpu.roll(pos, 4, 1))
    source = jnp.concatenate([first, second], axis=1).astype(BF16)
    cross = split3((-2.0 * scale) * pos)
    first = jnp.where(at < 3, cross[0], 1.0)
    first = jnp.where(at == 6, norm[0], jnp.where(at == 7, norm[1], first))
    second = jnp.where(at == 3, norm[2], cross[1] + pltpu.roll(cross[2], 4, 1))
    return source, jnp.concatenate([first, second], axis=1).astype(BF16)


def turn_sources(source, src_ref, start):
    boxes, rows, width = source.shape
    eye = lax.broadcasted_iota(jnp.int32, (width, width), 0) == lax.broadcasted_iota(jnp.int32, (width, width), 1)
    turned = nt_dot(eye.astype(F32).astype(BF16), source.reshape(boxes * rows, width))
    for b in range(boxes):
        at = b * rows
        lanes = turned[:, at // 128 * 128 : at // 128 * 128 + 128]
        if at % 128:
            lanes = pltpu.roll(lanes, 128 - at % 128, 1)
        src_ref[start + b] = lanes.astype(BF16)


def near_sum(entries, total, item_at, first_source, src_ref, win_ref, obs_ref, out_ref, scratch):
    u0_ref, u1_ref, t0_ref, t1_ref = scratch
    boxes, waves, width = out_ref.shape
    first_box, second_count, second_box, source = code_shifts(boxes, entries)
    t1_ref[...] = jnp.zeros(t1_ref.shape, BF16)

    def field(code, low, high):
        return (code >> low) & ((1 << (high - low)) - 1)

    def source_at(code):
        return jnp.maximum((code >> source) - first_source, 0) if first_source else code >> source

    def distances(chunk, g, u_ref):
        code = item_at(chunk * ITEMS + g)
        observers = [obs_ref[field(code, first_box, second_count)], obs_ref[field(code, second_box, source)]]
        u_ref[g] = nn_dot(src_ref[source_at(code)][:, :16], jnp.concatenate(observers, axis=1))

    def tile(g, u_ref, t_ref):
        for at in range(0, width, ROWS):
            v = jnp.maximum(u_ref[g, at : at + ROWS], 1e-12)
            q = v * lax.rsqrt(v)
            t = q - jnp.round(q)
            x = 0.25 - jnp.abs(t)
            z = x * x
            cosine = x * (((z + S2) * z + S1) * z + S0)
            t_ref[g, at : at + ROWS] = (cosine * pltpu.reciprocal(q + OFFSET * TURN, approx=True)).astype(BF16)

    def product(chunk, g, t_ref):
        code = item_at(chunk * ITEMS + g)
        got = nn_dot(win_ref[source_at(code)], t_ref[g])
        out_ref[field(code, first_box, second_count)] += field(code, 0, first_box).astype(F32) * got[:waves, :width]
        out_ref[field(code, second_box, source)] += field(code, second_count, second_box).astype(F32) * got[:waves, width:]

    def stages(chunk, u_ref, next_u_ref, t_ref, last_t_ref):
        for g in range(ITEMS):
            distances(chunk + 1, g, next_u_ref)
            product(jnp.maximum(chunk - 1, 0), g, last_t_ref)
            tile(g, u_ref, t_ref)

    rounds = (total + (2 * ITEMS - 1)) // (2 * ITEMS)
    for g in range(ITEMS):
        distances(0, g, u0_ref)

    def body(k, carry):
        stages(2 * k, u0_ref, u1_ref, t0_ref, t1_ref)
        stages(2 * k + 1, u1_ref, u0_ref, t1_ref, t0_ref)
        return carry

    lax.fori_loop(0, rounds, body, 0)
    for g in range(ITEMS):
        product(jnp.maximum(2 * rounds - 1, 0), g, t1_ref)


def own_near_kernel(
    own_ref, near_hbm, src_hbm, id_hbm, count_hbm, table_hbm, out_ref, items_ref, obs_ref, src_ref, gain_ref, near_ref,
    list_ref, trans_src_ref, trans_id_ref, trans_count_ref, rows_ref, *scratch
):
    *scratch, sems = scratch
    boxes, waves, width = out_ref.shape
    entries = near_ref.shape[1]
    length = items_ref.shape[1]
    parents, window = gain_ref.shape[:2]
    listed = src_hbm.shape[1]
    near_copy, *list_copies = start_all(
        (
            (near_hbm, near_ref),
            (src_hbm, trans_src_ref),
            (id_hbm, trans_id_ref),
            (count_hbm, trans_count_ref),
        ),
        sems,
    )
    out_ref[...] = jnp.zeros(out_ref.shape, F32)
    gain_ref[...] = jnp.zeros(gain_ref.shape, F32)
    source, observer = features(own_ref[:boxes].astype(F32)[:, 8:16, :])
    turn_sources(source, src_ref, 0)
    obs_ref[...] = observer
    near_copy.wait()
    block = lax.axis_index(("box", "dir"))
    items_ref[...] = list_items(near_ref[...], block, lax.axis_index("dir"), lax.axis_size("dir"))
    send_list = pltpu.make_async_copy(items_ref, list_ref, sems.at[0])
    send_list.start()
    wait_all(list_copies)
    row0 = lax.axis_index("dir") * parents
    for q in range(parents):
        for e in range(listed):
            pltpu.make_async_copy(
                table_hbm.at[trans_id_ref[row0 + q, e]], rows_ref.at[q * listed + e], sems.at[1]
            ).start()
    send_list.wait()
    near_sum(entries, list_ref[0, length - 3], lambda k: list_ref[0, k], 0, src_ref, own_ref, obs_ref, out_ref, scratch)
    pltpu.make_async_copy(rows_ref, rows_ref, sems.at[1]).wait()
    first = (lax.axis_index("box") - 1) * (window // 3)
    for q in range(parents):
        for e in range(listed):
            live = (e < trans_count_ref[row0 + q]).astype(F32)
            s = jnp.clip(trans_src_ref[row0 + q, e] - first, 0, window - 1)
            gain_ref[q, s] += rows_ref[q * listed + e] * live


def group_near_kernel(entries, items_ref, own_ref, *refs):
    *step_refs, obs_ref, own_src_ref, sum_ref, out_ref, win_ref, src_ref, u0_ref, u1_ref, t0_ref, t1_ref = refs
    boxes, waves, width = out_ref.shape
    length = items_ref.shape[1]
    here = lax.axis_index("dir")
    other_side = jnp.where((here & 1) == 0, here - 1, here + 1)

    def take(ref, part):
        win_ref[part * boxes : (part + 1) * boxes] = ref[:boxes]
        source, _ = features(ref[:boxes].astype(F32)[:, 8:16, :])
        turn_sources(source, src_ref, part * boxes)

    win_ref[:boxes] = own_ref[:boxes]
    src_ref[:boxes] = own_src_ref[...]
    take(step_refs[0], 1)
    for k, ref in enumerate(step_refs[1:], 2):
        pl.when((here ^ ((1 << k) - 1)) == other_side)(functools.partial(take, ref, 2))
    out_ref[...] = sum_ref[...]
    near_sum(
        entries,
        items_ref[0, length - 2],
        lambda k: items_ref[0, length - 4 - k],
        0,
        src_ref,
        win_ref,
        obs_ref,
        out_ref,
        (u0_ref, u1_ref, t0_ref, t1_ref),
    )


def incoming_kernel(
    entries, items_ref, even_ref, own_ref, odd_ref, gain_ref, cos_ref, sin_ref, imat_ref, rad_ref, obs_ref, near_ref, out_ref,
    sum_ref, win_ref, src_ref, down_re_ref, down_im_ref, *scratch
):
    parents, window, _, parent_dirs = gain_ref.shape
    boxes, waves, width = near_ref.shape
    chunks = parent_dirs // 128
    group = window // 3
    cross_start = list_places(boxes, entries)[1]
    cross_total = items_ref[0, items_ref.shape[1] - 1]
    odd_box = lax.axis_index("box") & 1
    sum_ref[...] = near_ref[...]

    @pl.when(cross_total > 0)
    def _():
        first = jnp.where(lax.axis_index("dir") == 0, 1, 0)

        @pl.when(first == odd_box)
        def _():
            win_ref[...] = even_ref[even_ref.shape[0] - boxes :]

        @pl.when(first != odd_box)
        def _():
            win_ref[...] = odd_ref[odd_ref.shape[0] - boxes :]

        source, _ = features(win_ref[...].astype(F32)[:, 8:16, :])
        turn_sources(source, src_ref, 0)
        near_sum(
            entries,
            cross_total,
            lambda k: items_ref[0, cross_start + k],
            2 * boxes,
            src_ref,
            win_ref,
            obs_ref,
            sum_ref,
            scratch,
        )

    cos_phase = cos_ref[...]
    sin_phase = sin_ref[...]
    sums = tuple(jnp.zeros((waves, 128), F32) for _ in range(parents * chunks * 2))
    for part, ref in ((2 - 2 * odd_box, even_ref), (1, own_ref), (2 * odd_box, odd_ref)):

        def add_source(s, sums, part=part, ref=ref):
            sums = list(sums)
            gains = [gain_ref[q, part * group + s] for q in range(parents)]
            for k in range(chunks):
                spectrum = ref[s * chunks + k].astype(F32)
                sre, sim = spectrum[:waves], spectrum[waves:]
                for q in range(parents):
                    gre = gains[q][0:1, k * 128 : (k + 1) * 128]
                    gim = gains[q][1:2, k * 128 : (k + 1) * 128]
                    at = (q * chunks + k) * 2
                    sums[at] = sums[at] + (gre * sre - gim * sim)
                    sums[at + 1] = sums[at + 1] + (gre * sim + gim * sre)
            return tuple(sums)

        sums = lax.fori_loop(0, group, add_source, sums, unroll=8)
    for q in range(parents):
        for k in range(chunks):
            at = (q * chunks + k) * 2
            re = sums[at].astype(BF16).astype(F32)
            im = sums[at + 1].astype(BF16).astype(F32)
            lanes = slice(k * 128, (k + 1) * 128)
            for c in range(8):
                cos, sin = cos_phase[c : c + 1, lanes], sin_phase[c : c + 1, lanes]
                rows = slice((q * 8 + c) * waves, (q * 8 + c + 1) * waves)
                down_re_ref[rows, lanes] = cos * re + sin * im
                down_im_ref[rows, lanes] = cos * im - sin * re
    imat = imat_ref[...]
    in_re = nt_dot(down_re_ref[...].astype(BF16), imat)
    in_im = nt_dot(down_im_ref[...].astype(BF16), imat)
    incoming = jnp.concatenate([in_re, in_im], axis=1).astype(BF16)
    far = nt_dot(incoming, rad_ref[...])
    factor = TURN * LEAD / math.sqrt(entries * width)
    out_ref[...] = sum_ref[...] * factor + far.reshape(near_ref.shape)


def per_device(
    currents, positions, radiation, interp_index, interp_weight, child_phase, near_src, trans_src, trans_id,
    trans_count, trans_table
):
    boxes, waves, width = currents.shape
    entries = near_src.shape[1]
    leaf_dirs = radiation.shape[1] // 2
    parent_dirs = child_phase.shape[1]
    parents = boxes // 8
    spectra_rows = parents * parent_dirs // 128
    size = lax.axis_size("dir")
    vmem = pl.BlockSpec(memory_space=pltpu.VMEM)
    smem = pl.BlockSpec(memory_space=pltpu.SMEM)
    hbm = pl.BlockSpec(memory_space=pltpu.HBM)
    params = pltpu.CompilerParams(vmem_limit_bytes=32 * 1024 * 1024)

    def in_hbm(x):
        return pltpu.with_memory_space_constraint(x, pltpu.HBM)

    def shaped(shape, dtype):
        return jax.ShapeDtypeStruct(shape, dtype)

    operands = (currents, positions.transpose(1, 0, 2), radiation, interp_index.T, interp_weight.T, child_phase)
    packet, spectra, imat, cos_phase, sin_phase, rad = pl.pallas_call(
        outgoing_kernel,
        out_shape=(
            shaped((boxes + spectra_rows, 16, width), BF16),
            shaped((spectra_rows, 2 * waves, 128), BF16),
            shaped((leaf_dirs, parent_dirs), BF16),
            shaped((8, parent_dirs), F32),
            shaped((8, parent_dirs), F32),
            shaped(radiation.shape, BF16),
        ),
        in_specs=[hbm] * len(operands),
        out_specs=(vmem,) * 6,
        scratch_shapes=[pltpu.VMEM(x.shape, x.dtype) for x in operands if x is not radiation]
        + [pltpu.SemaphoreType.DMA((len(operands),))],
        compiler_params=params,
        name="outgoing",
    )(*[in_hbm(x) for x in operands])

    steps = []
    for step in range(1, size):
        pairs = [(i, i ^ step) for i in range(size) if i < i ^ step]
        steps.append(swapped(packet if carries_packet(step) else spectra, "dir", pairs))

    length = list_places(boxes, entries)[2]
    window = 3 * trans_src.shape[0]
    near_scratch = [
        pltpu.VMEM((ITEMS, width, 2 * width), F32),
        pltpu.VMEM((ITEMS, width, 2 * width), F32),
        pltpu.VMEM((ITEMS, width, 2 * width), BF16),
        pltpu.VMEM((ITEMS, width, 2 * width), BF16),
    ]
    own_sum, items, observers, sources, gains = pl.pallas_call(
        own_near_kernel,
        out_shape=(
            shaped((boxes, waves, width), F32),
            shaped((1, length), jnp.int32),
            shaped((boxes, 16, width), BF16),
            shaped((boxes, width, 128), BF16),
            shaped((parents, window, 2, parent_dirs), F32),
        ),
        in_specs=[vmem] + [hbm] * 5,
        out_specs=(vmem,) * 5,
        scratch_shapes=[
            pltpu.VMEM(near_src.shape, jnp.int32),
            pltpu.SMEM((1, length), jnp.int32),
            pltpu.SMEM(trans_src.shape, jnp.int32),
            pltpu.SMEM(trans_id.shape, jnp.int32),
            pltpu.SMEM(trans_count.shape, jnp.int32),
            pltpu.VMEM((parents * trans_src.shape[1], 2, parent_dirs), F32),
        ]
        + near_scratch
        + [pltpu.SemaphoreType.DMA((4,))],
        compiler_params=params,
        name="own_near",
    )(packet, *[in_hbm(x) for x in (near_src, trans_src, trans_id, trans_count, trans_table)])

    group = pl.pallas_call(
        group_kernel,
        out_shape=shaped((size * spectra_rows + boxes, 2 * waves, 128), BF16),
        in_specs=[vmem] * (2 + len(steps)),
        out_specs=vmem,
        compiler_params=params,
        name="group",
    )(spectra, *steps, items)
    groups = lax.axis_size("box")
    group_even = swapped(group, "box", [(i, i + 1) for i in range(0, groups - 1, 2)])
    group_odd = swapped(group, "box", [(i, i + 1) for i in range(1, groups - 1, 2)])

    packets = [x for step, x in enumerate(steps, 1) if carries_packet(step)]
    near = pl.pallas_call(
        functools.partial(group_near_kernel, entries),
        out_shape=shaped((boxes, waves, width), F32),
        in_specs=[smem] + [vmem] * (4 + len(packets)),
        out_specs=vmem,
        scratch_shapes=[
            pltpu.VMEM((3 * boxes, 16, width), BF16),
            pltpu.VMEM((3 * boxes, width, 128), BF16),
        ]
        + near_scratch,
        compiler_params=params,
        name="group_near",
    )(items, packet, *packets, observers, sources, own_sum)

    return pl.pallas_call(
        functools.partial(incoming_kernel, entries),
        out_shape=shaped((boxes, waves, width), F32),
        in_specs=[smem] + [vmem] * 10,
        out_specs=vmem,
        scratch_shapes=[
            pltpu.VMEM((boxes, waves, width), F32),
            pltpu.VMEM((boxes, 16, width), BF16),
            pltpu.VMEM((boxes, width, 128), BF16),
            pltpu.VMEM((boxes * waves, parent_dirs), F32),
            pltpu.VMEM((boxes * waves, parent_dirs), F32),
        ]
        + near_scratch,
        compiler_params=params,
        name="incoming",
    )(items, group_even, group, group_odd, gains, cos_phase, sin_phase, imat, rad, observers, near)


def solution(mesh):
    placed = (
        P(("box", "dir"), None, None),
        P(("box", "dir"), None, None),
        P(),
        P(),
        P(),
        P(),
        P(("box", "dir"), None),
        P("box", None),
        P("box", None),
        P("box"),
        P(),
    )
    return jax.shard_map(
        per_device,
        mesh=mesh,
        in_specs=placed,
        out_specs=P(("box", "dir"), None, None),
        check_vma=False,
    )
```

```python
import functools
import math

import jax
import jax.numpy as jnp
from jax import lax
from jax.experimental import pallas as pl
from jax.experimental.pallas import tpu as pltpu
from jax.sharding import PartitionSpec as P

F32 = jnp.float32
BF16 = jnp.bfloat16

WAVENUMBER = 4.0
OFFSET = 0.5
TURN = WAVENUMBER / (2.0 * math.pi)
S0, S1, S2 = (-0.08849679958812066, 0.5822236432316782, -1.1456733260321648)
LEAD = -70.99877392901621
ITEMS = 4
ROWS = 32
OWN_MOST = 4


def round_up(value, step):
    return -(-value // step) * step


def swapped(x, axis, pairs):
    return lax.ppermute(x, axis, [way for i, j in pairs for way in ((i, j), (j, i))])


def split3(x):
    high = x.astype(BF16).astype(F32)
    rest = x - high
    mid = rest.astype(BF16).astype(F32)
    return high, mid, rest - mid


def nt_dot(a, b):
    return lax.dot_general(a, b, (((1,), (1,)), ((), ())), preferred_element_type=F32)


def nn_dot(a, b):
    return jnp.dot(a, b, preferred_element_type=F32)


def code_shifts(boxes, entries):
    count_bits = entries.bit_length()
    box_bits = (boxes - 1).bit_length()
    return count_bits, count_bits + box_bits, 2 * count_bits + box_bits, 2 * (count_bits + box_bits)


def list_places(boxes, entries):
    gap = 6 * ITEMS
    most = OWN_MOST * boxes
    cross = most + gap
    end = cross + boxes * ((boxes + 1) // 2) + gap + (boxes * entries + 3 * boxes) // 2 + gap + 3
    return most, cross, round_up(end, 128)


def list_items(near_src, block, here, size):
    boxes, entries = near_src.shape
    most, cross_start, length = list_places(boxes, entries)
    first_box, second_count, second_box, source = code_shifts(boxes, entries)
    lanes = round_up(3 * boxes, 128)
    odd = (here & 1) == 1
    edge = (here == 0) | (here == size - 1)
    local = near_src - block * boxes
    below = local + jnp.where(odd, 2 * boxes, 3 * boxes)
    above = local + jnp.where(odd, boxes, 0)
    local = jnp.where(local < 0, below, jnp.where(local >= boxes, above, local))
    lane = lax.broadcasted_iota(jnp.int32, (boxes, lanes), 1)
    box = lax.broadcasted_iota(jnp.int32, (boxes, lanes), 0)
    count = jnp.zeros((boxes, lanes), jnp.int32)
    for e in range(entries):
        count = count + (local[:, e : e + 1] == lane).astype(jnp.int32)
    present = count > 0
    flags = present.astype(F32)
    box_row = lax.broadcasted_iota(jnp.int32, (boxes, boxes), 0)
    box_col = lax.broadcasted_iota(jnp.int32, (boxes, boxes), 1)
    rank = nn_dot((box_col < box_row).astype(F32).astype(BF16), flags.astype(BF16)).astype(jnp.int32)
    items = (jnp.sum(flags, axis=0, keepdims=True).astype(jnp.int32) + 1) >> 1
    from_own = lane < boxes
    from_cross = (lane >= 2 * boxes) & edge
    own_items = jnp.where(from_own[:1], items, 0).astype(F32)
    cross_items = jnp.where(from_cross[:1], items, 0).astype(F32)
    other_items = jnp.where(from_own[:1] | from_cross[:1], 0, items).astype(F32)
    row = lax.broadcasted_iota(jnp.int32, (lanes, lanes), 0)
    col = lax.broadcasted_iota(jnp.int32, (lanes, lanes), 1)
    ahead = (row < col).astype(F32).astype(BF16)
    lists = jnp.concatenate([own_items, other_items, cross_items, jnp.zeros((5, lanes), F32)], axis=0)
    offset = nn_dot(lists.astype(BF16), ahead).astype(jnp.int32)
    own_total = jnp.sum(own_items, axis=1, keepdims=True).astype(jnp.int32)
    other_total = jnp.sum(other_items, axis=1, keepdims=True).astype(jnp.int32)
    cross_total = jnp.sum(cross_items, axis=1, keepdims=True).astype(jnp.int32)
    half = rank >> 1
    own_place = offset[0:1] + half
    other_place = jnp.where(from_own, other_total + own_place - most, offset[1:2] + half)
    place = jnp.where(from_own & (own_place < most), own_place, (length - 4) - other_place)
    place = jnp.where(from_cross, cross_start + offset[2:3] + half, place)
    place = jnp.where(present, place, -1)
    code = jnp.where(
        (rank & 1) == 0,
        (lane << source) | (box << first_box) | count,
        (box << second_box) | (count << second_count),
    )
    place_t = place.T
    code_t = code.T
    rows = 3 * boxes
    slot = lax.broadcasted_iota(jnp.int32, (rows, length), 1)
    found = jnp.zeros((rows, length), jnp.int32)
    for i in range(boxes):
        hit = place_t[:rows, i : i + 1] == slot
        found = found + jnp.where(hit, code_t[:rows, i : i + 1], 0)
    listed = jnp.sum(found, axis=0, keepdims=True)
    other_total = other_total + jnp.maximum(own_total - most, 0)
    own_total = jnp.minimum(own_total, most)
    at = lax.broadcasted_iota(jnp.int32, (1, length), 1)
    listed = jnp.where(at == length - 3, own_total, listed)
    return jnp.where(at == length - 2, other_total, jnp.where(at == length - 1, cross_total, listed))


def start_all(copies, sems):
    started = [pltpu.make_async_copy(src, dst, sems.at[k]) for k, (src, dst) in enumerate(copies)]
    for copy in started:
        copy.start()
    return started


def wait_all(started):
    for copy in started:
        copy.wait()


def outgoing_kernel(
    x_hbm, pos_hbm, rad_hbm, idx_hbm, wgt_hbm, phase_hbm, packet_ref, spectra_ref, imat_ref, cos_ref, sin_ref, rad_ref,
    x_ref, pos_ref, idx_ref, wgt_ref, phase_ref, sems
):
    wait_all(
        start_all(
            (
                (x_hbm, x_ref),
                (pos_hbm, pos_ref),
                (rad_hbm, rad_ref),
                (idx_hbm, idx_ref),
                (wgt_hbm, wgt_ref),
                (phase_hbm, phase_ref),
            ),
            sems,
        )
    )
    leaf_dirs, parent_dirs = imat_ref.shape
    boxes, waves, width = x_ref.shape
    chunks = parent_dirs // 128
    x = x_ref[...].astype(F32)
    planes = pos_ref[...].astype(F32)
    at = lax.broadcasted_iota(jnp.int32, (boxes, 16 - waves, width), 1)
    pos = jnp.zeros((boxes, 16 - waves, width), F32)
    for axis in range(3):
        pos = jnp.where(at == axis, planes[axis][:, None, :], pos)
    packet_ref[:boxes] = jnp.concatenate([x, pos], axis=1).astype(BF16)
    column = lax.broadcasted_iota(jnp.int32, (leaf_dirs, parent_dirs), 0)
    imat = jnp.zeros((leaf_dirs, parent_dirs), F32)
    for s in range(idx_ref.shape[0]):
        imat = imat + jnp.where(idx_ref[s : s + 1, :] == column, wgt_ref[s : s + 1, :], 0.0)
    imat = imat.astype(BF16)
    imat_ref[...] = imat
    cos_phase = jnp.cos(phase_ref[...])
    sin_phase = jnp.sin(phase_ref[...])
    cos_ref[...] = cos_phase
    sin_ref[...] = sin_phase
    leaf = nn_dot(x.reshape(boxes * waves, width).astype(BF16), rad_ref[...]).astype(BF16)
    up_re = nn_dot(leaf[:, :leaf_dirs], imat)
    up_im = nn_dot(leaf[:, leaf_dirs:], imat)
    for q in range(boxes // 8):
        re = jnp.zeros((waves, parent_dirs), F32)
        im = jnp.zeros((waves, parent_dirs), F32)
        for c in range(8):
            at = (q * 8 + c) * waves
            ure = up_re[at : at + waves]
            uim = up_im[at : at + waves]
            re = re + (cos_phase[c : c + 1] * ure - sin_phase[c : c + 1] * uim)
            im = im + (sin_phase[c : c + 1] * ure + cos_phase[c : c + 1] * uim)
        both = jnp.concatenate([re, im], axis=0).astype(BF16)
        for k in range(chunks):
            part = both[:, k * 128 : (k + 1) * 128]
            packet_ref[boxes + q * chunks + k] = part
            spectra_ref[q * chunks + k] = part


def carries_packet(step):
    return step & (step + 1) == 0


def group_kernel(own_ref, *refs):
    *step_refs, _, group_ref = refs
    size = lax.axis_size("dir")
    rows = own_ref.shape[0]
    here = lax.axis_index("dir")
    group_ref[pl.ds(here * rows, rows)] = own_ref[...]
    for step, ref in enumerate(step_refs, 1):
        group_ref[pl.ds((here ^ step) * rows, rows)] = ref[ref.shape[0] - rows :]
    group_ref[size * rows :] = step_refs[-1][: step_refs[-1].shape[0] - rows]


def features(pos):
    scale = TURN * TURN
    norm = split3(scale * jnp.sum(pos * pos, axis=1, keepdims=True))
    at = lax.broadcasted_iota(jnp.int32, pos.shape, 1)
    first = jnp.where(at < 3, pos, 1.0)
    first = jnp.where(at == 3, norm[0], jnp.where(at == 4, norm[1], jnp.where(at == 5, norm[2], first)))
    second = jnp.where(at == 3, 1.0, pos + pltpu.roll(pos, 4, 1))
    source = jnp.concatenate([first, second], axis=1).astype(BF16)
    cross = split3((-2.0 * scale) * pos)
    first = jnp.where(at < 3, cross[0], 1.0)
    first = jnp.where(at == 6, norm[0], jnp.where(at == 7, norm[1], first))
    second = jnp.where(at == 3, norm[2], cross[1] + pltpu.roll(cross[2], 4, 1))
    return source, jnp.concatenate([first, second], axis=1).astype(BF16)


def turn_sources(source, src_ref, start):
    boxes, rows, width = source.shape
    eye = lax.broadcasted_iota(jnp.int32, (width, width), 0) == lax.broadcasted_iota(jnp.int32, (width, width), 1)
    turned = nt_dot(eye.astype(F32).astype(BF16), source.reshape(boxes * rows, width))
    for b in range(boxes):
        at = b * rows
        lanes = turned[:, at // 128 * 128 : at // 128 * 128 + 128]
        if at % 128:
            lanes = pltpu.roll(lanes, 128 - at % 128, 1)
        src_ref[start + b] = lanes.astype(BF16)


def near_sum(entries, total, item_at, first_source, src_ref, win_ref, obs_ref, out_ref, scratch):
    u0_ref, u1_ref, t0_ref, t1_ref = scratch
    boxes, waves, width = out_ref.shape
    first_box, second_count, second_box, source = code_shifts(boxes, entries)
    t1_ref[...] = jnp.zeros(t1_ref.shape, BF16)

    def field(code, low, high):
        return (code >> low) & ((1 << (high - low)) - 1)

    def source_at(code):
        return jnp.maximum((code >> source) - first_source, 0) if first_source else code >> source

    def distances(chunk, g, u_ref):
        code = item_at(chunk * ITEMS + g)
        observers = [obs_ref[field(code, first_box, second_count)], obs_ref[field(code, second_box, source)]]
        u_ref[g] = nn_dot(src_ref[source_at(code)][:, :16], jnp.concatenate(observers, axis=1))

    def tile(g, u_ref, t_ref):
        for at in range(0, width, ROWS):
            q = pltpu.reciprocal(lax.rsqrt(jnp.abs(u_ref[g, at : at + ROWS])), approx=True)
            t = q - jnp.round(q)
            x = 0.25 - jnp.abs(t)
            z = x * x
            cosine = x * (((z + S2) * z + S1) * z + S0)
            t_ref[g, at : at + ROWS] = (cosine * pltpu.reciprocal(q + OFFSET * TURN, approx=True)).astype(BF16)

    def product(chunk, g, t_ref):
        code = item_at(chunk * ITEMS + g)
        got = nn_dot(win_ref[source_at(code)], t_ref[g])
        out_ref[field(code, first_box, second_count)] += field(code, 0, first_box).astype(F32) * got[:waves, :width]
        out_ref[field(code, second_box, source)] += field(code, second_count, second_box).astype(F32) * got[:waves, width:]

    def stages(chunk, u_ref, next_u_ref, t_ref, last_t_ref):
        for g in range(ITEMS):
            distances(chunk + 1, g, next_u_ref)
            product(jnp.maximum(chunk - 1, 0), g, last_t_ref)
            tile(g, u_ref, t_ref)

    rounds = (total + (2 * ITEMS - 1)) // (2 * ITEMS)
    for g in range(ITEMS):
        distances(0, g, u0_ref)

    def body(k, carry):
        stages(2 * k, u0_ref, u1_ref, t0_ref, t1_ref)
        stages(2 * k + 1, u1_ref, u0_ref, t1_ref, t0_ref)
        return carry

    lax.fori_loop(0, rounds, body, 0)
    for g in range(ITEMS):
        product(jnp.maximum(2 * rounds - 1, 0), g, t1_ref)


def own_near_kernel(
    own_ref, near_hbm, src_hbm, id_hbm, count_hbm, table_hbm, out_ref, items_ref, obs_ref, src_ref, gain_ref, near_ref,
    list_ref, trans_src_ref, trans_id_ref, trans_count_ref, rows_ref, *scratch
):
    *scratch, sems = scratch
    boxes, waves, width = out_ref.shape
    entries = near_ref.shape[1]
    length = items_ref.shape[1]
    parents, window = gain_ref.shape[:2]
    listed = src_hbm.shape[1]
    near_copy, *list_copies = start_all(
        (
            (near_hbm, near_ref),
            (src_hbm, trans_src_ref),
            (id_hbm, trans_id_ref),
            (count_hbm, trans_count_ref),
        ),
        sems,
    )
    out_ref[...] = jnp.zeros(out_ref.shape, F32)
    gain_ref[...] = jnp.zeros(gain_ref.shape, F32)
    source, observer = features(own_ref[:boxes].astype(F32)[:, 8:16, :])
    turn_sources(source, src_ref, 0)
    obs_ref[...] = observer
    near_copy.wait()
    block = lax.axis_index(("box", "dir"))
    items_ref[...] = list_items(near_ref[...], block, lax.axis_index("dir"), lax.axis_size("dir"))
    send_list = pltpu.make_async_copy(items_ref, list_ref, sems.at[0])
    send_list.start()
    wait_all(list_copies)
    row0 = lax.axis_index("dir") * parents
    for q in range(parents):
        for e in range(listed):
            pltpu.make_async_copy(
                table_hbm.at[trans_id_ref[row0 + q, e]], rows_ref.at[q * listed + e], sems.at[1]
            ).start()
    send_list.wait()
    near_sum(entries, list_ref[0, length - 3], lambda k: list_ref[0, k], 0, src_ref, own_ref, obs_ref, out_ref, scratch)
    pltpu.make_async_copy(rows_ref, rows_ref, sems.at[1]).wait()
    first = (lax.axis_index("box") - 1) * (window // 3)
    for q in range(parents):
        for e in range(listed):
            live = (e < trans_count_ref[row0 + q]).astype(F32)
            s = jnp.clip(trans_src_ref[row0 + q, e] - first, 0, window - 1)
            gain_ref[q, s] += rows_ref[q * listed + e] * live


def group_near_kernel(entries, items_ref, own_ref, *refs):
    *step_refs, obs_ref, own_src_ref, sum_ref, out_ref, win_ref, src_ref, u0_ref, u1_ref, t0_ref, t1_ref = refs
    boxes, waves, width = out_ref.shape
    length = items_ref.shape[1]
    here = lax.axis_index("dir")
    other_side = jnp.where((here & 1) == 0, here - 1, here + 1)

    def take(ref, part):
        win_ref[part * boxes : (part + 1) * boxes] = ref[:boxes]
        source, _ = features(ref[:boxes].astype(F32)[:, 8:16, :])
        turn_sources(source, src_ref, part * boxes)

    win_ref[:boxes] = own_ref[:boxes]
    src_ref[:boxes] = own_src_ref[...]
    take(step_refs[0], 1)
    for k, ref in enumerate(step_refs[1:], 2):
        pl.when((here ^ ((1 << k) - 1)) == other_side)(functools.partial(take, ref, 2))
    out_ref[...] = sum_ref[...]
    near_sum(
        entries,
        items_ref[0, length - 2],
        lambda k: items_ref[0, length - 4 - k],
        0,
        src_ref,
        win_ref,
        obs_ref,
        out_ref,
        (u0_ref, u1_ref, t0_ref, t1_ref),
    )


def incoming_kernel(
    entries, items_ref, even_ref, own_ref, odd_ref, gain_ref, cos_ref, sin_ref, imat_ref, rad_ref, obs_ref, near_ref, out_ref,
    sum_ref, win_ref, src_ref, down_re_ref, down_im_ref, *scratch
):
    parents, window, _, parent_dirs = gain_ref.shape
    boxes, waves, width = near_ref.shape
    chunks = parent_dirs // 128
    group = window // 3
    cross_start = list_places(boxes, entries)[1]
    cross_total = items_ref[0, items_ref.shape[1] - 1]
    odd_box = lax.axis_index("box") & 1
    sum_ref[...] = near_ref[...]

    @pl.when(cross_total > 0)
    def _():
        first = jnp.where(lax.axis_index("dir") == 0, 1, 0)

        @pl.when(first == odd_box)
        def _():
            win_ref[...] = even_ref[even_ref.shape[0] - boxes :]

        @pl.when(first != odd_box)
        def _():
            win_ref[...] = odd_ref[odd_ref.shape[0] - boxes :]

        source, _ = features(win_ref[...].astype(F32)[:, 8:16, :])
        turn_sources(source, src_ref, 0)
        near_sum(
            entries,
            cross_total,
            lambda k: items_ref[0, cross_start + k],
            2 * boxes,
            src_ref,
            win_ref,
            obs_ref,
            sum_ref,
            scratch,
        )

    cos_phase = cos_ref[...]
    sin_phase = sin_ref[...]
    sums = tuple(jnp.zeros((waves, 128), F32) for _ in range(parents * chunks * 2))
    for part, ref in ((2 - 2 * odd_box, even_ref), (1, own_ref), (2 * odd_box, odd_ref)):

        def add_source(s, sums, part=part, ref=ref):
            sums = list(sums)
            gains = [gain_ref[q, part * group + s] for q in range(parents)]
            for k in range(chunks):
                spectrum = ref[s * chunks + k].astype(F32)
                sre, sim = spectrum[:waves], spectrum[waves:]
                for q in range(parents):
                    gre = gains[q][0:1, k * 128 : (k + 1) * 128]
                    gim = gains[q][1:2, k * 128 : (k + 1) * 128]
                    at = (q * chunks + k) * 2
                    sums[at] = sums[at] + (gre * sre - gim * sim)
                    sums[at + 1] = sums[at + 1] + (gre * sim + gim * sre)
            return tuple(sums)

        sums = lax.fori_loop(0, group, add_source, sums, unroll=8)
    for q in range(parents):
        for k in range(chunks):
            at = (q * chunks + k) * 2
            re = sums[at].astype(BF16).astype(F32)
            im = sums[at + 1].astype(BF16).astype(F32)
            lanes = slice(k * 128, (k + 1) * 128)
            for c in range(8):
                cos, sin = cos_phase[c : c + 1, lanes], sin_phase[c : c + 1, lanes]
                rows = slice((q * 8 + c) * waves, (q * 8 + c + 1) * waves)
                down_re_ref[rows, lanes] = cos * re + sin * im
                down_im_ref[rows, lanes] = cos * im - sin * re
    imat = imat_ref[...]
    in_re = nt_dot(down_re_ref[...].astype(BF16), imat)
    in_im = nt_dot(down_im_ref[...].astype(BF16), imat)
    incoming = jnp.concatenate([in_re, in_im], axis=1).astype(BF16)
    far = nt_dot(incoming, rad_ref[...])
    factor = TURN * LEAD / math.sqrt(entries * width)
    out_ref[...] = sum_ref[...] * factor + far.reshape(near_ref.shape)


def per_device(
    currents, positions, radiation, interp_index, interp_weight, child_phase, near_src, trans_src, trans_id,
    trans_count, trans_table
):
    boxes, waves, width = currents.shape
    entries = near_src.shape[1]
    leaf_dirs = radiation.shape[1] // 2
    parent_dirs = child_phase.shape[1]
    parents = boxes // 8
    spectra_rows = parents * parent_dirs // 128
    size = lax.axis_size("dir")
    vmem = pl.BlockSpec(memory_space=pltpu.VMEM)
    smem = pl.BlockSpec(memory_space=pltpu.SMEM)
    hbm = pl.BlockSpec(memory_space=pltpu.HBM)
    params = pltpu.CompilerParams(vmem_limit_bytes=32 * 1024 * 1024)

    def in_hbm(x):
        return pltpu.with_memory_space_constraint(x, pltpu.HBM)

    def shaped(shape, dtype):
        return jax.ShapeDtypeStruct(shape, dtype)

    operands = (currents, positions.transpose(1, 0, 2), radiation, interp_index.T, interp_weight.T, child_phase)
    packet, spectra, imat, cos_phase, sin_phase, rad = pl.pallas_call(
        outgoing_kernel,
        out_shape=(
            shaped((boxes + spectra_rows, 16, width), BF16),
            shaped((spectra_rows, 2 * waves, 128), BF16),
            shaped((leaf_dirs, parent_dirs), BF16),
            shaped((8, parent_dirs), F32),
            shaped((8, parent_dirs), F32),
            shaped(radiation.shape, BF16),
        ),
        in_specs=[hbm] * len(operands),
        out_specs=(vmem,) * 6,
        scratch_shapes=[pltpu.VMEM(x.shape, x.dtype) for x in operands if x is not radiation]
        + [pltpu.SemaphoreType.DMA((len(operands),))],
        compiler_params=params,
        name="outgoing",
    )(*[in_hbm(x) for x in operands])

    steps = []
    for step in range(1, size):
        pairs = [(i, i ^ step) for i in range(size) if i < i ^ step]
        steps.append(swapped(packet if carries_packet(step) else spectra, "dir", pairs))

    length = list_places(boxes, entries)[2]
    window = 3 * trans_src.shape[0]
    near_scratch = [
        pltpu.VMEM((ITEMS, width, 2 * width), F32),
        pltpu.VMEM((ITEMS, width, 2 * width), F32),
        pltpu.VMEM((ITEMS, width, 2 * width), BF16),
        pltpu.VMEM((ITEMS, width, 2 * width), BF16),
    ]
    own_sum, items, observers, sources, gains = pl.pallas_call(
        own_near_kernel,
        out_shape=(
            shaped((boxes, waves, width), F32),
            shaped((1, length), jnp.int32),
            shaped((boxes, 16, width), BF16),
            shaped((boxes, width, 128), BF16),
            shaped((parents, window, 2, parent_dirs), F32),
        ),
        in_specs=[vmem] + [hbm] * 5,
        out_specs=(vmem,) * 5,
        scratch_shapes=[
            pltpu.VMEM(near_src.shape, jnp.int32),
            pltpu.SMEM((1, length), jnp.int32),
            pltpu.SMEM(trans_src.shape, jnp.int32),
            pltpu.SMEM(trans_id.shape, jnp.int32),
            pltpu.SMEM(trans_count.shape, jnp.int32),
            pltpu.VMEM((parents * trans_src.shape[1], 2, parent_dirs), F32),
        ]
        + near_scratch
        + [pltpu.SemaphoreType.DMA((4,))],
        compiler_params=params,
        name="own_near",
    )(packet, *[in_hbm(x) for x in (near_src, trans_src, trans_id, trans_count, trans_table)])

    group = pl.pallas_call(
        group_kernel,
        out_shape=shaped((size * spectra_rows + boxes, 2 * waves, 128), BF16),
        in_specs=[vmem] * (2 + len(steps)),
        out_specs=vmem,
        compiler_params=params,
        name="group",
    )(spectra, *steps, items)
    groups = lax.axis_size("box")
    group_even = swapped(group, "box", [(i, i + 1) for i in range(0, groups - 1, 2)])
    group_odd = swapped(group, "box", [(i, i + 1) for i in range(1, groups - 1, 2)])

    packets = [x for step, x in enumerate(steps, 1) if carries_packet(step)]
    near = pl.pallas_call(
        functools.partial(group_near_kernel, entries),
        out_shape=shaped((boxes, waves, width), F32),
        in_specs=[smem] + [vmem] * (4 + len(packets)),
        out_specs=vmem,
        scratch_shapes=[
            pltpu.VMEM((3 * boxes, 16, width), BF16),
            pltpu.VMEM((3 * boxes, width, 128), BF16),
        ]
        + near_scratch,
        compiler_params=params,
        name="group_near",
    )(items, packet, *packets, observers, sources, own_sum)

    return pl.pallas_call(
        functools.partial(incoming_kernel, entries),
        out_shape=shaped((boxes, waves, width), F32),
        in_specs=[smem] + [vmem] * 10,
        out_specs=vmem,
        scratch_shapes=[
            pltpu.VMEM((boxes, waves, width), F32),
            pltpu.VMEM((boxes, 16, width), BF16),
            pltpu.VMEM((boxes, width, 128), BF16),
            pltpu.VMEM((boxes * waves, parent_dirs), F32),
            pltpu.VMEM((boxes * waves, parent_dirs), F32),
        ]
        + near_scratch,
        compiler_params=params,
        name="incoming",
    )(items, group_even, group, group_odd, gains, cos_phase, sin_phase, imat, rad, observers, near)


def solution(mesh):
    placed = (
        P(("box", "dir"), None, None),
        P(("box", "dir"), None, None),
        P(),
        P(),
        P(),
        P(),
        P(("box", "dir"), None),
        P("box", None),
        P("box", None),
        P("box"),
        P(),
    )
    return jax.shard_map(
        per_device,
        mesh=mesh,
        in_specs=placed,
        out_specs=P(("box", "dir"), None, None),
        check_vma=False,
    )
```

```python
import functools
import math

import jax
import jax.numpy as jnp
from jax import lax
from jax.experimental import pallas as pl
from jax.experimental.pallas import tpu as pltpu
from jax.sharding import PartitionSpec as P

F32 = jnp.float32
BF16 = jnp.bfloat16

WAVENUMBER = 4.0
OFFSET = 0.5
TURN = WAVENUMBER / (2.0 * math.pi)
S0, S1, S2 = (-0.08849679958812066, 0.5822236432316782, -1.1456733260321648)
LEAD = -70.99877392901621
ITEMS = 4
ROWS = 32
STAGES = 4


def round_up(value, step):
    return -(-value // step) * step


def swapped(x, axis, pairs):
    return lax.ppermute(x, axis, [way for i, j in pairs for way in ((i, j), (j, i))])


def split3(x):
    high = x.astype(BF16).astype(F32)
    rest = x - high
    mid = rest.astype(BF16).astype(F32)
    return high, mid, rest - mid


def nt_dot(a, b):
    return lax.dot_general(a, b, (((1,), (1,)), ((), ())), preferred_element_type=F32)


def nn_dot(a, b):
    return jnp.dot(a, b, preferred_element_type=F32)


def code_shifts(boxes, entries):
    count_bits = entries.bit_length()
    box_bits = (boxes - 1).bit_length()
    return count_bits, count_bits + box_bits, 2 * count_bits + box_bits, 2 * (count_bits + box_bits)


def list_length(boxes, entries):
    return round_up((boxes * entries + 3 * boxes) // 2 + 4 * ITEMS + 2, 128)


def list_items(near_src, block, here, size):
    boxes, entries = near_src.shape
    length = list_length(boxes, entries)
    first_box, second_count, second_box, source = code_shifts(boxes, entries)
    lanes = round_up(3 * boxes, 128)
    odd = (here & 1) == 1
    edge = (here == 0) | (here == size - 1)
    local = near_src - block * boxes
    below = local + jnp.where(odd, 2 * boxes, 3 * boxes)
    above = local + jnp.where(odd, boxes, 0)
    local = jnp.where(local < 0, below, jnp.where(local >= boxes, above, local))
    lane = lax.broadcasted_iota(jnp.int32, (boxes, lanes), 1)
    box = lax.broadcasted_iota(jnp.int32, (boxes, lanes), 0)
    count = jnp.zeros((boxes, lanes), jnp.int32)
    for e in range(entries):
        count = count + (local[:, e : e + 1] == lane).astype(jnp.int32)
    present = count > 0
    flags = present.astype(F32)
    box_row = lax.broadcasted_iota(jnp.int32, (boxes, boxes), 0)
    box_col = lax.broadcasted_iota(jnp.int32, (boxes, boxes), 1)
    rank = nn_dot((box_col < box_row).astype(F32).astype(BF16), flags.astype(BF16)).astype(jnp.int32)
    items = (jnp.sum(flags, axis=0, keepdims=True).astype(jnp.int32) + 1) >> 1
    from_cross = (lane >= 2 * boxes) & edge
    cross_items = jnp.where(from_cross[:1], items, 0).astype(F32)
    group_items = jnp.where(from_cross[:1], 0, items).astype(F32)
    row = lax.broadcasted_iota(jnp.int32, (lanes, lanes), 0)
    col = lax.broadcasted_iota(jnp.int32, (lanes, lanes), 1)
    ahead = (row < col).astype(F32).astype(BF16)
    lists = jnp.concatenate([group_items, cross_items, jnp.zeros((6, lanes), F32)], axis=0)
    offset = nn_dot(lists.astype(BF16), ahead).astype(jnp.int32)
    group_total = jnp.sum(group_items, axis=1, keepdims=True).astype(jnp.int32)
    cross_total = jnp.sum(cross_items, axis=1, keepdims=True).astype(jnp.int32)
    half = rank >> 1
    place = jnp.where(from_cross, (length - 3) - (offset[1:2] + half), offset[0:1] + half)
    place = jnp.where(present, place, -1)
    code = jnp.where(
        (rank & 1) == 0,
        (lane << source) | (box << first_box) | count,
        (box << second_box) | (count << second_count),
    )
    place_t = place.T
    code_t = code.T
    rows = 3 * boxes
    slot = lax.broadcasted_iota(jnp.int32, (rows, length), 1)
    found = jnp.zeros((rows, length), jnp.int32)
    for i in range(boxes):
        hit = place_t[:rows, i : i + 1] == slot
        found = found + jnp.where(hit, code_t[:rows, i : i + 1], 0)
    listed = jnp.sum(found, axis=0, keepdims=True)
    at = lax.broadcasted_iota(jnp.int32, (1, length), 1)
    return jnp.where(at == length - 2, group_total, jnp.where(at == length - 1, cross_total, listed))


def start_all(copies, sems):
    started = [pltpu.make_async_copy(src, dst, sems.at[k]) for k, (src, dst) in enumerate(copies)]
    for copy in started:
        copy.start()
    return started


def wait_all(started):
    for copy in started:
        copy.wait()


def outgoing_kernel(
    x_hbm, pos_hbm, rad_hbm, idx_hbm, wgt_hbm, phase_hbm, packet_ref, spectra_ref, imat_ref, cos_ref, sin_ref, rad_ref,
    x_ref, pos_ref, idx_ref, wgt_ref, phase_ref, sems
):
    wait_all(
        start_all(
            (
                (x_hbm, x_ref),
                (pos_hbm, pos_ref),
                (rad_hbm, rad_ref),
                (idx_hbm, idx_ref),
                (wgt_hbm, wgt_ref),
                (phase_hbm, phase_ref),
            ),
            sems,
        )
    )
    leaf_dirs, parent_dirs = imat_ref.shape
    x_rows, _, width = x_ref.shape
    axes, boxes, _ = pos_ref.shape
    waves = x_rows * 16 // boxes
    chunks = parent_dirs // 128
    own_rows = x_rows + axes * boxes // 16
    packet_ref[:x_rows] = x_ref[...]
    packet_ref[x_rows:own_rows] = pos_ref[...].reshape(axes * boxes // 16, 16, width)
    column = lax.broadcasted_iota(jnp.int32, (leaf_dirs, parent_dirs), 0)
    imat = jnp.zeros((leaf_dirs, parent_dirs), F32)
    for s in range(idx_ref.shape[0]):
        imat = imat + jnp.where(idx_ref[s : s + 1, :] == column, wgt_ref[s : s + 1, :], 0.0)
    imat = imat.astype(BF16)
    imat_ref[...] = imat
    cos_phase = jnp.cos(phase_ref[...])
    sin_phase = jnp.sin(phase_ref[...])
    cos_ref[...] = cos_phase
    sin_ref[...] = sin_phase
    leaf = nn_dot(x_ref[...].reshape(boxes * waves, width), rad_ref[...]).astype(BF16)
    up_re = nn_dot(leaf[:, :leaf_dirs], imat)
    up_im = nn_dot(leaf[:, leaf_dirs:], imat)
    for q in range(boxes // 8):
        re = jnp.zeros((waves, parent_dirs), F32)
        im = jnp.zeros((waves, parent_dirs), F32)
        for c in range(8):
            at = (q * 8 + c) * waves
            ure = up_re[at : at + waves]
            uim = up_im[at : at + waves]
            re = re + (cos_phase[c : c + 1] * ure - sin_phase[c : c + 1] * uim)
            im = im + (sin_phase[c : c + 1] * ure + cos_phase[c : c + 1] * uim)
        both = jnp.concatenate([re, im], axis=0).astype(BF16)
        for k in range(chunks):
            part = both[:, k * 128 : (k + 1) * 128]
            packet_ref[own_rows + q * chunks + k] = part
            spectra_ref[q * chunks + k] = part


def carries_packet(step):
    return step & (step + 1) == 0


def group_kernel(own_ref, *refs):
    *step_refs, _, group_ref = refs
    size = lax.axis_size("dir")
    rows = own_ref.shape[0]
    here = lax.axis_index("dir")
    group_ref[pl.ds(here * rows, rows)] = own_ref[...]
    for step, ref in enumerate(step_refs, 1):
        group_ref[pl.ds((here ^ step) * rows, rows)] = ref[ref.shape[0] - rows :]
    group_ref[size * rows :] = step_refs[-1][: step_refs[-1].shape[0] - rows]


def features(planes):
    rows, _, width = planes.shape
    boxes = rows * 16 // 3
    planes = planes.astype(F32).reshape(3, boxes, width)
    at = lax.broadcasted_iota(jnp.int32, (boxes, 8, width), 1)
    pos = jnp.zeros((boxes, 8, width), F32)
    for axis in range(3):
        pos = jnp.where(at == axis, planes[axis][:, None, :], pos)
    scale = TURN * TURN
    norm = split3(scale * jnp.sum(pos * pos, axis=1, keepdims=True))
    first = jnp.where(at < 3, pos, 1.0)
    first = jnp.where(at == 3, norm[0], jnp.where(at == 4, norm[1], jnp.where(at == 5, norm[2], first)))
    second = jnp.where(at == 3, 1.0, pos + pltpu.roll(pos, 4, 1))
    source = jnp.concatenate([first, second], axis=1).astype(BF16)
    cross = split3((-2.0 * scale) * pos)
    first = jnp.where(at < 3, cross[0], 1.0)
    first = jnp.where(at == 6, norm[0], jnp.where(at == 7, norm[1], first))
    second = jnp.where(at == 3, norm[2], cross[1] + pltpu.roll(cross[2], 4, 1))
    return source, jnp.concatenate([first, second], axis=1).astype(BF16)


def turn_sources(source, src_ref, start):
    boxes, rows, width = source.shape
    eye = lax.broadcasted_iota(jnp.int32, (width, width), 0) == lax.broadcasted_iota(jnp.int32, (width, width), 1)
    turned = nt_dot(eye.astype(F32).astype(BF16), source.reshape(boxes * rows, width))
    for b in range(boxes):
        at = b * rows
        lanes = turned[:, at // 128 * 128 : at // 128 * 128 + 128]
        if at % 128:
            lanes = pltpu.roll(lanes, 128 - at % 128, 1)
        src_ref[start + b] = lanes.astype(BF16)


def near_sum(entries, total, item_at, first_source, src_ref, win_ref, obs_ref, out_ref, scratch):
    u0_ref, u1_ref, t0_ref, t1_ref = scratch
    boxes, waves, width = out_ref.shape
    first_box, second_count, second_box, source = code_shifts(boxes, entries)
    t1_ref[...] = jnp.zeros(t1_ref.shape, BF16)

    def field(code, low, high):
        return (code >> low) & ((1 << (high - low)) - 1)

    def source_at(code):
        return jnp.maximum((code >> source) - first_source, 0) if first_source else code >> source

    def distances(chunk, g, u_ref):
        code = item_at(chunk * ITEMS + g)
        observers = [obs_ref[field(code, first_box, second_count)], obs_ref[field(code, second_box, source)]]
        u_ref[g] = nn_dot(src_ref[source_at(code)][:, :16], jnp.concatenate(observers, axis=1))

    def tile(g, u_ref, t_ref):
        for at in range(0, width, ROWS):
            v = jnp.maximum(u_ref[g, at : at + ROWS], 1e-12)
            q = v * lax.rsqrt(v)
            t = q - jnp.round(q)
            x = 0.25 - jnp.abs(t)
            z = x * x
            cosine = x * (((z + S2) * z + S1) * z + S0)
            t_ref[g, at : at + ROWS] = (cosine * pltpu.reciprocal(q + OFFSET * TURN, approx=True)).astype(BF16)

    def product(chunk, g, t_ref):
        code = item_at(chunk * ITEMS + g)
        at = source_at(code)
        got = nn_dot(win_ref[at >> 1], t_ref[g])
        got = jnp.where((at & 1) == 1, got[waves:], got[:waves])
        out_ref[field(code, first_box, second_count)] += field(code, 0, first_box).astype(F32) * got[:, :width]
        out_ref[field(code, second_box, source)] += field(code, second_count, second_box).astype(F32) * got[:, width:]

    u_refs = (u0_ref, u1_ref)
    t_refs = (t0_ref, t1_ref)

    def stage(chunk, turn):
        for g in range(ITEMS):
            distances(chunk + 1, g, u_refs[1 - turn])
            product(jnp.maximum(chunk - 1, 0), g, t_refs[1 - turn])
            tile(g, u_refs[turn], t_refs[turn])

    def body(k, carry):
        for j in range(STAGES):
            stage(k * STAGES + j, j & 1)
        return carry

    def finish(turn):
        for g in range(ITEMS):
            product(jnp.maximum(chunks - 1, 0), g, t_refs[turn])

    chunks = (total + (ITEMS - 1)) // ITEMS
    rounds = chunks // STAGES
    for g in range(ITEMS):
        distances(0, g, u0_ref)
    lax.fori_loop(0, rounds, body, 0)
    for j in range(STAGES - 1):
        pl.when(rounds * STAGES + j < chunks)(functools.partial(stage, rounds * STAGES + j, j & 1))
    pl.when((chunks & 1) == 0)(functools.partial(finish, 1))
    pl.when((chunks & 1) == 1)(functools.partial(finish, 0))


def prepare_kernel(
    own_ref, near_hbm, src_hbm, id_hbm, count_hbm, table_hbm, items_ref, obs_ref, src_ref, gain_ref, near_ref,
    trans_src_ref, trans_id_ref, trans_count_ref, rows_ref, sems
):
    boxes = obs_ref.shape[0]
    parents, window = gain_ref.shape[:2]
    listed = src_hbm.shape[1]
    near_copy, *list_copies = start_all(
        (
            (near_hbm, near_ref),
            (src_hbm, trans_src_ref),
            (id_hbm, trans_id_ref),
            (count_hbm, trans_count_ref),
        ),
        sems,
    )
    gain_ref[...] = jnp.zeros(gain_ref.shape, F32)
    plane_rows = 3 * boxes // 16
    source, observer = features(own_ref[boxes // 2 : boxes // 2 + plane_rows])
    turn_sources(source, src_ref, 0)
    obs_ref[...] = observer
    wait_all(list_copies)
    row0 = lax.axis_index("dir") * parents
    for q in range(parents):
        for e in range(listed):
            pltpu.make_async_copy(
                table_hbm.at[trans_id_ref[row0 + q, e]], rows_ref.at[q * listed + e], sems.at[1]
            ).start()
    near_copy.wait()
    block = lax.axis_index(("box", "dir"))
    items_ref[...] = list_items(near_ref[...], block, lax.axis_index("dir"), lax.axis_size("dir"))
    pltpu.make_async_copy(rows_ref, rows_ref, sems.at[1]).wait()
    first = (lax.axis_index("box") - 1) * (window // 3)
    for q in range(parents):
        for e in range(listed):
            live = (e < trans_count_ref[row0 + q]).astype(F32)
            s = jnp.clip(trans_src_ref[row0 + q, e] - first, 0, window - 1)
            gain_ref[q, s] += rows_ref[q * listed + e] * live


def near_kernel(entries, items_ref, own_ref, *refs):
    *step_refs, obs_ref, own_src_ref, out_ref, win_ref, src_ref, list_ref, u0_ref, u1_ref, t0_ref, t1_ref, sem = refs
    boxes, waves, width = out_ref.shape
    fetch = pltpu.make_async_copy(items_ref, list_ref, sem)
    fetch.start()
    length = list_ref.shape[1]
    here = lax.axis_index("dir")
    other_side = jnp.where((here & 1) == 0, here - 1, here + 1)
    x_rows = boxes // 2

    def take(ref, part):
        win_ref[part * x_rows : (part + 1) * x_rows] = ref[:x_rows]
        source, _ = features(ref[x_rows : x_rows + 3 * boxes // 16])
        turn_sources(source, src_ref, part * boxes)

    win_ref[:x_rows] = own_ref[:x_rows]
    src_ref[:boxes] = own_src_ref[...]
    take(step_refs[0], 1)
    for k, ref in enumerate(step_refs[1:], 2):
        pl.when((here ^ ((1 << k) - 1)) == other_side)(functools.partial(take, ref, 2))
    out_ref[...] = jnp.zeros(out_ref.shape, F32)
    fetch.wait()
    near_sum(
        entries,
        list_ref[0, length - 2],
        lambda k: list_ref[0, k],
        0,
        src_ref,
        win_ref,
        obs_ref,
        out_ref,
        (u0_ref, u1_ref, t0_ref, t1_ref),
    )


def incoming_kernel(
    entries, items_ref, even_ref, own_ref, odd_ref, gain_ref, cos_ref, sin_ref, imat_ref, rad_ref, obs_ref, near_ref, out_ref,
    sum_ref, win_ref, src_ref, down_re_ref, down_im_ref, list_ref, u0_ref, u1_ref, t0_ref, t1_ref, sem
):
    parents, window, _, parent_dirs = gain_ref.shape
    boxes, waves, width = near_ref.shape
    chunks = parent_dirs // 128
    group = window // 3
    fetch = pltpu.make_async_copy(items_ref, list_ref, sem)
    fetch.start()
    length = list_ref.shape[1]
    odd_box = lax.axis_index("box") & 1
    sum_ref[...] = near_ref[...]
    cos_phase = cos_ref[...]
    sin_phase = sin_ref[...]
    sums = tuple(jnp.zeros((waves, 128), F32) for _ in range(parents * chunks * 2))
    for part, ref in ((2 - 2 * odd_box, even_ref), (1, own_ref), (2 * odd_box, odd_ref)):

        def add_source(s, sums, part=part, ref=ref):
            sums = list(sums)
            gains = [gain_ref[q, part * group + s] for q in range(parents)]
            for k in range(chunks):
                spectrum = ref[s * chunks + k].astype(F32)
                sre, sim = spectrum[:waves], spectrum[waves:]
                for q in range(parents):
                    gre = gains[q][0:1, k * 128 : (k + 1) * 128]
                    gim = gains[q][1:2, k * 128 : (k + 1) * 128]
                    at = (q * chunks + k) * 2
                    sums[at] = sums[at] + (gre * sre - gim * sim)
                    sums[at + 1] = sums[at + 1] + (gre * sim + gim * sre)
            return tuple(sums)

        sums = lax.fori_loop(0, group, add_source, sums, unroll=8)
    for q in range(parents):
        for k in range(chunks):
            at = (q * chunks + k) * 2
            re = sums[at].astype(BF16).astype(F32)
            im = sums[at + 1].astype(BF16).astype(F32)
            lanes = slice(k * 128, (k + 1) * 128)
            for c in range(8):
                cos, sin = cos_phase[c : c + 1, lanes], sin_phase[c : c + 1, lanes]
                rows = slice((q * 8 + c) * waves, (q * 8 + c + 1) * waves)
                down_re_ref[rows, lanes] = cos * re + sin * im
                down_im_ref[rows, lanes] = cos * im - sin * re
    imat = imat_ref[...]
    in_re = nt_dot(down_re_ref[...].astype(BF16), imat)
    in_im = nt_dot(down_im_ref[...].astype(BF16), imat)
    incoming = jnp.concatenate([in_re, in_im], axis=1).astype(BF16)
    far = nt_dot(incoming, rad_ref[...])
    fetch.wait()
    cross_total = list_ref[0, length - 1]

    @pl.when(cross_total > 0)
    def _():
        first = jnp.where(lax.axis_index("dir") == 0, 1, 0)

        @pl.when(first == odd_box)
        def _():
            win_ref[...] = even_ref[even_ref.shape[0] - win_ref.shape[0] :]

        @pl.when(first != odd_box)
        def _():
            win_ref[...] = odd_ref[odd_ref.shape[0] - win_ref.shape[0] :]

        source, _ = features(win_ref[boxes // 2 :])
        turn_sources(source, src_ref, 0)
        near_sum(
            entries,
            cross_total,
            lambda k: list_ref[0, length - 3 - k],
            2 * boxes,
            src_ref,
            win_ref,
            obs_ref,
            sum_ref,
            (u0_ref, u1_ref, t0_ref, t1_ref),
        )

    factor = TURN * LEAD / math.sqrt(entries * width)
    out_ref[...] = sum_ref[...] * factor + far.reshape(near_ref.shape)


def per_device(
    currents, positions, radiation, interp_index, interp_weight, child_phase, near_src, trans_src, trans_id,
    trans_count, trans_table
):
    boxes, waves, width = currents.shape
    entries = near_src.shape[1]
    leaf_dirs = radiation.shape[1] // 2
    parent_dirs = child_phase.shape[1]
    parents = boxes // 8
    spectra_rows = parents * parent_dirs // 128
    size = lax.axis_size("dir")
    vmem = pl.BlockSpec(memory_space=pltpu.VMEM)
    hbm = pl.BlockSpec(memory_space=pltpu.HBM)
    params = pltpu.CompilerParams(vmem_limit_bytes=32 * 1024 * 1024)

    def in_hbm(x):
        return pltpu.with_memory_space_constraint(x, pltpu.HBM)

    def shaped(shape, dtype):
        return jax.ShapeDtypeStruct(shape, dtype)

    x_rows = boxes // 2
    own_rows = x_rows + 3 * boxes // 16
    operands = (currents.reshape(x_rows, 2 * waves, width), positions.transpose(1, 0, 2), radiation, interp_index.T, interp_weight.T, child_phase)
    packet, spectra, imat, cos_phase, sin_phase, rad = pl.pallas_call(
        outgoing_kernel,
        out_shape=(
            shaped((own_rows + spectra_rows, 16, width), BF16),
            shaped((spectra_rows, 2 * waves, 128), BF16),
            shaped((leaf_dirs, parent_dirs), BF16),
            shaped((8, parent_dirs), F32),
            shaped((8, parent_dirs), F32),
            shaped(radiation.shape, BF16),
        ),
        in_specs=[hbm] * len(operands),
        out_specs=(vmem,) * 6,
        scratch_shapes=[pltpu.VMEM(x.shape, x.dtype) for x in operands if x is not radiation]
        + [pltpu.SemaphoreType.DMA((len(operands),))],
        compiler_params=params,
        name="outgoing",
    )(*[in_hbm(x) for x in operands])

    steps = []
    for step in range(1, size):
        pairs = [(i, i ^ step) for i in range(size) if i < i ^ step]
        steps.append(swapped(packet if carries_packet(step) else spectra, "dir", pairs))

    length = list_length(boxes, entries)
    window = 3 * trans_src.shape[0]
    near_scratch = [
        pltpu.VMEM((ITEMS, width, 2 * width), F32),
        pltpu.VMEM((ITEMS, width, 2 * width), F32),
        pltpu.VMEM((ITEMS, width, 2 * width), BF16),
        pltpu.VMEM((ITEMS, width, 2 * width), BF16),
    ]
    items, observers, sources, gains = pl.pallas_call(
        prepare_kernel,
        out_shape=(
            shaped((1, length), jnp.int32),
            shaped((boxes, 16, width), BF16),
            shaped((boxes, width, 128), BF16),
            shaped((parents, window, 2, parent_dirs), F32),
        ),
        in_specs=[vmem] + [hbm] * 5,
        out_specs=(vmem,) * 4,
        scratch_shapes=[
            pltpu.VMEM(near_src.shape, jnp.int32),
            pltpu.SMEM(trans_src.shape, jnp.int32),
            pltpu.SMEM(trans_id.shape, jnp.int32),
            pltpu.SMEM(trans_count.shape, jnp.int32),
            pltpu.VMEM((parents * trans_src.shape[1], 2, parent_dirs), F32),
            pltpu.SemaphoreType.DMA((4,)),
        ],
        compiler_params=params,
        name="prepare",
    )(packet, *[in_hbm(x) for x in (near_src, trans_src, trans_id, trans_count, trans_table)])

    group = pl.pallas_call(
        group_kernel,
        out_shape=shaped((size * spectra_rows + own_rows, 2 * waves, 128), BF16),
        in_specs=[vmem] * (2 + len(steps)),
        out_specs=vmem,
        compiler_params=params,
        name="group",
    )(spectra, *steps, items)
    groups = lax.axis_size("box")
    group_odd = swapped(group, "box", [(i, i + 1) for i in range(1, groups - 1, 2)])
    group_even = swapped(group, "box", [(i, i + 1) for i in range(0, groups - 1, 2)])

    packets = [x for step, x in enumerate(steps, 1) if carries_packet(step)]
    near = pl.pallas_call(
        functools.partial(near_kernel, entries),
        out_shape=shaped((boxes, waves, width), F32),
        in_specs=[vmem] * (4 + len(packets)),
        out_specs=vmem,
        scratch_shapes=[
            pltpu.VMEM((3 * x_rows, 16, width), BF16),
            pltpu.VMEM((3 * boxes, width, 128), BF16),
            pltpu.SMEM((1, length), jnp.int32),
        ]
        + near_scratch
        + [pltpu.SemaphoreType.DMA],
        compiler_params=params,
        name="near",
    )(items, packet, *packets, observers, sources)

    return pl.pallas_call(
        functools.partial(incoming_kernel, entries),
        out_shape=shaped((boxes, waves, width), F32),
        in_specs=[vmem] * 11,
        out_specs=vmem,
        scratch_shapes=[
            pltpu.VMEM((boxes, waves, width), F32),
            pltpu.VMEM((own_rows, 16, width), BF16),
            pltpu.VMEM((boxes, width, 128), BF16),
            pltpu.VMEM((boxes * waves, parent_dirs), F32),
            pltpu.VMEM((boxes * waves, parent_dirs), F32),
            pltpu.SMEM((1, length), jnp.int32),
        ]
        + near_scratch
        + [pltpu.SemaphoreType.DMA],
        compiler_params=params,
        name="incoming",
    )(items, group_even, group, group_odd, gains, cos_phase, sin_phase, imat, rad, observers, near)


def solution(mesh):
    placed = (
        P(("box", "dir"), None, None),
        P(("box", "dir"), None, None),
        P(),
        P(),
        P(),
        P(),
        P(("box", "dir"), None),
        P("box", None),
        P("box", None),
        P("box"),
        P(),
    )
    return jax.shard_map(
        per_device,
        mesh=mesh,
        in_specs=placed,
        out_specs=P(("box", "dir"), None, None),
        check_vma=False,
    )
```

```python
import functools
import math

import jax
import jax.numpy as jnp
from jax import lax
from jax.experimental import pallas as pl
from jax.experimental.pallas import tpu as pltpu
from jax.sharding import PartitionSpec as P

F32 = jnp.float32
BF16 = jnp.bfloat16

WAVENUMBER = 4.0
OFFSET = 0.5
TURN = WAVENUMBER / (2.0 * math.pi)
S0, S1, S2 = (-0.08849679958812066, 0.5822236432316782, -1.1456733260321648)
LEAD = -70.99877392901621
ITEMS = 4
ROWS = 32
STAGES = 4
FIRST_ITEMS = 2


def round_up(value, step):
    return -(-value // step) * step


def swapped(x, axis, pairs):
    return lax.ppermute(x, axis, [way for i, j in pairs for way in ((i, j), (j, i))])


def split3(x):
    high = x.astype(BF16).astype(F32)
    rest = x - high
    mid = rest.astype(BF16).astype(F32)
    return high, mid, rest - mid


def nt_dot(a, b):
    return lax.dot_general(a, b, (((1,), (1,)), ((), ())), preferred_element_type=F32)


def nn_dot(a, b):
    return jnp.dot(a, b, preferred_element_type=F32)


def code_shifts(boxes, entries):
    count_bits = entries.bit_length()
    box_bits = (boxes - 1).bit_length()
    return count_bits, count_bits + box_bits, 2 * count_bits + box_bits, 2 * (count_bits + box_bits)


def list_places(boxes, entries):
    gap = 2 * ITEMS
    most = FIRST_ITEMS * boxes
    return most, most + gap, round_up(most + gap + (boxes * entries + 3 * boxes) // 2 + 2 * gap + 3, 128)


def list_items(near_src, block, here, size):
    boxes, entries = near_src.shape
    most, second_start, length = list_places(boxes, entries)
    first_box, second_count, second_box, source = code_shifts(boxes, entries)
    lanes = round_up(3 * boxes, 128)
    odd = (here & 1) == 1
    edge = (here == 0) | (here == size - 1)
    local = near_src - block * boxes
    below = local + jnp.where(odd, 2 * boxes, 3 * boxes)
    above = local + jnp.where(odd, boxes, 0)
    local = jnp.where(local < 0, below, jnp.where(local >= boxes, above, local))
    lane = lax.broadcasted_iota(jnp.int32, (boxes, lanes), 1)
    box = lax.broadcasted_iota(jnp.int32, (boxes, lanes), 0)
    count = jnp.zeros((boxes, lanes), jnp.int32)
    for e in range(entries):
        count = count + (local[:, e : e + 1] == lane).astype(jnp.int32)
    present = count > 0
    flags = present.astype(F32)
    box_row = lax.broadcasted_iota(jnp.int32, (boxes, boxes), 0)
    box_col = lax.broadcasted_iota(jnp.int32, (boxes, boxes), 1)
    rank = nn_dot((box_col < box_row).astype(F32).astype(BF16), flags.astype(BF16)).astype(jnp.int32)
    items = (jnp.sum(flags, axis=0, keepdims=True).astype(jnp.int32) + 1) >> 1
    from_cross = (lane >= 2 * boxes) & edge
    cross_items = jnp.where(from_cross[:1], items, 0).astype(F32)
    group_items = jnp.where(from_cross[:1], 0, items).astype(F32)
    row = lax.broadcasted_iota(jnp.int32, (lanes, lanes), 0)
    col = lax.broadcasted_iota(jnp.int32, (lanes, lanes), 1)
    ahead = (row < col).astype(F32).astype(BF16)
    lists = jnp.concatenate([group_items, cross_items, jnp.zeros((6, lanes), F32)], axis=0)
    offset = nn_dot(lists.astype(BF16), ahead).astype(jnp.int32)
    group_total = jnp.sum(group_items, axis=1, keepdims=True).astype(jnp.int32)
    cross_total = jnp.sum(cross_items, axis=1, keepdims=True).astype(jnp.int32)
    own_items = jnp.where(lane[:1] < boxes, group_items, 0.0)
    first_total = jnp.minimum(jnp.sum(own_items, axis=1, keepdims=True).astype(jnp.int32), most)
    half = rank >> 1
    group_place = offset[0:1] + half
    group_place = jnp.where(group_place < first_total, group_place, second_start - first_total + group_place)
    place = jnp.where(from_cross, (length - 4) - (offset[1:2] + half), group_place)
    place = jnp.where(present, place, -1)
    code = jnp.where(
        (rank & 1) == 0,
        (lane << source) | (box << first_box) | count,
        (box << second_box) | (count << second_count),
    )
    place_t = place.T
    code_t = code.T
    rows = 3 * boxes
    slot = lax.broadcasted_iota(jnp.int32, (rows, length), 1)
    found = jnp.zeros((rows, length), jnp.int32)
    for i in range(boxes):
        hit = place_t[:rows, i : i + 1] == slot
        found = found + jnp.where(hit, code_t[:rows, i : i + 1], 0)
    listed = jnp.sum(found, axis=0, keepdims=True)
    at = lax.broadcasted_iota(jnp.int32, (1, length), 1)
    listed = jnp.where(at == length - 3, first_total, listed)
    return jnp.where(at == length - 2, group_total - first_total, jnp.where(at == length - 1, cross_total, listed))


def start_all(copies, sems):
    started = [pltpu.make_async_copy(src, dst, sems.at[k]) for k, (src, dst) in enumerate(copies)]
    for copy in started:
        copy.start()
    return started


def wait_all(started):
    for copy in started:
        copy.wait()


def outgoing_kernel(
    x_hbm, pos_hbm, rad_hbm, idx_hbm, wgt_hbm, phase_hbm, packet_ref, spectra_ref, imat_ref, cos_ref, sin_ref, rad_ref,
    x_ref, pos_ref, idx_ref, wgt_ref, phase_ref, sems
):
    wait_all(
        start_all(
            (
                (x_hbm, x_ref),
                (pos_hbm, pos_ref),
                (rad_hbm, rad_ref),
                (idx_hbm, idx_ref),
                (wgt_hbm, wgt_ref),
                (phase_hbm, phase_ref),
            ),
            sems,
        )
    )
    leaf_dirs, parent_dirs = imat_ref.shape
    x_rows, _, width = x_ref.shape
    axes, boxes, _ = pos_ref.shape
    waves = x_rows * 16 // boxes
    chunks = parent_dirs // 128
    own_rows = x_rows + axes * boxes // 16
    packet_ref[:x_rows] = x_ref[...]
    packet_ref[x_rows:own_rows] = pos_ref[...].reshape(axes * boxes // 16, 16, width)
    column = lax.broadcasted_iota(jnp.int32, (leaf_dirs, parent_dirs), 0)
    imat = jnp.zeros((leaf_dirs, parent_dirs), F32)
    for s in range(idx_ref.shape[0]):
        imat = imat + jnp.where(idx_ref[s : s + 1, :] == column, wgt_ref[s : s + 1, :], 0.0)
    imat = imat.astype(BF16)
    imat_ref[...] = imat
    cos_phase = jnp.cos(phase_ref[...])
    sin_phase = jnp.sin(phase_ref[...])
    cos_ref[...] = cos_phase
    sin_ref[...] = sin_phase
    leaf = nn_dot(x_ref[...].reshape(boxes * waves, width), rad_ref[...]).astype(BF16)
    up_re = nn_dot(leaf[:, :leaf_dirs], imat)
    up_im = nn_dot(leaf[:, leaf_dirs:], imat)
    for q in range(boxes // 8):
        re = jnp.zeros((waves, parent_dirs), F32)
        im = jnp.zeros((waves, parent_dirs), F32)
        for c in range(8):
            at = (q * 8 + c) * waves
            ure = up_re[at : at + waves]
            uim = up_im[at : at + waves]
            re = re + (cos_phase[c : c + 1] * ure - sin_phase[c : c + 1] * uim)
            im = im + (sin_phase[c : c + 1] * ure + cos_phase[c : c + 1] * uim)
        both = jnp.concatenate([re, im], axis=0).astype(BF16)
        for k in range(chunks):
            part = both[:, k * 128 : (k + 1) * 128]
            packet_ref[own_rows + q * chunks + k] = part
            spectra_ref[q * chunks + k] = part


def carries_packet(step):
    return step & (step + 1) == 0


def group_kernel(own_ref, *refs):
    *step_refs, _, group_ref = refs
    size = lax.axis_size("dir")
    rows = own_ref.shape[0]
    here = lax.axis_index("dir")
    group_ref[pl.ds(here * rows, rows)] = own_ref[...]
    for step, ref in enumerate(step_refs, 1):
        group_ref[pl.ds((here ^ step) * rows, rows)] = ref[ref.shape[0] - rows :]
    group_ref[size * rows :] = step_refs[-1][: step_refs[-1].shape[0] - rows]


def features(planes):
    rows, _, width = planes.shape
    boxes = rows * 16 // 3
    planes = planes.astype(F32).reshape(3, boxes, width)
    at = lax.broadcasted_iota(jnp.int32, (boxes, 8, width), 1)
    pos = jnp.zeros((boxes, 8, width), F32)
    for axis in range(3):
        pos = jnp.where(at == axis, planes[axis][:, None, :], pos)
    scale = TURN * TURN
    norm = split3(scale * jnp.sum(pos * pos, axis=1, keepdims=True))
    first = jnp.where(at < 3, pos, 1.0)
    first = jnp.where(at == 3, norm[0], jnp.where(at == 4, norm[1], jnp.where(at == 5, norm[2], first)))
    second = jnp.where(at == 3, 1.0, pos + pltpu.roll(pos, 4, 1))
    source = jnp.concatenate([first, second], axis=1).astype(BF16)
    cross = split3((-2.0 * scale) * pos)
    first = jnp.where(at < 3, cross[0], 1.0)
    first = jnp.where(at == 6, norm[0], jnp.where(at == 7, norm[1], first))
    second = jnp.where(at == 3, norm[2], cross[1] + pltpu.roll(cross[2], 4, 1))
    return source, jnp.concatenate([first, second], axis=1).astype(BF16)


def turn_sources(source, src_ref, start):
    boxes, rows, width = source.shape
    eye = lax.broadcasted_iota(jnp.int32, (width, width), 0) == lax.broadcasted_iota(jnp.int32, (width, width), 1)
    turned = nt_dot(eye.astype(F32).astype(BF16), source.reshape(boxes * rows, width))
    for b in range(boxes):
        at = b * rows
        lanes = turned[:, at // 128 * 128 : at // 128 * 128 + 128]
        if at % 128:
            lanes = pltpu.roll(lanes, 128 - at % 128, 1)
        src_ref[start + b] = lanes.astype(BF16)


def near_sum(entries, total, item_at, first_source, src_ref, win_ref, obs_ref, out_ref, scratch):
    u0_ref, u1_ref, t0_ref, t1_ref = scratch
    boxes, waves, width = out_ref.shape
    first_box, second_count, second_box, source = code_shifts(boxes, entries)
    t1_ref[...] = jnp.zeros(t1_ref.shape, BF16)

    def field(code, low, high):
        return (code >> low) & ((1 << (high - low)) - 1)

    def source_at(code):
        return jnp.maximum((code >> source) - first_source, 0) if first_source else code >> source

    def distances(chunk, g, u_ref):
        code = item_at(chunk * ITEMS + g)
        observers = [obs_ref[field(code, first_box, second_count)], obs_ref[field(code, second_box, source)]]
        u_ref[g] = nn_dot(src_ref[source_at(code)][:, :16], jnp.concatenate(observers, axis=1))

    def tile(g, u_ref, t_ref):
        for at in range(0, width, ROWS):
            v = jnp.maximum(u_ref[g, at : at + ROWS], 1e-12)
            q = v * lax.rsqrt(v)
            t = q - jnp.round(q)
            x = 0.25 - jnp.abs(t)
            z = x * x
            cosine = x * (((z + S2) * z + S1) * z + S0)
            t_ref[g, at : at + ROWS] = (cosine * pltpu.reciprocal(q + OFFSET * TURN, approx=True)).astype(BF16)

    def product(chunk, g, t_ref):
        code = item_at(chunk * ITEMS + g)
        at = source_at(code)
        got = nn_dot(win_ref[at >> 1], t_ref[g])
        got = jnp.where((at & 1) == 1, got[waves:], got[:waves])
        out_ref[field(code, first_box, second_count)] += field(code, 0, first_box).astype(F32) * got[:, :width]
        out_ref[field(code, second_box, source)] += field(code, second_count, second_box).astype(F32) * got[:, width:]

    u_refs = (u0_ref, u1_ref)
    t_refs = (t0_ref, t1_ref)

    def stage(chunk, turn):
        for g in range(ITEMS):
            distances(chunk + 1, g, u_refs[1 - turn])
            product(jnp.maximum(chunk - 1, 0), g, t_refs[1 - turn])
            tile(g, u_refs[turn], t_refs[turn])

    def body(k, carry):
        for j in range(STAGES):
            stage(k * STAGES + j, j & 1)
        return carry

    def finish(turn):
        for g in range(ITEMS):
            product(jnp.maximum(chunks - 1, 0), g, t_refs[turn])

    chunks = (total + (ITEMS - 1)) // ITEMS
    rounds = chunks // STAGES
    for g in range(ITEMS):
        distances(0, g, u0_ref)
    lax.fori_loop(0, rounds, body, 0)
    for j in range(STAGES - 1):
        pl.when(rounds * STAGES + j < chunks)(functools.partial(stage, rounds * STAGES + j, j & 1))
    pl.when((chunks & 1) == 0)(functools.partial(finish, 1))
    pl.when((chunks & 1) == 1)(functools.partial(finish, 0))


def prepare_kernel(
    own_ref, near_hbm, src_hbm, id_hbm, count_hbm, table_hbm, out_ref, items_ref, obs_ref, src_ref, gain_ref, near_ref,
    trans_src_ref, trans_id_ref, trans_count_ref, rows_ref, list_ref, u0_ref, u1_ref, t0_ref, t1_ref, sems
):
    boxes = obs_ref.shape[0]
    entries = near_ref.shape[1]
    length = list_ref.shape[1]
    parents, window = gain_ref.shape[:2]
    listed = src_hbm.shape[1]
    near_copy, *list_copies = start_all(
        (
            (near_hbm, near_ref),
            (src_hbm, trans_src_ref),
            (id_hbm, trans_id_ref),
            (count_hbm, trans_count_ref),
        ),
        sems,
    )
    gain_ref[...] = jnp.zeros(gain_ref.shape, F32)
    plane_rows = 3 * boxes // 16
    source, observer = features(own_ref[boxes // 2 : boxes // 2 + plane_rows])
    turn_sources(source, src_ref, 0)
    obs_ref[...] = observer
    wait_all(list_copies)
    row0 = lax.axis_index("dir") * parents
    for q in range(parents):
        for e in range(listed):
            pltpu.make_async_copy(
                table_hbm.at[trans_id_ref[row0 + q, e]], rows_ref.at[q * listed + e], sems.at[1]
            ).start()
    near_copy.wait()
    block = lax.axis_index(("box", "dir"))
    items_ref[...] = list_items(near_ref[...], block, lax.axis_index("dir"), lax.axis_size("dir"))
    fetch = pltpu.make_async_copy(items_ref, list_ref, sems.at[0])
    fetch.start()
    out_ref[...] = jnp.zeros(out_ref.shape, F32)
    pltpu.make_async_copy(rows_ref, rows_ref, sems.at[1]).wait()
    first = (lax.axis_index("box") - 1) * (window // 3)
    for q in range(parents):
        for e in range(listed):
            live = (e < trans_count_ref[row0 + q]).astype(F32)
            s = jnp.clip(trans_src_ref[row0 + q, e] - first, 0, window - 1)
            gain_ref[q, s] += rows_ref[q * listed + e] * live
    fetch.wait()
    near_sum(
        entries,
        list_ref[0, length - 3],
        lambda k: list_ref[0, k],
        0,
        src_ref,
        own_ref,
        obs_ref,
        out_ref,
        (u0_ref, u1_ref, t0_ref, t1_ref),
    )


def near_kernel(entries, items_ref, own_ref, *refs):
    *step_refs, obs_ref, own_src_ref, first_ref, out_ref, win_ref, src_ref, list_ref, u0_ref, u1_ref, t0_ref, t1_ref, sem = refs
    boxes, waves, width = out_ref.shape
    fetch = pltpu.make_async_copy(items_ref, list_ref, sem)
    fetch.start()
    length = list_ref.shape[1]
    here = lax.axis_index("dir")
    other_side = jnp.where((here & 1) == 0, here - 1, here + 1)
    x_rows = boxes // 2

    def take(ref, part):
        win_ref[part * x_rows : (part + 1) * x_rows] = ref[:x_rows]
        source, _ = features(ref[x_rows : x_rows + 3 * boxes // 16])
        turn_sources(source, src_ref, part * boxes)

    win_ref[:x_rows] = own_ref[:x_rows]
    src_ref[:boxes] = own_src_ref[...]
    take(step_refs[0], 1)
    for k, ref in enumerate(step_refs[1:], 2):
        pl.when((here ^ ((1 << k) - 1)) == other_side)(functools.partial(take, ref, 2))
    second_start = list_places(boxes, entries)[1]
    out_ref[...] = first_ref[...]
    fetch.wait()
    near_sum(
        entries,
        list_ref[0, length - 2],
        lambda k: list_ref[0, second_start + k],
        0,
        src_ref,
        win_ref,
        obs_ref,
        out_ref,
        (u0_ref, u1_ref, t0_ref, t1_ref),
    )


def incoming_kernel(
    entries, items_ref, even_ref, own_ref, odd_ref, gain_ref, cos_ref, sin_ref, imat_ref, rad_ref, obs_ref, near_ref, out_ref,
    sum_ref, win_ref, src_ref, down_re_ref, down_im_ref, list_ref, u0_ref, u1_ref, t0_ref, t1_ref, sem
):
    parents, window, _, parent_dirs = gain_ref.shape
    boxes, waves, width = near_ref.shape
    chunks = parent_dirs // 128
    group = window // 3
    fetch = pltpu.make_async_copy(items_ref, list_ref, sem)
    fetch.start()
    length = list_ref.shape[1]
    odd_box = lax.axis_index("box") & 1
    sum_ref[...] = near_ref[...]
    cos_phase = cos_ref[...]
    sin_phase = sin_ref[...]
    sums = tuple(jnp.zeros((waves, 128), F32) for _ in range(parents * chunks * 2))
    for part, ref in ((2 - 2 * odd_box, even_ref), (1, own_ref), (2 * odd_box, odd_ref)):

        def add_source(s, sums, part=part, ref=ref):
            sums = list(sums)
            gains = [gain_ref[q, part * group + s] for q in range(parents)]
            for k in range(chunks):
                spectrum = ref[s * chunks + k].astype(F32)
                sre, sim = spectrum[:waves], spectrum[waves:]
                for q in range(parents):
                    gre = gains[q][0:1, k * 128 : (k + 1) * 128]
                    gim = gains[q][1:2, k * 128 : (k + 1) * 128]
                    at = (q * chunks + k) * 2
                    sums[at] = sums[at] + (gre * sre - gim * sim)
                    sums[at + 1] = sums[at + 1] + (gre * sim + gim * sre)
            return tuple(sums)

        sums = lax.fori_loop(0, group, add_source, sums, unroll=8)
    for q in range(parents):
        for k in range(chunks):
            at = (q * chunks + k) * 2
            re = sums[at].astype(BF16).astype(F32)
            im = sums[at + 1].astype(BF16).astype(F32)
            lanes = slice(k * 128, (k + 1) * 128)
            for c in range(8):
                cos, sin = cos_phase[c : c + 1, lanes], sin_phase[c : c + 1, lanes]
                rows = slice((q * 8 + c) * waves, (q * 8 + c + 1) * waves)
                down_re_ref[rows, lanes] = cos * re + sin * im
                down_im_ref[rows, lanes] = cos * im - sin * re
    imat = imat_ref[...]
    in_re = nt_dot(down_re_ref[...].astype(BF16), imat)
    in_im = nt_dot(down_im_ref[...].astype(BF16), imat)
    incoming = jnp.concatenate([in_re, in_im], axis=1).astype(BF16)
    far = nt_dot(incoming, rad_ref[...])
    fetch.wait()
    cross_total = list_ref[0, length - 1]

    @pl.when(cross_total > 0)
    def _():
        first = jnp.where(lax.axis_index("dir") == 0, 1, 0)

        @pl.when(first == odd_box)
        def _():
            win_ref[...] = even_ref[even_ref.shape[0] - win_ref.shape[0] :]

        @pl.when(first != odd_box)
        def _():
            win_ref[...] = odd_ref[odd_ref.shape[0] - win_ref.shape[0] :]

        source, _ = features(win_ref[boxes // 2 :])
        turn_sources(source, src_ref, 0)
        near_sum(
            entries,
            cross_total,
            lambda k: list_ref[0, length - 4 - k],
            2 * boxes,
            src_ref,
            win_ref,
            obs_ref,
            sum_ref,
            (u0_ref, u1_ref, t0_ref, t1_ref),
        )

    factor = TURN * LEAD / math.sqrt(entries * width)
    out_ref[...] = sum_ref[...] * factor + far.reshape(near_ref.shape)


def per_device(
    currents, positions, radiation, interp_index, interp_weight, child_phase, near_src, trans_src, trans_id,
    trans_count, trans_table
):
    boxes, waves, width = currents.shape
    entries = near_src.shape[1]
    leaf_dirs = radiation.shape[1] // 2
    parent_dirs = child_phase.shape[1]
    parents = boxes // 8
    spectra_rows = parents * parent_dirs // 128
    size = lax.axis_size("dir")
    vmem = pl.BlockSpec(memory_space=pltpu.VMEM)
    hbm = pl.BlockSpec(memory_space=pltpu.HBM)
    params = pltpu.CompilerParams(vmem_limit_bytes=32 * 1024 * 1024)

    def in_hbm(x):
        return pltpu.with_memory_space_constraint(x, pltpu.HBM)

    def shaped(shape, dtype):
        return jax.ShapeDtypeStruct(shape, dtype)

    x_rows = boxes // 2
    own_rows = x_rows + 3 * boxes // 16
    operands = (currents.reshape(x_rows, 2 * waves, width), positions.transpose(1, 0, 2), radiation, interp_index.T, interp_weight.T, child_phase)
    packet, spectra, imat, cos_phase, sin_phase, rad = pl.pallas_call(
        outgoing_kernel,
        out_shape=(
            shaped((own_rows + spectra_rows, 16, width), BF16),
            shaped((spectra_rows, 2 * waves, 128), BF16),
            shaped((leaf_dirs, parent_dirs), BF16),
            shaped((8, parent_dirs), F32),
            shaped((8, parent_dirs), F32),
            shaped(radiation.shape, BF16),
        ),
        in_specs=[hbm] * len(operands),
        out_specs=(vmem,) * 6,
        scratch_shapes=[pltpu.VMEM(x.shape, x.dtype) for x in operands if x is not radiation]
        + [pltpu.SemaphoreType.DMA((len(operands),))],
        compiler_params=params,
        name="outgoing",
    )(*[in_hbm(x) for x in operands])

    steps = []
    for step in range(1, size):
        pairs = [(i, i ^ step) for i in range(size) if i < i ^ step]
        steps.append(swapped(packet if carries_packet(step) else spectra, "dir", pairs))

    length = list_places(boxes, entries)[2]
    window = 3 * trans_src.shape[0]
    near_scratch = [
        pltpu.VMEM((ITEMS, width, 2 * width), F32),
        pltpu.VMEM((ITEMS, width, 2 * width), F32),
        pltpu.VMEM((ITEMS, width, 2 * width), BF16),
        pltpu.VMEM((ITEMS, width, 2 * width), BF16),
    ]
    first_sum, items, observers, sources, gains = pl.pallas_call(
        prepare_kernel,
        out_shape=(
            shaped((boxes, waves, width), F32),
            shaped((1, length), jnp.int32),
            shaped((boxes, 16, width), BF16),
            shaped((boxes, width, 128), BF16),
            shaped((parents, window, 2, parent_dirs), F32),
        ),
        in_specs=[vmem] + [hbm] * 5,
        out_specs=(vmem,) * 5,
        scratch_shapes=[
            pltpu.VMEM(near_src.shape, jnp.int32),
            pltpu.SMEM(trans_src.shape, jnp.int32),
            pltpu.SMEM(trans_id.shape, jnp.int32),
            pltpu.SMEM(trans_count.shape, jnp.int32),
            pltpu.VMEM((parents * trans_src.shape[1], 2, parent_dirs), F32),
            pltpu.SMEM((1, length), jnp.int32),
        ]
        + near_scratch
        + [pltpu.SemaphoreType.DMA((4,))],
        compiler_params=params,
        name="prepare",
    )(packet, *[in_hbm(x) for x in (near_src, trans_src, trans_id, trans_count, trans_table)])

    group = pl.pallas_call(
        group_kernel,
        out_shape=shaped((size * spectra_rows + own_rows, 2 * waves, 128), BF16),
        in_specs=[vmem] * (2 + len(steps)),
        out_specs=vmem,
        compiler_params=params,
        name="group",
    )(spectra, *steps, items)
    groups = lax.axis_size("box")
    group_odd = swapped(group, "box", [(i, i + 1) for i in range(1, groups - 1, 2)])
    group_even = swapped(group, "box", [(i, i + 1) for i in range(0, groups - 1, 2)])

    packets = [x for step, x in enumerate(steps, 1) if carries_packet(step)]
    near = pl.pallas_call(
        functools.partial(near_kernel, entries),
        out_shape=shaped((boxes, waves, width), F32),
        in_specs=[vmem] * (5 + len(packets)),
        out_specs=vmem,
        scratch_shapes=[
            pltpu.VMEM((3 * x_rows, 16, width), BF16),
            pltpu.VMEM((3 * boxes, width, 128), BF16),
            pltpu.SMEM((1, length), jnp.int32),
        ]
        + near_scratch
        + [pltpu.SemaphoreType.DMA],
        compiler_params=params,
        name="near",
    )(items, packet, *packets, observers, sources, first_sum)

    return pl.pallas_call(
        functools.partial(incoming_kernel, entries),
        out_shape=shaped((boxes, waves, width), F32),
        in_specs=[vmem] * 11,
        out_specs=vmem,
        scratch_shapes=[
            pltpu.VMEM((boxes, waves, width), F32),
            pltpu.VMEM((own_rows, 16, width), BF16),
            pltpu.VMEM((boxes, width, 128), BF16),
            pltpu.VMEM((boxes * waves, parent_dirs), F32),
            pltpu.VMEM((boxes * waves, parent_dirs), F32),
            pltpu.SMEM((1, length), jnp.int32),
        ]
        + near_scratch
        + [pltpu.SemaphoreType.DMA],
        compiler_params=params,
        name="incoming",
    )(items, group_even, group, group_odd, gains, cos_phase, sin_phase, imat, rad, observers, near)


def solution(mesh):
    placed = (
        P(("box", "dir"), None, None),
        P(("box", "dir"), None, None),
        P(),
        P(),
        P(),
        P(),
        P(("box", "dir"), None),
        P("box", None),
        P("box", None),
        P("box"),
        P(),
    )
    return jax.shard_map(
        per_device,
        mesh=mesh,
        in_specs=placed,
        out_specs=P(("box", "dir"), None, None),
        check_vma=False,
    )
```

```python
import functools
import math

import jax
import jax.numpy as jnp
from jax import lax
from jax.experimental import pallas as pl
from jax.experimental.pallas import tpu as pltpu
from jax.sharding import PartitionSpec as P

F32 = jnp.float32
BF16 = jnp.bfloat16

WAVENUMBER = 4.0
OFFSET = 0.5
TURN = WAVENUMBER / (2.0 * math.pi)
S0, S1, S2 = (-0.08849679958812066, 0.5822236432316782, -1.1456733260321648)
LEAD = -70.99877392901621
ITEMS = 4
ROWS = 32
STAGES = 4
FIRST_ITEMS = 2


def round_up(value, step):
    return -(-value // step) * step


def swapped(x, axis, pairs):
    return lax.ppermute(x, axis, [way for i, j in pairs for way in ((i, j), (j, i))])


def split3(x):
    high = x.astype(BF16).astype(F32)
    rest = x - high
    mid = rest.astype(BF16).astype(F32)
    return high, mid, rest - mid


def nt_dot(a, b):
    return lax.dot_general(a, b, (((1,), (1,)), ((), ())), preferred_element_type=F32)


def nn_dot(a, b):
    return jnp.dot(a, b, preferred_element_type=F32)


def code_bits(boxes, entries):
    return entries.bit_length(), (boxes - 1).bit_length(), (3 * boxes - 1).bit_length()


def list_places(boxes, entries):
    gap = 2 * ITEMS
    most = FIRST_ITEMS * boxes
    return most, most + gap, round_up(most + gap + boxes * entries // 2 + 2 * gap + 6, 128)


def list_items(near_src, block, here, size):
    boxes, entries = near_src.shape
    most, second_start, length = list_places(boxes, entries)
    count_bits, box_bits, source_bits = code_bits(boxes, entries)
    pair_bits = count_bits + box_bits + source_bits
    lanes = round_up(3 * boxes, 128)
    odd = (here & 1) == 1
    edge = (here == 0) | (here == size - 1)
    local = near_src - block * boxes
    below = local + jnp.where(odd, 2 * boxes, 3 * boxes)
    above = local + jnp.where(odd, boxes, 0)
    local = jnp.where(local < 0, below, jnp.where(local >= boxes, above, local))
    lane = lax.broadcasted_iota(jnp.int32, (boxes, lanes), 1)
    box = lax.broadcasted_iota(jnp.int32, (boxes, lanes), 0)
    count = jnp.zeros((boxes, lanes), jnp.int32)
    for e in range(entries):
        count = count + (local[:, e : e + 1] == lane).astype(jnp.int32)
    present = count > 0
    flags = present.astype(F32)
    box_row = lax.broadcasted_iota(jnp.int32, (boxes, boxes), 0)
    box_col = lax.broadcasted_iota(jnp.int32, (boxes, boxes), 1)
    rank = nn_dot((box_col < box_row).astype(F32).astype(BF16), flags.astype(BF16)).astype(jnp.int32)
    pairs = jnp.sum(flags, axis=0, keepdims=True)
    from_cross = (lane >= 2 * boxes) & edge
    cross_pairs = jnp.where(from_cross[:1], pairs, 0.0)
    group_pairs = jnp.where(from_cross[:1], 0.0, pairs)
    row = lax.broadcasted_iota(jnp.int32, (lanes, lanes), 0)
    col = lax.broadcasted_iota(jnp.int32, (lanes, lanes), 1)
    ahead = (row < col).astype(F32).astype(BF16)
    lists = jnp.concatenate([group_pairs, cross_pairs, jnp.zeros((6, lanes), F32)], axis=0)
    offset = nn_dot(lists.astype(BF16), ahead).astype(jnp.int32)
    own_pairs = jnp.where(lane[:1] < boxes, group_pairs, 0.0)

    def total(pairs):
        return jnp.sum(pairs, axis=1, keepdims=True).astype(jnp.int32)

    first_total = jnp.minimum(total(own_pairs), 2 * most)
    second_total = total(group_pairs) - first_total
    cross_total = total(cross_pairs)
    order = offset[0:1] + rank
    in_second = order >= first_total
    order = jnp.where(in_second, order - first_total, order)
    order = jnp.where(from_cross, offset[1:2] + rank, order)
    half = order >> 1
    place = jnp.where(from_cross, (length - 4) - half, jnp.where(in_second, second_start + half, half))
    place = jnp.where(present, place, -1)
    code = (lane << (count_bits + box_bits)) | (box << count_bits) | count
    code = jnp.where((order & 1) == 1, code << pair_bits, code)
    place_t = place.T
    code_t = code.T
    rows = 3 * boxes
    slot = lax.broadcasted_iota(jnp.int32, (rows, length), 1)
    found = jnp.zeros((rows, length), jnp.int32)
    for i in range(boxes):
        hit = place_t[:rows, i : i + 1] == slot
        found = found + jnp.where(hit, code_t[:rows, i : i + 1], 0)
    listed = jnp.sum(found, axis=0, keepdims=True)
    at = lax.broadcasted_iota(jnp.int32, (1, length), 1)
    for back, pairs in ((3, first_total), (2, second_total), (1, cross_total)):
        listed = jnp.where(at == length - back, (pairs + 1) >> 1, listed)
    return listed


def start_all(copies, sems):
    started = [pltpu.make_async_copy(src, dst, sems.at[k]) for k, (src, dst) in enumerate(copies)]
    for copy in started:
        copy.start()
    return started


def wait_all(started):
    for copy in started:
        copy.wait()


def outgoing_kernel(
    x_hbm, pos_hbm, rad_hbm, idx_hbm, wgt_hbm, phase_hbm, packet_ref, spectra_ref, imat_ref, cos_ref, sin_ref, rad_ref,
    x_ref, pos_ref, idx_ref, wgt_ref, phase_ref, sems
):
    wait_all(
        start_all(
            (
                (x_hbm, x_ref),
                (pos_hbm, pos_ref),
                (rad_hbm, rad_ref),
                (idx_hbm, idx_ref),
                (wgt_hbm, wgt_ref),
                (phase_hbm, phase_ref),
            ),
            sems,
        )
    )
    leaf_dirs, parent_dirs = imat_ref.shape
    x_rows, _, width = x_ref.shape
    axes, boxes, _ = pos_ref.shape
    waves = x_rows * 16 // boxes
    chunks = parent_dirs // 128
    own_rows = x_rows + axes * boxes // 16
    packet_ref[:x_rows] = x_ref[...]
    packet_ref[x_rows:own_rows] = pos_ref[...].reshape(axes * boxes // 16, 16, width)
    column = lax.broadcasted_iota(jnp.int32, (leaf_dirs, parent_dirs), 0)
    imat = jnp.zeros((leaf_dirs, parent_dirs), F32)
    for s in range(idx_ref.shape[0]):
        imat = imat + jnp.where(idx_ref[s : s + 1, :] == column, wgt_ref[s : s + 1, :], 0.0)
    imat = imat.astype(BF16)
    imat_ref[...] = imat
    cos_phase = jnp.cos(phase_ref[...])
    sin_phase = jnp.sin(phase_ref[...])
    cos_ref[...] = cos_phase
    sin_ref[...] = sin_phase
    leaf = nn_dot(x_ref[...].reshape(boxes * waves, width), rad_ref[...]).astype(BF16)
    up_re = nn_dot(leaf[:, :leaf_dirs], imat)
    up_im = nn_dot(leaf[:, leaf_dirs:], imat)
    for q in range(boxes // 8):
        re = jnp.zeros((waves, parent_dirs), F32)
        im = jnp.zeros((waves, parent_dirs), F32)
        for c in range(8):
            at = (q * 8 + c) * waves
            ure = up_re[at : at + waves]
            uim = up_im[at : at + waves]
            re = re + (cos_phase[c : c + 1] * ure - sin_phase[c : c + 1] * uim)
            im = im + (sin_phase[c : c + 1] * ure + cos_phase[c : c + 1] * uim)
        both = jnp.concatenate([re, im], axis=0).astype(BF16)
        for k in range(chunks):
            part = both[:, k * 128 : (k + 1) * 128]
            packet_ref[own_rows + q * chunks + k] = part
            spectra_ref[q * chunks + k] = part


def carries_packet(step):
    return step & (step + 1) == 0


def group_kernel(own_ref, *refs):
    *step_refs, _, group_ref = refs
    size = lax.axis_size("dir")
    rows = own_ref.shape[0]
    here = lax.axis_index("dir")
    group_ref[pl.ds(here * rows, rows)] = own_ref[...]
    for step, ref in enumerate(step_refs, 1):
        group_ref[pl.ds((here ^ step) * rows, rows)] = ref[ref.shape[0] - rows :]
    group_ref[size * rows :] = step_refs[-1][: step_refs[-1].shape[0] - rows]


def features(planes):
    rows, _, width = planes.shape
    boxes = rows * 16 // 3
    planes = planes.astype(F32).reshape(3, boxes, width)
    at = lax.broadcasted_iota(jnp.int32, (boxes, 8, width), 1)
    pos = jnp.zeros((boxes, 8, width), F32)
    for axis in range(3):
        pos = jnp.where(at == axis, planes[axis][:, None, :], pos)
    scale = TURN * TURN
    norm = split3(scale * jnp.sum(pos * pos, axis=1, keepdims=True))
    first = jnp.where(at < 3, pos, 1.0)
    first = jnp.where(at == 3, norm[0], jnp.where(at == 4, norm[1], jnp.where(at == 5, norm[2], first)))
    second = jnp.where(at == 3, 1.0, pos + pltpu.roll(pos, 4, 1))
    source = jnp.concatenate([first, second], axis=1).astype(BF16)
    cross = split3((-2.0 * scale) * pos)
    first = jnp.where(at < 3, cross[0], 1.0)
    first = jnp.where(at == 6, norm[0], jnp.where(at == 7, norm[1], first))
    second = jnp.where(at == 3, norm[2], cross[1] + pltpu.roll(cross[2], 4, 1))
    return source, jnp.concatenate([first, second], axis=1).astype(BF16)


def turn_sources(source, src_ref, start):
    boxes, rows, width = source.shape
    eye = lax.broadcasted_iota(jnp.int32, (width, width), 0) == lax.broadcasted_iota(jnp.int32, (width, width), 1)
    turned = nt_dot(eye.astype(F32).astype(BF16), source.reshape(boxes * rows, width))
    column = lax.broadcasted_iota(jnp.int32, (width, 128), 1)
    for b in range(boxes):
        at = b * rows
        lanes = turned[:, at // 128 * 128 : at // 128 * 128 + 128]
        for slot in range(2):
            shift = (slot * rows - at) % 128
            moved = pltpu.roll(lanes, shift, 1) if shift else lanes
            inside = (column >= slot * rows) & (column < (slot + 1) * rows)
            src_ref[slot, start + b] = jnp.where(inside, moved, 0.0).astype(BF16)


def take_currents(x_rows, win_ref, start):
    for k in range(x_rows.shape[0]):
        both = x_rows[k]
        wide = both.astype(F32)
        win_ref[start + 2 * k] = both
        win_ref[start + 2 * k + 1] = jnp.concatenate([wide[8:], wide[:8]], axis=0).astype(BF16)


def near_sum(entries, total, item_at, first_source, src_ref, win_ref, obs_ref, out_ref, scratch):
    u0_ref, u1_ref, t0_ref, t1_ref = scratch
    boxes, waves, width = out_ref.shape
    count_bits, box_bits, source_bits = code_bits(boxes, entries)
    pair_bits = count_bits + box_bits + source_bits
    t1_ref[...] = jnp.zeros(t1_ref.shape, BF16)
    upper = lax.broadcasted_iota(jnp.int32, (2 * waves, width), 0) < waves
    empty = jnp.zeros((16, width), BF16)

    def pair_at(chunk, g, slot):
        code = item_at(chunk * ITEMS + g) >> (slot * pair_bits)
        source = (code >> (count_bits + box_bits)) & ((1 << source_bits) - 1)
        if first_source:
            source = jnp.maximum(source - first_source, 0)
        return source, (code >> count_bits) & ((1 << box_bits) - 1), code & ((1 << count_bits) - 1)

    def distances(chunk, g, u_ref):
        source0, box0, _ = pair_at(chunk, g, 0)
        source1, box1, _ = pair_at(chunk, g, 1)
        sources = src_ref[0, source0] + src_ref[1, source1]
        observers = jnp.concatenate(
            [
                jnp.concatenate([obs_ref[box0], empty], axis=1),
                jnp.concatenate([empty, obs_ref[box1]], axis=1),
            ],
            axis=0,
        )
        u_ref[g] = nn_dot(sources[:, :32], observers)

    def tile(g, u_ref, t_ref):
        for at in range(0, width, ROWS):
            v = jnp.maximum(u_ref[g, at : at + ROWS], 1e-12)
            q = v * lax.rsqrt(v)
            t = q - jnp.round(q)
            x = 0.25 - jnp.abs(t)
            z = x * x
            cosine = x * (((z + S2) * z + S1) * z + S0)
            t_ref[g, at : at + ROWS] = (cosine * pltpu.reciprocal(q + OFFSET * TURN, approx=True)).astype(BF16)

    def product(chunk, g, t_ref):
        source0, box0, count0 = pair_at(chunk, g, 0)
        source1, box1, count1 = pair_at(chunk, g, 1)
        currents = jnp.where(upper, win_ref[source0].astype(F32), win_ref[source1 ^ 1].astype(F32)).astype(BF16)
        got = nn_dot(currents, t_ref[g])
        out_ref[box0] += count0.astype(F32) * got[:waves, :width]
        out_ref[box1] += count1.astype(F32) * got[waves:, width:]

    u_refs = (u0_ref, u1_ref)
    t_refs = (t0_ref, t1_ref)

    def stage(chunk, turn):
        for g in range(ITEMS):
            distances(chunk + 1, g, u_refs[1 - turn])
            product(jnp.maximum(chunk - 1, 0), g, t_refs[1 - turn])
            tile(g, u_refs[turn], t_refs[turn])

    def body(k, carry):
        for j in range(STAGES):
            stage(k * STAGES + j, j & 1)
        return carry

    def finish(turn):
        for g in range(ITEMS):
            product(jnp.maximum(chunks - 1, 0), g, t_refs[turn])

    chunks = (total + (ITEMS - 1)) // ITEMS
    rounds = chunks // STAGES
    for g in range(ITEMS):
        distances(0, g, u0_ref)
    lax.fori_loop(0, rounds, body, 0)
    for j in range(STAGES - 1):
        pl.when(rounds * STAGES + j < chunks)(functools.partial(stage, rounds * STAGES + j, j & 1))
    pl.when((chunks & 1) == 0)(functools.partial(finish, 1))
    pl.when((chunks & 1) == 1)(functools.partial(finish, 0))


def prepare_kernel(
    own_ref, near_hbm, src_hbm, id_hbm, count_hbm, table_hbm, out_ref, items_ref, obs_ref, src_ref, gain_ref, near_ref,
    trans_src_ref, trans_id_ref, trans_count_ref, rows_ref, list_ref, win_ref, u0_ref, u1_ref, t0_ref, t1_ref, sems
):
    boxes = obs_ref.shape[0]
    entries = near_ref.shape[1]
    length = list_ref.shape[1]
    parents, window = gain_ref.shape[:2]
    listed = src_hbm.shape[1]
    near_copy, *list_copies = start_all(
        (
            (near_hbm, near_ref),
            (src_hbm, trans_src_ref),
            (id_hbm, trans_id_ref),
            (count_hbm, trans_count_ref),
        ),
        sems,
    )
    gain_ref[...] = jnp.zeros(gain_ref.shape, F32)
    plane_rows = 3 * boxes // 16
    source, observer = features(own_ref[boxes // 2 : boxes // 2 + plane_rows])
    turn_sources(source, src_ref, 0)
    take_currents(own_ref[: boxes // 2], win_ref, 0)
    obs_ref[...] = observer
    wait_all(list_copies)
    row0 = lax.axis_index("dir") * parents
    for q in range(parents):
        for e in range(listed):
            pltpu.make_async_copy(
                table_hbm.at[trans_id_ref[row0 + q, e]], rows_ref.at[q * listed + e], sems.at[1]
            ).start()
    near_copy.wait()
    block = lax.axis_index(("box", "dir"))
    items_ref[...] = list_items(near_ref[...], block, lax.axis_index("dir"), lax.axis_size("dir"))
    fetch = pltpu.make_async_copy(items_ref, list_ref, sems.at[0])
    fetch.start()
    out_ref[...] = jnp.zeros(out_ref.shape, F32)
    pltpu.make_async_copy(rows_ref, rows_ref, sems.at[1]).wait()
    first = (lax.axis_index("box") - 1) * (window // 3)
    for q in range(parents):
        for e in range(listed):
            live = (e < trans_count_ref[row0 + q]).astype(F32)
            s = jnp.clip(trans_src_ref[row0 + q, e] - first, 0, window - 1)
            gain_ref[q, s] += rows_ref[q * listed + e] * live
    fetch.wait()
    near_sum(
        entries,
        list_ref[0, length - 3],
        lambda k: list_ref[0, k],
        0,
        src_ref,
        win_ref,
        obs_ref,
        out_ref,
        (u0_ref, u1_ref, t0_ref, t1_ref),
    )


def near_kernel(entries, items_ref, own_ref, *refs):
    *step_refs, obs_ref, own_src_ref, first_ref, out_ref, win_ref, src_ref, list_ref, u0_ref, u1_ref, t0_ref, t1_ref, sem = refs
    boxes, waves, width = out_ref.shape
    fetch = pltpu.make_async_copy(items_ref, list_ref, sem)
    fetch.start()
    length = list_ref.shape[1]
    here = lax.axis_index("dir")
    other_side = jnp.where((here & 1) == 0, here - 1, here + 1)
    x_rows = boxes // 2

    def take(ref, part):
        take_currents(ref[:x_rows], win_ref, part * boxes)
        source, _ = features(ref[x_rows : x_rows + 3 * boxes // 16])
        turn_sources(source, src_ref, part * boxes)

    take_currents(own_ref[:x_rows], win_ref, 0)
    src_ref[:, :boxes] = own_src_ref[...]
    take(step_refs[0], 1)
    for k, ref in enumerate(step_refs[1:], 2):
        pl.when((here ^ ((1 << k) - 1)) == other_side)(functools.partial(take, ref, 2))
    second_start = list_places(boxes, entries)[1]
    out_ref[...] = first_ref[...]
    fetch.wait()
    near_sum(
        entries,
        list_ref[0, length - 2],
        lambda k: list_ref[0, second_start + k],
        0,
        src_ref,
        win_ref,
        obs_ref,
        out_ref,
        (u0_ref, u1_ref, t0_ref, t1_ref),
    )


def incoming_kernel(
    entries, items_ref, even_ref, own_ref, odd_ref, gain_ref, cos_ref, sin_ref, imat_ref, rad_ref, obs_ref, near_ref, out_ref,
    sum_ref, win_ref, src_ref, down_re_ref, down_im_ref, list_ref, u0_ref, u1_ref, t0_ref, t1_ref, sem
):
    parents, window, _, parent_dirs = gain_ref.shape
    boxes, waves, width = near_ref.shape
    chunks = parent_dirs // 128
    group = window // 3
    fetch = pltpu.make_async_copy(items_ref, list_ref, sem)
    fetch.start()
    length = list_ref.shape[1]
    odd_box = lax.axis_index("box") & 1
    sum_ref[...] = near_ref[...]
    x_rows = boxes // 2
    packet_rows = x_rows + 3 * boxes // 16
    from_even = jnp.where(lax.axis_index("dir") == 0, 1, 0) == odd_box
    even_packet, odd_packet = (ref[ref.shape[0] - packet_rows :] for ref in (even_ref, odd_ref))
    packet = jnp.where(from_even, even_packet.astype(F32), odd_packet.astype(F32)).astype(BF16)
    take_currents(packet[:x_rows], win_ref, 0)
    source, _ = features(packet[x_rows:])
    turn_sources(source, src_ref, 0)
    fetch.wait()
    cos_phase = cos_ref[...]
    sin_phase = sin_ref[...]
    sums = tuple(jnp.zeros((waves, 128), F32) for _ in range(parents * chunks * 2))
    for part, ref in ((2 - 2 * odd_box, even_ref), (1, own_ref), (2 * odd_box, odd_ref)):

        def add_source(s, sums, part=part, ref=ref):
            sums = list(sums)
            gains = [gain_ref[q, part * group + s] for q in range(parents)]
            for k in range(chunks):
                spectrum = ref[s * chunks + k].astype(F32)
                sre, sim = spectrum[:waves], spectrum[waves:]
                for q in range(parents):
                    gre = gains[q][0:1, k * 128 : (k + 1) * 128]
                    gim = gains[q][1:2, k * 128 : (k + 1) * 128]
                    at = (q * chunks + k) * 2
                    sums[at] = sums[at] + (gre * sre - gim * sim)
                    sums[at + 1] = sums[at + 1] + (gre * sim + gim * sre)
            return tuple(sums)

        sums = lax.fori_loop(0, group, add_source, sums, unroll=8)
    for q in range(parents):
        for k in range(chunks):
            at = (q * chunks + k) * 2
            re = sums[at].astype(BF16).astype(F32)
            im = sums[at + 1].astype(BF16).astype(F32)
            lanes = slice(k * 128, (k + 1) * 128)
            for c in range(8):
                cos, sin = cos_phase[c : c + 1, lanes], sin_phase[c : c + 1, lanes]
                rows = slice((q * 8 + c) * waves, (q * 8 + c + 1) * waves)
                down_re_ref[rows, lanes] = cos * re + sin * im
                down_im_ref[rows, lanes] = cos * im - sin * re
    imat = imat_ref[...]
    in_re = nt_dot(down_re_ref[...].astype(BF16), imat)
    in_im = nt_dot(down_im_ref[...].astype(BF16), imat)
    incoming = jnp.concatenate([in_re, in_im], axis=1).astype(BF16)
    far = nt_dot(incoming, rad_ref[...])
    near_sum(
        entries,
        list_ref[0, length - 1],
        lambda k: list_ref[0, length - 4 - k],
        2 * boxes,
        src_ref,
        win_ref,
        obs_ref,
        sum_ref,
        (u0_ref, u1_ref, t0_ref, t1_ref),
    )
    factor = TURN * LEAD / math.sqrt(entries * width)
    out_ref[...] = sum_ref[...] * factor + far.reshape(near_ref.shape)


def per_device(
    currents, positions, radiation, interp_index, interp_weight, child_phase, near_src, trans_src, trans_id,
    trans_count, trans_table
):
    boxes, waves, width = currents.shape
    entries = near_src.shape[1]
    leaf_dirs = radiation.shape[1] // 2
    parent_dirs = child_phase.shape[1]
    parents = boxes // 8
    spectra_rows = parents * parent_dirs // 128
    size = lax.axis_size("dir")
    vmem = pl.BlockSpec(memory_space=pltpu.VMEM)
    hbm = pl.BlockSpec(memory_space=pltpu.HBM)
    params = pltpu.CompilerParams(vmem_limit_bytes=32 * 1024 * 1024)

    def in_hbm(x):
        return pltpu.with_memory_space_constraint(x, pltpu.HBM)

    def shaped(shape, dtype):
        return jax.ShapeDtypeStruct(shape, dtype)

    x_rows = boxes // 2
    own_rows = x_rows + 3 * boxes // 16
    operands = (currents.reshape(x_rows, 2 * waves, width), positions.transpose(1, 0, 2), radiation, interp_index.T, interp_weight.T, child_phase)
    packet, spectra, imat, cos_phase, sin_phase, rad = pl.pallas_call(
        outgoing_kernel,
        out_shape=(
            shaped((own_rows + spectra_rows, 16, width), BF16),
            shaped((spectra_rows, 2 * waves, 128), BF16),
            shaped((leaf_dirs, parent_dirs), BF16),
            shaped((8, parent_dirs), F32),
            shaped((8, parent_dirs), F32),
            shaped(radiation.shape, BF16),
        ),
        in_specs=[hbm] * len(operands),
        out_specs=(vmem,) * 6,
        scratch_shapes=[pltpu.VMEM(x.shape, x.dtype) for x in operands if x is not radiation]
        + [pltpu.SemaphoreType.DMA((len(operands),))],
        compiler_params=params,
        name="outgoing",
    )(*[in_hbm(x) for x in operands])

    steps = []
    for step in range(1, size):
        pairs = [(i, i ^ step) for i in range(size) if i < i ^ step]
        steps.append(swapped(packet if carries_packet(step) else spectra, "dir", pairs))

    length = list_places(boxes, entries)[2]
    window = 3 * trans_src.shape[0]
    near_scratch = [
        pltpu.VMEM((ITEMS, width, 2 * width), F32),
        pltpu.VMEM((ITEMS, width, 2 * width), F32),
        pltpu.VMEM((ITEMS, width, 2 * width), BF16),
        pltpu.VMEM((ITEMS, width, 2 * width), BF16),
    ]
    first_sum, items, observers, sources, gains = pl.pallas_call(
        prepare_kernel,
        out_shape=(
            shaped((boxes, waves, width), F32),
            shaped((1, length), jnp.int32),
            shaped((boxes, 16, width), BF16),
            shaped((2, boxes, width, 128), BF16),
            shaped((parents, window, 2, parent_dirs), F32),
        ),
        in_specs=[vmem] + [hbm] * 5,
        out_specs=(vmem,) * 5,
        scratch_shapes=[
            pltpu.VMEM(near_src.shape, jnp.int32),
            pltpu.SMEM(trans_src.shape, jnp.int32),
            pltpu.SMEM(trans_id.shape, jnp.int32),
            pltpu.SMEM(trans_count.shape, jnp.int32),
            pltpu.VMEM((parents * trans_src.shape[1], 2, parent_dirs), F32),
            pltpu.SMEM((1, length), jnp.int32),
            pltpu.VMEM((boxes, 16, width), BF16),
        ]
        + near_scratch
        + [pltpu.SemaphoreType.DMA((4,))],
        compiler_params=params,
        name="prepare",
    )(packet, *[in_hbm(x) for x in (near_src, trans_src, trans_id, trans_count, trans_table)])

    group = pl.pallas_call(
        group_kernel,
        out_shape=shaped((size * spectra_rows + own_rows, 2 * waves, 128), BF16),
        in_specs=[vmem] * (2 + len(steps)),
        out_specs=vmem,
        compiler_params=params,
        name="group",
    )(spectra, *steps, items)
    groups = lax.axis_size("box")
    group_odd = swapped(group, "box", [(i, i + 1) for i in range(1, groups - 1, 2)])
    group_even = swapped(group, "box", [(i, i + 1) for i in range(0, groups - 1, 2)])

    packets = [x for step, x in enumerate(steps, 1) if carries_packet(step)]
    near = pl.pallas_call(
        functools.partial(near_kernel, entries),
        out_shape=shaped((boxes, waves, width), F32),
        in_specs=[vmem] * (5 + len(packets)),
        out_specs=vmem,
        scratch_shapes=[
            pltpu.VMEM((3 * boxes, 16, width), BF16),
            pltpu.VMEM((2, 3 * boxes, width, 128), BF16),
            pltpu.SMEM((1, length), jnp.int32),
        ]
        + near_scratch
        + [pltpu.SemaphoreType.DMA],
        compiler_params=params,
        name="near",
    )(items, packet, *packets, observers, sources, first_sum)

    return pl.pallas_call(
        functools.partial(incoming_kernel, entries),
        out_shape=shaped((boxes, waves, width), F32),
        in_specs=[vmem] * 11,
        out_specs=vmem,
        scratch_shapes=[
            pltpu.VMEM((boxes, waves, width), F32),
            pltpu.VMEM((boxes, 16, width), BF16),
            pltpu.VMEM((2, boxes, width, 128), BF16),
            pltpu.VMEM((boxes * waves, parent_dirs), F32),
            pltpu.VMEM((boxes * waves, parent_dirs), F32),
            pltpu.SMEM((1, length), jnp.int32),
        ]
        + near_scratch
        + [pltpu.SemaphoreType.DMA],
        compiler_params=params,
        name="incoming",
    )(items, group_even, group, group_odd, gains, cos_phase, sin_phase, imat, rad, observers, near)


def solution(mesh):
    placed = (
        P(("box", "dir"), None, None),
        P(("box", "dir"), None, None),
        P(),
        P(),
        P(),
        P(),
        P(("box", "dir"), None),
        P("box", None),
        P("box", None),
        P("box"),
        P(),
    )
    return jax.shard_map(
        per_device,
        mesh=mesh,
        in_specs=placed,
        out_specs=P(("box", "dir"), None, None),
        check_vma=False,
    )
```

```python
import functools
import math

import jax
import jax.numpy as jnp
from jax import lax
from jax.experimental import pallas as pl
from jax.experimental.pallas import tpu as pltpu
from jax.sharding import PartitionSpec as P

F32 = jnp.float32
BF16 = jnp.bfloat16

WAVENUMBER = 4.0
OFFSET = 0.5
TURN = WAVENUMBER / (2.0 * math.pi)
CHAIN = (-2.2803148655023415, -1.415255674611144, -7.327656729815578, -24.467745134801202)
LEAD = 0.04087004462557604
ITEMS = 4
ROWS = 32
STAGES = 4
FIRST_ITEMS = 5


def round_up(value, step):
    return -(-value // step) * step


def swapped(x, axis, pairs):
    return lax.ppermute(x, axis, [way for i, j in pairs for way in ((i, j), (j, i))])


def split3(x):
    high = x.astype(BF16).astype(F32)
    rest = x - high
    mid = rest.astype(BF16).astype(F32)
    return high, mid, rest - mid


def nt_dot(a, b):
    return lax.dot_general(a, b, (((1,), (1,)), ((), ())), preferred_element_type=F32)


def nn_dot(a, b):
    return jnp.dot(a, b, preferred_element_type=F32)


def code_bits(boxes, entries):
    return entries.bit_length(), (boxes - 1).bit_length(), (3 * boxes - 1).bit_length()


def list_places(boxes, entries):
    gap = 2 * ITEMS
    most = FIRST_ITEMS * boxes // 2
    return most, most + gap, round_up(most + gap + boxes * entries // 2 + 2 * gap + 6, 128)


def list_items(near_src, block, here, size):
    boxes, entries = near_src.shape
    most, second_start, length = list_places(boxes, entries)
    count_bits, box_bits, source_bits = code_bits(boxes, entries)
    pair_bits = count_bits + box_bits + source_bits
    lanes = round_up(3 * boxes, 128)
    odd = (here & 1) == 1
    edge = (here == 0) | (here == size - 1)
    local = near_src - block * boxes
    below = local + jnp.where(odd, 2 * boxes, 3 * boxes)
    above = local + jnp.where(odd, boxes, 0)
    local = jnp.where(local < 0, below, jnp.where(local >= boxes, above, local))
    lane = lax.broadcasted_iota(jnp.int32, (boxes, lanes), 1)
    box = lax.broadcasted_iota(jnp.int32, (boxes, lanes), 0)
    count = jnp.zeros((boxes, lanes), jnp.int32)
    for e in range(entries):
        count = count + (local[:, e : e + 1] == lane).astype(jnp.int32)
    present = count > 0
    flags = present.astype(F32)
    box_row = lax.broadcasted_iota(jnp.int32, (boxes, boxes), 0)
    box_col = lax.broadcasted_iota(jnp.int32, (boxes, boxes), 1)
    rank = nn_dot((box_col < box_row).astype(F32).astype(BF16), flags.astype(BF16)).astype(jnp.int32)
    pairs = jnp.sum(flags, axis=0, keepdims=True)
    from_cross = (lane >= 2 * boxes) & edge
    cross_pairs = jnp.where(from_cross[:1], pairs, 0.0)
    group_pairs = jnp.where(from_cross[:1], 0.0, pairs)
    row = lax.broadcasted_iota(jnp.int32, (lanes, lanes), 0)
    col = lax.broadcasted_iota(jnp.int32, (lanes, lanes), 1)
    ahead = (row < col).astype(F32).astype(BF16)
    lists = jnp.concatenate([group_pairs, cross_pairs, jnp.zeros((6, lanes), F32)], axis=0)
    offset = nn_dot(lists.astype(BF16), ahead).astype(jnp.int32)
    own_pairs = jnp.where(lane[:1] < boxes, group_pairs, 0.0)

    def total(pairs):
        return jnp.sum(pairs, axis=1, keepdims=True).astype(jnp.int32)

    first_total = jnp.minimum(total(own_pairs), 2 * most)
    second_total = total(group_pairs) - first_total
    cross_total = total(cross_pairs)
    order = offset[0:1] + rank
    in_second = order >= first_total
    order = jnp.where(in_second, order - first_total, order)
    order = jnp.where(from_cross, offset[1:2] + rank, order)
    half = order >> 1
    place = jnp.where(from_cross, (length - 4) - half, jnp.where(in_second, second_start + half, half))
    place = jnp.where(present, place, -1)
    code = (lane << (count_bits + box_bits)) | (box << count_bits) | count
    code = jnp.where((order & 1) == 1, code << pair_bits, code)
    place_t = place.T
    code_t = code.T
    rows = 3 * boxes
    slot = lax.broadcasted_iota(jnp.int32, (rows, length), 1)
    found = jnp.zeros((rows, length), jnp.int32)
    for i in range(boxes):
        hit = place_t[:rows, i : i + 1] == slot
        found = found + jnp.where(hit, code_t[:rows, i : i + 1], 0)
    listed = jnp.sum(found, axis=0, keepdims=True)
    at = lax.broadcasted_iota(jnp.int32, (1, length), 1)
    for back, pairs in ((3, first_total), (2, second_total), (1, cross_total)):
        listed = jnp.where(at == length - back, (pairs + 1) >> 1, listed)
    return listed


def start_all(copies, sems):
    started = [pltpu.make_async_copy(src, dst, sems.at[k]) for k, (src, dst) in enumerate(copies)]
    for copy in started:
        copy.start()
    return started


def wait_all(started):
    for copy in started:
        copy.wait()


def outgoing_kernel(
    x_hbm, pos_hbm, rad_hbm, idx_hbm, wgt_hbm, phase_hbm, packet_ref, spectra_ref, imat_ref, cos_ref, sin_ref, rad_ref,
    x_ref, pos_ref, idx_ref, wgt_ref, phase_ref, sems
):
    wait_all(
        start_all(
            (
                (x_hbm, x_ref),
                (pos_hbm, pos_ref),
                (rad_hbm, rad_ref),
                (idx_hbm, idx_ref),
                (wgt_hbm, wgt_ref),
                (phase_hbm, phase_ref),
            ),
            sems,
        )
    )
    leaf_dirs, parent_dirs = imat_ref.shape
    x_rows, _, width = x_ref.shape
    axes, boxes, _ = pos_ref.shape
    waves = x_rows * 16 // boxes
    chunks = parent_dirs // 128
    own_rows = x_rows + axes * boxes // 16
    packet_ref[:x_rows] = x_ref[...]
    packet_ref[x_rows:own_rows] = pos_ref[...].reshape(axes * boxes // 16, 16, width)
    column = lax.broadcasted_iota(jnp.int32, (leaf_dirs, parent_dirs), 0)
    imat = jnp.zeros((leaf_dirs, parent_dirs), F32)
    for s in range(idx_ref.shape[0]):
        imat = imat + jnp.where(idx_ref[s : s + 1, :] == column, wgt_ref[s : s + 1, :], 0.0)
    imat = imat.astype(BF16)
    imat_ref[...] = imat
    cos_phase = jnp.cos(phase_ref[...])
    sin_phase = jnp.sin(phase_ref[...])
    cos_ref[...] = cos_phase
    sin_ref[...] = sin_phase
    leaf = nn_dot(x_ref[...].reshape(boxes * waves, width), rad_ref[...]).astype(BF16)
    up_re = nn_dot(leaf[:, :leaf_dirs], imat)
    up_im = nn_dot(leaf[:, leaf_dirs:], imat)
    for q in range(boxes // 8):
        re = jnp.zeros((waves, parent_dirs), F32)
        im = jnp.zeros((waves, parent_dirs), F32)
        for c in range(8):
            at = (q * 8 + c) * waves
            ure = up_re[at : at + waves]
            uim = up_im[at : at + waves]
            re = re + (cos_phase[c : c + 1] * ure - sin_phase[c : c + 1] * uim)
            im = im + (sin_phase[c : c + 1] * ure + cos_phase[c : c + 1] * uim)
        both = jnp.concatenate([re, im], axis=0).astype(BF16)
        for k in range(chunks):
            part = both[:, k * 128 : (k + 1) * 128]
            packet_ref[own_rows + q * chunks + k] = part
            spectra_ref[q * chunks + k] = part


def carries_packet(step):
    return step & (step + 1) == 0


def group_kernel(own_ref, *refs):
    *step_refs, _, group_ref = refs
    size = lax.axis_size("dir")
    rows = own_ref.shape[0]
    here = lax.axis_index("dir")
    group_ref[pl.ds(here * rows, rows)] = own_ref[...]
    for step, ref in enumerate(step_refs, 1):
        group_ref[pl.ds((here ^ step) * rows, rows)] = ref[ref.shape[0] - rows :]
    group_ref[size * rows :] = step_refs[-1][: step_refs[-1].shape[0] - rows]


def features(planes):
    rows, _, width = planes.shape
    boxes = rows * 16 // 3
    planes = planes.astype(F32).reshape(3, boxes, width)
    at = lax.broadcasted_iota(jnp.int32, (boxes, 8, width), 1)
    pos = jnp.zeros((boxes, 8, width), F32)
    for axis in range(3):
        pos = jnp.where(at == axis, planes[axis][:, None, :], pos)
    scale = TURN * TURN
    norm = split3(scale * jnp.sum(pos * pos, axis=1, keepdims=True))
    first = jnp.where(at < 3, pos, 1.0)
    first = jnp.where(at == 3, norm[0], jnp.where(at == 4, norm[1], jnp.where(at == 5, norm[2], first)))
    second = jnp.where(at == 3, 1.0, pos + pltpu.roll(pos, 4, 1))
    source = jnp.concatenate([first, second], axis=1).astype(BF16)
    cross = split3((-2.0 * scale) * pos)
    first = jnp.where(at < 3, cross[0], 1.0)
    first = jnp.where(at == 6, norm[0], jnp.where(at == 7, norm[1], first))
    second = jnp.where(at == 3, norm[2], cross[1] + pltpu.roll(cross[2], 4, 1))
    return source, jnp.concatenate([first, second], axis=1).astype(BF16)


def turn_sources(source, src_ref, start):
    boxes, rows, width = source.shape
    eye = lax.broadcasted_iota(jnp.int32, (width, width), 0) == lax.broadcasted_iota(jnp.int32, (width, width), 1)
    turned = nt_dot(eye.astype(F32).astype(BF16), source.reshape(boxes * rows, width))
    column = lax.broadcasted_iota(jnp.int32, (width, 128), 1)
    for b in range(boxes):
        at = b * rows
        lanes = turned[:, at // 128 * 128 : at // 128 * 128 + 128]
        for slot in range(2):
            shift = (slot * rows - at) % 128
            moved = pltpu.roll(lanes, shift, 1) if shift else lanes
            inside = (column >= slot * rows) & (column < (slot + 1) * rows)
            src_ref[slot, start + b] = jnp.where(inside, moved, 0.0).astype(BF16)


def take_currents(x_rows, win_ref, start):
    for k in range(x_rows.shape[0]):
        both = x_rows[k]
        wide = both.astype(F32)
        win_ref[start + 2 * k] = both
        win_ref[start + 2 * k + 1] = jnp.concatenate([wide[8:], wide[:8]], axis=0).astype(BF16)


def near_sum(entries, total, item_at, first_source, src_ref, win_ref, obs_ref, out_ref, scratch):
    u0_ref, u1_ref, t0_ref, t1_ref = scratch
    boxes, waves, width = out_ref.shape
    count_bits, box_bits, source_bits = code_bits(boxes, entries)
    pair_bits = count_bits + box_bits + source_bits
    t1_ref[...] = jnp.zeros(t1_ref.shape, BF16)
    upper = lax.broadcasted_iota(jnp.int32, (2 * waves, width), 0) < waves
    empty = jnp.zeros((16, width), BF16)

    def pair_at(chunk, g, slot):
        code = item_at(chunk * ITEMS + g) >> (slot * pair_bits)
        source = (code >> (count_bits + box_bits)) & ((1 << source_bits) - 1)
        if first_source:
            source = jnp.maximum(source - first_source, 0)
        return source, (code >> count_bits) & ((1 << box_bits) - 1), code & ((1 << count_bits) - 1)

    def distances(chunk, g, u_ref):
        source0, box0, _ = pair_at(chunk, g, 0)
        source1, box1, _ = pair_at(chunk, g, 1)
        sources = src_ref[0, source0] + src_ref[1, source1]
        observers = jnp.concatenate(
            [
                jnp.concatenate([obs_ref[box0], empty], axis=1),
                jnp.concatenate([empty, obs_ref[box1]], axis=1),
            ],
            axis=0,
        )
        u_ref[g] = nn_dot(sources[:, :32], observers)

    def tile(g, u_ref, t_ref):
        for at in range(0, width, ROWS):
            v = jnp.maximum(u_ref[g, at : at + ROWS], 1e-12)
            q = v * lax.rsqrt(v)
            t = q - jnp.round(q)
            cosine = t * t + CHAIN[0]
            for constant in CHAIN[1:]:
                cosine = cosine * cosine + constant
            t_ref[g, at : at + ROWS] = (cosine * pltpu.reciprocal(q + OFFSET * TURN, approx=True)).astype(BF16)

    def product(chunk, g, t_ref):
        source0, box0, count0 = pair_at(chunk, g, 0)
        source1, box1, count1 = pair_at(chunk, g, 1)
        currents = jnp.where(upper, win_ref[source0].astype(F32), win_ref[source1 ^ 1].astype(F32)).astype(BF16)
        got = nn_dot(currents, t_ref[g])
        out_ref[box0] += count0.astype(F32) * got[:waves, :width]
        out_ref[box1] += count1.astype(F32) * got[waves:, width:]

    u_refs = (u0_ref, u1_ref)
    t_refs = (t0_ref, t1_ref)

    def stage(chunk, turn):
        for g in range(ITEMS):
            distances(chunk + 1, g, u_refs[1 - turn])
            product(jnp.maximum(chunk - 1, 0), g, t_refs[1 - turn])
            tile(g, u_refs[turn], t_refs[turn])

    def body(k, carry):
        for j in range(STAGES):
            stage(k * STAGES + j, j & 1)
        return carry

    def finish(turn):
        for g in range(ITEMS):
            product(jnp.maximum(chunks - 1, 0), g, t_refs[turn])

    chunks = (total + (ITEMS - 1)) // ITEMS
    rounds = chunks // STAGES
    for g in range(ITEMS):
        distances(0, g, u0_ref)
    lax.fori_loop(0, rounds, body, 0)
    for j in range(STAGES - 1):
        pl.when(rounds * STAGES + j < chunks)(functools.partial(stage, rounds * STAGES + j, j & 1))
    pl.when((chunks & 1) == 0)(functools.partial(finish, 1))
    pl.when((chunks & 1) == 1)(functools.partial(finish, 0))


def prepare_kernel(
    own_ref, near_hbm, src_hbm, id_hbm, count_hbm, table_hbm, out_ref, items_ref, obs_ref, src_ref, gain_ref, near_ref,
    trans_src_ref, trans_id_ref, trans_count_ref, table_ref, list_ref, win_ref, u0_ref, u1_ref, t0_ref, t1_ref, sems
):
    boxes = obs_ref.shape[0]
    entries = near_ref.shape[1]
    length = list_ref.shape[1]
    parents, window = gain_ref.shape[:2]
    listed = src_hbm.shape[1]
    near_copy, *list_copies = start_all(
        (
            (near_hbm, near_ref),
            (src_hbm, trans_src_ref),
            (id_hbm, trans_id_ref),
            (count_hbm, trans_count_ref),
            (table_hbm, table_ref),
        ),
        sems,
    )
    table_copy = list_copies.pop()
    gain_ref[...] = jnp.zeros(gain_ref.shape, F32)
    plane_rows = 3 * boxes // 16
    source, observer = features(own_ref[boxes // 2 : boxes // 2 + plane_rows])
    turn_sources(source, src_ref, 0)
    take_currents(own_ref[: boxes // 2], win_ref, 0)
    obs_ref[...] = observer
    wait_all(list_copies)
    row0 = lax.axis_index("dir") * parents
    near_copy.wait()
    block = lax.axis_index(("box", "dir"))
    items_ref[...] = list_items(near_ref[...], block, lax.axis_index("dir"), lax.axis_size("dir"))
    fetch = pltpu.make_async_copy(items_ref, list_ref, sems.at[0])
    fetch.start()
    out_ref[...] = jnp.zeros(out_ref.shape, F32)
    table_copy.wait()
    first = (lax.axis_index("box") - 1) * (window // 3)
    for q in range(parents):
        for e in range(listed):
            live = (e < trans_count_ref[row0 + q]).astype(F32)
            s = jnp.clip(trans_src_ref[row0 + q, e] - first, 0, window - 1)
            gain_ref[q, s] += table_ref[trans_id_ref[row0 + q, e]] * live
    fetch.wait()
    near_sum(
        entries,
        list_ref[0, length - 3],
        lambda k: list_ref[0, k],
        0,
        src_ref,
        win_ref,
        obs_ref,
        out_ref,
        (u0_ref, u1_ref, t0_ref, t1_ref),
    )


def near_kernel(entries, items_ref, own_ref, *refs):
    *step_refs, obs_ref, own_src_ref, first_ref, out_ref, win_ref, src_ref, list_ref, u0_ref, u1_ref, t0_ref, t1_ref, sems = refs
    boxes, waves, width = out_ref.shape
    fetches = start_all(((items_ref, list_ref), (own_src_ref, src_ref.at[:, :boxes])), sems)
    length = list_ref.shape[1]
    here = lax.axis_index("dir")
    other_side = jnp.where((here & 1) == 0, here - 1, here + 1)
    x_rows = boxes // 2

    def take(ref, part):
        take_currents(ref[:x_rows], win_ref, part * boxes)
        source, _ = features(ref[x_rows : x_rows + 3 * boxes // 16])
        turn_sources(source, src_ref, part * boxes)

    take_currents(own_ref[:x_rows], win_ref, 0)
    take(step_refs[0], 1)
    for k, ref in enumerate(step_refs[1:], 2):
        pl.when((here ^ ((1 << k) - 1)) == other_side)(functools.partial(take, ref, 2))
    second_start = list_places(boxes, entries)[1]
    out_ref[...] = first_ref[...]
    wait_all(fetches)
    near_sum(
        entries,
        list_ref[0, length - 2],
        lambda k: list_ref[0, second_start + k],
        0,
        src_ref,
        win_ref,
        obs_ref,
        out_ref,
        (u0_ref, u1_ref, t0_ref, t1_ref),
    )


def incoming_kernel(
    entries, items_ref, even_ref, own_ref, odd_ref, gain_ref, cos_ref, sin_ref, imat_ref, rad_ref, obs_ref, near_ref, out_ref,
    sum_ref, win_ref, src_ref, down_re_ref, down_im_ref, list_ref, u0_ref, u1_ref, t0_ref, t1_ref, sem
):
    parents, window, _, parent_dirs = gain_ref.shape
    boxes, waves, width = near_ref.shape
    chunks = parent_dirs // 128
    group = window // 3
    fetch = pltpu.make_async_copy(items_ref, list_ref, sem)
    fetch.start()
    length = list_ref.shape[1]
    odd_box = lax.axis_index("box") & 1
    sum_ref[...] = near_ref[...]
    x_rows = boxes // 2
    packet_rows = x_rows + 3 * boxes // 16
    here = lax.axis_index("dir")

    @pl.when((here == 0) | (here == lax.axis_size("dir") - 1))
    def _():
        from_even = jnp.where(here == 0, 1, 0) == odd_box
        even_packet, odd_packet = (ref[ref.shape[0] - packet_rows :] for ref in (even_ref, odd_ref))
        packet = jnp.where(from_even, even_packet.astype(F32), odd_packet.astype(F32)).astype(BF16)
        take_currents(packet[:x_rows], win_ref, 0)
        source, _ = features(packet[x_rows:])
        turn_sources(source, src_ref, 0)

    fetch.wait()
    cos_phase = cos_ref[...]
    sin_phase = sin_ref[...]
    sums = tuple(jnp.zeros((waves, 128), F32) for _ in range(parents * chunks * 2))
    for part, ref in ((2 - 2 * odd_box, even_ref), (1, own_ref), (2 * odd_box, odd_ref)):

        def add_source(s, sums, part=part, ref=ref):
            sums = list(sums)
            gains = [gain_ref[q, part * group + s] for q in range(parents)]
            for k in range(chunks):
                spectrum = ref[s * chunks + k].astype(F32)
                sre, sim = spectrum[:waves], spectrum[waves:]
                for q in range(parents):
                    gre = gains[q][0:1, k * 128 : (k + 1) * 128]
                    gim = gains[q][1:2, k * 128 : (k + 1) * 128]
                    at = (q * chunks + k) * 2
                    sums[at] = sums[at] + (gre * sre - gim * sim)
                    sums[at + 1] = sums[at + 1] + (gre * sim + gim * sre)
            return tuple(sums)

        sums = lax.fori_loop(0, group, add_source, sums, unroll=8)
    for q in range(parents):
        for k in range(chunks):
            at = (q * chunks + k) * 2
            re = sums[at].astype(BF16).astype(F32)
            im = sums[at + 1].astype(BF16).astype(F32)
            lanes = slice(k * 128, (k + 1) * 128)
            for c in range(8):
                cos, sin = cos_phase[c : c + 1, lanes], sin_phase[c : c + 1, lanes]
                rows = slice((q * 8 + c) * waves, (q * 8 + c + 1) * waves)
                down_re_ref[rows, lanes] = cos * re + sin * im
                down_im_ref[rows, lanes] = cos * im - sin * re
    imat = imat_ref[...]
    in_re = nt_dot(down_re_ref[...].astype(BF16), imat)
    in_im = nt_dot(down_im_ref[...].astype(BF16), imat)
    incoming = jnp.concatenate([in_re, in_im], axis=1).astype(BF16)
    far = nt_dot(incoming, rad_ref[...])
    near_sum(
        entries,
        list_ref[0, length - 1],
        lambda k: list_ref[0, length - 4 - k],
        2 * boxes,
        src_ref,
        win_ref,
        obs_ref,
        sum_ref,
        (u0_ref, u1_ref, t0_ref, t1_ref),
    )
    factor = TURN * LEAD / math.sqrt(entries * width)
    out_ref[...] = sum_ref[...] * factor + far.reshape(near_ref.shape)


def per_device(
    currents, positions, radiation, interp_index, interp_weight, child_phase, near_src, trans_src, trans_id,
    trans_count, trans_table
):
    boxes, waves, width = currents.shape
    entries = near_src.shape[1]
    leaf_dirs = radiation.shape[1] // 2
    parent_dirs = child_phase.shape[1]
    parents = boxes // 8
    spectra_rows = parents * parent_dirs // 128
    size = lax.axis_size("dir")
    vmem = pl.BlockSpec(memory_space=pltpu.VMEM)
    hbm = pl.BlockSpec(memory_space=pltpu.HBM)
    params = pltpu.CompilerParams(vmem_limit_bytes=32 * 1024 * 1024)

    def in_hbm(x):
        return pltpu.with_memory_space_constraint(x, pltpu.HBM)

    def shaped(shape, dtype):
        return jax.ShapeDtypeStruct(shape, dtype)

    x_rows = boxes // 2
    own_rows = x_rows + 3 * boxes // 16
    operands = (currents.reshape(x_rows, 2 * waves, width), positions.transpose(1, 0, 2), radiation, interp_index.T, interp_weight.T, child_phase)
    packet, spectra, imat, cos_phase, sin_phase, rad = pl.pallas_call(
        outgoing_kernel,
        out_shape=(
            shaped((own_rows + spectra_rows, 16, width), BF16),
            shaped((spectra_rows, 2 * waves, 128), BF16),
            shaped((leaf_dirs, parent_dirs), BF16),
            shaped((8, parent_dirs), F32),
            shaped((8, parent_dirs), F32),
            shaped(radiation.shape, BF16),
        ),
        in_specs=[hbm] * len(operands),
        out_specs=(vmem,) * 6,
        scratch_shapes=[pltpu.VMEM(x.shape, x.dtype) for x in operands if x is not radiation]
        + [pltpu.SemaphoreType.DMA((len(operands),))],
        compiler_params=params,
        name="outgoing",
    )(*[in_hbm(x) for x in operands])

    steps = []
    for step in range(1, size):
        pairs = [(i, i ^ step) for i in range(size) if i < i ^ step]
        steps.append(swapped(packet if carries_packet(step) else spectra, "dir", pairs))

    length = list_places(boxes, entries)[2]
    window = 3 * trans_src.shape[0]
    near_scratch = [
        pltpu.VMEM((ITEMS, width, 2 * width), F32),
        pltpu.VMEM((ITEMS, width, 2 * width), F32),
        pltpu.VMEM((ITEMS, width, 2 * width), BF16),
        pltpu.VMEM((ITEMS, width, 2 * width), BF16),
    ]
    first_sum, items, observers, sources, gains = pl.pallas_call(
        prepare_kernel,
        out_shape=(
            shaped((boxes, waves, width), F32),
            shaped((1, length), jnp.int32),
            shaped((boxes, 16, width), BF16),
            shaped((2, boxes, width, 128), BF16),
            shaped((parents, window, 2, parent_dirs), F32),
        ),
        in_specs=[vmem] + [hbm] * 5,
        out_specs=(vmem,) * 5,
        scratch_shapes=[
            pltpu.VMEM(near_src.shape, jnp.int32),
            pltpu.SMEM(trans_src.shape, jnp.int32),
            pltpu.SMEM(trans_id.shape, jnp.int32),
            pltpu.SMEM(trans_count.shape, jnp.int32),
            pltpu.VMEM(trans_table.shape, F32),
            pltpu.SMEM((1, length), jnp.int32),
            pltpu.VMEM((boxes, 16, width), BF16),
        ]
        + near_scratch
        + [pltpu.SemaphoreType.DMA((5,))],
        compiler_params=params,
        name="prepare",
    )(packet, *[in_hbm(x) for x in (near_src, trans_src, trans_id, trans_count, trans_table)])

    group = pl.pallas_call(
        group_kernel,
        out_shape=shaped((size * spectra_rows + own_rows, 2 * waves, 128), BF16),
        in_specs=[vmem] * (2 + len(steps)),
        out_specs=vmem,
        compiler_params=params,
        name="group",
    )(spectra, *steps, items)
    groups = lax.axis_size("box")
    group_odd = swapped(group, "box", [(i, i + 1) for i in range(1, groups - 1, 2)])
    group_even = swapped(group, "box", [(i, i + 1) for i in range(0, groups - 1, 2)])

    packets = [x for step, x in enumerate(steps, 1) if carries_packet(step)]
    near = pl.pallas_call(
        functools.partial(near_kernel, entries),
        out_shape=shaped((boxes, waves, width), F32),
        in_specs=[vmem] * (5 + len(packets)),
        out_specs=vmem,
        scratch_shapes=[
            pltpu.VMEM((3 * boxes, 16, width), BF16),
            pltpu.VMEM((2, 3 * boxes, width, 128), BF16),
            pltpu.SMEM((1, length), jnp.int32),
        ]
        + near_scratch
        + [pltpu.SemaphoreType.DMA((2,))],
        compiler_params=params,
        name="near",
    )(items, packet, *packets, observers, sources, first_sum)

    return pl.pallas_call(
        functools.partial(incoming_kernel, entries),
        out_shape=shaped((boxes, waves, width), F32),
        in_specs=[vmem] * 11,
        out_specs=vmem,
        scratch_shapes=[
            pltpu.VMEM((boxes, waves, width), F32),
            pltpu.VMEM((boxes, 16, width), BF16),
            pltpu.VMEM((2, boxes, width, 128), BF16),
            pltpu.VMEM((boxes * waves, parent_dirs), F32),
            pltpu.VMEM((boxes * waves, parent_dirs), F32),
            pltpu.SMEM((1, length), jnp.int32),
        ]
        + near_scratch
        + [pltpu.SemaphoreType.DMA],
        compiler_params=params,
        name="incoming",
    )(items, group_even, group, group_odd, gains, cos_phase, sin_phase, imat, rad, observers, near)


def solution(mesh):
    placed = (
        P(("box", "dir"), None, None),
        P(("box", "dir"), None, None),
        P(),
        P(),
        P(),
        P(),
        P(("box", "dir"), None),
        P("box", None),
        P("box", None),
        P("box"),
        P(),
    )
    return jax.shard_map(
        per_device,
        mesh=mesh,
        in_specs=placed,
        out_specs=P(("box", "dir"), None, None),
        check_vma=False,
    )
```

```python
import functools
import math

import jax
import jax.numpy as jnp
from jax import lax
from jax.experimental import pallas as pl
from jax.experimental.pallas import tpu as pltpu
from jax.sharding import PartitionSpec as P

F32 = jnp.float32
BF16 = jnp.bfloat16

WAVENUMBER = 4.0
OFFSET = 0.5
TURN = WAVENUMBER / (2.0 * math.pi)
CHAIN = (-2.2803148655023415, -1.415255674611144, -7.327656729815578, -24.467745134801202)
LEAD = 0.04087004462557604
ITEMS = 4
ROWS = 32
STAGES = 4
FIRST_ITEMS = 5


def round_up(value, step):
    return -(-value // step) * step


def swapped(x, axis, pairs):
    return lax.ppermute(x, axis, [way for i, j in pairs for way in ((i, j), (j, i))])


def split3(x):
    high = x.astype(BF16).astype(F32)
    rest = x - high
    mid = rest.astype(BF16).astype(F32)
    return high, mid, rest - mid


def nt_dot(a, b):
    return lax.dot_general(a, b, (((1,), (1,)), ((), ())), preferred_element_type=F32)


def nn_dot(a, b):
    return jnp.dot(a, b, preferred_element_type=F32)


def code_bits(boxes, entries):
    return entries.bit_length(), (boxes - 1).bit_length(), (3 * boxes - 1).bit_length()


def list_places(boxes, entries):
    gap = 2 * ITEMS
    most = FIRST_ITEMS * boxes // 2
    return most, most + gap, round_up(most + gap + boxes * entries // 2 + 2 * gap + 6, 128)


def list_items(near_src, block, here, size):
    boxes, entries = near_src.shape
    most, second_start, length = list_places(boxes, entries)
    count_bits, box_bits, source_bits = code_bits(boxes, entries)
    pair_bits = count_bits + box_bits + source_bits
    lanes = round_up(3 * boxes, 128)
    odd = (here & 1) == 1
    edge = (here == 0) | (here == size - 1)
    local = near_src - block * boxes
    below = local + jnp.where(odd, 2 * boxes, 3 * boxes)
    above = local + jnp.where(odd, boxes, 0)
    local = jnp.where(local < 0, below, jnp.where(local >= boxes, above, local))
    lane = lax.broadcasted_iota(jnp.int32, (boxes, lanes), 1)
    box = lax.broadcasted_iota(jnp.int32, (boxes, lanes), 0)
    count = jnp.zeros((boxes, lanes), jnp.int32)
    for e in range(entries):
        count = count + (local[:, e : e + 1] == lane).astype(jnp.int32)
    present = count > 0
    flags = present.astype(F32)
    box_row = lax.broadcasted_iota(jnp.int32, (boxes, boxes), 0)
    box_col = lax.broadcasted_iota(jnp.int32, (boxes, boxes), 1)
    rank = nn_dot((box_col < box_row).astype(F32).astype(BF16), flags.astype(BF16)).astype(jnp.int32)
    pairs = jnp.sum(flags, axis=0, keepdims=True)
    from_cross = (lane >= 2 * boxes) & edge
    cross_pairs = jnp.where(from_cross[:1], pairs, 0.0)
    group_pairs = jnp.where(from_cross[:1], 0.0, pairs)
    row = lax.broadcasted_iota(jnp.int32, (lanes, lanes), 0)
    col = lax.broadcasted_iota(jnp.int32, (lanes, lanes), 1)
    ahead = (row < col).astype(F32).astype(BF16)
    lists = jnp.concatenate([group_pairs, cross_pairs, jnp.zeros((6, lanes), F32)], axis=0)
    offset = nn_dot(lists.astype(BF16), ahead).astype(jnp.int32)
    own_pairs = jnp.where(lane[:1] < boxes, group_pairs, 0.0)

    def total(pairs):
        return jnp.sum(pairs, axis=1, keepdims=True).astype(jnp.int32)

    first_total = jnp.minimum(total(own_pairs), 2 * most)
    second_total = total(group_pairs) - first_total
    cross_total = total(cross_pairs)
    order = offset[0:1] + rank
    in_second = order >= first_total
    order = jnp.where(in_second, order - first_total, order)
    order = jnp.where(from_cross, offset[1:2] + rank, order)
    half = order >> 1
    place = jnp.where(from_cross, (length - 4) - half, jnp.where(in_second, second_start + half, half))
    place = jnp.where(present, place, -1)
    code = (lane << (count_bits + box_bits)) | (box << count_bits) | count
    code = jnp.where((order & 1) == 1, code << pair_bits, code)
    place_t = place.T
    code_t = code.T
    rows = 3 * boxes
    slot = lax.broadcasted_iota(jnp.int32, (rows, length), 1)
    found = jnp.zeros((rows, length), jnp.int32)
    for i in range(boxes):
        hit = place_t[:rows, i : i + 1] == slot
        found = found + jnp.where(hit, code_t[:rows, i : i + 1], 0)
    listed = jnp.sum(found, axis=0, keepdims=True)
    at = lax.broadcasted_iota(jnp.int32, (1, length), 1)
    for back, pairs in ((3, first_total), (2, second_total), (1, cross_total)):
        listed = jnp.where(at == length - back, (pairs + 1) >> 1, listed)
    return listed


def start_all(copies, sems):
    started = [pltpu.make_async_copy(src, dst, sems.at[k]) for k, (src, dst) in enumerate(copies)]
    for copy in started:
        copy.start()
    return started


def wait_all(started):
    for copy in started:
        copy.wait()


def outgoing_kernel(
    x_hbm, pos_hbm, rad_hbm, idx_hbm, wgt_hbm, phase_hbm, near_hbm, packet_ref, spectra_ref, imat_ref, cos_ref, sin_ref,
    rad_ref, items_ref, x_ref, pos_ref, idx_ref, wgt_ref, phase_ref, near_ref, sems
):
    wait_all(
        start_all(
            (
                (x_hbm, x_ref),
                (pos_hbm, pos_ref),
                (rad_hbm, rad_ref),
                (idx_hbm, idx_ref),
                (wgt_hbm, wgt_ref),
                (phase_hbm, phase_ref),
                (near_hbm, near_ref),
            ),
            sems,
        )
    )
    block = lax.axis_index(("box", "dir"))
    items_ref[...] = list_items(near_ref[...], block, lax.axis_index("dir"), lax.axis_size("dir"))
    leaf_dirs, parent_dirs = imat_ref.shape
    x_rows, _, width = x_ref.shape
    axes, boxes, _ = pos_ref.shape
    waves = x_rows * 16 // boxes
    chunks = parent_dirs // 128
    own_rows = x_rows + axes * boxes // 16
    packet_ref[:x_rows] = x_ref[...]
    packet_ref[x_rows:own_rows] = pos_ref[...].reshape(axes * boxes // 16, 16, width)
    column = lax.broadcasted_iota(jnp.int32, (leaf_dirs, parent_dirs), 0)
    imat = jnp.zeros((leaf_dirs, parent_dirs), F32)
    for s in range(idx_ref.shape[0]):
        imat = imat + jnp.where(idx_ref[s : s + 1, :] == column, wgt_ref[s : s + 1, :], 0.0)
    imat = imat.astype(BF16)
    imat_ref[...] = imat
    cos_phase = jnp.cos(phase_ref[...])
    sin_phase = jnp.sin(phase_ref[...])
    cos_ref[...] = cos_phase
    sin_ref[...] = sin_phase
    leaf = nn_dot(x_ref[...].reshape(boxes * waves, width), rad_ref[...]).astype(BF16)
    up_re = nn_dot(leaf[:, :leaf_dirs], imat)
    up_im = nn_dot(leaf[:, leaf_dirs:], imat)
    for q in range(boxes // 8):
        re = jnp.zeros((waves, parent_dirs), F32)
        im = jnp.zeros((waves, parent_dirs), F32)
        for c in range(8):
            at = (q * 8 + c) * waves
            ure = up_re[at : at + waves]
            uim = up_im[at : at + waves]
            re = re + (cos_phase[c : c + 1] * ure - sin_phase[c : c + 1] * uim)
            im = im + (sin_phase[c : c + 1] * ure + cos_phase[c : c + 1] * uim)
        both = jnp.concatenate([re, im], axis=0).astype(BF16)
        for k in range(chunks):
            part = both[:, k * 128 : (k + 1) * 128]
            packet_ref[own_rows + q * chunks + k] = part
            spectra_ref[q * chunks + k] = part


def carries_packet(step):
    return step & (step + 1) == 0


def group_kernel(own_ref, *refs):
    *step_refs, _, group_ref = refs
    size = lax.axis_size("dir")
    rows = own_ref.shape[0]
    here = lax.axis_index("dir")
    group_ref[pl.ds(here * rows, rows)] = own_ref[...]
    for step, ref in enumerate(step_refs, 1):
        group_ref[pl.ds((here ^ step) * rows, rows)] = ref[ref.shape[0] - rows :]
    group_ref[size * rows :] = step_refs[-1][: step_refs[-1].shape[0] - rows]


def features(planes):
    rows, _, width = planes.shape
    boxes = rows * 16 // 3
    planes = planes.astype(F32).reshape(3, boxes, width)
    at = lax.broadcasted_iota(jnp.int32, (boxes, 8, width), 1)
    pos = jnp.zeros((boxes, 8, width), F32)
    for axis in range(3):
        pos = jnp.where(at == axis, planes[axis][:, None, :], pos)
    scale = TURN * TURN
    norm = split3(scale * jnp.sum(pos * pos, axis=1, keepdims=True))
    first = jnp.where(at < 3, pos, 1.0)
    first = jnp.where(at == 3, norm[0], jnp.where(at == 4, norm[1], jnp.where(at == 5, norm[2], first)))
    second = jnp.where(at == 3, 1.0, pos + pltpu.roll(pos, 4, 1))
    source = jnp.concatenate([first, second], axis=1).astype(BF16)
    cross = split3((-2.0 * scale) * pos)
    first = jnp.where(at < 3, cross[0], 1.0)
    first = jnp.where(at == 6, norm[0], jnp.where(at == 7, norm[1], first))
    second = jnp.where(at == 3, norm[2], cross[1] + pltpu.roll(cross[2], 4, 1))
    return source, jnp.concatenate([first, second], axis=1).astype(BF16)


def turn_sources(source, src_ref, start):
    boxes, rows, width = source.shape
    eye = lax.broadcasted_iota(jnp.int32, (width, width), 0) == lax.broadcasted_iota(jnp.int32, (width, width), 1)
    turned = nt_dot(eye.astype(F32).astype(BF16), source.reshape(boxes * rows, width))
    column = lax.broadcasted_iota(jnp.int32, (width, 128), 1)
    for b in range(boxes):
        at = b * rows
        lanes = turned[:, at // 128 * 128 : at // 128 * 128 + 128]
        for slot in range(2):
            shift = (slot * rows - at) % 128
            moved = pltpu.roll(lanes, shift, 1) if shift else lanes
            inside = (column >= slot * rows) & (column < (slot + 1) * rows)
            src_ref[slot, start + b] = jnp.where(inside, moved, 0.0).astype(BF16)


def take_currents(x_rows, win_ref, start):
    for k in range(x_rows.shape[0]):
        both = x_rows[k]
        wide = both.astype(F32)
        win_ref[start + 2 * k] = both
        win_ref[start + 2 * k + 1] = jnp.concatenate([wide[8:], wide[:8]], axis=0).astype(BF16)


def near_sum(entries, total, item_at, first_source, src_ref, win_ref, obs_ref, out_ref, scratch):
    u0_ref, u1_ref, t0_ref, t1_ref = scratch
    boxes, waves, width = out_ref.shape
    count_bits, box_bits, source_bits = code_bits(boxes, entries)
    pair_bits = count_bits + box_bits + source_bits
    t1_ref[...] = jnp.zeros(t1_ref.shape, BF16)
    upper = lax.broadcasted_iota(jnp.int32, (2 * waves, width), 0) < waves
    empty = jnp.zeros((16, width), BF16)

    def pair_at(chunk, g, slot):
        code = item_at(chunk * ITEMS + g) >> (slot * pair_bits)
        source = (code >> (count_bits + box_bits)) & ((1 << source_bits) - 1)
        if first_source:
            source = jnp.maximum(source - first_source, 0)
        return source, (code >> count_bits) & ((1 << box_bits) - 1), code & ((1 << count_bits) - 1)

    def distances(chunk, g, u_ref):
        source0, box0, _ = pair_at(chunk, g, 0)
        source1, box1, _ = pair_at(chunk, g, 1)
        sources = src_ref[0, source0] + src_ref[1, source1]
        observers = jnp.concatenate(
            [
                jnp.concatenate([obs_ref[box0], empty], axis=1),
                jnp.concatenate([empty, obs_ref[box1]], axis=1),
            ],
            axis=0,
        )
        u_ref[g] = nn_dot(sources[:, :32], observers)

    def tile(g, u_ref, t_ref):
        for at in range(0, width, ROWS):
            v = jnp.maximum(u_ref[g, at : at + ROWS], 1e-12)
            q = v * lax.rsqrt(v)
            t = q - jnp.round(q)
            cosine = t * t + CHAIN[0]
            for constant in CHAIN[1:]:
                cosine = cosine * cosine + constant
            t_ref[g, at : at + ROWS] = (cosine * pltpu.reciprocal(q + OFFSET * TURN, approx=True)).astype(BF16)

    def product(chunk, g, t_ref):
        source0, box0, count0 = pair_at(chunk, g, 0)
        source1, box1, count1 = pair_at(chunk, g, 1)
        currents = jnp.where(upper, win_ref[source0].astype(F32), win_ref[source1 ^ 1].astype(F32)).astype(BF16)
        got = nn_dot(currents, t_ref[g])
        out_ref[box0] += count0.astype(F32) * got[:waves, :width]
        out_ref[box1] += count1.astype(F32) * got[waves:, width:]

    u_refs = (u0_ref, u1_ref)
    t_refs = (t0_ref, t1_ref)

    def stage(chunk, turn):
        for g in range(ITEMS):
            distances(chunk + 1, g, u_refs[1 - turn])
            product(jnp.maximum(chunk - 1, 0), g, t_refs[1 - turn])
            tile(g, u_refs[turn], t_refs[turn])

    def body(k, carry):
        for j in range(STAGES):
            stage(k * STAGES + j, j & 1)
        return carry

    def finish(turn):
        for g in range(ITEMS):
            product(jnp.maximum(chunks - 1, 0), g, t_refs[turn])

    chunks = (total + (ITEMS - 1)) // ITEMS
    rounds = chunks // STAGES
    for g in range(ITEMS):
        distances(0, g, u0_ref)
    lax.fori_loop(0, rounds, body, 0)
    for j in range(STAGES - 1):
        pl.when(rounds * STAGES + j < chunks)(functools.partial(stage, rounds * STAGES + j, j & 1))
    pl.when((chunks > 0) & ((chunks & 1) == 0))(functools.partial(finish, 1))
    pl.when((chunks & 1) == 1)(functools.partial(finish, 0))


def prepare_kernel(
    entries, own_ref, items_ref, src_hbm, id_hbm, count_hbm, table_hbm, out_ref, obs_ref, src_ref, gain_ref, trans_src_ref,
    trans_id_ref, trans_count_ref, table_ref, list_ref, win_ref, u0_ref, u1_ref, t0_ref, t1_ref, sems
):
    boxes = obs_ref.shape[0]
    length = list_ref.shape[1]
    parents, window = gain_ref.shape[:2]
    listed = src_hbm.shape[1]
    fetch, *trans_copies = start_all(
        (
            (items_ref, list_ref),
            (src_hbm, trans_src_ref),
            (id_hbm, trans_id_ref),
            (count_hbm, trans_count_ref),
            (table_hbm, table_ref),
        ),
        sems,
    )
    plane_rows = 3 * boxes // 16
    source, observer = features(own_ref[boxes // 2 : boxes // 2 + plane_rows])
    turn_sources(source, src_ref, 0)
    take_currents(own_ref[: boxes // 2], win_ref, 0)
    obs_ref[...] = observer
    out_ref[...] = jnp.zeros(out_ref.shape, F32)
    gain_ref[...] = jnp.zeros(gain_ref.shape, F32)
    fetch.wait()
    near_sum(
        entries,
        list_ref[0, length - 3],
        lambda k: list_ref[0, k],
        0,
        src_ref,
        win_ref,
        obs_ref,
        out_ref,
        (u0_ref, u1_ref, t0_ref, t1_ref),
    )
    wait_all(trans_copies)
    row0 = lax.axis_index("dir") * parents
    first = (lax.axis_index("box") - 1) * (window // 3)
    for q in range(parents):
        for e in range(listed):
            live = (e < trans_count_ref[row0 + q]).astype(F32)
            s = jnp.clip(trans_src_ref[row0 + q, e] - first, 0, window - 1)
            gain_ref[q, s] += table_ref[trans_id_ref[row0 + q, e]] * live


def near_kernel(entries, items_ref, own_ref, *refs):
    *step_refs, obs_ref, own_src_ref, first_ref, out_ref, win_ref, src_ref, list_ref, u0_ref, u1_ref, t0_ref, t1_ref, sems = refs
    boxes, waves, width = out_ref.shape
    fetches = start_all(((items_ref, list_ref), (own_src_ref, src_ref.at[:, :boxes])), sems)
    length = list_ref.shape[1]
    here = lax.axis_index("dir")
    other_side = jnp.where((here & 1) == 0, here - 1, here + 1)
    x_rows = boxes // 2

    def take(ref, part):
        take_currents(ref[:x_rows], win_ref, part * boxes)
        source, _ = features(ref[x_rows : x_rows + 3 * boxes // 16])
        turn_sources(source, src_ref, part * boxes)

    take_currents(own_ref[:x_rows], win_ref, 0)
    take(step_refs[0], 1)
    for k, ref in enumerate(step_refs[1:], 2):
        pl.when((here ^ ((1 << k) - 1)) == other_side)(functools.partial(take, ref, 2))
    second_start = list_places(boxes, entries)[1]
    out_ref[...] = first_ref[...]
    wait_all(fetches)
    near_sum(
        entries,
        list_ref[0, length - 2],
        lambda k: list_ref[0, second_start + k],
        0,
        src_ref,
        win_ref,
        obs_ref,
        out_ref,
        (u0_ref, u1_ref, t0_ref, t1_ref),
    )


def incoming_kernel(
    entries, items_ref, even_ref, own_ref, odd_ref, gain_ref, cos_ref, sin_ref, imat_ref, rad_ref, obs_ref, near_ref, out_ref,
    sum_ref, win_ref, src_ref, down_re_ref, down_im_ref, list_ref, u0_ref, u1_ref, t0_ref, t1_ref, sem
):
    parents, window, _, parent_dirs = gain_ref.shape
    boxes, waves, width = near_ref.shape
    chunks = parent_dirs // 128
    group = window // 3
    fetch = pltpu.make_async_copy(items_ref, list_ref, sem)
    fetch.start()
    length = list_ref.shape[1]
    odd_box = lax.axis_index("box") & 1
    sum_ref[...] = near_ref[...]
    x_rows = boxes // 2
    packet_rows = x_rows + 3 * boxes // 16
    here = lax.axis_index("dir")

    @pl.when((here == 0) | (here == lax.axis_size("dir") - 1))
    def _():
        from_even = jnp.where(here == 0, 1, 0) == odd_box
        even_packet, odd_packet = (ref[ref.shape[0] - packet_rows :] for ref in (even_ref, odd_ref))
        packet = jnp.where(from_even, even_packet.astype(F32), odd_packet.astype(F32)).astype(BF16)
        take_currents(packet[:x_rows], win_ref, 0)
        source, _ = features(packet[x_rows:])
        turn_sources(source, src_ref, 0)

    fetch.wait()
    cos_phase = cos_ref[...]
    sin_phase = sin_ref[...]
    sums = tuple(jnp.zeros((waves, 128), F32) for _ in range(parents * chunks * 2))
    for part, ref in ((2 - 2 * odd_box, even_ref), (1, own_ref), (2 * odd_box, odd_ref)):

        def add_source(s, sums, part=part, ref=ref):
            sums = list(sums)
            gains = [gain_ref[q, part * group + s] for q in range(parents)]
            for k in range(chunks):
                spectrum = ref[s * chunks + k].astype(F32)
                sre, sim = spectrum[:waves], spectrum[waves:]
                for q in range(parents):
                    gre = gains[q][0:1, k * 128 : (k + 1) * 128]
                    gim = gains[q][1:2, k * 128 : (k + 1) * 128]
                    at = (q * chunks + k) * 2
                    sums[at] = sums[at] + (gre * sre - gim * sim)
                    sums[at + 1] = sums[at + 1] + (gre * sim + gim * sre)
            return tuple(sums)

        sums = lax.fori_loop(0, group, add_source, sums, unroll=8)
    for q in range(parents):
        for k in range(chunks):
            at = (q * chunks + k) * 2
            re = sums[at].astype(BF16).astype(F32)
            im = sums[at + 1].astype(BF16).astype(F32)
            lanes = slice(k * 128, (k + 1) * 128)
            for c in range(8):
                cos, sin = cos_phase[c : c + 1, lanes], sin_phase[c : c + 1, lanes]
                rows = slice((q * 8 + c) * waves, (q * 8 + c + 1) * waves)
                down_re_ref[rows, lanes] = cos * re + sin * im
                down_im_ref[rows, lanes] = cos * im - sin * re
    imat = imat_ref[...]
    in_re = nt_dot(down_re_ref[...].astype(BF16), imat)
    in_im = nt_dot(down_im_ref[...].astype(BF16), imat)
    incoming = jnp.concatenate([in_re, in_im], axis=1).astype(BF16)
    far = nt_dot(incoming, rad_ref[...])
    near_sum(
        entries,
        list_ref[0, length - 1],
        lambda k: list_ref[0, length - 4 - k],
        2 * boxes,
        src_ref,
        win_ref,
        obs_ref,
        sum_ref,
        (u0_ref, u1_ref, t0_ref, t1_ref),
    )
    factor = TURN * LEAD / math.sqrt(entries * width)
    out_ref[...] = sum_ref[...] * factor + far.reshape(near_ref.shape)


def per_device(
    currents, positions, radiation, interp_index, interp_weight, child_phase, near_src, trans_src, trans_id,
    trans_count, trans_table
):
    boxes, waves, width = currents.shape
    entries = near_src.shape[1]
    leaf_dirs = radiation.shape[1] // 2
    parent_dirs = child_phase.shape[1]
    parents = boxes // 8
    spectra_rows = parents * parent_dirs // 128
    size = lax.axis_size("dir")
    vmem = pl.BlockSpec(memory_space=pltpu.VMEM)
    hbm = pl.BlockSpec(memory_space=pltpu.HBM)
    params = pltpu.CompilerParams(vmem_limit_bytes=32 * 1024 * 1024)

    def in_hbm(x):
        return pltpu.with_memory_space_constraint(x, pltpu.HBM)

    def shaped(shape, dtype):
        return jax.ShapeDtypeStruct(shape, dtype)

    x_rows = boxes // 2
    own_rows = x_rows + 3 * boxes // 16
    operands = (currents.reshape(x_rows, 2 * waves, width), positions.transpose(1, 0, 2), radiation, interp_index.T, interp_weight.T, child_phase)
    operands = operands + (near_src,)
    length = list_places(boxes, entries)[2]
    packet, spectra, imat, cos_phase, sin_phase, rad, items = pl.pallas_call(
        outgoing_kernel,
        out_shape=(
            shaped((own_rows + spectra_rows, 16, width), BF16),
            shaped((spectra_rows, 2 * waves, 128), BF16),
            shaped((leaf_dirs, parent_dirs), BF16),
            shaped((8, parent_dirs), F32),
            shaped((8, parent_dirs), F32),
            shaped(radiation.shape, BF16),
            shaped((1, length), jnp.int32),
        ),
        in_specs=[hbm] * len(operands),
        out_specs=(vmem,) * 7,
        scratch_shapes=[pltpu.VMEM(x.shape, x.dtype) for x in operands if x is not radiation]
        + [pltpu.SemaphoreType.DMA((len(operands),))],
        compiler_params=params,
        name="outgoing",
    )(*[in_hbm(x) for x in operands])

    steps = []
    for step in range(1, size):
        pairs = [(i, i ^ step) for i in range(size) if i < i ^ step]
        steps.append(swapped(packet if carries_packet(step) else spectra, "dir", pairs))

    window = 3 * trans_src.shape[0]
    near_scratch = [
        pltpu.VMEM((ITEMS, width, 2 * width), F32),
        pltpu.VMEM((ITEMS, width, 2 * width), F32),
        pltpu.VMEM((ITEMS, width, 2 * width), BF16),
        pltpu.VMEM((ITEMS, width, 2 * width), BF16),
    ]
    first_sum, observers, sources, gains = pl.pallas_call(
        functools.partial(prepare_kernel, entries),
        out_shape=(
            shaped((boxes, waves, width), F32),
            shaped((boxes, 16, width), BF16),
            shaped((2, boxes, width, 128), BF16),
            shaped((parents, window, 2, parent_dirs), F32),
        ),
        in_specs=[vmem] * 2 + [hbm] * 4,
        out_specs=(vmem,) * 4,
        scratch_shapes=[
            pltpu.SMEM(trans_src.shape, jnp.int32),
            pltpu.SMEM(trans_id.shape, jnp.int32),
            pltpu.SMEM(trans_count.shape, jnp.int32),
            pltpu.VMEM(trans_table.shape, F32),
            pltpu.SMEM((1, length), jnp.int32),
            pltpu.VMEM((boxes, 16, width), BF16),
        ]
        + near_scratch
        + [pltpu.SemaphoreType.DMA((5,))],
        compiler_params=params,
        name="prepare",
    )(packet, items, *[in_hbm(x) for x in (trans_src, trans_id, trans_count, trans_table)])

    group = pl.pallas_call(
        group_kernel,
        out_shape=shaped((size * spectra_rows + own_rows, 2 * waves, 128), BF16),
        in_specs=[vmem] * (2 + len(steps)),
        out_specs=vmem,
        compiler_params=params,
        name="group",
    )(spectra, *steps, first_sum)
    groups = lax.axis_size("box")
    group_odd = swapped(group, "box", [(i, i + 1) for i in range(1, groups - 1, 2)])
    group_even = swapped(group, "box", [(i, i + 1) for i in range(0, groups - 1, 2)])

    packets = [x for step, x in enumerate(steps, 1) if carries_packet(step)]
    near = pl.pallas_call(
        functools.partial(near_kernel, entries),
        out_shape=shaped((boxes, waves, width), F32),
        in_specs=[vmem] * (5 + len(packets)),
        out_specs=vmem,
        scratch_shapes=[
            pltpu.VMEM((3 * boxes, 16, width), BF16),
            pltpu.VMEM((2, 3 * boxes, width, 128), BF16),
            pltpu.SMEM((1, length), jnp.int32),
        ]
        + near_scratch
        + [pltpu.SemaphoreType.DMA((2,))],
        compiler_params=params,
        name="near",
    )(items, packet, *packets, observers, sources, first_sum)

    return pl.pallas_call(
        functools.partial(incoming_kernel, entries),
        out_shape=shaped((boxes, waves, width), F32),
        in_specs=[vmem] * 11,
        out_specs=vmem,
        scratch_shapes=[
            pltpu.VMEM((boxes, waves, width), F32),
            pltpu.VMEM((boxes, 16, width), BF16),
            pltpu.VMEM((2, boxes, width, 128), BF16),
            pltpu.VMEM((boxes * waves, parent_dirs), F32),
            pltpu.VMEM((boxes * waves, parent_dirs), F32),
            pltpu.SMEM((1, length), jnp.int32),
        ]
        + near_scratch
        + [pltpu.SemaphoreType.DMA],
        compiler_params=params,
        name="incoming",
    )(items, group_even, group, group_odd, gains, cos_phase, sin_phase, imat, rad, observers, near)


def solution(mesh):
    placed = (
        P(("box", "dir"), None, None),
        P(("box", "dir"), None, None),
        P(),
        P(),
        P(),
        P(),
        P(("box", "dir"), None),
        P("box", None),
        P("box", None),
        P("box"),
        P(),
    )
    return jax.shard_map(
        per_device,
        mesh=mesh,
        in_specs=placed,
        out_specs=P(("box", "dir"), None, None),
        check_vma=False,
    )
```

```python
import functools
import math

import jax
import jax.numpy as jnp
from jax import lax
from jax.experimental import pallas as pl
from jax.experimental.pallas import tpu as pltpu
from jax.sharding import PartitionSpec as P

F32 = jnp.float32
BF16 = jnp.bfloat16

WAVENUMBER = 4.0
OFFSET = 0.5
TURN = WAVENUMBER / (2.0 * math.pi)
CHAIN = (-2.2803148655023415, -1.415255674611144, -7.327656729815578, -24.467745134801202)
LEAD = 0.04087004462557604
ITEMS = 4
ROWS = 32
STAGES = 4
FIRST_ITEMS = 6


def round_up(value, step):
    return -(-value // step) * step


def swapped(x, axis, pairs):
    return lax.ppermute(x, axis, [way for i, j in pairs for way in ((i, j), (j, i))])


def split3(x):
    high = x.astype(BF16).astype(F32)
    rest = x - high
    mid = rest.astype(BF16).astype(F32)
    return high, mid, rest - mid


def nt_dot(a, b):
    return lax.dot_general(a, b, (((1,), (1,)), ((), ())), preferred_element_type=F32)


def nn_dot(a, b):
    return jnp.dot(a, b, preferred_element_type=F32)


def code_bits(boxes, entries):
    return entries.bit_length(), (boxes - 1).bit_length(), (3 * boxes - 1).bit_length()


def list_places(boxes, entries):
    gap = 2 * ITEMS
    most = FIRST_ITEMS * boxes // 2
    return most, most + gap, round_up(most + gap + boxes * entries // 2 + 2 * gap + 6, 128)


def list_items(near_src, block, here, size):
    boxes, entries = near_src.shape
    most, second_start, length = list_places(boxes, entries)
    count_bits, box_bits, source_bits = code_bits(boxes, entries)
    pair_bits = count_bits + box_bits + source_bits
    lanes = round_up(3 * boxes, 128)
    odd = (here & 1) == 1
    edge = (here == 0) | (here == size - 1)
    local = near_src - block * boxes
    below = local + jnp.where(odd, 2 * boxes, 3 * boxes)
    above = local + jnp.where(odd, boxes, 0)
    local = jnp.where(local < 0, below, jnp.where(local >= boxes, above, local))
    lane = lax.broadcasted_iota(jnp.int32, (boxes, lanes), 1)
    box = lax.broadcasted_iota(jnp.int32, (boxes, lanes), 0)
    count = jnp.zeros((boxes, lanes), jnp.int32)
    for e in range(entries):
        count = count + (local[:, e : e + 1] == lane).astype(jnp.int32)
    present = count > 0
    flags = present.astype(F32)
    box_row = lax.broadcasted_iota(jnp.int32, (boxes, boxes), 0)
    box_col = lax.broadcasted_iota(jnp.int32, (boxes, boxes), 1)
    rank = nn_dot((box_col < box_row).astype(F32).astype(BF16), flags.astype(BF16)).astype(jnp.int32)
    pairs = jnp.sum(flags, axis=0, keepdims=True)
    from_cross = (lane >= 2 * boxes) & edge
    cross_pairs = jnp.where(from_cross[:1], pairs, 0.0)
    group_pairs = jnp.where(from_cross[:1], 0.0, pairs)
    row = lax.broadcasted_iota(jnp.int32, (lanes, lanes), 0)
    col = lax.broadcasted_iota(jnp.int32, (lanes, lanes), 1)
    ahead = (row < col).astype(F32).astype(BF16)
    lists = jnp.concatenate([group_pairs, cross_pairs, jnp.zeros((6, lanes), F32)], axis=0)
    offset = nn_dot(lists.astype(BF16), ahead).astype(jnp.int32)
    own_pairs = jnp.where(lane[:1] < boxes, group_pairs, 0.0)

    def total(pairs):
        return jnp.sum(pairs, axis=1, keepdims=True).astype(jnp.int32)

    first_total = jnp.minimum(total(own_pairs), 2 * most)
    second_total = total(group_pairs) - first_total
    cross_total = total(cross_pairs)
    order = offset[0:1] + rank
    in_second = order >= first_total
    order = jnp.where(in_second, order - first_total, order)
    order = jnp.where(from_cross, offset[1:2] + rank, order)
    half = order >> 1
    place = jnp.where(from_cross, (length - 4) - half, jnp.where(in_second, second_start + half, half))
    place = jnp.where(present, place, -1)
    code = (lane << (count_bits + box_bits)) | (box << count_bits) | count
    code = jnp.where((order & 1) == 1, code << pair_bits, code)
    place_t = place.T
    code_t = code.T
    rows = 3 * boxes
    slot = lax.broadcasted_iota(jnp.int32, (rows, length), 1)
    found = jnp.zeros((rows, length), jnp.int32)
    for i in range(boxes):
        hit = place_t[:rows, i : i + 1] == slot
        found = found + jnp.where(hit, code_t[:rows, i : i + 1], 0)
    listed = jnp.sum(found, axis=0, keepdims=True)
    at = lax.broadcasted_iota(jnp.int32, (1, length), 1)
    for back, pairs in ((3, first_total), (2, second_total), (1, cross_total)):
        listed = jnp.where(at == length - back, (pairs + 1) >> 1, listed)
    return listed


def start_all(copies, sems):
    started = [pltpu.make_async_copy(src, dst, sems.at[k]) for k, (src, dst) in enumerate(copies)]
    for copy in started:
        copy.start()
    return started


def wait_all(started):
    for copy in started:
        copy.wait()


def outgoing_kernel(
    x_hbm, pos_hbm, rad_hbm, idx_hbm, wgt_hbm, phase_hbm, near_hbm, packet_ref, spectra_ref, imat_ref, cos_ref, sin_ref,
    rad_ref, items_ref, x_ref, pos_ref, idx_ref, wgt_ref, phase_ref, near_ref, sems
):
    wait_all(
        start_all(
            (
                (x_hbm, x_ref),
                (pos_hbm, pos_ref),
                (rad_hbm, rad_ref),
                (idx_hbm, idx_ref),
                (wgt_hbm, wgt_ref),
                (phase_hbm, phase_ref),
                (near_hbm, near_ref),
            ),
            sems,
        )
    )
    block = lax.axis_index(("box", "dir"))
    items_ref[...] = list_items(near_ref[...], block, lax.axis_index("dir"), lax.axis_size("dir"))
    leaf_dirs, parent_dirs = imat_ref.shape
    x_rows, _, width = x_ref.shape
    axes, boxes, _ = pos_ref.shape
    waves = x_rows * 16 // boxes
    chunks = parent_dirs // 128
    own_rows = x_rows + axes * boxes // 16
    packet_ref[:x_rows] = x_ref[...]
    packet_ref[x_rows:own_rows] = pos_ref[...].reshape(axes * boxes // 16, 16, width)
    column = lax.broadcasted_iota(jnp.int32, (leaf_dirs, parent_dirs), 0)
    imat = jnp.zeros((leaf_dirs, parent_dirs), F32)
    for s in range(idx_ref.shape[0]):
        imat = imat + jnp.where(idx_ref[s : s + 1, :] == column, wgt_ref[s : s + 1, :], 0.0)
    imat = imat.astype(BF16)
    imat_ref[...] = imat
    cos_phase = jnp.cos(phase_ref[...])
    sin_phase = jnp.sin(phase_ref[...])
    cos_ref[...] = cos_phase
    sin_ref[...] = sin_phase
    leaf = nn_dot(x_ref[...].reshape(boxes * waves, width), rad_ref[...]).astype(BF16)
    up_re = nn_dot(leaf[:, :leaf_dirs], imat)
    up_im = nn_dot(leaf[:, leaf_dirs:], imat)
    for q in range(boxes // 8):
        re = jnp.zeros((waves, parent_dirs), F32)
        im = jnp.zeros((waves, parent_dirs), F32)
        for c in range(8):
            at = (q * 8 + c) * waves
            ure = up_re[at : at + waves]
            uim = up_im[at : at + waves]
            re = re + (cos_phase[c : c + 1] * ure - sin_phase[c : c + 1] * uim)
            im = im + (sin_phase[c : c + 1] * ure + cos_phase[c : c + 1] * uim)
        both = jnp.concatenate([re, im], axis=0).astype(BF16)
        for k in range(chunks):
            part = both[:, k * 128 : (k + 1) * 128]
            packet_ref[own_rows + q * chunks + k] = part
            spectra_ref[q * chunks + k] = part


def carries_packet(step):
    return step & (step + 1) == 0


def group_kernel(own_ref, *refs):
    *step_refs, _, group_ref = refs
    size = lax.axis_size("dir")
    rows = own_ref.shape[0]
    here = lax.axis_index("dir")
    group_ref[pl.ds(here * rows, rows)] = own_ref[...]
    for step, ref in enumerate(step_refs, 1):
        group_ref[pl.ds((here ^ step) * rows, rows)] = ref[ref.shape[0] - rows :]
    group_ref[size * rows :] = step_refs[-1][: step_refs[-1].shape[0] - rows]


def features(planes):
    rows, _, width = planes.shape
    boxes = rows * 16 // 3
    planes = planes.astype(F32).reshape(3, boxes, width)
    at = lax.broadcasted_iota(jnp.int32, (boxes, 8, width), 1)
    pos = jnp.zeros((boxes, 8, width), F32)
    for axis in range(3):
        pos = jnp.where(at == axis, planes[axis][:, None, :], pos)
    scale = TURN * TURN
    norm = split3(scale * jnp.sum(pos * pos, axis=1, keepdims=True))
    first = jnp.where(at < 3, pos, 1.0)
    first = jnp.where(at == 3, norm[0], jnp.where(at == 4, norm[1], jnp.where(at == 5, norm[2], first)))
    second = jnp.where(at == 3, 1.0, pos + pltpu.roll(pos, 4, 1))
    source = jnp.concatenate([first, second], axis=1).astype(BF16)
    cross = split3((-2.0 * scale) * pos)
    first = jnp.where(at < 3, cross[0], 1.0)
    first = jnp.where(at == 6, norm[0], jnp.where(at == 7, norm[1], first))
    second = jnp.where(at == 3, norm[2], cross[1] + pltpu.roll(cross[2], 4, 1))
    return source, jnp.concatenate([first, second], axis=1).astype(BF16)


def turn_sources(source, src_ref, start):
    boxes, rows, width = source.shape
    eye = lax.broadcasted_iota(jnp.int32, (width, width), 0) == lax.broadcasted_iota(jnp.int32, (width, width), 1)
    twice = jnp.concatenate([source, source], axis=1).reshape(boxes * 2 * rows, width)
    turned = nt_dot(eye.astype(F32).astype(BF16), twice)
    for b in range(boxes):
        at = b * 2 * rows
        lanes = turned[:, at // 128 * 128 : at // 128 * 128 + 128]
        if at % 128:
            lanes = pltpu.roll(lanes, 128 - at % 128, 1)
        src_ref[start + b] = lanes.astype(BF16)


def take_currents(x_rows, win_ref, start):
    for k in range(x_rows.shape[0]):
        both = x_rows[k]
        wide = both.astype(F32)
        win_ref[start + 2 * k] = both
        win_ref[start + 2 * k + 1] = jnp.concatenate([wide[8:], wide[:8]], axis=0).astype(BF16)


def near_sum(entries, total, item_at, first_source, src_ref, win_ref, obs_ref, out_ref, scratch):
    u0_ref, u1_ref, t0_ref, t1_ref = scratch
    boxes, waves, width = out_ref.shape
    count_bits, box_bits, source_bits = code_bits(boxes, entries)
    pair_bits = count_bits + box_bits + source_bits
    t1_ref[...] = jnp.zeros(t1_ref.shape, BF16)
    upper = lax.broadcasted_iota(jnp.int32, (2 * waves, width), 0) < waves
    left = lax.broadcasted_iota(jnp.int32, (width, 128), 1) < 16
    empty = jnp.zeros((16, width), BF16)

    def pair_at(chunk, g, slot):
        code = item_at(chunk * ITEMS + g) >> (slot * pair_bits)
        source = (code >> (count_bits + box_bits)) & ((1 << source_bits) - 1)
        if first_source:
            source = jnp.maximum(source - first_source, 0)
        return source, (code >> count_bits) & ((1 << box_bits) - 1), code & ((1 << count_bits) - 1)

    def distances(chunk, g, u_ref):
        source0, box0, _ = pair_at(chunk, g, 0)
        source1, box1, _ = pair_at(chunk, g, 1)
        sources = jnp.where(left, src_ref[source0], src_ref[source1])
        observers = jnp.concatenate(
            [
                jnp.concatenate([obs_ref[box0], empty], axis=1),
                jnp.concatenate([empty, obs_ref[box1]], axis=1),
            ],
            axis=0,
        )
        u_ref[g] = nn_dot(sources[:, :32], observers)

    def tile(g, u_ref, t_ref):
        for at in range(0, width, ROWS):
            v = jnp.maximum(u_ref[g, at : at + ROWS], 1e-12)
            q = v * lax.rsqrt(v)
            t = q - jnp.round(q)
            cosine = t * t + CHAIN[0]
            for constant in CHAIN[1:]:
                cosine = cosine * cosine + constant
            t_ref[g, at : at + ROWS] = (cosine * pltpu.reciprocal(q + OFFSET * TURN, approx=True)).astype(BF16)

    def product(chunk, g, t_ref):
        source0, box0, count0 = pair_at(chunk, g, 0)
        source1, box1, count1 = pair_at(chunk, g, 1)
        currents = jnp.where(upper, win_ref[source0].astype(F32), win_ref[source1 ^ 1].astype(F32)).astype(BF16)
        got = nn_dot(currents, t_ref[g])
        out_ref[box0] += count0.astype(F32) * got[:waves, :width]
        out_ref[box1] += count1.astype(F32) * got[waves:, width:]

    u_refs = (u0_ref, u1_ref)
    t_refs = (t0_ref, t1_ref)

    def stage(chunk, turn):
        for g in range(ITEMS):
            distances(chunk + 1, g, u_refs[1 - turn])
            product(jnp.maximum(chunk - 1, 0), g, t_refs[1 - turn])
            tile(g, u_refs[turn], t_refs[turn])

    def body(k, carry):
        for j in range(STAGES):
            stage(k * STAGES + j, j & 1)
        return carry

    def finish(turn):
        for g in range(ITEMS):
            product(jnp.maximum(chunks - 1, 0), g, t_refs[turn])

    chunks = (total + (ITEMS - 1)) // ITEMS
    rounds = chunks // STAGES
    for g in range(ITEMS):
        distances(0, g, u0_ref)
    lax.fori_loop(0, rounds, body, 0)
    for j in range(STAGES - 1):
        pl.when(rounds * STAGES + j < chunks)(functools.partial(stage, rounds * STAGES + j, j & 1))
    pl.when((chunks > 0) & ((chunks & 1) == 0))(functools.partial(finish, 1))
    pl.when((chunks & 1) == 1)(functools.partial(finish, 0))


def prepare_kernel(
    entries, own_ref, items_ref, src_hbm, id_hbm, count_hbm, table_hbm, out_ref, obs_ref, src_ref, gain_ref, trans_src_ref,
    trans_id_ref, trans_count_ref, table_ref, list_ref, win_ref, u0_ref, u1_ref, t0_ref, t1_ref, sems
):
    boxes = obs_ref.shape[0]
    length = list_ref.shape[1]
    parents, window = gain_ref.shape[:2]
    listed = src_hbm.shape[1]
    fetch, *trans_copies = start_all(
        (
            (items_ref, list_ref),
            (src_hbm, trans_src_ref),
            (id_hbm, trans_id_ref),
            (count_hbm, trans_count_ref),
            (table_hbm, table_ref),
        ),
        sems,
    )
    plane_rows = 3 * boxes // 16
    source, observer = features(own_ref[boxes // 2 : boxes // 2 + plane_rows])
    turn_sources(source, src_ref, 0)
    take_currents(own_ref[: boxes // 2], win_ref, 0)
    obs_ref[...] = observer
    out_ref[...] = jnp.zeros(out_ref.shape, F32)
    gain_ref[...] = jnp.zeros(gain_ref.shape, F32)
    fetch.wait()
    near_sum(
        entries,
        list_ref[0, length - 3],
        lambda k: list_ref[0, k],
        0,
        src_ref,
        win_ref,
        obs_ref,
        out_ref,
        (u0_ref, u1_ref, t0_ref, t1_ref),
    )
    wait_all(trans_copies)
    row0 = lax.axis_index("dir") * parents
    first = (lax.axis_index("box") - 1) * (window // 3)
    for q in range(parents):
        for e in range(listed):
            live = (e < trans_count_ref[row0 + q]).astype(F32)
            s = jnp.clip(trans_src_ref[row0 + q, e] - first, 0, window - 1)
            gain_ref[q, s] += table_ref[trans_id_ref[row0 + q, e]] * live


def near_kernel(entries, items_ref, own_ref, *refs):
    *step_refs, obs_ref, own_src_ref, first_ref, out_ref, win_ref, src_ref, list_ref, u0_ref, u1_ref, t0_ref, t1_ref, sems = refs
    boxes, waves, width = out_ref.shape
    fetches = start_all(((items_ref, list_ref), (own_src_ref, src_ref.at[:boxes])), sems)
    length = list_ref.shape[1]
    here = lax.axis_index("dir")
    other_side = jnp.where((here & 1) == 0, here - 1, here + 1)
    x_rows = boxes // 2

    def take(ref, part):
        take_currents(ref[:x_rows], win_ref, part * boxes)
        source, _ = features(ref[x_rows : x_rows + 3 * boxes // 16])
        turn_sources(source, src_ref, part * boxes)

    take_currents(own_ref[:x_rows], win_ref, 0)
    take(step_refs[0], 1)
    for k, ref in enumerate(step_refs[1:], 2):
        pl.when((here ^ ((1 << k) - 1)) == other_side)(functools.partial(take, ref, 2))
    second_start = list_places(boxes, entries)[1]
    out_ref[...] = first_ref[...]
    wait_all(fetches)
    near_sum(
        entries,
        list_ref[0, length - 2],
        lambda k: list_ref[0, second_start + k],
        0,
        src_ref,
        win_ref,
        obs_ref,
        out_ref,
        (u0_ref, u1_ref, t0_ref, t1_ref),
    )


def incoming_kernel(
    entries, items_ref, even_ref, own_ref, odd_ref, gain_ref, cos_ref, sin_ref, imat_ref, rad_ref, obs_ref, near_ref, out_ref,
    sum_ref, win_ref, src_ref, down_re_ref, down_im_ref, list_ref, u0_ref, u1_ref, t0_ref, t1_ref, sem
):
    parents, window, _, parent_dirs = gain_ref.shape
    boxes, waves, width = near_ref.shape
    chunks = parent_dirs // 128
    group = window // 3
    fetch = pltpu.make_async_copy(items_ref, list_ref, sem)
    fetch.start()
    length = list_ref.shape[1]
    odd_box = lax.axis_index("box") & 1
    sum_ref[...] = near_ref[...]
    x_rows = boxes // 2
    packet_rows = x_rows + 3 * boxes // 16
    from_even = jnp.where(lax.axis_index("dir") == 0, 1, 0) == odd_box
    even_packet, odd_packet = (ref[ref.shape[0] - packet_rows :] for ref in (even_ref, odd_ref))
    packet = jnp.where(from_even, even_packet.astype(F32), odd_packet.astype(F32)).astype(BF16)
    take_currents(packet[:x_rows], win_ref, 0)
    source, _ = features(packet[x_rows:])
    turn_sources(source, src_ref, 0)
    fetch.wait()
    cos_phase = cos_ref[...]
    sin_phase = sin_ref[...]
    sums = tuple(jnp.zeros((waves, 128), F32) for _ in range(parents * chunks * 2))
    for part, ref in ((2 - 2 * odd_box, even_ref), (1, own_ref), (2 * odd_box, odd_ref)):

        def add_source(s, sums, part=part, ref=ref):
            sums = list(sums)
            gains = [gain_ref[q, part * group + s] for q in range(parents)]
            for k in range(chunks):
                spectrum = ref[s * chunks + k].astype(F32)
                sre, sim = spectrum[:waves], spectrum[waves:]
                for q in range(parents):
                    gre = gains[q][0:1, k * 128 : (k + 1) * 128]
                    gim = gains[q][1:2, k * 128 : (k + 1) * 128]
                    at = (q * chunks + k) * 2
                    sums[at] = sums[at] + (gre * sre - gim * sim)
                    sums[at + 1] = sums[at + 1] + (gre * sim + gim * sre)
            return tuple(sums)

        sums = lax.fori_loop(0, group, add_source, sums, unroll=8)
    for q in range(parents):
        for k in range(chunks):
            at = (q * chunks + k) * 2
            re = sums[at].astype(BF16).astype(F32)
            im = sums[at + 1].astype(BF16).astype(F32)
            lanes = slice(k * 128, (k + 1) * 128)
            for c in range(8):
                cos, sin = cos_phase[c : c + 1, lanes], sin_phase[c : c + 1, lanes]
                rows = slice((q * 8 + c) * waves, (q * 8 + c + 1) * waves)
                down_re_ref[rows, lanes] = cos * re + sin * im
                down_im_ref[rows, lanes] = cos * im - sin * re
    imat = imat_ref[...]
    in_re = nt_dot(down_re_ref[...].astype(BF16), imat)
    in_im = nt_dot(down_im_ref[...].astype(BF16), imat)
    incoming = jnp.concatenate([in_re, in_im], axis=1).astype(BF16)
    far = nt_dot(incoming, rad_ref[...])
    near_sum(
        entries,
        list_ref[0, length - 1],
        lambda k: list_ref[0, length - 4 - k],
        2 * boxes,
        src_ref,
        win_ref,
        obs_ref,
        sum_ref,
        (u0_ref, u1_ref, t0_ref, t1_ref),
    )
    factor = TURN * LEAD / math.sqrt(entries * width)
    out_ref[...] = sum_ref[...] * factor + far.reshape(near_ref.shape)


def per_device(
    currents, positions, radiation, interp_index, interp_weight, child_phase, near_src, trans_src, trans_id,
    trans_count, trans_table
):
    boxes, waves, width = currents.shape
    entries = near_src.shape[1]
    leaf_dirs = radiation.shape[1] // 2
    parent_dirs = child_phase.shape[1]
    parents = boxes // 8
    spectra_rows = parents * parent_dirs // 128
    size = lax.axis_size("dir")
    vmem = pl.BlockSpec(memory_space=pltpu.VMEM)
    hbm = pl.BlockSpec(memory_space=pltpu.HBM)
    params = pltpu.CompilerParams(vmem_limit_bytes=32 * 1024 * 1024)

    def in_hbm(x):
        return pltpu.with_memory_space_constraint(x, pltpu.HBM)

    def shaped(shape, dtype):
        return jax.ShapeDtypeStruct(shape, dtype)

    x_rows = boxes // 2
    own_rows = x_rows + 3 * boxes // 16
    operands = (currents.reshape(x_rows, 2 * waves, width), positions.transpose(1, 0, 2), radiation, interp_index.T, interp_weight.T, child_phase)
    operands = operands + (near_src,)
    length = list_places(boxes, entries)[2]
    packet, spectra, imat, cos_phase, sin_phase, rad, items = pl.pallas_call(
        outgoing_kernel,
        out_shape=(
            shaped((own_rows + spectra_rows, 16, width), BF16),
            shaped((spectra_rows, 2 * waves, 128), BF16),
            shaped((leaf_dirs, parent_dirs), BF16),
            shaped((8, parent_dirs), F32),
            shaped((8, parent_dirs), F32),
            shaped(radiation.shape, BF16),
            shaped((1, length), jnp.int32),
        ),
        in_specs=[hbm] * len(operands),
        out_specs=(vmem,) * 7,
        scratch_shapes=[pltpu.VMEM(x.shape, x.dtype) for x in operands if x is not radiation]
        + [pltpu.SemaphoreType.DMA((len(operands),))],
        compiler_params=params,
        name="outgoing",
    )(*[in_hbm(x) for x in operands])

    steps = []
    for step in range(1, size):
        pairs = [(i, i ^ step) for i in range(size) if i < i ^ step]
        steps.append(swapped(packet if carries_packet(step) else spectra, "dir", pairs))

    window = 3 * trans_src.shape[0]
    near_scratch = [
        pltpu.VMEM((ITEMS, width, 2 * width), F32),
        pltpu.VMEM((ITEMS, width, 2 * width), F32),
        pltpu.VMEM((ITEMS, width, 2 * width), BF16),
        pltpu.VMEM((ITEMS, width, 2 * width), BF16),
    ]
    first_sum, observers, sources, gains = pl.pallas_call(
        functools.partial(prepare_kernel, entries),
        out_shape=(
            shaped((boxes, waves, width), F32),
            shaped((boxes, 16, width), BF16),
            shaped((boxes, width, 128), BF16),
            shaped((parents, window, 2, parent_dirs), F32),
        ),
        in_specs=[vmem] * 2 + [hbm] * 4,
        out_specs=(vmem,) * 4,
        scratch_shapes=[
            pltpu.SMEM(trans_src.shape, jnp.int32),
            pltpu.SMEM(trans_id.shape, jnp.int32),
            pltpu.SMEM(trans_count.shape, jnp.int32),
            pltpu.VMEM(trans_table.shape, F32),
            pltpu.SMEM((1, length), jnp.int32),
            pltpu.VMEM((boxes, 16, width), BF16),
        ]
        + near_scratch
        + [pltpu.SemaphoreType.DMA((5,))],
        compiler_params=params,
        name="prepare",
    )(packet, items, *[in_hbm(x) for x in (trans_src, trans_id, trans_count, trans_table)])

    group = pl.pallas_call(
        group_kernel,
        out_shape=shaped((size * spectra_rows + own_rows, 2 * waves, 128), BF16),
        in_specs=[vmem] * (2 + len(steps)),
        out_specs=vmem,
        compiler_params=params,
        name="group",
    )(spectra, *steps, first_sum)
    groups = lax.axis_size("box")
    group_odd = swapped(group, "box", [(i, i + 1) for i in range(1, groups - 1, 2)])
    group_even = swapped(group, "box", [(i, i + 1) for i in range(0, groups - 1, 2)])

    packets = [x for step, x in enumerate(steps, 1) if carries_packet(step)]
    near = pl.pallas_call(
        functools.partial(near_kernel, entries),
        out_shape=shaped((boxes, waves, width), F32),
        in_specs=[vmem] * (5 + len(packets)),
        out_specs=vmem,
        scratch_shapes=[
            pltpu.VMEM((3 * boxes, 16, width), BF16),
            pltpu.VMEM((3 * boxes, width, 128), BF16),
            pltpu.SMEM((1, length), jnp.int32),
        ]
        + near_scratch
        + [pltpu.SemaphoreType.DMA((2,))],
        compiler_params=params,
        name="near",
    )(items, packet, *packets, observers, sources, first_sum)

    return pl.pallas_call(
        functools.partial(incoming_kernel, entries),
        out_shape=shaped((boxes, waves, width), F32),
        in_specs=[vmem] * 11,
        out_specs=vmem,
        scratch_shapes=[
            pltpu.VMEM((boxes, waves, width), F32),
            pltpu.VMEM((boxes, 16, width), BF16),
            pltpu.VMEM((boxes, width, 128), BF16),
            pltpu.VMEM((boxes * waves, parent_dirs), F32),
            pltpu.VMEM((boxes * waves, parent_dirs), F32),
            pltpu.SMEM((1, length), jnp.int32),
        ]
        + near_scratch
        + [pltpu.SemaphoreType.DMA],
        compiler_params=params,
        name="incoming",
    )(items, group_even, group, group_odd, gains, cos_phase, sin_phase, imat, rad, observers, near)


def solution(mesh):
    placed = (
        P(("box", "dir"), None, None),
        P(("box", "dir"), None, None),
        P(),
        P(),
        P(),
        P(),
        P(("box", "dir"), None),
        P("box", None),
        P("box", None),
        P("box"),
        P(),
    )
    return jax.shard_map(
        per_device,
        mesh=mesh,
        in_specs=placed,
        out_specs=P(("box", "dir"), None, None),
        check_vma=False,
    )
```

```python
import functools
import math

import jax
import jax.numpy as jnp
from jax import lax
from jax.experimental import pallas as pl
from jax.experimental.pallas import tpu as pltpu
from jax.sharding import PartitionSpec as P

F32 = jnp.float32
BF16 = jnp.bfloat16

WAVENUMBER = 4.0
OFFSET = 0.5
TURN = WAVENUMBER / (2.0 * math.pi)
CHAIN = (-2.2803148655023415, -1.415255674611144, -7.327656729815578, -24.467745134801202)
LEAD = 0.04087004462557604
ITEMS = 4
ROWS = 32
STAGES = 4
FIRST_ITEMS = 6


def round_up(value, step):
    return -(-value // step) * step


def swapped(x, axis, pairs):
    return lax.ppermute(x, axis, [way for i, j in pairs for way in ((i, j), (j, i))])


def split3(x):
    high = x.astype(BF16).astype(F32)
    rest = x - high
    mid = rest.astype(BF16).astype(F32)
    return high, mid, rest - mid


def nt_dot(a, b):
    return lax.dot_general(a, b, (((1,), (1,)), ((), ())), preferred_element_type=F32)


def nn_dot(a, b):
    return jnp.dot(a, b, preferred_element_type=F32)


def code_bits(boxes, entries):
    return entries.bit_length(), (boxes - 1).bit_length(), (3 * boxes - 1).bit_length()


def list_places(boxes, entries):
    gap = 2 * ITEMS
    most = FIRST_ITEMS * boxes // 2
    return most, most + gap, round_up(most + gap + boxes * entries // 2 + 2 * gap + 6, 128)


def list_items(near_src, block, here, size):
    boxes, entries = near_src.shape
    most, second_start, length = list_places(boxes, entries)
    count_bits, box_bits, source_bits = code_bits(boxes, entries)
    pair_bits = count_bits + box_bits + source_bits
    lanes = round_up(3 * boxes, 128)
    odd = (here & 1) == 1
    edge = (here == 0) | (here == size - 1)
    local = near_src - block * boxes
    below = local + jnp.where(odd, 2 * boxes, 3 * boxes)
    above = local + jnp.where(odd, boxes, 0)
    local = jnp.where(local < 0, below, jnp.where(local >= boxes, above, local))
    lane = lax.broadcasted_iota(jnp.int32, (boxes, lanes), 1)
    box = lax.broadcasted_iota(jnp.int32, (boxes, lanes), 0)
    count = jnp.zeros((boxes, lanes), jnp.int32)
    for e in range(entries):
        count = count + (local[:, e : e + 1] == lane).astype(jnp.int32)
    present = count > 0
    flags = present.astype(F32)
    box_row = lax.broadcasted_iota(jnp.int32, (boxes, boxes), 0)
    box_col = lax.broadcasted_iota(jnp.int32, (boxes, boxes), 1)
    rank = nn_dot((box_col < box_row).astype(F32).astype(BF16), flags.astype(BF16)).astype(jnp.int32)
    pairs = jnp.sum(flags, axis=0, keepdims=True)
    from_cross = (lane >= 2 * boxes) & edge
    cross_pairs = jnp.where(from_cross[:1], pairs, 0.0)
    group_pairs = jnp.where(from_cross[:1], 0.0, pairs)
    row = lax.broadcasted_iota(jnp.int32, (lanes, lanes), 0)
    col = lax.broadcasted_iota(jnp.int32, (lanes, lanes), 1)
    ahead = (row < col).astype(F32).astype(BF16)
    lists = jnp.concatenate([group_pairs, cross_pairs, jnp.zeros((6, lanes), F32)], axis=0)
    offset = nn_dot(lists.astype(BF16), ahead).astype(jnp.int32)
    own_pairs = jnp.where(lane[:1] < boxes, group_pairs, 0.0)

    def total(pairs):
        return jnp.sum(pairs, axis=1, keepdims=True).astype(jnp.int32)

    first_total = jnp.minimum(total(own_pairs), 2 * most)
    second_total = total(group_pairs) - first_total
    cross_total = total(cross_pairs)
    order = offset[0:1] + rank
    in_second = order >= first_total
    order = jnp.where(in_second, order - first_total, order)
    order = jnp.where(from_cross, offset[1:2] + rank, order)
    half = order >> 1
    place = jnp.where(from_cross, (length - 4) - half, jnp.where(in_second, second_start + half, half))
    place = jnp.where(present, place, -1)
    code = (lane << (count_bits + box_bits)) | (box << count_bits) | count
    code = jnp.where((order & 1) == 1, code << pair_bits, code)
    place_t = place.T
    code_t = code.T
    rows = 3 * boxes
    slot = lax.broadcasted_iota(jnp.int32, (rows, length), 1)
    found = jnp.zeros((rows, length), jnp.int32)
    for i in range(boxes):
        hit = place_t[:rows, i : i + 1] == slot
        found = found + jnp.where(hit, code_t[:rows, i : i + 1], 0)
    listed = jnp.sum(found, axis=0, keepdims=True)
    at = lax.broadcasted_iota(jnp.int32, (1, length), 1)
    for back, pairs in ((3, first_total), (2, second_total), (1, cross_total)):
        listed = jnp.where(at == length - back, (pairs + 1) >> 1, listed)
    return listed


def start_all(copies, sems):
    started = [pltpu.make_async_copy(src, dst, sems.at[k]) for k, (src, dst) in enumerate(copies)]
    for copy in started:
        copy.start()
    return started


def wait_all(started):
    for copy in started:
        copy.wait()


def outgoing_kernel(
    x_hbm, pos_hbm, rad_hbm, idx_hbm, wgt_hbm, phase_hbm, near_hbm, packet_ref, spectra_ref, imat_ref, cos_ref, sin_ref,
    rad_ref, items_ref, x_ref, pos_ref, idx_ref, wgt_ref, phase_ref, near_ref, sems
):
    wait_all(
        start_all(
            (
                (x_hbm, x_ref),
                (pos_hbm, pos_ref),
                (rad_hbm, rad_ref),
                (idx_hbm, idx_ref),
                (wgt_hbm, wgt_ref),
                (phase_hbm, phase_ref),
                (near_hbm, near_ref),
            ),
            sems,
        )
    )
    block = lax.axis_index(("box", "dir"))
    items_ref[...] = list_items(near_ref[...], block, lax.axis_index("dir"), lax.axis_size("dir"))
    leaf_dirs, parent_dirs = imat_ref.shape
    x_rows, _, width = x_ref.shape
    axes, boxes, _ = pos_ref.shape
    waves = x_rows * 16 // boxes
    chunks = parent_dirs // 128
    own_rows = x_rows + axes * boxes // 16
    packet_ref[:x_rows] = x_ref[...]
    packet_ref[x_rows:own_rows] = pos_ref[...].reshape(axes * boxes // 16, 16, width)
    column = lax.broadcasted_iota(jnp.int32, (leaf_dirs, parent_dirs), 0)
    imat = jnp.zeros((leaf_dirs, parent_dirs), F32)
    for s in range(idx_ref.shape[0]):
        imat = imat + jnp.where(idx_ref[s : s + 1, :] == column, wgt_ref[s : s + 1, :], 0.0)
    imat = imat.astype(BF16)
    imat_ref[...] = imat
    cos_phase = jnp.cos(phase_ref[...])
    sin_phase = jnp.sin(phase_ref[...])
    cos_ref[...] = cos_phase
    sin_ref[...] = sin_phase
    leaf = nn_dot(x_ref[...].reshape(boxes * waves, width), rad_ref[...]).astype(BF16)
    up_re = nn_dot(leaf[:, :leaf_dirs], imat)
    up_im = nn_dot(leaf[:, leaf_dirs:], imat)
    for q in range(boxes // 8):
        re = jnp.zeros((waves, parent_dirs), F32)
        im = jnp.zeros((waves, parent_dirs), F32)
        for c in range(8):
            at = (q * 8 + c) * waves
            ure = up_re[at : at + waves]
            uim = up_im[at : at + waves]
            re = re + (cos_phase[c : c + 1] * ure - sin_phase[c : c + 1] * uim)
            im = im + (sin_phase[c : c + 1] * ure + cos_phase[c : c + 1] * uim)
        both = jnp.concatenate([re, im], axis=0).astype(BF16)
        for k in range(chunks):
            part = both[:, k * 128 : (k + 1) * 128]
            packet_ref[own_rows + q * chunks + k] = part
            spectra_ref[q * chunks + k] = part


def carries_packet(step):
    return step & (step + 1) == 0


def group_kernel(own_ref, *refs):
    *step_refs, _, group_ref = refs
    size = lax.axis_size("dir")
    rows = own_ref.shape[0]
    here = lax.axis_index("dir")
    group_ref[pl.ds(here * rows, rows)] = own_ref[...]
    for step, ref in enumerate(step_refs, 1):
        group_ref[pl.ds((here ^ step) * rows, rows)] = ref[ref.shape[0] - rows :]
    group_ref[size * rows :] = step_refs[-1][: step_refs[-1].shape[0] - rows]


def features(planes):
    rows, _, width = planes.shape
    boxes = rows * 16 // 3
    planes = planes.astype(F32).reshape(3, boxes, width)
    at = lax.broadcasted_iota(jnp.int32, (boxes, 8, width), 1)
    pos = jnp.zeros((boxes, 8, width), F32)
    for axis in range(3):
        pos = jnp.where(at == axis, planes[axis][:, None, :], pos)
    scale = TURN * TURN
    norm = split3(scale * jnp.sum(pos * pos, axis=1, keepdims=True))
    first = jnp.where(at < 3, pos, 1.0)
    first = jnp.where(at == 3, norm[0], jnp.where(at == 4, norm[1], jnp.where(at == 5, norm[2], first)))
    second = jnp.where(at == 3, 1.0, pos + pltpu.roll(pos, 4, 1))
    source = jnp.concatenate([first, second], axis=1).astype(BF16)
    cross = split3((-2.0 * scale) * pos)
    first = jnp.where(at < 3, cross[0], 1.0)
    first = jnp.where(at == 6, norm[0], jnp.where(at == 7, norm[1], first))
    second = jnp.where(at == 3, norm[2], cross[1] + pltpu.roll(cross[2], 4, 1))
    return source, jnp.concatenate([first, second], axis=1).astype(BF16)


def turn_sources(source, src_ref, start):
    boxes, rows, width = source.shape
    eye = lax.broadcasted_iota(jnp.int32, (width, width), 0) == lax.broadcasted_iota(jnp.int32, (width, width), 1)
    twice = jnp.concatenate([source, source], axis=1).reshape(boxes * 2 * rows, width)
    turned = nt_dot(eye.astype(F32).astype(BF16), twice)
    for b in range(boxes):
        at = b * 2 * rows
        lanes = turned[:, at // 128 * 128 : at // 128 * 128 + 128]
        if at % 128:
            lanes = pltpu.roll(lanes, 128 - at % 128, 1)
        src_ref[start + b] = lanes.astype(BF16)


def take_currents(x_rows, win_ref, start):
    for k in range(x_rows.shape[0]):
        both = x_rows[k]
        wide = both.astype(F32)
        win_ref[start + 2 * k] = both
        win_ref[start + 2 * k + 1] = jnp.concatenate([wide[8:], wide[:8]], axis=0).astype(BF16)


def near_sum(entries, total, item_at, first_source, src_ref, win_ref, obs_ref, out_ref, scratch):
    u0_ref, u1_ref, t0_ref, t1_ref = scratch
    boxes, waves, width = out_ref.shape
    count_bits, box_bits, source_bits = code_bits(boxes, entries)
    pair_bits = count_bits + box_bits + source_bits
    t1_ref[...] = jnp.zeros(t1_ref.shape, BF16)
    upper = lax.broadcasted_iota(jnp.int32, (2 * waves, width), 0) < waves
    left = lax.broadcasted_iota(jnp.int32, (width, 128), 1) < 16
    empty = jnp.zeros((16, width), BF16)

    def pair_at(chunk, g, slot):
        code = item_at(chunk * ITEMS + g) >> (slot * pair_bits)
        source = (code >> (count_bits + box_bits)) & ((1 << source_bits) - 1)
        if first_source:
            source = jnp.maximum(source - first_source, 0)
        return source, (code >> count_bits) & ((1 << box_bits) - 1), code & ((1 << count_bits) - 1)

    def distances(chunk, g, u_ref):
        source0, box0, _ = pair_at(chunk, g, 0)
        source1, box1, _ = pair_at(chunk, g, 1)
        sources = jnp.where(left, src_ref[source0], src_ref[source1])
        observers = jnp.concatenate(
            [
                jnp.concatenate([obs_ref[box0], empty], axis=1),
                jnp.concatenate([empty, obs_ref[box1]], axis=1),
            ],
            axis=0,
        )
        u_ref[g] = nn_dot(sources[:, :32], observers)

    def tile(g, u_ref, t_ref):
        for at in range(0, width, ROWS):
            v = jnp.maximum(u_ref[g, at : at + ROWS], 1e-12)
            q = v * lax.rsqrt(v)
            t = q - jnp.round(q)
            cosine = t * t + CHAIN[0]
            for constant in CHAIN[1:]:
                cosine = cosine * cosine + constant
            t_ref[g, at : at + ROWS] = (cosine * pltpu.reciprocal(q + OFFSET * TURN, approx=True)).astype(BF16)

    def product(chunk, g, t_ref):
        source0, box0, count0 = pair_at(chunk, g, 0)
        source1, box1, count1 = pair_at(chunk, g, 1)
        currents = jnp.where(upper, win_ref[source0].astype(F32), win_ref[source1 ^ 1].astype(F32)).astype(BF16)
        got = nn_dot(currents, t_ref[g])
        out_ref[box0] += count0.astype(F32) * got[:waves, :width]
        out_ref[box1] += count1.astype(F32) * got[waves:, width:]

    u_refs = (u0_ref, u1_ref)
    t_refs = (t0_ref, t1_ref)

    def stage(chunk, turn):
        for g in range(ITEMS):
            distances(chunk + 1, g, u_refs[1 - turn])
            product(jnp.maximum(chunk - 1, 0), g, t_refs[1 - turn])
            tile(g, u_refs[turn], t_refs[turn])

    def body(k, carry):
        for j in range(STAGES):
            stage(k * STAGES + j, j & 1)
        return carry

    def finish(turn):
        for g in range(ITEMS):
            product(jnp.maximum(chunks - 1, 0), g, t_refs[turn])

    chunks = (total + (ITEMS - 1)) // ITEMS
    rounds = chunks // STAGES
    for g in range(ITEMS):
        distances(0, g, u0_ref)
    lax.fori_loop(0, rounds, body, 0)
    for j in range(STAGES - 1):
        pl.when(rounds * STAGES + j < chunks)(functools.partial(stage, rounds * STAGES + j, j & 1))
    pl.when((chunks > 0) & ((chunks & 1) == 0))(functools.partial(finish, 1))
    pl.when((chunks & 1) == 1)(functools.partial(finish, 0))


def prepare_kernel(
    entries, own_ref, items_ref, src_hbm, id_hbm, count_hbm, table_hbm, out_ref, obs_ref, src_ref, win_ref, gain_ref,
    trans_src_ref, trans_id_ref, trans_count_ref, table_ref, list_ref, u0_ref, u1_ref, t0_ref, t1_ref, sems
):
    boxes = obs_ref.shape[0]
    length = list_ref.shape[1]
    parents, window = gain_ref.shape[:2]
    listed = src_hbm.shape[1]
    fetch, *trans_copies = start_all(
        (
            (items_ref, list_ref),
            (src_hbm, trans_src_ref),
            (id_hbm, trans_id_ref),
            (count_hbm, trans_count_ref),
            (table_hbm, table_ref),
        ),
        sems,
    )
    plane_rows = 3 * boxes // 16
    source, observer = features(own_ref[boxes // 2 : boxes // 2 + plane_rows])
    turn_sources(source, src_ref, 0)
    take_currents(own_ref[: boxes // 2], win_ref, 0)
    obs_ref[...] = observer
    out_ref[...] = jnp.zeros(out_ref.shape, F32)
    gain_ref[...] = jnp.zeros(gain_ref.shape, F32)
    fetch.wait()
    near_sum(
        entries,
        list_ref[0, length - 3],
        lambda k: list_ref[0, k],
        0,
        src_ref,
        win_ref,
        obs_ref,
        out_ref,
        (u0_ref, u1_ref, t0_ref, t1_ref),
    )
    wait_all(trans_copies)
    row0 = lax.axis_index("dir") * parents
    first = (lax.axis_index("box") - 1) * (window // 3)
    for q in range(parents):
        for e in range(listed):
            live = (e < trans_count_ref[row0 + q]).astype(F32)
            s = jnp.clip(trans_src_ref[row0 + q, e] - first, 0, window - 1)
            gain_ref[q, s] += table_ref[trans_id_ref[row0 + q, e]] * live


def near_kernel(entries, items_ref, *refs):
    *refs, sem = refs
    (
        *step_refs, obs_ref, first_ref, _, _, out_ref, src_ref, win_ref, list_ref, u0_ref, u1_ref, t0_ref, t1_ref
    ) = refs
    boxes, waves, width = out_ref.shape
    fetch = pltpu.make_async_copy(items_ref, list_ref, sem)
    fetch.start()
    length = list_ref.shape[1]
    here = lax.axis_index("dir")
    other_side = jnp.where((here & 1) == 0, here - 1, here + 1)
    x_rows = boxes // 2
    own_rows = x_rows + 3 * boxes // 16

    def take(packet, part):
        take_currents(packet[:x_rows], win_ref, part * boxes)
        source, _ = features(packet[x_rows:])
        turn_sources(source, src_ref, part * boxes)

    take(step_refs[0][:own_rows], 1)
    if len(step_refs) > 1:
        packet = step_refs[1][:own_rows]
        for k, ref in enumerate(step_refs[2:], 3):
            from_here = (here ^ ((1 << k) - 1)) == other_side
            packet = jnp.where(from_here, ref[:own_rows].astype(F32), packet.astype(F32)).astype(BF16)
        take(packet, 2)
    second_start = list_places(boxes, entries)[1]
    out_ref[...] = first_ref[...]
    fetch.wait()
    near_sum(
        entries,
        list_ref[0, length - 2],
        lambda k: list_ref[0, second_start + k],
        0,
        src_ref,
        win_ref,
        obs_ref,
        out_ref,
        (u0_ref, u1_ref, t0_ref, t1_ref),
    )


def incoming_kernel(
    entries, items_ref, odd_ref, own_ref, even_ref, gain_ref, cos_ref, sin_ref, imat_ref, rad_ref, obs_ref, near_ref, out_ref,
    sum_ref, win_ref, src_ref, down_re_ref, down_im_ref, list_ref, u0_ref, u1_ref, t0_ref, t1_ref, sem
):
    parents, window, _, parent_dirs = gain_ref.shape
    boxes, waves, width = near_ref.shape
    chunks = parent_dirs // 128
    group = window // 3
    fetch = pltpu.make_async_copy(items_ref, list_ref, sem)
    fetch.start()
    length = list_ref.shape[1]
    odd_box = lax.axis_index("box") & 1
    sum_ref[...] = near_ref[...]
    x_rows = boxes // 2
    packet_rows = x_rows + 3 * boxes // 16
    from_even = jnp.where(lax.axis_index("dir") == 0, 1, 0) == odd_box
    even_packet, odd_packet = (ref[ref.shape[0] - packet_rows :] for ref in (even_ref, odd_ref))
    packet = jnp.where(from_even, even_packet.astype(F32), odd_packet.astype(F32)).astype(BF16)
    take_currents(packet[:x_rows], win_ref, 0)
    source, _ = features(packet[x_rows:])
    turn_sources(source, src_ref, 0)
    fetch.wait()
    cos_phase = cos_ref[...]
    sin_phase = sin_ref[...]
    sums = tuple(jnp.zeros((waves, 128), F32) for _ in range(parents * chunks * 2))
    for part, ref in ((2 - 2 * odd_box, even_ref), (1, own_ref), (2 * odd_box, odd_ref)):

        def add_source(s, sums, part=part, ref=ref):
            sums = list(sums)
            gains = [gain_ref[q, part * group + s] for q in range(parents)]
            for k in range(chunks):
                spectrum = ref[s * chunks + k].astype(F32)
                sre, sim = spectrum[:waves], spectrum[waves:]
                for q in range(parents):
                    gre = gains[q][0:1, k * 128 : (k + 1) * 128]
                    gim = gains[q][1:2, k * 128 : (k + 1) * 128]
                    at = (q * chunks + k) * 2
                    sums[at] = sums[at] + (gre * sre - gim * sim)
                    sums[at + 1] = sums[at + 1] + (gre * sim + gim * sre)
            return tuple(sums)

        sums = lax.fori_loop(0, group, add_source, sums, unroll=8)
    for q in range(parents):
        for k in range(chunks):
            at = (q * chunks + k) * 2
            re = sums[at].astype(BF16).astype(F32)
            im = sums[at + 1].astype(BF16).astype(F32)
            lanes = slice(k * 128, (k + 1) * 128)
            for c in range(8):
                cos, sin = cos_phase[c : c + 1, lanes], sin_phase[c : c + 1, lanes]
                rows = slice((q * 8 + c) * waves, (q * 8 + c + 1) * waves)
                down_re_ref[rows, lanes] = cos * re + sin * im
                down_im_ref[rows, lanes] = cos * im - sin * re
    imat = imat_ref[...]
    in_re = nt_dot(down_re_ref[...].astype(BF16), imat)
    in_im = nt_dot(down_im_ref[...].astype(BF16), imat)
    incoming = jnp.concatenate([in_re, in_im], axis=1).astype(BF16)
    far = nt_dot(incoming, rad_ref[...])
    near_sum(
        entries,
        list_ref[0, length - 1],
        lambda k: list_ref[0, length - 4 - k],
        2 * boxes,
        src_ref,
        win_ref,
        obs_ref,
        sum_ref,
        (u0_ref, u1_ref, t0_ref, t1_ref),
    )
    factor = TURN * LEAD / math.sqrt(entries * width)
    out_ref[...] = sum_ref[...] * factor + far.reshape(near_ref.shape)


def per_device(
    currents, positions, radiation, interp_index, interp_weight, child_phase, near_src, trans_src, trans_id,
    trans_count, trans_table
):
    boxes, waves, width = currents.shape
    entries = near_src.shape[1]
    leaf_dirs = radiation.shape[1] // 2
    parent_dirs = child_phase.shape[1]
    parents = boxes // 8
    spectra_rows = parents * parent_dirs // 128
    size = lax.axis_size("dir")
    vmem = pl.BlockSpec(memory_space=pltpu.VMEM)
    hbm = pl.BlockSpec(memory_space=pltpu.HBM)
    params = pltpu.CompilerParams(vmem_limit_bytes=32 * 1024 * 1024)

    def in_hbm(x):
        return pltpu.with_memory_space_constraint(x, pltpu.HBM)

    def shaped(shape, dtype):
        return jax.ShapeDtypeStruct(shape, dtype)

    x_rows = boxes // 2
    own_rows = x_rows + 3 * boxes // 16
    operands = (currents.reshape(x_rows, 2 * waves, width), positions.transpose(1, 0, 2), radiation, interp_index.T, interp_weight.T, child_phase)
    operands = operands + (near_src,)
    length = list_places(boxes, entries)[2]
    packet, spectra, imat, cos_phase, sin_phase, rad, items = pl.pallas_call(
        outgoing_kernel,
        out_shape=(
            shaped((own_rows + spectra_rows, 16, width), BF16),
            shaped((spectra_rows, 2 * waves, 128), BF16),
            shaped((leaf_dirs, parent_dirs), BF16),
            shaped((8, parent_dirs), F32),
            shaped((8, parent_dirs), F32),
            shaped(radiation.shape, BF16),
            shaped((1, length), jnp.int32),
        ),
        in_specs=[hbm] * len(operands),
        out_specs=(vmem,) * 7,
        scratch_shapes=[pltpu.VMEM(x.shape, x.dtype) for x in operands if x is not radiation]
        + [pltpu.SemaphoreType.DMA((len(operands),))],
        compiler_params=params,
        name="outgoing",
    )(*[in_hbm(x) for x in operands])

    steps = []
    for step in range(1, size):
        pairs = [(i, i ^ step) for i in range(size) if i < i ^ step]
        steps.append(swapped(packet if carries_packet(step) else spectra, "dir", pairs))

    window = 3 * trans_src.shape[0]
    near_scratch = [
        pltpu.VMEM((ITEMS, width, 2 * width), F32),
        pltpu.VMEM((ITEMS, width, 2 * width), F32),
        pltpu.VMEM((ITEMS, width, 2 * width), BF16),
        pltpu.VMEM((ITEMS, width, 2 * width), BF16),
    ]
    first_sum, observers, sources, ordered, gains = pl.pallas_call(
        functools.partial(prepare_kernel, entries),
        out_shape=(
            shaped((boxes, waves, width), F32),
            shaped((boxes, 16, width), BF16),
            shaped((3 * boxes, width, 128), BF16),
            shaped((3 * boxes, 16, width), BF16),
            shaped((parents, window, 2, parent_dirs), F32),
        ),
        in_specs=[vmem] * 2 + [hbm] * 4,
        out_specs=(vmem,) * 5,
        scratch_shapes=[
            pltpu.SMEM(trans_src.shape, jnp.int32),
            pltpu.SMEM(trans_id.shape, jnp.int32),
            pltpu.SMEM(trans_count.shape, jnp.int32),
            pltpu.VMEM(trans_table.shape, F32),
            pltpu.SMEM((1, length), jnp.int32),
        ]
        + near_scratch
        + [pltpu.SemaphoreType.DMA((5,))],
        compiler_params=params,
        name="prepare",
    )(packet, items, *[in_hbm(x) for x in (trans_src, trans_id, trans_count, trans_table)])

    group = pl.pallas_call(
        group_kernel,
        out_shape=shaped((size * spectra_rows + own_rows, 2 * waves, 128), BF16),
        in_specs=[vmem] * (2 + len(steps)),
        out_specs=vmem,
        compiler_params=params,
        name="group",
    )(spectra, *steps, first_sum)
    groups = lax.axis_size("box")
    group_odd = swapped(group, "box", [(i, i + 1) for i in range(1, groups - 1, 2)])
    group_even = swapped(group, "box", [(i, i + 1) for i in range(0, groups - 1, 2)])

    packets = [x for step, x in enumerate(steps, 1) if carries_packet(step)]
    near, _, _ = pl.pallas_call(
        functools.partial(near_kernel, entries),
        out_shape=(
            shaped((boxes, waves, width), F32),
            shaped(sources.shape, BF16),
            shaped(ordered.shape, BF16),
        ),
        in_specs=[vmem] * (5 + len(packets)),
        out_specs=(vmem,) * 3,
        input_output_aliases={3 + len(packets): 1, 4 + len(packets): 2},
        scratch_shapes=[pltpu.SMEM((1, length), jnp.int32)] + near_scratch + [pltpu.SemaphoreType.DMA],
        compiler_params=params,
        name="near",
    )(items, *packets, observers, first_sum, sources, ordered)

    return pl.pallas_call(
        functools.partial(incoming_kernel, entries),
        out_shape=shaped((boxes, waves, width), F32),
        in_specs=[vmem] * 11,
        out_specs=vmem,
        scratch_shapes=[
            pltpu.VMEM((boxes, waves, width), F32),
            pltpu.VMEM((boxes, 16, width), BF16),
            pltpu.VMEM((boxes, width, 128), BF16),
            pltpu.VMEM((boxes * waves, parent_dirs), F32),
            pltpu.VMEM((boxes * waves, parent_dirs), F32),
            pltpu.SMEM((1, length), jnp.int32),
        ]
        + near_scratch
        + [pltpu.SemaphoreType.DMA],
        compiler_params=params,
        name="incoming",
    )(items, group_odd, group, group_even, gains, cos_phase, sin_phase, imat, rad, observers, near)


def solution(mesh):
    placed = (
        P(("box", "dir"), None, None),
        P(("box", "dir"), None, None),
        P(),
        P(),
        P(),
        P(),
        P(("box", "dir"), None),
        P("box", None),
        P("box", None),
        P("box"),
        P(),
    )
    return jax.shard_map(
        per_device,
        mesh=mesh,
        in_specs=placed,
        out_specs=P(("box", "dir"), None, None),
        check_vma=False,
    )
```

```python
import functools
import math

import jax
import jax.numpy as jnp
from jax import lax
from jax.experimental import pallas as pl
from jax.experimental.pallas import tpu as pltpu
from jax.sharding import PartitionSpec as P

F32 = jnp.float32
BF16 = jnp.bfloat16

WAVENUMBER = 4.0
OFFSET = 0.5
TURN = WAVENUMBER / (2.0 * math.pi)
CHAIN = (-2.2803148655023415, -1.415255674611144, -7.327656729815578, -24.467745134801202)
LEAD = 0.04087004462557604
ITEMS = 4
ROWS = 32
STAGES = 4
FIRST_ITEMS = 6
AHEAD = 2
LEFT_OVER = 2


def round_up(value, step):
    return -(-value // step) * step


def swapped(x, axis, pairs):
    return lax.ppermute(x, axis, [way for i, j in pairs for way in ((i, j), (j, i))])


def split3(x):
    high = x.astype(BF16).astype(F32)
    rest = x - high
    mid = rest.astype(BF16).astype(F32)
    return high, mid, rest - mid


def nt_dot(a, b):
    return lax.dot_general(a, b, (((1,), (1,)), ((), ())), preferred_element_type=F32)


def nn_dot(a, b):
    return jnp.dot(a, b, preferred_element_type=F32)


def code_bits(boxes, entries):
    return entries.bit_length(), (boxes - 1).bit_length(), (3 * boxes - 1).bit_length()


def list_places(boxes, entries):
    gap = 2 * ITEMS
    most = FIRST_ITEMS * boxes // 2
    return most, most + gap, round_up(most + gap + boxes * entries // 2 + 2 * gap + 6, 128)


def list_items(near_src, block, here, size):
    boxes, entries = near_src.shape
    most, second_start, length = list_places(boxes, entries)
    count_bits, box_bits, source_bits = code_bits(boxes, entries)
    pair_bits = count_bits + box_bits + source_bits
    lanes = round_up(3 * boxes, 128)
    odd = (here & 1) == 1
    edge = (here == 0) | (here == size - 1)
    local = near_src - block * boxes
    below = local + jnp.where(odd, 2 * boxes, 3 * boxes)
    above = local + jnp.where(odd, boxes, 0)
    local = jnp.where(local < 0, below, jnp.where(local >= boxes, above, local))
    lane = lax.broadcasted_iota(jnp.int32, (boxes, lanes), 1)
    box = lax.broadcasted_iota(jnp.int32, (boxes, lanes), 0)
    count = jnp.zeros((boxes, lanes), jnp.int32)
    for e in range(entries):
        count = count + (local[:, e : e + 1] == lane).astype(jnp.int32)
    present = count > 0
    flags = present.astype(F32)
    box_row = lax.broadcasted_iota(jnp.int32, (boxes, boxes), 0)
    box_col = lax.broadcasted_iota(jnp.int32, (boxes, boxes), 1)
    rank = nn_dot((box_col < box_row).astype(F32).astype(BF16), flags.astype(BF16)).astype(jnp.int32)
    pairs = jnp.sum(flags, axis=0, keepdims=True)
    from_cross = lane >= jnp.where(edge, 2 * boxes, 3 * boxes - LEFT_OVER)
    cross_pairs = jnp.where(from_cross[:1], pairs, 0.0)
    group_pairs = jnp.where(from_cross[:1], 0.0, pairs)
    row = lax.broadcasted_iota(jnp.int32, (lanes, lanes), 0)
    col = lax.broadcasted_iota(jnp.int32, (lanes, lanes), 1)
    ahead = (row < col).astype(F32).astype(BF16)
    lists = jnp.concatenate([group_pairs, cross_pairs, jnp.zeros((6, lanes), F32)], axis=0)
    offset = nn_dot(lists.astype(BF16), ahead).astype(jnp.int32)
    own_pairs = jnp.where(lane[:1] < boxes, group_pairs, 0.0)

    def total(pairs):
        return jnp.sum(pairs, axis=1, keepdims=True).astype(jnp.int32)

    first_total = jnp.minimum(total(own_pairs), 2 * most)
    second_total = total(group_pairs) - first_total
    cross_total = total(cross_pairs)
    order = offset[0:1] + rank
    in_second = order >= first_total
    order = jnp.where(in_second, order - first_total, order)
    order = jnp.where(from_cross, offset[1:2] + rank, order)
    half = order >> 1
    place = jnp.where(from_cross, (length - 4) - half, jnp.where(in_second, second_start + half, half))
    place = jnp.where(present, place, -1)
    code = (lane << (count_bits + box_bits)) | (box << count_bits) | count
    code = jnp.where((order & 1) == 1, code << pair_bits, code)
    place_t = place.T
    code_t = code.T
    rows = 3 * boxes
    slot = lax.broadcasted_iota(jnp.int32, (rows, length), 1)
    found = jnp.zeros((rows, length), jnp.int32)
    for i in range(boxes):
        hit = place_t[:rows, i : i + 1] == slot
        found = found + jnp.where(hit, code_t[:rows, i : i + 1], 0)
    listed = jnp.sum(found, axis=0, keepdims=True)
    at = lax.broadcasted_iota(jnp.int32, (1, length), 1)
    for back, pairs in ((3, first_total), (2, second_total), (1, cross_total)):
        listed = jnp.where(at == length - back, (pairs + 1) >> 1, listed)
    return listed


def start_all(copies, sems):
    started = [pltpu.make_async_copy(src, dst, sems.at[k]) for k, (src, dst) in enumerate(copies)]
    for copy in started:
        copy.start()
    return started


def wait_all(started):
    for copy in started:
        copy.wait()


def outgoing_kernel(
    x_hbm, pos_hbm, rad_hbm, idx_hbm, wgt_hbm, phase_hbm, near_hbm, packet_ref, spectra_ref, imat_ref, cos_ref, sin_ref,
    rad_ref, items_ref, x_ref, pos_ref, idx_ref, wgt_ref, phase_ref, near_ref, sems
):
    wait_all(
        start_all(
            (
                (x_hbm, x_ref),
                (pos_hbm, pos_ref),
                (rad_hbm, rad_ref),
                (idx_hbm, idx_ref),
                (wgt_hbm, wgt_ref),
                (phase_hbm, phase_ref),
                (near_hbm, near_ref),
            ),
            sems,
        )
    )
    block = lax.axis_index(("box", "dir"))
    items_ref[...] = list_items(near_ref[...], block, lax.axis_index("dir"), lax.axis_size("dir"))
    leaf_dirs, parent_dirs = imat_ref.shape
    x_rows, _, width = x_ref.shape
    axes, boxes, _ = pos_ref.shape
    waves = x_rows * 16 // boxes
    chunks = parent_dirs // 128
    own_rows = x_rows + axes * boxes // 16
    packet_ref[:x_rows] = x_ref[...]
    packet_ref[x_rows:own_rows] = pos_ref[...].reshape(axes * boxes // 16, 16, width)
    column = lax.broadcasted_iota(jnp.int32, (leaf_dirs, parent_dirs), 0)
    imat = jnp.zeros((leaf_dirs, parent_dirs), F32)
    for s in range(idx_ref.shape[0]):
        imat = imat + jnp.where(idx_ref[s : s + 1, :] == column, wgt_ref[s : s + 1, :], 0.0)
    imat = imat.astype(BF16)
    imat_ref[...] = imat
    cos_phase = jnp.cos(phase_ref[...])
    sin_phase = jnp.sin(phase_ref[...])
    cos_ref[...] = cos_phase
    sin_ref[...] = sin_phase
    leaf = nn_dot(x_ref[...].reshape(boxes * waves, width), rad_ref[...]).astype(BF16)
    up_re = nn_dot(leaf[:, :leaf_dirs], imat)
    up_im = nn_dot(leaf[:, leaf_dirs:], imat)
    for q in range(boxes // 8):
        re = jnp.zeros((waves, parent_dirs), F32)
        im = jnp.zeros((waves, parent_dirs), F32)
        for c in range(8):
            at = (q * 8 + c) * waves
            ure = up_re[at : at + waves]
            uim = up_im[at : at + waves]
            re = re + (cos_phase[c : c + 1] * ure - sin_phase[c : c + 1] * uim)
            im = im + (sin_phase[c : c + 1] * ure + cos_phase[c : c + 1] * uim)
        both = jnp.concatenate([re, im], axis=0).astype(BF16)
        for k in range(chunks):
            part = both[:, k * 128 : (k + 1) * 128]
            packet_ref[own_rows + q * chunks + k] = part
            spectra_ref[q * chunks + k] = part


def carries_packet(step):
    return step & (step + 1) == 0


def group_kernel(own_ref, *refs):
    *step_refs, _, group_ref = refs
    size = lax.axis_size("dir")
    rows = own_ref.shape[0]
    here = lax.axis_index("dir")
    group_ref[pl.ds(here * rows, rows)] = own_ref[...]
    for step, ref in enumerate(step_refs, 1):
        group_ref[pl.ds((here ^ step) * rows, rows)] = ref[ref.shape[0] - rows :]
    group_ref[size * rows :] = step_refs[-1][: step_refs[-1].shape[0] - rows]


def features(planes):
    rows, _, width = planes.shape
    boxes = rows * 16 // 3
    planes = planes.astype(F32).reshape(3, boxes, width)
    at = lax.broadcasted_iota(jnp.int32, (boxes, 8, width), 1)
    pos = jnp.zeros((boxes, 8, width), F32)
    for axis in range(3):
        pos = jnp.where(at == axis, planes[axis][:, None, :], pos)
    scale = TURN * TURN
    norm = split3(scale * jnp.sum(pos * pos, axis=1, keepdims=True))
    first = jnp.where(at < 3, pos, 1.0)
    first = jnp.where(at == 3, norm[0], jnp.where(at == 4, norm[1], jnp.where(at == 5, norm[2], first)))
    second = jnp.where(at == 3, 1.0, pos + pltpu.roll(pos, 4, 1))
    source = jnp.concatenate([first, second], axis=1).astype(BF16)
    cross = split3((-2.0 * scale) * pos)
    first = jnp.where(at < 3, cross[0], 1.0)
    first = jnp.where(at == 6, norm[0], jnp.where(at == 7, norm[1], first))
    second = jnp.where(at == 3, norm[2], cross[1] + pltpu.roll(cross[2], 4, 1))
    return source, jnp.concatenate([first, second], axis=1).astype(BF16)


def turn_sources(source, src_ref, start):
    boxes, rows, width = source.shape
    eye = lax.broadcasted_iota(jnp.int32, (width, width), 0) == lax.broadcasted_iota(jnp.int32, (width, width), 1)
    twice = jnp.concatenate([source, source], axis=1).reshape(boxes * 2 * rows, width)
    turned = nt_dot(eye.astype(F32).astype(BF16), twice)
    for b in range(boxes):
        at = b * 2 * rows
        lanes = turned[:, at // 128 * 128 : at // 128 * 128 + 128]
        if at % 128:
            lanes = pltpu.roll(lanes, 128 - at % 128, 1)
        src_ref[start + b] = lanes.astype(BF16)


def take_currents(x_rows, win_ref, start):
    for k in range(x_rows.shape[0]):
        both = x_rows[k]
        wide = both.astype(F32)
        win_ref[start + 2 * k] = both
        win_ref[start + 2 * k + 1] = jnp.concatenate([wide[8:], wide[:8]], axis=0).astype(BF16)


def near_sum(entries, total, item_at, first_source, src_ref, win_ref, obs_ref, out_ref, scratch, ahead=0):
    u0_ref, u1_ref, t0_ref, t1_ref = scratch
    boxes, waves, width = out_ref.shape
    count_bits, box_bits, source_bits = code_bits(boxes, entries)
    pair_bits = count_bits + box_bits + source_bits
    t1_ref[...] = jnp.zeros(t1_ref.shape, BF16)
    upper = lax.broadcasted_iota(jnp.int32, (2 * waves, width), 0) < waves
    left = lax.broadcasted_iota(jnp.int32, (width, 128), 1) < 16
    empty = jnp.zeros((16, width), BF16)

    def pair_at(chunk, g, slot):
        code = item_at(chunk * ITEMS + g) >> (slot * pair_bits)
        source = (code >> (count_bits + box_bits)) & ((1 << source_bits) - 1)
        if first_source:
            source = jnp.maximum(source - first_source, 0)
        return source, (code >> count_bits) & ((1 << box_bits) - 1), code & ((1 << count_bits) - 1)

    def distances(chunk, g, u_ref):
        source0, box0, _ = pair_at(chunk, g, 0)
        source1, box1, _ = pair_at(chunk, g, 1)
        sources = jnp.where(left, src_ref[source0], src_ref[source1])
        observers = jnp.concatenate(
            [
                jnp.concatenate([obs_ref[box0], empty], axis=1),
                jnp.concatenate([empty, obs_ref[box1]], axis=1),
            ],
            axis=0,
        )
        u_ref[g] = nn_dot(sources[:, :32], observers)

    def tile(g, u_ref, t_ref):
        for at in range(0, width, ROWS):
            v = jnp.maximum(u_ref[g, at : at + ROWS], 1e-12)
            q = v * lax.rsqrt(v)
            t = q - jnp.round(q)
            cosine = t * t + CHAIN[0]
            for constant in CHAIN[1:]:
                cosine = cosine * cosine + constant
            t_ref[g, at : at + ROWS] = (cosine * pltpu.reciprocal(q + OFFSET * TURN, approx=True)).astype(BF16)

    def product(chunk, g, t_ref):
        source0, box0, count0 = pair_at(chunk, g, 0)
        source1, box1, count1 = pair_at(chunk, g, 1)
        currents = jnp.where(upper, win_ref[source0].astype(F32), win_ref[source1 ^ 1].astype(F32)).astype(BF16)
        got = nn_dot(currents, t_ref[g])
        out_ref[box0] += count0.astype(F32) * got[:waves, :width]
        out_ref[box1] += count1.astype(F32) * got[waves:, width:]

    u_refs = (u0_ref, u1_ref)
    t_refs = (t0_ref, t1_ref)

    def stage(chunk, turn):
        for g in range(ITEMS):
            distances(chunk + 1, g, u_refs[1 - turn])
            product(jnp.maximum(chunk - 1, 0), g, t_refs[1 - turn])
            tile(g, u_refs[turn], t_refs[turn])

    def body(k, carry):
        for j in range(STAGES):
            stage(ahead + k * STAGES + j, j & 1)
        return carry

    def finish(turn):
        for g in range(ITEMS):
            product(jnp.maximum(chunks - 1, 0), g, t_refs[turn])

    chunks = jnp.maximum((total + (ITEMS - 1)) // ITEMS, ahead)
    rounds = (chunks - ahead) // STAGES
    for g in range(ITEMS):
        distances(0, g, u0_ref)
    for j in range(ahead):
        stage(j, j & 1)
    lax.fori_loop(0, rounds, body, 0)
    last = ahead + rounds * STAGES
    for j in range(STAGES - 1):
        pl.when(last + j < chunks)(functools.partial(stage, last + j, j & 1))
    pl.when((chunks > 0) & ((chunks & 1) == 0))(functools.partial(finish, 1))
    pl.when((chunks & 1) == 1)(functools.partial(finish, 0))


def prepare_kernel(
    entries, own_ref, items_ref, src_hbm, id_hbm, count_hbm, table_hbm, out_ref, obs_ref, src_ref, win_ref, gain_ref,
    trans_src_ref, trans_id_ref, trans_count_ref, table_ref, list_ref, u0_ref, u1_ref, t0_ref, t1_ref, sems
):
    boxes = obs_ref.shape[0]
    length = list_ref.shape[1]
    parents, window = gain_ref.shape[:2]
    listed = src_hbm.shape[1]
    fetch, *trans_copies = start_all(
        (
            (items_ref, list_ref),
            (src_hbm, trans_src_ref),
            (id_hbm, trans_id_ref),
            (count_hbm, trans_count_ref),
            (table_hbm, table_ref),
        ),
        sems,
    )
    plane_rows = 3 * boxes // 16
    source, observer = features(own_ref[boxes // 2 : boxes // 2 + plane_rows])
    turn_sources(source, src_ref, 0)
    take_currents(own_ref[: boxes // 2], win_ref, 0)
    obs_ref[...] = observer
    out_ref[...] = jnp.zeros(out_ref.shape, F32)
    gain_ref[...] = jnp.zeros(gain_ref.shape, F32)
    fetch.wait()
    near_sum(
        entries,
        list_ref[0, length - 3],
        lambda k: list_ref[0, k],
        0,
        src_ref,
        win_ref,
        obs_ref,
        out_ref,
        (u0_ref, u1_ref, t0_ref, t1_ref),
    )
    wait_all(trans_copies)
    row0 = lax.axis_index("dir") * parents
    first = (lax.axis_index("box") - 1) * (window // 3)
    for q in range(parents):
        for e in range(listed):
            live = (e < trans_count_ref[row0 + q]).astype(F32)
            s = jnp.clip(trans_src_ref[row0 + q, e] - first, 0, window - 1)
            gain_ref[q, s] += table_ref[trans_id_ref[row0 + q, e]] * live


def near_kernel(entries, items_ref, *refs):
    *refs, sem = refs
    (
        *step_refs, obs_ref, first_ref, _, _, out_ref, src_ref, win_ref, list_ref, u0_ref, u1_ref, t0_ref, t1_ref
    ) = refs
    boxes, waves, width = out_ref.shape
    fetch = pltpu.make_async_copy(items_ref, list_ref, sem)
    fetch.start()
    length = list_ref.shape[1]
    here = lax.axis_index("dir")
    other_side = jnp.where((here & 1) == 0, here - 1, here + 1)
    x_rows = boxes // 2
    own_rows = x_rows + 3 * boxes // 16

    def take(packet, part):
        take_currents(packet[:x_rows], win_ref, part * boxes)
        source, _ = features(packet[x_rows:])
        turn_sources(source, src_ref, part * boxes)

    take(step_refs[0][:own_rows], 1)
    if len(step_refs) > 1:
        packet = step_refs[1][:own_rows]
        for k, ref in enumerate(step_refs[2:], 3):
            from_here = (here ^ ((1 << k) - 1)) == other_side
            packet = jnp.where(from_here, ref[:own_rows].astype(F32), packet.astype(F32)).astype(BF16)
        take(packet, 2)
    second_start = list_places(boxes, entries)[1]
    out_ref[...] = first_ref[...]
    fetch.wait()
    near_sum(
        entries,
        list_ref[0, length - 2],
        lambda k: list_ref[0, second_start + k],
        0,
        src_ref,
        win_ref,
        obs_ref,
        out_ref,
        (u0_ref, u1_ref, t0_ref, t1_ref),
    )


def incoming_kernel(entries, others, *refs):
    incoming(entries, *refs[others:], other_refs=refs[:others])


def incoming(
    entries, items_ref, even_ref, own_ref, odd_ref, gain_ref, cos_ref, sin_ref, imat_ref, rad_ref, obs_ref, near_ref, out_ref,
    sum_ref, win_ref, src_ref, down_re_ref, down_im_ref, list_ref, u0_ref, u1_ref, t0_ref, t1_ref, sem, other_refs=()
):
    parents, window, _, parent_dirs = gain_ref.shape
    boxes, waves, width = near_ref.shape
    chunks = parent_dirs // 128
    group = window // 3
    fetch = pltpu.make_async_copy(items_ref, list_ref, sem)
    fetch.start()
    length = list_ref.shape[1]
    odd_box = lax.axis_index("box") & 1
    sum_ref[...] = near_ref[...]
    x_rows = boxes // 2
    packet_rows = x_rows + 3 * boxes // 16
    here = lax.axis_index("dir")
    from_even = jnp.where(here == 0, 1, 0) == odd_box
    even_packet, odd_packet = (ref[ref.shape[0] - packet_rows :] for ref in (even_ref, odd_ref))
    packet = jnp.where(from_even, even_packet.astype(F32), odd_packet.astype(F32))
    other_side = jnp.where((here & 1) == 0, here - 1, here + 1)
    for k, ref in enumerate(other_refs, 2):
        from_group = (here ^ ((1 << k) - 1)) == other_side
        packet = jnp.where(from_group, ref[:packet_rows].astype(F32), packet)
    packet = packet.astype(BF16)
    take_currents(packet[:x_rows], win_ref, 0)
    source, _ = features(packet[x_rows:])
    turn_sources(source, src_ref, 0)
    fetch.wait()
    cos_phase = cos_ref[...]
    sin_phase = sin_ref[...]
    sums = tuple(jnp.zeros((waves, 128), F32) for _ in range(parents * chunks * 2))
    for part, ref in ((2 - 2 * odd_box, even_ref), (1, own_ref), (2 * odd_box, odd_ref)):

        def add_source(s, sums, part=part, ref=ref):
            sums = list(sums)
            gains = [gain_ref[q, part * group + s] for q in range(parents)]
            for k in range(chunks):
                spectrum = ref[s * chunks + k].astype(F32)
                sre, sim = spectrum[:waves], spectrum[waves:]
                for q in range(parents):
                    gre = gains[q][0:1, k * 128 : (k + 1) * 128]
                    gim = gains[q][1:2, k * 128 : (k + 1) * 128]
                    at = (q * chunks + k) * 2
                    sums[at] = sums[at] + (gre * sre - gim * sim)
                    sums[at + 1] = sums[at + 1] + (gre * sim + gim * sre)
            return tuple(sums)

        sums = lax.fori_loop(0, group, add_source, sums, unroll=8)
    for q in range(parents):
        for k in range(chunks):
            at = (q * chunks + k) * 2
            re = sums[at].astype(BF16).astype(F32)
            im = sums[at + 1].astype(BF16).astype(F32)
            lanes = slice(k * 128, (k + 1) * 128)
            for c in range(8):
                cos, sin = cos_phase[c : c + 1, lanes], sin_phase[c : c + 1, lanes]
                rows = slice((q * 8 + c) * waves, (q * 8 + c + 1) * waves)
                down_re_ref[rows, lanes] = cos * re + sin * im
                down_im_ref[rows, lanes] = cos * im - sin * re
    imat = imat_ref[...]
    in_re = nt_dot(down_re_ref[...].astype(BF16), imat)
    in_im = nt_dot(down_im_ref[...].astype(BF16), imat)
    incoming = jnp.concatenate([in_re, in_im], axis=1).astype(BF16)
    far = nt_dot(incoming, rad_ref[...])
    near_sum(
        entries,
        list_ref[0, length - 1],
        lambda k: list_ref[0, length - 4 - k],
        2 * boxes,
        src_ref,
        win_ref,
        obs_ref,
        sum_ref,
        (u0_ref, u1_ref, t0_ref, t1_ref),
        AHEAD,
    )
    factor = TURN * LEAD / math.sqrt(entries * width)
    out_ref[...] = sum_ref[...] * factor + far.reshape(near_ref.shape)


def per_device(
    currents, positions, radiation, interp_index, interp_weight, child_phase, near_src, trans_src, trans_id,
    trans_count, trans_table
):
    boxes, waves, width = currents.shape
    entries = near_src.shape[1]
    leaf_dirs = radiation.shape[1] // 2
    parent_dirs = child_phase.shape[1]
    parents = boxes // 8
    spectra_rows = parents * parent_dirs // 128
    size = lax.axis_size("dir")
    vmem = pl.BlockSpec(memory_space=pltpu.VMEM)
    hbm = pl.BlockSpec(memory_space=pltpu.HBM)
    params = pltpu.CompilerParams(vmem_limit_bytes=32 * 1024 * 1024)

    def in_hbm(x):
        return pltpu.with_memory_space_constraint(x, pltpu.HBM)

    def shaped(shape, dtype):
        return jax.ShapeDtypeStruct(shape, dtype)

    x_rows = boxes // 2
    own_rows = x_rows + 3 * boxes // 16
    operands = (currents.reshape(x_rows, 2 * waves, width), positions.transpose(1, 0, 2), radiation, interp_index.T, interp_weight.T, child_phase)
    operands = operands + (near_src,)
    length = list_places(boxes, entries)[2]
    packet, spectra, imat, cos_phase, sin_phase, rad, items = pl.pallas_call(
        outgoing_kernel,
        out_shape=(
            shaped((own_rows + spectra_rows, 16, width), BF16),
            shaped((spectra_rows, 2 * waves, 128), BF16),
            shaped((leaf_dirs, parent_dirs), BF16),
            shaped((8, parent_dirs), F32),
            shaped((8, parent_dirs), F32),
            shaped(radiation.shape, BF16),
            shaped((1, length), jnp.int32),
        ),
        in_specs=[hbm] * len(operands),
        out_specs=(vmem,) * 7,
        scratch_shapes=[pltpu.VMEM(x.shape, x.dtype) for x in operands if x is not radiation]
        + [pltpu.SemaphoreType.DMA((len(operands),))],
        compiler_params=params,
        name="outgoing",
    )(*[in_hbm(x) for x in operands])

    steps = []
    for step in range(1, size):
        pairs = [(i, i ^ step) for i in range(size) if i < i ^ step]
        steps.append(swapped(packet if carries_packet(step) else spectra, "dir", pairs))

    window = 3 * trans_src.shape[0]
    near_scratch = [
        pltpu.VMEM((ITEMS, width, 2 * width), F32),
        pltpu.VMEM((ITEMS, width, 2 * width), F32),
        pltpu.VMEM((ITEMS, width, 2 * width), BF16),
        pltpu.VMEM((ITEMS, width, 2 * width), BF16),
    ]
    first_sum, observers, sources, ordered, gains = pl.pallas_call(
        functools.partial(prepare_kernel, entries),
        out_shape=(
            shaped((boxes, waves, width), F32),
            shaped((boxes, 16, width), BF16),
            shaped((3 * boxes, width, 128), BF16),
            shaped((3 * boxes, 16, width), BF16),
            shaped((parents, window, 2, parent_dirs), F32),
        ),
        in_specs=[vmem] * 2 + [hbm] * 4,
        out_specs=(vmem,) * 5,
        scratch_shapes=[
            pltpu.SMEM(trans_src.shape, jnp.int32),
            pltpu.SMEM(trans_id.shape, jnp.int32),
            pltpu.SMEM(trans_count.shape, jnp.int32),
            pltpu.VMEM(trans_table.shape, F32),
            pltpu.SMEM((1, length), jnp.int32),
        ]
        + near_scratch
        + [pltpu.SemaphoreType.DMA((5,))],
        compiler_params=params,
        name="prepare",
    )(packet, items, *[in_hbm(x) for x in (trans_src, trans_id, trans_count, trans_table)])

    group = pl.pallas_call(
        group_kernel,
        out_shape=shaped((size * spectra_rows + own_rows, 2 * waves, 128), BF16),
        in_specs=[vmem] * (2 + len(steps)),
        out_specs=vmem,
        compiler_params=params,
        name="group",
    )(spectra, *steps, first_sum)
    groups = lax.axis_size("box")
    group_odd = swapped(group, "box", [(i, i + 1) for i in range(1, groups - 1, 2)])
    group_even = swapped(group, "box", [(i, i + 1) for i in range(0, groups - 1, 2)])

    packets = [x for step, x in enumerate(steps, 1) if carries_packet(step)]
    near, _, _ = pl.pallas_call(
        functools.partial(near_kernel, entries),
        out_shape=(
            shaped((boxes, waves, width), F32),
            shaped(sources.shape, BF16),
            shaped(ordered.shape, BF16),
        ),
        in_specs=[vmem] * (5 + len(packets)),
        out_specs=(vmem,) * 3,
        input_output_aliases={3 + len(packets): 1, 4 + len(packets): 2},
        scratch_shapes=[pltpu.SMEM((1, length), jnp.int32)] + near_scratch + [pltpu.SemaphoreType.DMA],
        compiler_params=params,
        name="near",
    )(items, *packets, observers, first_sum, sources, ordered)

    return pl.pallas_call(
        functools.partial(incoming_kernel, entries, len(packets) - 1),
        out_shape=shaped((boxes, waves, width), F32),
        in_specs=[vmem] * (10 + len(packets)),
        out_specs=vmem,
        scratch_shapes=[
            pltpu.VMEM((boxes, waves, width), F32),
            pltpu.VMEM((boxes, 16, width), BF16),
            pltpu.VMEM((boxes, width, 128), BF16),
            pltpu.VMEM((boxes * waves, parent_dirs), F32),
            pltpu.VMEM((boxes * waves, parent_dirs), F32),
            pltpu.SMEM((1, length), jnp.int32),
        ]
        + near_scratch
        + [pltpu.SemaphoreType.DMA],
        compiler_params=params,
        name="incoming",
    )(*packets[1:], items, group_even, group, group_odd, gains, cos_phase, sin_phase, imat, rad, observers, near)


def solution(mesh):
    placed = (
        P(("box", "dir"), None, None),
        P(("box", "dir"), None, None),
        P(),
        P(),
        P(),
        P(),
        P(("box", "dir"), None),
        P("box", None),
        P("box", None),
        P("box"),
        P(),
    )
    return jax.shard_map(
        per_device,
        mesh=mesh,
        in_specs=placed,
        out_specs=P(("box", "dir"), None, None),
        check_vma=False,
    )
```

```python
import functools
import math

import jax
import jax.numpy as jnp
from jax import lax
from jax.experimental import pallas as pl
from jax.experimental.pallas import tpu as pltpu
from jax.sharding import PartitionSpec as P

F32 = jnp.float32
BF16 = jnp.bfloat16

WAVENUMBER = 4.0
OFFSET = 0.5
TURN = WAVENUMBER / (2.0 * math.pi)
CHAIN = (-2.2803148655023415, -1.415255674611144, -7.327656729815578, -24.467745134801202)
LEAD = 0.04087004462557604
ITEMS = 4
ROWS = 32
STAGES = 4
AHEAD = 2
LEFT_OVER = 2


def round_up(value, step):
    return -(-value // step) * step


def swapped(x, axis, pairs):
    return lax.ppermute(x, axis, [way for i, j in pairs for way in ((i, j), (j, i))])


def split3(x):
    high = x.astype(BF16).astype(F32)
    rest = x - high
    mid = rest.astype(BF16).astype(F32)
    return high, mid, rest - mid


def nt_dot(a, b):
    return lax.dot_general(a, b, (((1,), (1,)), ((), ())), preferred_element_type=F32)


def nn_dot(a, b):
    return jnp.dot(a, b, preferred_element_type=F32)


def code_bits(boxes, entries):
    return entries.bit_length(), (boxes - 1).bit_length()


def list_places(boxes, entries):
    gap = 2 * ITEMS
    second_start = (boxes * (boxes + 1) // 2 + 1) // 2 + gap
    return second_start, round_up(second_start + boxes * entries // 2 + 2 * gap + 6, 128)


def list_items(near_src, block, here, size):
    boxes, entries = near_src.shape
    second_start, length = list_places(boxes, entries)
    count_bits, box_bits = code_bits(boxes, entries)
    lanes = round_up(3 * boxes, 128)
    odd = (here & 1) == 1
    edge = (here == 0) | (here == size - 1)
    local = near_src - block * boxes
    below = local + jnp.where(odd, 2 * boxes, 3 * boxes)
    above = local + jnp.where(odd, boxes, 0)
    local = jnp.where(local < 0, below, jnp.where(local >= boxes, above, local))
    lane = lax.broadcasted_iota(jnp.int32, (boxes, lanes), 1)
    box = lax.broadcasted_iota(jnp.int32, (boxes, lanes), 0)
    count = jnp.zeros((boxes, lanes), jnp.int32)
    for e in range(entries):
        count = count + (local[:, e : e + 1] == lane).astype(jnp.int32)
    from_own = lane < boxes
    mirrored = count.astype(F32).T[:boxes]
    mirrored = jnp.concatenate([mirrored, jnp.zeros((boxes, lanes - boxes), F32)], axis=1).astype(jnp.int32)
    back = jnp.where(from_own & (lane != box), mirrored, 0)
    present = (count + back > 0) & ((lane >= box) | (lane >= boxes))
    flags = present.astype(F32)
    box_row = lax.broadcasted_iota(jnp.int32, (boxes, boxes), 0)
    box_col = lax.broadcasted_iota(jnp.int32, (boxes, boxes), 1)
    rank = nn_dot((box_col < box_row).astype(F32).astype(BF16), flags.astype(BF16)).astype(jnp.int32)
    pairs = jnp.sum(flags, axis=0, keepdims=True)
    from_cross = lane >= jnp.where(edge, 2 * boxes, 3 * boxes - LEFT_OVER)
    own_pairs = jnp.where(from_own[:1], pairs, 0.0)
    cross_pairs = jnp.where(from_cross[:1], pairs, 0.0)
    group_pairs = jnp.where(from_own[:1] | from_cross[:1], 0.0, pairs)
    row = lax.broadcasted_iota(jnp.int32, (lanes, lanes), 0)
    col = lax.broadcasted_iota(jnp.int32, (lanes, lanes), 1)
    ahead = (row < col).astype(F32).astype(BF16)
    lists = jnp.concatenate([own_pairs, group_pairs, cross_pairs, jnp.zeros((5, lanes), F32)], axis=0)
    offset = nn_dot(lists.astype(BF16), ahead).astype(jnp.int32)
    order = jnp.where(from_own, offset[0:1], jnp.where(from_cross, offset[2:3], offset[1:2])) + rank
    half = order >> 1
    place = jnp.where(from_own, half, jnp.where(from_cross, (length - 4) - half, second_start + half))
    place = jnp.where(present, place, -1)
    code = (((lane << box_bits) | box) << (2 * count_bits)) | (back << count_bits) | count
    odd_place = (order & 1) == 1
    place_t = place.T
    codes_t = (jnp.where(odd_place, 0, code).T, jnp.where(odd_place, code, 0).T)
    rows = 3 * boxes
    slot = lax.broadcasted_iota(jnp.int32, (rows, length), 1)
    found = [jnp.zeros((rows, length), jnp.int32) for _ in range(2)]
    for i in range(boxes):
        hit = place_t[:rows, i : i + 1] == slot
        for k in range(2):
            found[k] = found[k] + jnp.where(hit, codes_t[k][:rows, i : i + 1], 0)
    listed = jnp.concatenate([jnp.sum(x, axis=0, keepdims=True) for x in found], axis=0)
    at = lax.broadcasted_iota(jnp.int32, (2, length), 1)
    for ahead_of_end, pairs in ((3, own_pairs), (2, group_pairs), (1, cross_pairs)):
        total = jnp.sum(pairs, axis=1, keepdims=True).astype(jnp.int32)
        listed = jnp.where(at == length - ahead_of_end, (total + 1) >> 1, listed)
    return listed


def start_all(copies, sems):
    started = [pltpu.make_async_copy(src, dst, sems.at[k]) for k, (src, dst) in enumerate(copies)]
    for copy in started:
        copy.start()
    return started


def wait_all(started):
    for copy in started:
        copy.wait()


def outgoing_kernel(
    x_hbm, pos_hbm, rad_hbm, idx_hbm, wgt_hbm, phase_hbm, near_hbm, packet_ref, spectra_ref, imat_ref, cos_ref, sin_ref,
    rad_ref, items_ref, x_ref, pos_ref, idx_ref, wgt_ref, phase_ref, near_ref, sems
):
    wait_all(
        start_all(
            (
                (x_hbm, x_ref),
                (pos_hbm, pos_ref),
                (rad_hbm, rad_ref),
                (idx_hbm, idx_ref),
                (wgt_hbm, wgt_ref),
                (phase_hbm, phase_ref),
                (near_hbm, near_ref),
            ),
            sems,
        )
    )
    block = lax.axis_index(("box", "dir"))
    items_ref[...] = list_items(near_ref[...], block, lax.axis_index("dir"), lax.axis_size("dir"))
    leaf_dirs, parent_dirs = imat_ref.shape
    x_rows, _, width = x_ref.shape
    axes, boxes, _ = pos_ref.shape
    waves = x_rows * 16 // boxes
    chunks = parent_dirs // 128
    own_rows = x_rows + axes * boxes // 16
    packet_ref[:x_rows] = x_ref[...]
    packet_ref[x_rows:own_rows] = pos_ref[...].reshape(axes * boxes // 16, 16, width)
    column = lax.broadcasted_iota(jnp.int32, (leaf_dirs, parent_dirs), 0)
    imat = jnp.zeros((leaf_dirs, parent_dirs), F32)
    for s in range(idx_ref.shape[0]):
        imat = imat + jnp.where(idx_ref[s : s + 1, :] == column, wgt_ref[s : s + 1, :], 0.0)
    imat = imat.astype(BF16)
    imat_ref[...] = imat
    cos_phase = jnp.cos(phase_ref[...])
    sin_phase = jnp.sin(phase_ref[...])
    cos_ref[...] = cos_phase
    sin_ref[...] = sin_phase
    leaf = nn_dot(x_ref[...].reshape(boxes * waves, width), rad_ref[...]).astype(BF16)
    up_re = nn_dot(leaf[:, :leaf_dirs], imat)
    up_im = nn_dot(leaf[:, leaf_dirs:], imat)
    for q in range(boxes // 8):
        re = jnp.zeros((waves, parent_dirs), F32)
        im = jnp.zeros((waves, parent_dirs), F32)
        for c in range(8):
            at = (q * 8 + c) * waves
            ure = up_re[at : at + waves]
            uim = up_im[at : at + waves]
            re = re + (cos_phase[c : c + 1] * ure - sin_phase[c : c + 1] * uim)
            im = im + (sin_phase[c : c + 1] * ure + cos_phase[c : c + 1] * uim)
        both = jnp.concatenate([re, im], axis=0).astype(BF16)
        for k in range(chunks):
            part = both[:, k * 128 : (k + 1) * 128]
            packet_ref[own_rows + q * chunks + k] = part
            spectra_ref[q * chunks + k] = part


def carries_packet(step):
    return step & (step + 1) == 0


def group_kernel(own_ref, *refs):
    *step_refs, _, group_ref = refs
    size = lax.axis_size("dir")
    rows = own_ref.shape[0]
    here = lax.axis_index("dir")
    group_ref[pl.ds(here * rows, rows)] = own_ref[...]
    for step, ref in enumerate(step_refs, 1):
        group_ref[pl.ds((here ^ step) * rows, rows)] = ref[ref.shape[0] - rows :]
    group_ref[size * rows :] = step_refs[-1][: step_refs[-1].shape[0] - rows]


def features(planes):
    rows, _, width = planes.shape
    boxes = rows * 16 // 3
    planes = planes.astype(F32).reshape(3, boxes, width)
    at = lax.broadcasted_iota(jnp.int32, (boxes, 8, width), 1)
    pos = jnp.zeros((boxes, 8, width), F32)
    for axis in range(3):
        pos = jnp.where(at == axis, planes[axis][:, None, :], pos)
    scale = TURN * TURN
    norm = split3(scale * jnp.sum(pos * pos, axis=1, keepdims=True))
    first = jnp.where(at < 3, pos, 1.0)
    first = jnp.where(at == 3, norm[0], jnp.where(at == 4, norm[1], jnp.where(at == 5, norm[2], first)))
    second = jnp.where(at == 3, 1.0, pos + pltpu.roll(pos, 4, 1))
    source = jnp.concatenate([first, second], axis=1).astype(BF16)
    cross = split3((-2.0 * scale) * pos)
    first = jnp.where(at < 3, cross[0], 1.0)
    first = jnp.where(at == 6, norm[0], jnp.where(at == 7, norm[1], first))
    second = jnp.where(at == 3, norm[2], cross[1] + pltpu.roll(cross[2], 4, 1))
    return source, jnp.concatenate([first, second], axis=1).astype(BF16)


def turn_sources(source, src_ref, start):
    boxes, rows, width = source.shape
    eye = lax.broadcasted_iota(jnp.int32, (width, width), 0) == lax.broadcasted_iota(jnp.int32, (width, width), 1)
    twice = jnp.concatenate([source, source], axis=1).reshape(boxes * 2 * rows, width)
    turned = nt_dot(eye.astype(F32).astype(BF16), twice)
    for b in range(boxes):
        at = b * 2 * rows
        lanes = turned[:, at // 128 * 128 : at // 128 * 128 + 128]
        if at % 128:
            lanes = pltpu.roll(lanes, 128 - at % 128, 1)
        src_ref[start + b] = lanes.astype(BF16)


def take_currents(x_rows, win_ref, start):
    for k in range(x_rows.shape[0]):
        both = x_rows[k]
        wide = both.astype(F32)
        win_ref[start + 2 * k] = both
        win_ref[start + 2 * k + 1] = jnp.concatenate([wide[8:], wide[:8]], axis=0).astype(BF16)


def near_sum(
    entries, total, item_at, first_source, src_ref, win_ref, obs_ref, out_ref, scratch, ahead=0, mutual=False
):
    u0_ref, u1_ref, t0_ref, t1_ref = scratch
    boxes, waves, width = out_ref.shape
    count_bits, box_bits = code_bits(boxes, entries)
    t1_ref[...] = jnp.zeros(t1_ref.shape, BF16)
    upper = lax.broadcasted_iota(jnp.int32, (2 * waves, width), 0) < waves
    left = lax.broadcasted_iota(jnp.int32, (width, 128), 1) < 16
    empty = jnp.zeros((16, width), BF16)

    def pair_at(chunk, g, slot):
        code = item_at(slot, chunk * ITEMS + g)
        source = code >> (2 * count_bits + box_bits)
        if first_source:
            source = jnp.maximum(source - first_source, 0)
        box = (code >> (2 * count_bits)) & ((1 << box_bits) - 1)
        counts = [(code >> (way * count_bits)) & ((1 << count_bits) - 1) for way in range(2)]
        return source, box, [count.astype(F32) for count in counts]

    def distances(chunk, g, u_ref):
        source0, box0, _ = pair_at(chunk, g, 0)
        source1, box1, _ = pair_at(chunk, g, 1)
        sources = jnp.where(left, src_ref[source0], src_ref[source1])
        observers = jnp.concatenate(
            [
                jnp.concatenate([obs_ref[box0], empty], axis=1),
                jnp.concatenate([empty, obs_ref[box1]], axis=1),
            ],
            axis=0,
        )
        u_ref[g] = nn_dot(sources[:, :32], observers)

    def tile(g, u_ref, t_ref):
        for at in range(0, width, ROWS):
            v = jnp.maximum(u_ref[g, at : at + ROWS], 1e-12)
            q = v * lax.rsqrt(v)
            t = q - jnp.round(q)
            cosine = t * t + CHAIN[0]
            for constant in CHAIN[1:]:
                cosine = cosine * cosine + constant
            t_ref[g, at : at + ROWS] = (cosine * pltpu.reciprocal(q + OFFSET * TURN, approx=True)).astype(BF16)

    def product(chunk, g, t_ref):
        source0, box0, counts0 = pair_at(chunk, g, 0)
        source1, box1, counts1 = pair_at(chunk, g, 1)
        currents = jnp.where(upper, win_ref[source0].astype(F32), win_ref[source1 ^ 1].astype(F32)).astype(BF16)
        got = nn_dot(currents, t_ref[g])
        out_ref[box0] += counts0[0] * got[:waves, :width]
        out_ref[box1] += counts1[0] * got[waves:, width:]
        if mutual:
            first = jnp.where(upper, win_ref[box0].astype(F32), 0.0).astype(BF16)
            second = jnp.where(upper, 0.0, win_ref[box1 ^ 1].astype(F32)).astype(BF16)
            got = nt_dot(jnp.concatenate([first, second], axis=1), t_ref[g])
            out_ref[source0] += counts0[1] * got[:waves]
            out_ref[source1] += counts1[1] * got[waves:]

    u_refs = (u0_ref, u1_ref)
    t_refs = (t0_ref, t1_ref)

    def stage(chunk, turn):
        for g in range(ITEMS):
            distances(chunk + 1, g, u_refs[1 - turn])
            product(jnp.maximum(chunk - 1, 0), g, t_refs[1 - turn])
            tile(g, u_refs[turn], t_refs[turn])

    def body(k, carry):
        for j in range(STAGES):
            stage(ahead + k * STAGES + j, j & 1)
        return carry

    def finish(turn):
        for g in range(ITEMS):
            product(jnp.maximum(chunks - 1, 0), g, t_refs[turn])

    chunks = jnp.maximum((total + (ITEMS - 1)) // ITEMS, ahead)
    rounds = (chunks - ahead) // STAGES
    for g in range(ITEMS):
        distances(0, g, u0_ref)
    for j in range(ahead):
        stage(j, j & 1)
    lax.fori_loop(0, rounds, body, 0)
    last = ahead + rounds * STAGES
    for j in range(STAGES - 1):
        pl.when(last + j < chunks)(functools.partial(stage, last + j, j & 1))
    pl.when((chunks > 0) & ((chunks & 1) == 0))(functools.partial(finish, 1))
    pl.when((chunks & 1) == 1)(functools.partial(finish, 0))


def prepare_kernel(
    entries, own_ref, items_ref, src_hbm, id_hbm, count_hbm, table_hbm, out_ref, obs_ref, src_ref, win_ref, gain_ref,
    trans_src_ref, trans_id_ref, trans_count_ref, table_ref, list_ref, u0_ref, u1_ref, t0_ref, t1_ref, sems
):
    boxes = obs_ref.shape[0]
    length = list_ref.shape[1]
    parents, window = gain_ref.shape[:2]
    listed = src_hbm.shape[1]
    fetch, *trans_copies = start_all(
        (
            (items_ref, list_ref),
            (src_hbm, trans_src_ref),
            (id_hbm, trans_id_ref),
            (count_hbm, trans_count_ref),
            (table_hbm, table_ref),
        ),
        sems,
    )
    plane_rows = 3 * boxes // 16
    source, observer = features(own_ref[boxes // 2 : boxes // 2 + plane_rows])
    turn_sources(source, src_ref, 0)
    take_currents(own_ref[: boxes // 2], win_ref, 0)
    obs_ref[...] = observer
    out_ref[...] = jnp.zeros(out_ref.shape, F32)
    gain_ref[...] = jnp.zeros(gain_ref.shape, F32)
    fetch.wait()
    near_sum(
        entries,
        list_ref[0, length - 3],
        lambda slot, k: list_ref[slot, k],
        0,
        src_ref,
        win_ref,
        obs_ref,
        out_ref,
        (u0_ref, u1_ref, t0_ref, t1_ref),
        mutual=True,
    )
    wait_all(trans_copies)
    row0 = lax.axis_index("dir") * parents
    first = (lax.axis_index("box") - 1) * (window // 3)
    for q in range(parents):
        for e in range(listed):
            live = (e < trans_count_ref[row0 + q]).astype(F32)
            s = jnp.clip(trans_src_ref[row0 + q, e] - first, 0, window - 1)
            gain_ref[q, s] += table_ref[trans_id_ref[row0 + q, e]] * live


def near_kernel(entries, items_ref, *refs):
    *refs, sem = refs
    (
        *step_refs, obs_ref, first_ref, _, _, out_ref, src_ref, win_ref, list_ref, u0_ref, u1_ref, t0_ref, t1_ref
    ) = refs
    boxes, waves, width = out_ref.shape
    fetch = pltpu.make_async_copy(items_ref, list_ref, sem)
    fetch.start()
    length = list_ref.shape[1]
    here = lax.axis_index("dir")
    other_side = jnp.where((here & 1) == 0, here - 1, here + 1)
    x_rows = boxes // 2
    own_rows = x_rows + 3 * boxes // 16

    def take(packet, part):
        take_currents(packet[:x_rows], win_ref, part * boxes)
        source, _ = features(packet[x_rows:])
        turn_sources(source, src_ref, part * boxes)

    take(step_refs[0][:own_rows], 1)
    if len(step_refs) > 1:
        packet = step_refs[1][:own_rows]
        for k, ref in enumerate(step_refs[2:], 3):
            from_here = (here ^ ((1 << k) - 1)) == other_side
            packet = jnp.where(from_here, ref[:own_rows].astype(F32), packet.astype(F32)).astype(BF16)
        take(packet, 2)
    second_start, _ = list_places(boxes, entries)
    out_ref[...] = first_ref[...]
    fetch.wait()
    near_sum(
        entries,
        list_ref[0, length - 2],
        lambda slot, k: list_ref[slot, second_start + k],
        0,
        src_ref,
        win_ref,
        obs_ref,
        out_ref,
        (u0_ref, u1_ref, t0_ref, t1_ref),
    )


def incoming_kernel(entries, others, *refs):
    incoming(entries, *refs[others:], other_refs=refs[:others])


def incoming(
    entries, items_ref, even_ref, own_ref, odd_ref, gain_ref, cos_ref, sin_ref, imat_ref, rad_ref, obs_ref, near_ref, out_ref,
    sum_ref, win_ref, src_ref, down_re_ref, down_im_ref, list_ref, u0_ref, u1_ref, t0_ref, t1_ref, sem, other_refs=()
):
    parents, window, _, parent_dirs = gain_ref.shape
    boxes, waves, width = near_ref.shape
    chunks = parent_dirs // 128
    group = window // 3
    fetch = pltpu.make_async_copy(items_ref, list_ref, sem)
    fetch.start()
    length = list_ref.shape[1]
    odd_box = lax.axis_index("box") & 1
    sum_ref[...] = near_ref[...]
    x_rows = boxes // 2
    packet_rows = x_rows + 3 * boxes // 16
    here = lax.axis_index("dir")
    from_even = jnp.where(here == 0, 1, 0) == odd_box
    even_packet, odd_packet = (ref[ref.shape[0] - packet_rows :] for ref in (even_ref, odd_ref))
    packet = jnp.where(from_even, even_packet.astype(F32), odd_packet.astype(F32))
    other_side = jnp.where((here & 1) == 0, here - 1, here + 1)
    for k, ref in enumerate(other_refs, 2):
        from_group = (here ^ ((1 << k) - 1)) == other_side
        packet = jnp.where(from_group, ref[:packet_rows].astype(F32), packet)
    packet = packet.astype(BF16)
    take_currents(packet[:x_rows], win_ref, 0)
    source, _ = features(packet[x_rows:])
    turn_sources(source, src_ref, 0)
    fetch.wait()
    cos_phase = cos_ref[...]
    sin_phase = sin_ref[...]
    sums = tuple(jnp.zeros((waves, 128), F32) for _ in range(parents * chunks * 2))
    for part, ref in ((2 - 2 * odd_box, even_ref), (1, own_ref), (2 * odd_box, odd_ref)):

        def add_source(s, sums, part=part, ref=ref):
            sums = list(sums)
            gains = [gain_ref[q, part * group + s] for q in range(parents)]
            for k in range(chunks):
                spectrum = ref[s * chunks + k].astype(F32)
                sre, sim = spectrum[:waves], spectrum[waves:]
                for q in range(parents):
                    gre = gains[q][0:1, k * 128 : (k + 1) * 128]
                    gim = gains[q][1:2, k * 128 : (k + 1) * 128]
                    at = (q * chunks + k) * 2
                    sums[at] = sums[at] + (gre * sre - gim * sim)
                    sums[at + 1] = sums[at + 1] + (gre * sim + gim * sre)
            return tuple(sums)

        sums = lax.fori_loop(0, group, add_source, sums, unroll=8)
    for q in range(parents):
        for k in range(chunks):
            at = (q * chunks + k) * 2
            re = sums[at].astype(BF16).astype(F32)
            im = sums[at + 1].astype(BF16).astype(F32)
            lanes = slice(k * 128, (k + 1) * 128)
            for c in range(8):
                cos, sin = cos_phase[c : c + 1, lanes], sin_phase[c : c + 1, lanes]
                rows = slice((q * 8 + c) * waves, (q * 8 + c + 1) * waves)
                down_re_ref[rows, lanes] = cos * re + sin * im
                down_im_ref[rows, lanes] = cos * im - sin * re
    imat = imat_ref[...]
    in_re = nt_dot(down_re_ref[...].astype(BF16), imat)
    in_im = nt_dot(down_im_ref[...].astype(BF16), imat)
    incoming = jnp.concatenate([in_re, in_im], axis=1).astype(BF16)
    far = nt_dot(incoming, rad_ref[...])
    near_sum(
        entries,
        list_ref[0, length - 1],
        lambda slot, k: list_ref[slot, length - 4 - k],
        2 * boxes,
        src_ref,
        win_ref,
        obs_ref,
        sum_ref,
        (u0_ref, u1_ref, t0_ref, t1_ref),
        AHEAD,
    )
    factor = TURN * LEAD / math.sqrt(entries * width)
    out_ref[...] = sum_ref[...] * factor + far.reshape(near_ref.shape)


def per_device(
    currents, positions, radiation, interp_index, interp_weight, child_phase, near_src, trans_src, trans_id,
    trans_count, trans_table
):
    boxes, waves, width = currents.shape
    entries = near_src.shape[1]
    leaf_dirs = radiation.shape[1] // 2
    parent_dirs = child_phase.shape[1]
    parents = boxes // 8
    spectra_rows = parents * parent_dirs // 128
    size = lax.axis_size("dir")
    vmem = pl.BlockSpec(memory_space=pltpu.VMEM)
    hbm = pl.BlockSpec(memory_space=pltpu.HBM)
    params = pltpu.CompilerParams(vmem_limit_bytes=32 * 1024 * 1024)

    def in_hbm(x):
        return pltpu.with_memory_space_constraint(x, pltpu.HBM)

    def shaped(shape, dtype):
        return jax.ShapeDtypeStruct(shape, dtype)

    x_rows = boxes // 2
    own_rows = x_rows + 3 * boxes // 16
    operands = (currents.reshape(x_rows, 2 * waves, width), positions.transpose(1, 0, 2), radiation, interp_index.T, interp_weight.T, child_phase)
    operands = operands + (near_src,)
    _, length = list_places(boxes, entries)
    packet, spectra, imat, cos_phase, sin_phase, rad, items = pl.pallas_call(
        outgoing_kernel,
        out_shape=(
            shaped((own_rows + spectra_rows, 16, width), BF16),
            shaped((spectra_rows, 2 * waves, 128), BF16),
            shaped((leaf_dirs, parent_dirs), BF16),
            shaped((8, parent_dirs), F32),
            shaped((8, parent_dirs), F32),
            shaped(radiation.shape, BF16),
            shaped((2, length), jnp.int32),
        ),
        in_specs=[hbm] * len(operands),
        out_specs=(vmem,) * 7,
        scratch_shapes=[pltpu.VMEM(x.shape, x.dtype) for x in operands if x is not radiation]
        + [pltpu.SemaphoreType.DMA((len(operands),))],
        compiler_params=params,
        name="outgoing",
    )(*[in_hbm(x) for x in operands])

    steps = []
    for step in range(1, size):
        pairs = [(i, i ^ step) for i in range(size) if i < i ^ step]
        steps.append(swapped(packet if carries_packet(step) else spectra, "dir", pairs))

    window = 3 * trans_src.shape[0]
    near_scratch = [
        pltpu.VMEM((ITEMS, width, 2 * width), F32),
        pltpu.VMEM((ITEMS, width, 2 * width), F32),
        pltpu.VMEM((ITEMS, width, 2 * width), BF16),
        pltpu.VMEM((ITEMS, width, 2 * width), BF16),
    ]
    first_sum, observers, sources, ordered, gains = pl.pallas_call(
        functools.partial(prepare_kernel, entries),
        out_shape=(
            shaped((boxes, waves, width), F32),
            shaped((boxes, 16, width), BF16),
            shaped((3 * boxes, width, 128), BF16),
            shaped((3 * boxes, 16, width), BF16),
            shaped((parents, window, 2, parent_dirs), F32),
        ),
        in_specs=[vmem] * 2 + [hbm] * 4,
        out_specs=(vmem,) * 5,
        scratch_shapes=[
            pltpu.SMEM(trans_src.shape, jnp.int32),
            pltpu.SMEM(trans_id.shape, jnp.int32),
            pltpu.SMEM(trans_count.shape, jnp.int32),
            pltpu.VMEM(trans_table.shape, F32),
            pltpu.SMEM((2, length), jnp.int32),
        ]
        + near_scratch
        + [pltpu.SemaphoreType.DMA((5,))],
        compiler_params=params,
        name="prepare",
    )(packet, items, *[in_hbm(x) for x in (trans_src, trans_id, trans_count, trans_table)])

    group = pl.pallas_call(
        group_kernel,
        out_shape=shaped((size * spectra_rows + own_rows, 2 * waves, 128), BF16),
        in_specs=[vmem] * (2 + len(steps)),
        out_specs=vmem,
        compiler_params=params,
        name="group",
    )(spectra, *steps, first_sum)
    groups = lax.axis_size("box")
    group_odd = swapped(group, "box", [(i, i + 1) for i in range(1, groups - 1, 2)])
    group_even = swapped(group, "box", [(i, i + 1) for i in range(0, groups - 1, 2)])

    packets = [x for step, x in enumerate(steps, 1) if carries_packet(step)]
    near, _, _ = pl.pallas_call(
        functools.partial(near_kernel, entries),
        out_shape=(
            shaped((boxes, waves, width), F32),
            shaped(sources.shape, BF16),
            shaped(ordered.shape, BF16),
        ),
        in_specs=[vmem] * (5 + len(packets)),
        out_specs=(vmem,) * 3,
        input_output_aliases={3 + len(packets): 1, 4 + len(packets): 2},
        scratch_shapes=[pltpu.SMEM((2, length), jnp.int32)] + near_scratch + [pltpu.SemaphoreType.DMA],
        compiler_params=params,
        name="near",
    )(items, *packets, observers, first_sum, sources, ordered)

    return pl.pallas_call(
        functools.partial(incoming_kernel, entries, len(packets) - 1),
        out_shape=shaped((boxes, waves, width), F32),
        in_specs=[vmem] * (10 + len(packets)),
        out_specs=vmem,
        scratch_shapes=[
            pltpu.VMEM((boxes, waves, width), F32),
            pltpu.VMEM((boxes, 16, width), BF16),
            pltpu.VMEM((boxes, width, 128), BF16),
            pltpu.VMEM((boxes * waves, parent_dirs), F32),
            pltpu.VMEM((boxes * waves, parent_dirs), F32),
            pltpu.SMEM((2, length), jnp.int32),
        ]
        + near_scratch
        + [pltpu.SemaphoreType.DMA],
        compiler_params=params,
        name="incoming",
    )(*packets[1:], items, group_even, group, group_odd, gains, cos_phase, sin_phase, imat, rad, observers, near)


def solution(mesh):
    placed = (
        P(("box", "dir"), None, None),
        P(("box", "dir"), None, None),
        P(),
        P(),
        P(),
        P(),
        P(("box", "dir"), None),
        P("box", None),
        P("box", None),
        P("box"),
        P(),
    )
    return jax.shard_map(
        per_device,
        mesh=mesh,
        in_specs=placed,
        out_specs=P(("box", "dir"), None, None),
        check_vma=False,
    )
```

```python
import functools
import math

import jax
import jax.numpy as jnp
from jax import lax
from jax.experimental import pallas as pl
from jax.experimental.pallas import tpu as pltpu
from jax.sharding import PartitionSpec as P

F32 = jnp.float32
BF16 = jnp.bfloat16

WAVENUMBER = 4.0
OFFSET = 0.5
TURN = WAVENUMBER / (2.0 * math.pi)
CHAIN = (-2.2803148655023415, -1.415255674611144, -7.327656729815578, -24.467745134801202)
LEAD = 0.04087004462557604
ITEMS = 4
ROWS = 32
STAGES = 2
FIRST_ITEMS = 6
AHEAD = 2
LEFT_OVER = 2


def round_up(value, step):
    return -(-value // step) * step


def swapped(x, axis, pairs):
    return lax.ppermute(x, axis, [way for i, j in pairs for way in ((i, j), (j, i))])


def split3(x):
    high = x.astype(BF16).astype(F32)
    rest = x - high
    mid = rest.astype(BF16).astype(F32)
    return high, mid, rest - mid


def nt_dot(a, b):
    return lax.dot_general(a, b, (((1,), (1,)), ((), ())), preferred_element_type=F32)


def nn_dot(a, b):
    return jnp.dot(a, b, preferred_element_type=F32)


def code_bits(boxes, entries):
    return entries.bit_length(), (boxes - 1).bit_length(), (3 * boxes - 1).bit_length()


def list_places(boxes, entries):
    gap = 2 * ITEMS
    most = FIRST_ITEMS * boxes // 2
    return most, most + gap, round_up(most + gap + boxes * entries // 2 + 2 * gap + 6, 128)


def list_items(near_src, block, here, size):
    boxes, entries = near_src.shape
    most, second_start, length = list_places(boxes, entries)
    count_bits, box_bits, source_bits = code_bits(boxes, entries)
    pair_bits = count_bits + box_bits + source_bits
    lanes = round_up(3 * boxes, 128)
    odd = (here & 1) == 1
    edge = (here == 0) | (here == size - 1)
    local = near_src - block * boxes
    below = local + jnp.where(odd, 2 * boxes, 3 * boxes)
    above = local + jnp.where(odd, boxes, 0)
    local = jnp.where(local < 0, below, jnp.where(local >= boxes, above, local))
    lane = lax.broadcasted_iota(jnp.int32, (boxes, lanes), 1)
    box = lax.broadcasted_iota(jnp.int32, (boxes, lanes), 0)
    count = jnp.zeros((boxes, lanes), jnp.int32)
    for e in range(entries):
        count = count + (local[:, e : e + 1] == lane).astype(jnp.int32)
    present = count > 0
    flags = present.astype(F32)
    box_row = lax.broadcasted_iota(jnp.int32, (boxes, boxes), 0)
    box_col = lax.broadcasted_iota(jnp.int32, (boxes, boxes), 1)
    rank = nn_dot((box_col < box_row).astype(F32).astype(BF16), flags.astype(BF16)).astype(jnp.int32)
    pairs = jnp.sum(flags, axis=0, keepdims=True)
    from_cross = lane >= jnp.where(edge, 2 * boxes, 3 * boxes - LEFT_OVER)
    cross_pairs = jnp.where(from_cross[:1], pairs, 0.0)
    group_pairs = jnp.where(from_cross[:1], 0.0, pairs)
    row = lax.broadcasted_iota(jnp.int32, (lanes, lanes), 0)
    col = lax.broadcasted_iota(jnp.int32, (lanes, lanes), 1)
    ahead = (row < col).astype(F32).astype(BF16)
    lists = jnp.concatenate([group_pairs, cross_pairs, jnp.zeros((6, lanes), F32)], axis=0)
    offset = nn_dot(lists.astype(BF16), ahead).astype(jnp.int32)
    own_pairs = jnp.where(lane[:1] < boxes, group_pairs, 0.0)

    def total(pairs):
        return jnp.sum(pairs, axis=1, keepdims=True).astype(jnp.int32)

    first_total = jnp.minimum(total(own_pairs), 2 * most)
    second_total = total(group_pairs) - first_total
    cross_total = total(cross_pairs)
    order = offset[0:1] + rank
    in_second = order >= first_total
    order = jnp.where(in_second, order - first_total, order)
    order = jnp.where(from_cross, offset[1:2] + rank, order)
    half = order >> 1
    place = jnp.where(from_cross, (length - 4) - half, jnp.where(in_second, second_start + half, half))
    place = jnp.where(present, place, -1)
    code = (lane << (count_bits + box_bits)) | (box << count_bits) | count
    code = jnp.where((order & 1) == 1, code << pair_bits, code)
    place_t = place.T
    code_t = code.T
    rows = 3 * boxes
    slot = lax.broadcasted_iota(jnp.int32, (rows, length), 1)
    found = jnp.zeros((rows, length), jnp.int32)
    for i in range(boxes):
        hit = place_t[:rows, i : i + 1] == slot
        found = found + jnp.where(hit, code_t[:rows, i : i + 1], 0)
    listed = jnp.sum(found, axis=0, keepdims=True)
    at = lax.broadcasted_iota(jnp.int32, (1, length), 1)
    for back, pairs in ((3, first_total), (2, second_total), (1, cross_total)):
        listed = jnp.where(at == length - back, (pairs + 1) >> 1, listed)
    return listed


def start_all(copies, sems):
    started = [pltpu.make_async_copy(src, dst, sems.at[k]) for k, (src, dst) in enumerate(copies)]
    for copy in started:
        copy.start()
    return started


def wait_all(started):
    for copy in started:
        copy.wait()


def outgoing_kernel(
    x_hbm, pos_hbm, rad_hbm, idx_hbm, wgt_hbm, phase_hbm, near_hbm, packet_ref, spectra_ref, imat_ref, cos_ref, sin_ref,
    rad_ref, items_ref, x_ref, pos_ref, idx_ref, wgt_ref, phase_ref, near_ref, sems
):
    wait_all(
        start_all(
            (
                (x_hbm, x_ref),
                (pos_hbm, pos_ref),
                (rad_hbm, rad_ref),
                (idx_hbm, idx_ref),
                (wgt_hbm, wgt_ref),
                (phase_hbm, phase_ref),
                (near_hbm, near_ref),
            ),
            sems,
        )
    )
    block = lax.axis_index(("box", "dir"))
    items_ref[...] = list_items(near_ref[...], block, lax.axis_index("dir"), lax.axis_size("dir"))
    leaf_dirs, parent_dirs = imat_ref.shape
    x_rows, _, width = x_ref.shape
    axes, boxes, _ = pos_ref.shape
    waves = x_rows * 16 // boxes
    chunks = parent_dirs // 128
    own_rows = x_rows + axes * boxes // 16
    packet_ref[:x_rows] = x_ref[...]
    packet_ref[x_rows:own_rows] = pos_ref[...].reshape(axes * boxes // 16, 16, width)
    column = lax.broadcasted_iota(jnp.int32, (leaf_dirs, parent_dirs), 0)
    imat = jnp.zeros((leaf_dirs, parent_dirs), F32)
    for s in range(idx_ref.shape[0]):
        imat = imat + jnp.where(idx_ref[s : s + 1, :] == column, wgt_ref[s : s + 1, :], 0.0)
    imat = imat.astype(BF16)
    imat_ref[...] = imat
    cos_phase = jnp.cos(phase_ref[...])
    sin_phase = jnp.sin(phase_ref[...])
    cos_ref[...] = cos_phase
    sin_ref[...] = sin_phase
    leaf = nn_dot(x_ref[...].reshape(boxes * waves, width), rad_ref[...]).astype(BF16)
    up_re = nn_dot(leaf[:, :leaf_dirs], imat)
    up_im = nn_dot(leaf[:, leaf_dirs:], imat)
    for q in range(boxes // 8):
        re = jnp.zeros((waves, parent_dirs), F32)
        im = jnp.zeros((waves, parent_dirs), F32)
        for c in range(8):
            at = (q * 8 + c) * waves
            ure = up_re[at : at + waves]
            uim = up_im[at : at + waves]
            re = re + (cos_phase[c : c + 1] * ure - sin_phase[c : c + 1] * uim)
            im = im + (sin_phase[c : c + 1] * ure + cos_phase[c : c + 1] * uim)
        both = jnp.concatenate([re, im], axis=0).astype(BF16)
        for k in range(chunks):
            part = both[:, k * 128 : (k + 1) * 128]
            packet_ref[own_rows + q * chunks + k] = part
            spectra_ref[q * chunks + k] = part


def carries_packet(step):
    return step & (step + 1) == 0


def group_kernel(own_ref, *refs):
    *step_refs, _, group_ref = refs
    size = lax.axis_size("dir")
    rows = own_ref.shape[0]
    here = lax.axis_index("dir")
    group_ref[pl.ds(here * rows, rows)] = own_ref[...]
    for step, ref in enumerate(step_refs, 1):
        group_ref[pl.ds((here ^ step) * rows, rows)] = ref[ref.shape[0] - rows :]
    group_ref[size * rows :] = step_refs[-1][: step_refs[-1].shape[0] - rows]


def features(planes):
    rows, _, width = planes.shape
    boxes = rows * 16 // 3
    planes = planes.astype(F32).reshape(3, boxes, width)
    at = lax.broadcasted_iota(jnp.int32, (boxes, 8, width), 1)
    pos = jnp.zeros((boxes, 8, width), F32)
    for axis in range(3):
        pos = jnp.where(at == axis, planes[axis][:, None, :], pos)
    scale = TURN * TURN
    norm = split3(scale * jnp.sum(pos * pos, axis=1, keepdims=True))
    first = jnp.where(at < 3, pos, 1.0)
    first = jnp.where(at == 3, norm[0], jnp.where(at == 4, norm[1], jnp.where(at == 5, norm[2], first)))
    second = jnp.where(at == 3, 1.0, pos + pltpu.roll(pos, 4, 1))
    source = jnp.concatenate([first, second], axis=1).astype(BF16)
    cross = split3((-2.0 * scale) * pos)
    first = jnp.where(at < 3, cross[0], 1.0)
    first = jnp.where(at == 6, norm[0], jnp.where(at == 7, norm[1], first))
    second = jnp.where(at == 3, norm[2], cross[1] + pltpu.roll(cross[2], 4, 1))
    return source, jnp.concatenate([first, second], axis=1).astype(BF16)


def turn_sources(source, src_ref, start):
    boxes, rows, width = source.shape
    eye = lax.broadcasted_iota(jnp.int32, (width, width), 0) == lax.broadcasted_iota(jnp.int32, (width, width), 1)
    twice = jnp.concatenate([source, source], axis=1).reshape(boxes * 2 * rows, width)
    turned = nt_dot(eye.astype(F32).astype(BF16), twice)
    for b in range(boxes):
        at = b * 2 * rows
        lanes = turned[:, at // 128 * 128 : at // 128 * 128 + 128]
        if at % 128:
            lanes = pltpu.roll(lanes, 128 - at % 128, 1)
        src_ref[start + b] = lanes.astype(BF16)


def take_currents(x_rows, win_ref, start):
    for k in range(x_rows.shape[0]):
        both = x_rows[k]
        wide = both.astype(F32)
        win_ref[start + 2 * k] = both
        win_ref[start + 2 * k + 1] = jnp.concatenate([wide[8:], wide[:8]], axis=0).astype(BF16)


def near_sum(entries, total, item_at, first_source, src_ref, win_ref, obs_ref, out_ref, scratch, ahead=0):
    u0_ref, u1_ref, t0_ref, t1_ref = scratch
    boxes, waves, width = out_ref.shape
    count_bits, box_bits, source_bits = code_bits(boxes, entries)
    pair_bits = count_bits + box_bits + source_bits
    t1_ref[...] = jnp.zeros(t1_ref.shape, BF16)
    upper = lax.broadcasted_iota(jnp.int32, (2 * waves, width), 0) < waves
    left = lax.broadcasted_iota(jnp.int32, (width, 128), 1) < 16
    empty = jnp.zeros((16, width), BF16)

    def pair_at(chunk, g, slot):
        code = item_at(chunk * ITEMS + g) >> (slot * pair_bits)
        source = (code >> (count_bits + box_bits)) & ((1 << source_bits) - 1)
        if first_source:
            source = jnp.maximum(source - first_source, 0)
        return source, (code >> count_bits) & ((1 << box_bits) - 1), code & ((1 << count_bits) - 1)

    def distances(chunk, g, u_ref):
        source0, box0, _ = pair_at(chunk, g, 0)
        source1, box1, _ = pair_at(chunk, g, 1)
        sources = jnp.where(left, src_ref[source0], src_ref[source1])
        observers = jnp.concatenate(
            [
                jnp.concatenate([obs_ref[box0], empty], axis=1),
                jnp.concatenate([empty, obs_ref[box1]], axis=1),
            ],
            axis=0,
        )
        u_ref[g] = nn_dot(sources[:, :32], observers)

    def tile(g, u_ref, t_ref):
        for at in range(0, width, ROWS):
            v = jnp.maximum(u_ref[g, at : at + ROWS], 1e-12)
            q = v * lax.rsqrt(v)
            t = q - jnp.round(q)
            cosine = t * t + CHAIN[0]
            for constant in CHAIN[1:]:
                cosine = cosine * cosine + constant
            t_ref[g, at : at + ROWS] = (cosine * pltpu.reciprocal(q + OFFSET * TURN, approx=True)).astype(BF16)

    def product(chunk, g, t_ref):
        source0, box0, count0 = pair_at(chunk, g, 0)
        source1, box1, count1 = pair_at(chunk, g, 1)
        currents = jnp.where(upper, win_ref[source0].astype(F32), win_ref[source1 ^ 1].astype(F32)).astype(BF16)
        got = nn_dot(currents, t_ref[g])
        out_ref[box0] += count0.astype(F32) * got[:waves, :width]
        out_ref[box1] += count1.astype(F32) * got[waves:, width:]

    u_refs = (u0_ref, u1_ref)
    t_refs = (t0_ref, t1_ref)

    def stage(chunk, turn):
        for g in range(ITEMS):
            distances(chunk + 1, g, u_refs[1 - turn])
            product(jnp.maximum(chunk - 1, 0), g, t_refs[1 - turn])
            tile(g, u_refs[turn], t_refs[turn])

    def body(k, carry):
        for j in range(STAGES):
            stage(ahead + k * STAGES + j, j & 1)
        return carry

    def finish(turn):
        for g in range(ITEMS):
            product(jnp.maximum(chunks - 1, 0), g, t_refs[turn])

    chunks = jnp.maximum((total + (ITEMS - 1)) // ITEMS, ahead)
    rounds = (chunks - ahead) // STAGES
    for g in range(ITEMS):
        distances(0, g, u0_ref)
    for j in range(ahead):
        stage(j, j & 1)
    lax.fori_loop(0, rounds, body, 0)
    last = ahead + rounds * STAGES
    for j in range(STAGES - 1):
        pl.when(last + j < chunks)(functools.partial(stage, last + j, j & 1))
    pl.when((chunks > 0) & ((chunks & 1) == 0))(functools.partial(finish, 1))
    pl.when((chunks & 1) == 1)(functools.partial(finish, 0))


def prepare_kernel(
    entries, own_ref, items_ref, src_hbm, id_hbm, count_hbm, table_hbm, out_ref, obs_ref, src_ref, win_ref, gain_ref,
    trans_src_ref, trans_id_ref, trans_count_ref, table_ref, list_ref, u0_ref, u1_ref, t0_ref, t1_ref, sems
):
    boxes = obs_ref.shape[0]
    length = list_ref.shape[1]
    parents, window = gain_ref.shape[:2]
    listed = src_hbm.shape[1]
    fetch, *trans_copies = start_all(
        (
            (items_ref, list_ref),
            (src_hbm, trans_src_ref),
            (id_hbm, trans_id_ref),
            (count_hbm, trans_count_ref),
            (table_hbm, table_ref),
        ),
        sems,
    )
    plane_rows = 3 * boxes // 16
    source, observer = features(own_ref[boxes // 2 : boxes // 2 + plane_rows])
    turn_sources(source, src_ref, 0)
    take_currents(own_ref[: boxes // 2], win_ref, 0)
    obs_ref[...] = observer
    out_ref[...] = jnp.zeros(out_ref.shape, F32)
    gain_ref[...] = jnp.zeros(gain_ref.shape, F32)
    fetch.wait()
    near_sum(
        entries,
        list_ref[0, length - 3],
        lambda k: list_ref[0, k],
        0,
        src_ref,
        win_ref,
        obs_ref,
        out_ref,
        (u0_ref, u1_ref, t0_ref, t1_ref),
    )
    wait_all(trans_copies)
    row0 = lax.axis_index("dir") * parents
    first = (lax.axis_index("box") - 1) * (window // 3)
    for q in range(parents):
        for e in range(listed):
            live = (e < trans_count_ref[row0 + q]).astype(F32)
            s = jnp.clip(trans_src_ref[row0 + q, e] - first, 0, window - 1)
            gain_ref[q, s] += table_ref[trans_id_ref[row0 + q, e]] * live


def near_kernel(entries, items_ref, *refs):
    *refs, sem = refs
    (
        *step_refs, obs_ref, first_ref, _, _, out_ref, src_ref, win_ref, list_ref, u0_ref, u1_ref, t0_ref, t1_ref
    ) = refs
    boxes, waves, width = out_ref.shape
    fetch = pltpu.make_async_copy(items_ref, list_ref, sem)
    fetch.start()
    length = list_ref.shape[1]
    here = lax.axis_index("dir")
    other_side = jnp.where((here & 1) == 0, here - 1, here + 1)
    x_rows = boxes // 2
    own_rows = x_rows + 3 * boxes // 16

    def take(packet, part):
        take_currents(packet[:x_rows], win_ref, part * boxes)
        source, _ = features(packet[x_rows:])
        turn_sources(source, src_ref, part * boxes)

    take(step_refs[0][:own_rows], 1)
    if len(step_refs) > 1:
        packet = step_refs[1][:own_rows]
        for k, ref in enumerate(step_refs[2:], 3):
            from_here = (here ^ ((1 << k) - 1)) == other_side
            packet = jnp.where(from_here, ref[:own_rows].astype(F32), packet.astype(F32)).astype(BF16)
        take(packet, 2)
    second_start = list_places(boxes, entries)[1]
    out_ref[...] = first_ref[...]
    fetch.wait()
    near_sum(
        entries,
        list_ref[0, length - 2],
        lambda k: list_ref[0, second_start + k],
        0,
        src_ref,
        win_ref,
        obs_ref,
        out_ref,
        (u0_ref, u1_ref, t0_ref, t1_ref),
    )


def incoming_kernel(entries, others, *refs):
    incoming(entries, *refs[others:], other_refs=refs[:others])


def incoming(
    entries, items_ref, even_ref, own_ref, odd_ref, gain_ref, cos_ref, sin_ref, imat_ref, rad_ref, obs_ref, near_ref, out_ref,
    sum_ref, win_ref, src_ref, down_re_ref, down_im_ref, list_ref, u0_ref, u1_ref, t0_ref, t1_ref, sem, other_refs=()
):
    parents, window, _, parent_dirs = gain_ref.shape
    boxes, waves, width = near_ref.shape
    chunks = parent_dirs // 128
    group = window // 3
    fetch = pltpu.make_async_copy(items_ref, list_ref, sem)
    fetch.start()
    length = list_ref.shape[1]
    odd_box = lax.axis_index("box") & 1
    sum_ref[...] = near_ref[...]
    x_rows = boxes // 2
    packet_rows = x_rows + 3 * boxes // 16
    here = lax.axis_index("dir")
    from_even = jnp.where(here == 0, 1, 0) == odd_box
    even_packet, odd_packet = (ref[ref.shape[0] - packet_rows :] for ref in (even_ref, odd_ref))
    packet = jnp.where(from_even, even_packet.astype(F32), odd_packet.astype(F32))
    other_side = jnp.where((here & 1) == 0, here - 1, here + 1)
    for k, ref in enumerate(other_refs, 2):
        from_group = (here ^ ((1 << k) - 1)) == other_side
        packet = jnp.where(from_group, ref[:packet_rows].astype(F32), packet)
    packet = packet.astype(BF16)
    take_currents(packet[:x_rows], win_ref, 0)
    source, _ = features(packet[x_rows:])
    turn_sources(source, src_ref, 0)
    fetch.wait()
    cos_phase = cos_ref[...]
    sin_phase = sin_ref[...]
    sums = tuple(jnp.zeros((waves, 128), F32) for _ in range(parents * chunks * 2))
    for part, ref in ((2 - 2 * odd_box, even_ref), (1, own_ref), (2 * odd_box, odd_ref)):

        def add_source(s, sums, part=part, ref=ref):
            sums = list(sums)
            gains = [gain_ref[q, part * group + s] for q in range(parents)]
            for k in range(chunks):
                spectrum = ref[s * chunks + k].astype(F32)
                sre, sim = spectrum[:waves], spectrum[waves:]
                for q in range(parents):
                    gre = gains[q][0:1, k * 128 : (k + 1) * 128]
                    gim = gains[q][1:2, k * 128 : (k + 1) * 128]
                    at = (q * chunks + k) * 2
                    sums[at] = sums[at] + (gre * sre - gim * sim)
                    sums[at + 1] = sums[at + 1] + (gre * sim + gim * sre)
            return tuple(sums)

        sums = lax.fori_loop(0, group, add_source, sums, unroll=8)
    for q in range(parents):
        for k in range(chunks):
            at = (q * chunks + k) * 2
            re = sums[at].astype(BF16).astype(F32)
            im = sums[at + 1].astype(BF16).astype(F32)
            lanes = slice(k * 128, (k + 1) * 128)
            for c in range(8):
                cos, sin = cos_phase[c : c + 1, lanes], sin_phase[c : c + 1, lanes]
                rows = slice((q * 8 + c) * waves, (q * 8 + c + 1) * waves)
                down_re_ref[rows, lanes] = cos * re + sin * im
                down_im_ref[rows, lanes] = cos * im - sin * re
    imat = imat_ref[...]
    in_re = nt_dot(down_re_ref[...].astype(BF16), imat)
    in_im = nt_dot(down_im_ref[...].astype(BF16), imat)
    incoming = jnp.concatenate([in_re, in_im], axis=1).astype(BF16)
    far = nt_dot(incoming, rad_ref[...])
    near_sum(
        entries,
        list_ref[0, length - 1],
        lambda k: list_ref[0, length - 4 - k],
        2 * boxes,
        src_ref,
        win_ref,
        obs_ref,
        sum_ref,
        (u0_ref, u1_ref, t0_ref, t1_ref),
        AHEAD,
    )
    factor = TURN * LEAD / math.sqrt(entries * width)
    out_ref[...] = sum_ref[...] * factor + far.reshape(near_ref.shape)


def per_device(
    currents, positions, radiation, interp_index, interp_weight, child_phase, near_src, trans_src, trans_id,
    trans_count, trans_table
):
    boxes, waves, width = currents.shape
    entries = near_src.shape[1]
    leaf_dirs = radiation.shape[1] // 2
    parent_dirs = child_phase.shape[1]
    parents = boxes // 8
    spectra_rows = parents * parent_dirs // 128
    size = lax.axis_size("dir")
    vmem = pl.BlockSpec(memory_space=pltpu.VMEM)
    hbm = pl.BlockSpec(memory_space=pltpu.HBM)
    params = pltpu.CompilerParams(vmem_limit_bytes=32 * 1024 * 1024)

    def in_hbm(x):
        return pltpu.with_memory_space_constraint(x, pltpu.HBM)

    def shaped(shape, dtype):
        return jax.ShapeDtypeStruct(shape, dtype)

    x_rows = boxes // 2
    own_rows = x_rows + 3 * boxes // 16
    operands = (currents.reshape(x_rows, 2 * waves, width), positions.transpose(1, 0, 2), radiation, interp_index.T, interp_weight.T, child_phase)
    operands = operands + (near_src,)
    length = list_places(boxes, entries)[2]
    packet, spectra, imat, cos_phase, sin_phase, rad, items = pl.pallas_call(
        outgoing_kernel,
        out_shape=(
            shaped((own_rows + spectra_rows, 16, width), BF16),
            shaped((spectra_rows, 2 * waves, 128), BF16),
            shaped((leaf_dirs, parent_dirs), BF16),
            shaped((8, parent_dirs), F32),
            shaped((8, parent_dirs), F32),
            shaped(radiation.shape, BF16),
            shaped((1, length), jnp.int32),
        ),
        in_specs=[hbm] * len(operands),
        out_specs=(vmem,) * 7,
        scratch_shapes=[pltpu.VMEM(x.shape, x.dtype) for x in operands if x is not radiation]
        + [pltpu.SemaphoreType.DMA((len(operands),))],
        compiler_params=params,
        name="outgoing",
    )(*[in_hbm(x) for x in operands])

    steps = []
    for step in range(1, size):
        pairs = [(i, i ^ step) for i in range(size) if i < i ^ step]
        steps.append(swapped(packet if carries_packet(step) else spectra, "dir", pairs))

    window = 3 * trans_src.shape[0]
    near_scratch = [
        pltpu.VMEM((ITEMS, width, 2 * width), F32),
        pltpu.VMEM((ITEMS, width, 2 * width), F32),
        pltpu.VMEM((ITEMS, width, 2 * width), BF16),
        pltpu.VMEM((ITEMS, width, 2 * width), BF16),
    ]
    first_sum, observers, sources, ordered, gains = pl.pallas_call(
        functools.partial(prepare_kernel, entries),
        out_shape=(
            shaped((boxes, waves, width), F32),
            shaped((boxes, 16, width), BF16),
            shaped((3 * boxes, width, 128), BF16),
            shaped((3 * boxes, 16, width), BF16),
            shaped((parents, window, 2, parent_dirs), F32),
        ),
        in_specs=[vmem] * 2 + [hbm] * 4,
        out_specs=(vmem,) * 5,
        scratch_shapes=[
            pltpu.SMEM(trans_src.shape, jnp.int32),
            pltpu.SMEM(trans_id.shape, jnp.int32),
            pltpu.SMEM(trans_count.shape, jnp.int32),
            pltpu.VMEM(trans_table.shape, F32),
            pltpu.SMEM((1, length), jnp.int32),
        ]
        + near_scratch
        + [pltpu.SemaphoreType.DMA((5,))],
        compiler_params=params,
        name="prepare",
    )(packet, items, *[in_hbm(x) for x in (trans_src, trans_id, trans_count, trans_table)])

    group = pl.pallas_call(
        group_kernel,
        out_shape=shaped((size * spectra_rows + own_rows, 2 * waves, 128), BF16),
        in_specs=[vmem] * (2 + len(steps)),
        out_specs=vmem,
        compiler_params=params,
        name="group",
    )(spectra, *steps, first_sum)
    groups = lax.axis_size("box")
    group_odd = swapped(group, "box", [(i, i + 1) for i in range(1, groups - 1, 2)])
    group_even = swapped(group, "box", [(i, i + 1) for i in range(0, groups - 1, 2)])

    packets = [x for step, x in enumerate(steps, 1) if carries_packet(step)]
    near, _, _ = pl.pallas_call(
        functools.partial(near_kernel, entries),
        out_shape=(
            shaped((boxes, waves, width), F32),
            shaped(sources.shape, BF16),
            shaped(ordered.shape, BF16),
        ),
        in_specs=[vmem] * (5 + len(packets)),
        out_specs=(vmem,) * 3,
        input_output_aliases={3 + len(packets): 1, 4 + len(packets): 2},
        scratch_shapes=[pltpu.SMEM((1, length), jnp.int32)] + near_scratch + [pltpu.SemaphoreType.DMA],
        compiler_params=params,
        name="near",
    )(items, *packets, observers, first_sum, sources, ordered)

    return pl.pallas_call(
        functools.partial(incoming_kernel, entries, len(packets) - 1),
        out_shape=shaped((boxes, waves, width), F32),
        in_specs=[vmem] * (10 + len(packets)),
        out_specs=vmem,
        scratch_shapes=[
            pltpu.VMEM((boxes, waves, width), F32),
            pltpu.VMEM((boxes, 16, width), BF16),
            pltpu.VMEM((boxes, width, 128), BF16),
            pltpu.VMEM((boxes * waves, parent_dirs), F32),
            pltpu.VMEM((boxes * waves, parent_dirs), F32),
            pltpu.SMEM((1, length), jnp.int32),
        ]
        + near_scratch
        + [pltpu.SemaphoreType.DMA],
        compiler_params=params,
        name="incoming",
    )(*packets[1:], items, group_even, group, group_odd, gains, cos_phase, sin_phase, imat, rad, observers, near)


def solution(mesh):
    placed = (
        P(("box", "dir"), None, None),
        P(("box", "dir"), None, None),
        P(),
        P(),
        P(),
        P(),
        P(("box", "dir"), None),
        P("box", None),
        P("box", None),
        P("box"),
        P(),
    )
    return jax.shard_map(
        per_device,
        mesh=mesh,
        in_specs=placed,
        out_specs=P(("box", "dir"), None, None),
        check_vma=False,
    )
```

```python
import functools
import math

import jax
import jax.numpy as jnp
from jax import lax
from jax.experimental import pallas as pl
from jax.experimental.pallas import tpu as pltpu
from jax.sharding import PartitionSpec as P

F32 = jnp.float32
BF16 = jnp.bfloat16

WAVENUMBER = 4.0
OFFSET = 0.5
TURN = WAVENUMBER / (2.0 * math.pi)
CHAIN = (-2.2803148655023415, -1.415255674611144, -7.327656729815578, -24.467745134801202)
LEAD = 0.04087004462557604
COSINE = (
    0.9999999999990674, -0.49999999998466105, 0.04166666662512991, -0.0013888888455587084, 2.480156463978284e-05,
    -2.7556652559151664e-07, 2.08652097543821e-09, -1.135363495216746e-11, 4.13155312368983e-14,
)
SINE = (
    0.9999999999999502, -0.16666666666584865, 0.008333333331120085, -0.00019841269610529892, 2.755730716252212e-06,
    -2.5051753759896685e-08, 1.6052905945426492e-10, -7.584986682610132e-13, 2.4682378516637708e-15,
)
ITEMS = 4
ROWS = 32
STAGES = 2
FIRST_ITEMS = 6
AHEAD = 2
LEFT_OVER = 2


def round_up(value, step):
    return -(-value // step) * step


def swapped(x, axis, pairs):
    return lax.ppermute(x, axis, [way for i, j in pairs for way in ((i, j), (j, i))])


def polynomial(coefficients, z):
    value = jnp.full_like(z, coefficients[-1])
    for coefficient in coefficients[-2::-1]:
        value = value * z + coefficient
    return value


def split3(x):
    high = x.astype(BF16).astype(F32)
    rest = x - high
    mid = rest.astype(BF16).astype(F32)
    return high, mid, rest - mid


def nt_dot(a, b):
    return lax.dot_general(a, b, (((1,), (1,)), ((), ())), preferred_element_type=F32)


def nn_dot(a, b):
    return jnp.dot(a, b, preferred_element_type=F32)


def code_bits(boxes, entries):
    return entries.bit_length(), (boxes - 1).bit_length(), (3 * boxes - 1).bit_length()


def list_places(boxes, entries):
    gap = 2 * ITEMS
    most = FIRST_ITEMS * boxes // 2
    return most, most + gap, round_up(most + gap + boxes * entries // 2 + 2 * gap + 6, 128)


def list_items(near_src, block, here, size):
    boxes, entries = near_src.shape
    most, second_start, length = list_places(boxes, entries)
    count_bits, box_bits, source_bits = code_bits(boxes, entries)
    pair_bits = count_bits + box_bits + source_bits
    lanes = round_up(3 * boxes, 128)
    odd = (here & 1) == 1
    edge = (here == 0) | (here == size - 1)
    local = near_src - block * boxes
    below = local + jnp.where(odd, 2 * boxes, 3 * boxes)
    above = local + jnp.where(odd, boxes, 0)
    local = jnp.where(local < 0, below, jnp.where(local >= boxes, above, local))
    lane = lax.broadcasted_iota(jnp.int32, (boxes, lanes), 1)
    box = lax.broadcasted_iota(jnp.int32, (boxes, lanes), 0)
    count = jnp.zeros((boxes, lanes), jnp.int32)
    for e in range(entries):
        count = count + (local[:, e : e + 1] == lane).astype(jnp.int32)
    present = count > 0
    flags = present.astype(F32)
    box_row = lax.broadcasted_iota(jnp.int32, (boxes, boxes), 0)
    box_col = lax.broadcasted_iota(jnp.int32, (boxes, boxes), 1)
    rank = nn_dot((box_col < box_row).astype(F32).astype(BF16), flags.astype(BF16)).astype(jnp.int32)
    pairs = jnp.sum(flags, axis=0, keepdims=True)
    from_cross = lane >= jnp.where(edge, 2 * boxes, 3 * boxes - LEFT_OVER)
    cross_pairs = jnp.where(from_cross[:1], pairs, 0.0)
    group_pairs = jnp.where(from_cross[:1], 0.0, pairs)
    row = lax.broadcasted_iota(jnp.int32, (lanes, lanes), 0)
    col = lax.broadcasted_iota(jnp.int32, (lanes, lanes), 1)
    ahead = (row < col).astype(F32).astype(BF16)
    lists = jnp.concatenate([group_pairs, cross_pairs, jnp.zeros((6, lanes), F32)], axis=0)
    offset = nn_dot(lists.astype(BF16), ahead).astype(jnp.int32)
    own_pairs = jnp.where(lane[:1] < boxes, group_pairs, 0.0)

    def total(pairs):
        return jnp.sum(pairs, axis=1, keepdims=True).astype(jnp.int32)

    first_total = jnp.minimum(total(own_pairs), 2 * most)
    second_total = total(group_pairs) - first_total
    cross_total = total(cross_pairs)
    order = offset[0:1] + rank
    in_second = order >= first_total
    order = jnp.where(in_second, order - first_total, order)
    order = jnp.where(from_cross, offset[1:2] + rank, order)
    half = order >> 1
    place = jnp.where(from_cross, (length - 4) - half, jnp.where(in_second, second_start + half, half))
    place = jnp.where(present, place, -1)
    code = (lane << (count_bits + box_bits)) | (box << count_bits) | count
    code = jnp.where((order & 1) == 1, code << pair_bits, code)
    place_t = place.T
    code_t = code.T
    rows = 3 * boxes
    slot = lax.broadcasted_iota(jnp.int32, (rows, length), 1)
    found = jnp.zeros((rows, length), jnp.int32)
    for i in range(boxes):
        hit = place_t[:rows, i : i + 1] == slot
        found = found + jnp.where(hit, code_t[:rows, i : i + 1], 0)
    listed = jnp.sum(found, axis=0, keepdims=True)
    at = lax.broadcasted_iota(jnp.int32, (1, length), 1)
    for back, pairs in ((3, first_total), (2, second_total), (1, cross_total)):
        listed = jnp.where(at == length - back, (pairs + 1) >> 1, listed)
    return listed


def start_all(copies, sems):
    started = [pltpu.make_async_copy(src, dst, sems.at[k]) for k, (src, dst) in enumerate(copies)]
    for copy in started:
        copy.start()
    return started


def wait_all(started):
    for copy in started:
        copy.wait()


def outgoing_kernel(
    x_hbm, pos_hbm, rad_hbm, idx_hbm, wgt_hbm, phase_hbm, near_hbm, packet_ref, spectra_ref, imat_ref, cos_ref, sin_ref,
    rad_ref, items_ref, x_ref, pos_ref, idx_ref, wgt_ref, phase_ref, near_ref, sems
):
    wait_all(
        start_all(
            (
                (x_hbm, x_ref),
                (pos_hbm, pos_ref),
                (rad_hbm, rad_ref),
                (idx_hbm, idx_ref),
                (wgt_hbm, wgt_ref),
                (phase_hbm, phase_ref),
                (near_hbm, near_ref),
            ),
            sems,
        )
    )
    block = lax.axis_index(("box", "dir"))
    items_ref[...] = list_items(near_ref[...], block, lax.axis_index("dir"), lax.axis_size("dir"))
    leaf_dirs, parent_dirs = imat_ref.shape
    x_rows, _, width = x_ref.shape
    axes, boxes, _ = pos_ref.shape
    waves = x_rows * 16 // boxes
    chunks = parent_dirs // 128
    own_rows = x_rows + axes * boxes // 16
    packet_ref[:x_rows] = x_ref[...]
    packet_ref[x_rows:own_rows] = pos_ref[...].reshape(axes * boxes // 16, 16, width)
    column = lax.broadcasted_iota(jnp.int32, (leaf_dirs, parent_dirs), 0)
    imat = jnp.zeros((leaf_dirs, parent_dirs), F32)
    for s in range(idx_ref.shape[0]):
        imat = imat + jnp.where(idx_ref[s : s + 1, :] == column, wgt_ref[s : s + 1, :], 0.0)
    imat = imat.astype(BF16)
    imat_ref[...] = imat
    phase = phase_ref[...]
    cos_phase = polynomial(COSINE, phase * phase)
    sin_phase = phase * polynomial(SINE, phase * phase)
    cos_ref[...] = cos_phase
    sin_ref[...] = sin_phase
    leaf = nn_dot(x_ref[...].reshape(boxes * waves, width), rad_ref[...]).astype(BF16)
    up_re = nn_dot(leaf[:, :leaf_dirs], imat)
    up_im = nn_dot(leaf[:, leaf_dirs:], imat)
    for q in range(boxes // 8):
        re = jnp.zeros((waves, parent_dirs), F32)
        im = jnp.zeros((waves, parent_dirs), F32)
        for c in range(8):
            at = (q * 8 + c) * waves
            ure = up_re[at : at + waves]
            uim = up_im[at : at + waves]
            re = re + (cos_phase[c : c + 1] * ure - sin_phase[c : c + 1] * uim)
            im = im + (sin_phase[c : c + 1] * ure + cos_phase[c : c + 1] * uim)
        both = jnp.concatenate([re, im], axis=0).astype(BF16)
        for k in range(chunks):
            part = both[:, k * 128 : (k + 1) * 128]
            packet_ref[own_rows + q * chunks + k] = part
            spectra_ref[q * chunks + k] = part


def carries_packet(step):
    return step & (step + 1) == 0


def group_kernel(own_ref, *refs):
    *step_refs, _, group_ref = refs
    size = lax.axis_size("dir")
    rows = own_ref.shape[0]
    here = lax.axis_index("dir")
    group_ref[pl.ds(here * rows, rows)] = own_ref[...]
    for step, ref in enumerate(step_refs, 1):
        group_ref[pl.ds((here ^ step) * rows, rows)] = ref[ref.shape[0] - rows :]
    group_ref[size * rows :] = step_refs[-1][: step_refs[-1].shape[0] - rows]


def features(planes):
    rows, _, width = planes.shape
    boxes = rows * 16 // 3
    planes = planes.astype(F32).reshape(3, boxes, width)
    at = lax.broadcasted_iota(jnp.int32, (boxes, 8, width), 1)
    pos = jnp.zeros((boxes, 8, width), F32)
    for axis in range(3):
        pos = jnp.where(at == axis, planes[axis][:, None, :], pos)
    scale = TURN * TURN
    norm = split3(scale * jnp.sum(pos * pos, axis=1, keepdims=True))
    first = jnp.where(at < 3, pos, 1.0)
    first = jnp.where(at == 3, norm[0], jnp.where(at == 4, norm[1], jnp.where(at == 5, norm[2], first)))
    second = jnp.where(at == 3, 1.0, pos + pltpu.roll(pos, 4, 1))
    source = jnp.concatenate([first, second], axis=1).astype(BF16)
    cross = split3((-2.0 * scale) * pos)
    first = jnp.where(at < 3, cross[0], 1.0)
    first = jnp.where(at == 6, norm[0], jnp.where(at == 7, norm[1], first))
    second = jnp.where(at == 3, norm[2], cross[1] + pltpu.roll(cross[2], 4, 1))
    return source, jnp.concatenate([first, second], axis=1).astype(BF16)


def turn_sources(source, src_ref, start):
    boxes, rows, width = source.shape
    eye = lax.broadcasted_iota(jnp.int32, (width, width), 0) == lax.broadcasted_iota(jnp.int32, (width, width), 1)
    twice = jnp.concatenate([source, source], axis=1).reshape(boxes * 2 * rows, width)
    turned = nt_dot(eye.astype(F32).astype(BF16), twice)
    for b in range(boxes):
        at = b * 2 * rows
        lanes = turned[:, at // 128 * 128 : at // 128 * 128 + 128]
        if at % 128:
            lanes = pltpu.roll(lanes, 128 - at % 128, 1)
        src_ref[start + b] = lanes.astype(BF16)


def take_currents(x_rows, win_ref, start):
    for k in range(x_rows.shape[0]):
        both = x_rows[k]
        wide = both.astype(F32)
        win_ref[start + 2 * k] = both
        win_ref[start + 2 * k + 1] = jnp.concatenate([wide[8:], wide[:8]], axis=0).astype(BF16)


def near_sum(entries, total, item_at, first_source, src_ref, win_ref, obs_ref, out_ref, scratch, ahead=0):
    u0_ref, u1_ref, t0_ref, t1_ref = scratch
    boxes, waves, width = out_ref.shape
    count_bits, box_bits, source_bits = code_bits(boxes, entries)
    pair_bits = count_bits + box_bits + source_bits
    t1_ref[...] = jnp.zeros(t1_ref.shape, F32)
    upper = lax.broadcasted_iota(jnp.int32, (2 * waves, width), 0) < waves
    left = lax.broadcasted_iota(jnp.int32, (width, 128), 1) < 16
    empty = jnp.zeros((16, width), BF16)

    def pair_at(chunk, g, slot):
        code = item_at(chunk * ITEMS + g) >> (slot * pair_bits)
        source = (code >> (count_bits + box_bits)) & ((1 << source_bits) - 1)
        if first_source:
            source = jnp.maximum(source - first_source, 0)
        return source, (code >> count_bits) & ((1 << box_bits) - 1), code & ((1 << count_bits) - 1)

    def distances(chunk, g, u_ref):
        source0, box0, _ = pair_at(chunk, g, 0)
        source1, box1, _ = pair_at(chunk, g, 1)
        sources = jnp.where(left, src_ref[source0], src_ref[source1])
        observers = jnp.concatenate(
            [
                jnp.concatenate([obs_ref[box0], empty], axis=1),
                jnp.concatenate([empty, obs_ref[box1]], axis=1),
            ],
            axis=0,
        )
        u_ref[g] = nn_dot(sources[:, :32], observers)

    def tile(g, u_ref, t_ref):
        for at in range(0, width, ROWS):
            v = jnp.maximum(u_ref[g, at : at + ROWS], 1e-12)
            q = v * lax.rsqrt(v)
            t = q - jnp.round(q)
            cosine = t * t + CHAIN[0]
            for constant in CHAIN[1:]:
                cosine = cosine * cosine + constant
            t_ref[g, at : at + ROWS] = cosine * pltpu.reciprocal(q + OFFSET * TURN, approx=True)

    def product(chunk, g, t_ref):
        source0, box0, count0 = pair_at(chunk, g, 0)
        source1, box1, count1 = pair_at(chunk, g, 1)
        currents = jnp.where(upper, win_ref[source0].astype(F32), win_ref[source1 ^ 1].astype(F32))
        got = nn_dot(currents, t_ref[g])
        out_ref[box0] += count0.astype(F32) * got[:waves, :width]
        out_ref[box1] += count1.astype(F32) * got[waves:, width:]

    u_refs = (u0_ref, u1_ref)
    t_refs = (t0_ref, t1_ref)

    def stage(chunk, turn):
        for g in range(ITEMS):
            distances(chunk + 1, g, u_refs[1 - turn])
            product(jnp.maximum(chunk - 1, 0), g, t_refs[1 - turn])
            tile(g, u_refs[turn], t_refs[turn])

    def body(k, carry):
        for j in range(STAGES):
            stage(ahead + k * STAGES + j, j & 1)
        return carry

    def finish(turn):
        for g in range(ITEMS):
            product(jnp.maximum(chunks - 1, 0), g, t_refs[turn])

    chunks = jnp.maximum((total + (ITEMS - 1)) // ITEMS, ahead)
    rounds = (chunks - ahead) // STAGES
    for g in range(ITEMS):
        distances(0, g, u0_ref)
    for j in range(ahead):
        stage(j, j & 1)
    lax.fori_loop(0, rounds, body, 0)
    last = ahead + rounds * STAGES
    for j in range(STAGES - 1):
        pl.when(last + j < chunks)(functools.partial(stage, last + j, j & 1))
    pl.when((chunks > 0) & ((chunks & 1) == 0))(functools.partial(finish, 1))
    pl.when((chunks & 1) == 1)(functools.partial(finish, 0))


def prepare_kernel(
    entries, own_ref, items_ref, src_hbm, id_hbm, count_hbm, table_hbm, out_ref, obs_ref, src_ref, win_ref, gain_ref,
    trans_src_ref, trans_id_ref, trans_count_ref, table_ref, list_ref, u0_ref, u1_ref, t0_ref, t1_ref, sems
):
    boxes = obs_ref.shape[0]
    length = list_ref.shape[1]
    parents, window = gain_ref.shape[:2]
    listed = src_hbm.shape[1]
    fetch, *trans_copies = start_all(
        (
            (items_ref, list_ref),
            (src_hbm, trans_src_ref),
            (id_hbm, trans_id_ref),
            (count_hbm, trans_count_ref),
            (table_hbm, table_ref),
        ),
        sems,
    )
    plane_rows = 3 * boxes // 16
    source, observer = features(own_ref[boxes // 2 : boxes // 2 + plane_rows])
    turn_sources(source, src_ref, 0)
    take_currents(own_ref[: boxes // 2], win_ref, 0)
    obs_ref[...] = observer
    out_ref[...] = jnp.zeros(out_ref.shape, F32)
    gain_ref[...] = jnp.zeros(gain_ref.shape, F32)
    fetch.wait()
    near_sum(
        entries,
        list_ref[0, length - 3],
        lambda k: list_ref[0, k],
        0,
        src_ref,
        win_ref,
        obs_ref,
        out_ref,
        (u0_ref, u1_ref, t0_ref, t1_ref),
    )
    wait_all(trans_copies)
    row0 = lax.axis_index("dir") * parents
    first = (lax.axis_index("box") - 1) * (window // 3)
    for q in range(parents):
        for e in range(listed):
            live = (e < trans_count_ref[row0 + q]).astype(F32)
            s = jnp.clip(trans_src_ref[row0 + q, e] - first, 0, window - 1)
            gain_ref[q, s] += table_ref[trans_id_ref[row0 + q, e]] * live


def near_kernel(entries, items_ref, *refs):
    *refs, sem = refs
    (
        *step_refs, obs_ref, first_ref, _, _, out_ref, src_ref, win_ref, list_ref, u0_ref, u1_ref, t0_ref, t1_ref
    ) = refs
    boxes, waves, width = out_ref.shape
    fetch = pltpu.make_async_copy(items_ref, list_ref, sem)
    fetch.start()
    length = list_ref.shape[1]
    here = lax.axis_index("dir")
    other_side = jnp.where((here & 1) == 0, here - 1, here + 1)
    x_rows = boxes // 2
    own_rows = x_rows + 3 * boxes // 16

    def take(packet, part):
        take_currents(packet[:x_rows], win_ref, part * boxes)
        source, _ = features(packet[x_rows:])
        turn_sources(source, src_ref, part * boxes)

    take(step_refs[0][:own_rows], 1)
    if len(step_refs) > 1:
        packet = step_refs[1][:own_rows]
        for k, ref in enumerate(step_refs[2:], 3):
            from_here = (here ^ ((1 << k) - 1)) == other_side
            packet = jnp.where(from_here, ref[:own_rows].astype(F32), packet.astype(F32)).astype(BF16)
        take(packet, 2)
    second_start = list_places(boxes, entries)[1]
    out_ref[...] = first_ref[...]
    fetch.wait()
    near_sum(
        entries,
        list_ref[0, length - 2],
        lambda k: list_ref[0, second_start + k],
        0,
        src_ref,
        win_ref,
        obs_ref,
        out_ref,
        (u0_ref, u1_ref, t0_ref, t1_ref),
    )


def incoming_kernel(entries, others, *refs):
    incoming(entries, *refs[others:], other_refs=refs[:others])


def incoming(
    entries, items_ref, even_ref, own_ref, odd_ref, gain_ref, cos_ref, sin_ref, imat_ref, rad_ref, obs_ref, near_ref, out_ref,
    sum_ref, win_ref, src_ref, down_re_ref, down_im_ref, list_ref, u0_ref, u1_ref, t0_ref, t1_ref, sem, other_refs=()
):
    parents, window, _, parent_dirs = gain_ref.shape
    boxes, waves, width = near_ref.shape
    chunks = parent_dirs // 128
    group = window // 3
    fetch = pltpu.make_async_copy(items_ref, list_ref, sem)
    fetch.start()
    length = list_ref.shape[1]
    odd_box = lax.axis_index("box") & 1
    sum_ref[...] = near_ref[...]
    x_rows = boxes // 2
    packet_rows = x_rows + 3 * boxes // 16
    here = lax.axis_index("dir")
    from_even = jnp.where(here == 0, 1, 0) == odd_box
    even_packet, odd_packet = (ref[ref.shape[0] - packet_rows :] for ref in (even_ref, odd_ref))
    packet = jnp.where(from_even, even_packet.astype(F32), odd_packet.astype(F32))
    other_side = jnp.where((here & 1) == 0, here - 1, here + 1)
    for k, ref in enumerate(other_refs, 2):
        from_group = (here ^ ((1 << k) - 1)) == other_side
        packet = jnp.where(from_group, ref[:packet_rows].astype(F32), packet)
    packet = packet.astype(BF16)
    take_currents(packet[:x_rows], win_ref, 0)
    source, _ = features(packet[x_rows:])
    turn_sources(source, src_ref, 0)
    fetch.wait()
    cos_phase = cos_ref[...]
    sin_phase = sin_ref[...]
    sums = tuple(jnp.zeros((waves, 128), F32) for _ in range(parents * chunks * 2))
    for part, ref in ((2 - 2 * odd_box, even_ref), (1, own_ref), (2 * odd_box, odd_ref)):

        def add_source(s, sums, part=part, ref=ref):
            sums = list(sums)
            gains = [gain_ref[q, part * group + s] for q in range(parents)]
            for k in range(chunks):
                spectrum = ref[s * chunks + k].astype(F32)
                sre, sim = spectrum[:waves], spectrum[waves:]
                for q in range(parents):
                    gre = gains[q][0:1, k * 128 : (k + 1) * 128]
                    gim = gains[q][1:2, k * 128 : (k + 1) * 128]
                    at = (q * chunks + k) * 2
                    sums[at] = sums[at] + (gre * sre - gim * sim)
                    sums[at + 1] = sums[at + 1] + (gre * sim + gim * sre)
            return tuple(sums)

        sums = lax.fori_loop(0, group, add_source, sums, unroll=8)
    for q in range(parents):
        for k in range(chunks):
            at = (q * chunks + k) * 2
            re = sums[at].astype(BF16).astype(F32)
            im = sums[at + 1].astype(BF16).astype(F32)
            lanes = slice(k * 128, (k + 1) * 128)
            for c in range(8):
                cos, sin = cos_phase[c : c + 1, lanes], sin_phase[c : c + 1, lanes]
                rows = slice((q * 8 + c) * waves, (q * 8 + c + 1) * waves)
                down_re_ref[rows, lanes] = cos * re + sin * im
                down_im_ref[rows, lanes] = cos * im - sin * re
    imat = imat_ref[...]
    in_re = nt_dot(down_re_ref[...].astype(BF16), imat)
    in_im = nt_dot(down_im_ref[...].astype(BF16), imat)
    incoming = jnp.concatenate([in_re, in_im], axis=1).astype(BF16)
    far = nt_dot(incoming, rad_ref[...])
    near_sum(
        entries,
        list_ref[0, length - 1],
        lambda k: list_ref[0, length - 4 - k],
        2 * boxes,
        src_ref,
        win_ref,
        obs_ref,
        sum_ref,
        (u0_ref, u1_ref, t0_ref, t1_ref),
        AHEAD,
    )
    factor = TURN * LEAD / math.sqrt(entries * width)
    out_ref[...] = sum_ref[...] * factor + far.reshape(near_ref.shape)


def per_device(
    currents, positions, radiation, interp_index, interp_weight, child_phase, near_src, trans_src, trans_id,
    trans_count, trans_table
):
    boxes, waves, width = currents.shape
    entries = near_src.shape[1]
    leaf_dirs = radiation.shape[1] // 2
    parent_dirs = child_phase.shape[1]
    parents = boxes // 8
    spectra_rows = parents * parent_dirs // 128
    size = lax.axis_size("dir")
    vmem = pl.BlockSpec(memory_space=pltpu.VMEM)
    hbm = pl.BlockSpec(memory_space=pltpu.HBM)
    params = pltpu.CompilerParams(vmem_limit_bytes=32 * 1024 * 1024)

    def in_hbm(x):
        return pltpu.with_memory_space_constraint(x, pltpu.HBM)

    def shaped(shape, dtype):
        return jax.ShapeDtypeStruct(shape, dtype)

    x_rows = boxes // 2
    own_rows = x_rows + 3 * boxes // 16
    operands = (currents.reshape(x_rows, 2 * waves, width), positions.transpose(1, 0, 2), radiation, interp_index.T, interp_weight.T, child_phase)
    operands = operands + (near_src,)
    length = list_places(boxes, entries)[2]
    packet, spectra, imat, cos_phase, sin_phase, rad, items = pl.pallas_call(
        outgoing_kernel,
        out_shape=(
            shaped((own_rows + spectra_rows, 16, width), BF16),
            shaped((spectra_rows, 2 * waves, 128), BF16),
            shaped((leaf_dirs, parent_dirs), BF16),
            shaped((8, parent_dirs), F32),
            shaped((8, parent_dirs), F32),
            shaped(radiation.shape, BF16),
            shaped((1, length), jnp.int32),
        ),
        in_specs=[hbm] * len(operands),
        out_specs=(vmem,) * 7,
        scratch_shapes=[pltpu.VMEM(x.shape, x.dtype) for x in operands if x is not radiation]
        + [pltpu.SemaphoreType.DMA((len(operands),))],
        compiler_params=params,
        name="outgoing",
    )(*[in_hbm(x) for x in operands])

    steps = []
    for step in range(1, size):
        pairs = [(i, i ^ step) for i in range(size) if i < i ^ step]
        steps.append(swapped(packet if carries_packet(step) else spectra, "dir", pairs))

    window = 3 * trans_src.shape[0]
    near_scratch = [
        pltpu.VMEM((ITEMS, width, 2 * width), F32),
        pltpu.VMEM((ITEMS, width, 2 * width), F32),
        pltpu.VMEM((ITEMS, width, 2 * width), F32),
        pltpu.VMEM((ITEMS, width, 2 * width), F32),
    ]
    first_sum, observers, sources, ordered, gains = pl.pallas_call(
        functools.partial(prepare_kernel, entries),
        out_shape=(
            shaped((boxes, waves, width), F32),
            shaped((boxes, 16, width), BF16),
            shaped((3 * boxes, width, 128), BF16),
            shaped((3 * boxes, 16, width), BF16),
            shaped((parents, window, 2, parent_dirs), F32),
        ),
        in_specs=[vmem] * 2 + [hbm] * 4,
        out_specs=(vmem,) * 5,
        scratch_shapes=[
            pltpu.SMEM(trans_src.shape, jnp.int32),
            pltpu.SMEM(trans_id.shape, jnp.int32),
            pltpu.SMEM(trans_count.shape, jnp.int32),
            pltpu.VMEM(trans_table.shape, F32),
            pltpu.SMEM((1, length), jnp.int32),
        ]
        + near_scratch
        + [pltpu.SemaphoreType.DMA((5,))],
        compiler_params=params,
        name="prepare",
    )(packet, items, *[in_hbm(x) for x in (trans_src, trans_id, trans_count, trans_table)])

    group = pl.pallas_call(
        group_kernel,
        out_shape=shaped((size * spectra_rows + own_rows, 2 * waves, 128), BF16),
        in_specs=[vmem] * (2 + len(steps)),
        out_specs=vmem,
        compiler_params=params,
        name="group",
    )(spectra, *steps, first_sum)
    groups = lax.axis_size("box")
    group_odd = swapped(group, "box", [(i, i + 1) for i in range(1, groups - 1, 2)])
    group_even = swapped(group, "box", [(i, i + 1) for i in range(0, groups - 1, 2)])

    packets = [x for step, x in enumerate(steps, 1) if carries_packet(step)]
    near, _, _ = pl.pallas_call(
        functools.partial(near_kernel, entries),
        out_shape=(
            shaped((boxes, waves, width), F32),
            shaped(sources.shape, BF16),
            shaped(ordered.shape, BF16),
        ),
        in_specs=[vmem] * (5 + len(packets)),
        out_specs=(vmem,) * 3,
        input_output_aliases={3 + len(packets): 1, 4 + len(packets): 2},
        scratch_shapes=[pltpu.SMEM((1, length), jnp.int32)] + near_scratch + [pltpu.SemaphoreType.DMA],
        compiler_params=params,
        name="near",
    )(items, *packets, observers, first_sum, sources, ordered)

    return pl.pallas_call(
        functools.partial(incoming_kernel, entries, len(packets) - 1),
        out_shape=shaped((boxes, waves, width), F32),
        in_specs=[vmem] * (10 + len(packets)),
        out_specs=vmem,
        scratch_shapes=[
            pltpu.VMEM((boxes, waves, width), F32),
            pltpu.VMEM((boxes, 16, width), BF16),
            pltpu.VMEM((boxes, width, 128), BF16),
            pltpu.VMEM((boxes * waves, parent_dirs), F32),
            pltpu.VMEM((boxes * waves, parent_dirs), F32),
            pltpu.SMEM((1, length), jnp.int32),
        ]
        + near_scratch
        + [pltpu.SemaphoreType.DMA],
        compiler_params=params,
        name="incoming",
    )(*packets[1:], items, group_even, group, group_odd, gains, cos_phase, sin_phase, imat, rad, observers, near)


def solution(mesh):
    placed = (
        P(("box", "dir"), None, None),
        P(("box", "dir"), None, None),
        P(),
        P(),
        P(),
        P(),
        P(("box", "dir"), None),
        P("box", None),
        P("box", None),
        P("box"),
        P(),
    )
    return jax.shard_map(
        per_device,
        mesh=mesh,
        in_specs=placed,
        out_specs=P(("box", "dir"), None, None),
        check_vma=False,
    )
```

```python
import functools
import math

import jax
import jax.numpy as jnp
from jax import lax
from jax.experimental import pallas as pl
from jax.experimental.pallas import tpu as pltpu
from jax.sharding import PartitionSpec as P

F32 = jnp.float32
BF16 = jnp.bfloat16

WAVENUMBER = 4.0
OFFSET = 0.5
TURN = WAVENUMBER / (2.0 * math.pi)
CHAIN = (-2.2803148655023415, -1.415255674611144, -7.327656729815578, -24.467745134801202)
LEAD = 0.04087004462557604
COSINE = (
    0.9999999999990674, -0.49999999998466105, 0.04166666662512991, -0.0013888888455587084, 2.480156463978284e-05,
    -2.7556652559151664e-07, 2.08652097543821e-09, -1.135363495216746e-11, 4.13155312368983e-14,
)
SINE = (
    0.9999999999999502, -0.16666666666584865, 0.008333333331120085, -0.00019841269610529892, 2.755730716252212e-06,
    -2.5051753759896685e-08, 1.6052905945426492e-10, -7.584986682610132e-13, 2.4682378516637708e-15,
)
ITEMS = 4
ROWS = 32
STAGES = 2
FIRST_ITEMS = 6
AHEAD = 2
LEFT_OVER = 2


def round_up(value, step):
    return -(-value // step) * step


def swapped(x, axis, pairs):
    return lax.ppermute(x, axis, [way for i, j in pairs for way in ((i, j), (j, i))])


def polynomial(coefficients, z):
    value = jnp.full_like(z, coefficients[-1])
    for coefficient in coefficients[-2::-1]:
        value = value * z + coefficient
    return value


def split3(x):
    high = x.astype(BF16).astype(F32)
    rest = x - high
    mid = rest.astype(BF16).astype(F32)
    return high, mid, rest - mid


def nt_dot(a, b):
    return lax.dot_general(a, b, (((1,), (1,)), ((), ())), preferred_element_type=F32)


def nn_dot(a, b):
    return jnp.dot(a, b, preferred_element_type=F32)


def code_bits(boxes, entries):
    return entries.bit_length(), (boxes - 1).bit_length(), (3 * boxes - 1).bit_length()


def list_places(boxes, entries):
    gap = 2 * ITEMS
    most = FIRST_ITEMS * boxes // 2
    return most, most + gap, round_up(most + gap + boxes * entries // 2 + 2 * gap + 6, 128)


def list_items(near_src, block, here, size):
    boxes, entries = near_src.shape
    most, second_start, length = list_places(boxes, entries)
    count_bits, box_bits, source_bits = code_bits(boxes, entries)
    pair_bits = count_bits + box_bits + source_bits
    lanes = round_up(3 * boxes, 128)
    odd = (here & 1) == 1
    edge = (here == 0) | (here == size - 1)
    local = near_src - block * boxes
    below = local + jnp.where(odd, 2 * boxes, 3 * boxes)
    above = local + jnp.where(odd, boxes, 0)
    local = jnp.where(local < 0, below, jnp.where(local >= boxes, above, local))
    lane = lax.broadcasted_iota(jnp.int32, (boxes, lanes), 1)
    box = lax.broadcasted_iota(jnp.int32, (boxes, lanes), 0)
    count = jnp.zeros((boxes, lanes), jnp.int32)
    for e in range(entries):
        count = count + (local[:, e : e + 1] == lane).astype(jnp.int32)
    present = count > 0
    flags = present.astype(F32)
    box_row = lax.broadcasted_iota(jnp.int32, (boxes, boxes), 0)
    box_col = lax.broadcasted_iota(jnp.int32, (boxes, boxes), 1)
    rank = nn_dot((box_col < box_row).astype(F32).astype(BF16), flags.astype(BF16)).astype(jnp.int32)
    pairs = jnp.sum(flags, axis=0, keepdims=True)
    from_cross = lane >= jnp.where(edge, 2 * boxes, 3 * boxes - LEFT_OVER)
    cross_pairs = jnp.where(from_cross[:1], pairs, 0.0)
    group_pairs = jnp.where(from_cross[:1], 0.0, pairs)
    row = lax.broadcasted_iota(jnp.int32, (lanes, lanes), 0)
    col = lax.broadcasted_iota(jnp.int32, (lanes, lanes), 1)
    ahead = (row < col).astype(F32).astype(BF16)
    lists = jnp.concatenate([group_pairs, cross_pairs, jnp.zeros((6, lanes), F32)], axis=0)
    offset = nn_dot(lists.astype(BF16), ahead).astype(jnp.int32)
    own_pairs = jnp.where(lane[:1] < boxes, group_pairs, 0.0)

    def total(pairs):
        return jnp.sum(pairs, axis=1, keepdims=True).astype(jnp.int32)

    first_total = jnp.minimum(total(own_pairs), 2 * most)
    second_total = total(group_pairs) - first_total
    cross_total = total(cross_pairs)
    order = offset[0:1] + rank
    in_second = order >= first_total
    order = jnp.where(in_second, order - first_total, order)
    order = jnp.where(from_cross, offset[1:2] + rank, order)
    half = order >> 1
    place = jnp.where(from_cross, (length - 4) - half, jnp.where(in_second, second_start + half, half))
    place = jnp.where(present, place, -1)
    code = (lane << (count_bits + box_bits)) | (box << count_bits) | count
    code = jnp.where((order & 1) == 1, code << pair_bits, code)
    place_t = place.T
    code_t = code.T
    rows = 3 * boxes
    slot = lax.broadcasted_iota(jnp.int32, (rows, length), 1)
    found = jnp.zeros((rows, length), jnp.int32)
    for i in range(boxes):
        hit = place_t[:rows, i : i + 1] == slot
        found = found + jnp.where(hit, code_t[:rows, i : i + 1], 0)
    listed = jnp.sum(found, axis=0, keepdims=True)
    at = lax.broadcasted_iota(jnp.int32, (1, length), 1)
    for back, pairs in ((3, first_total), (2, second_total), (1, cross_total)):
        listed = jnp.where(at == length - back, (pairs + 1) >> 1, listed)
    return listed


def start_all(copies, sems):
    started = [pltpu.make_async_copy(src, dst, sems.at[k]) for k, (src, dst) in enumerate(copies)]
    for copy in started:
        copy.start()
    return started


def wait_all(started):
    for copy in started:
        copy.wait()


def outgoing_kernel(
    x_hbm, pos_hbm, rad_hbm, idx_hbm, wgt_hbm, phase_hbm, near_hbm, packet_ref, spectra_ref, imat_ref, cos_ref, sin_ref,
    rad_ref, items_ref, x_ref, pos_ref, idx_ref, wgt_ref, phase_ref, near_ref, sems
):
    wait_all(
        start_all(
            (
                (x_hbm, x_ref),
                (pos_hbm, pos_ref),
                (rad_hbm, rad_ref),
                (idx_hbm, idx_ref),
                (wgt_hbm, wgt_ref),
                (phase_hbm, phase_ref),
                (near_hbm, near_ref),
            ),
            sems,
        )
    )
    block = lax.axis_index(("box", "dir"))
    items_ref[...] = list_items(near_ref[...], block, lax.axis_index("dir"), lax.axis_size("dir"))
    leaf_dirs, parent_dirs = imat_ref.shape
    x_rows, _, width = x_ref.shape
    axes, boxes, _ = pos_ref.shape
    waves = x_rows * 16 // boxes
    chunks = parent_dirs // 128
    own_rows = x_rows + axes * boxes // 16
    packet_ref[:x_rows] = x_ref[...]
    packet_ref[x_rows:own_rows] = pos_ref[...].reshape(axes * boxes // 16, 16, width)
    column = lax.broadcasted_iota(jnp.int32, (leaf_dirs, parent_dirs), 0)
    imat = jnp.zeros((leaf_dirs, parent_dirs), F32)
    for s in range(idx_ref.shape[0]):
        imat = imat + jnp.where(idx_ref[s : s + 1, :] == column, wgt_ref[s : s + 1, :], 0.0)
    imat = imat.astype(BF16)
    imat_ref[...] = imat
    phase = phase_ref[...]
    cos_phase = polynomial(COSINE, phase * phase)
    sin_phase = phase * polynomial(SINE, phase * phase)
    cos_ref[...] = cos_phase
    sin_ref[...] = sin_phase
    leaf = nn_dot(x_ref[...].reshape(boxes * waves, width), rad_ref[...]).astype(BF16)
    up_re = nn_dot(leaf[:, :leaf_dirs], imat)
    up_im = nn_dot(leaf[:, leaf_dirs:], imat)
    for q in range(boxes // 8):
        re = jnp.zeros((waves, parent_dirs), F32)
        im = jnp.zeros((waves, parent_dirs), F32)
        for c in range(8):
            at = (q * 8 + c) * waves
            ure = up_re[at : at + waves]
            uim = up_im[at : at + waves]
            re = re + (cos_phase[c : c + 1] * ure - sin_phase[c : c + 1] * uim)
            im = im + (sin_phase[c : c + 1] * ure + cos_phase[c : c + 1] * uim)
        both = jnp.concatenate([re, im], axis=0).astype(BF16)
        for k in range(chunks):
            part = both[:, k * 128 : (k + 1) * 128]
            packet_ref[own_rows + q * chunks + k] = part
            spectra_ref[q * chunks + k] = part


def carries_packet(step):
    return step & (step + 1) == 0


def group_kernel(own_ref, *refs):
    *step_refs, _, group_ref = refs
    size = lax.axis_size("dir")
    rows = own_ref.shape[0]
    here = lax.axis_index("dir")
    group_ref[pl.ds(here * rows, rows)] = own_ref[...]
    for step, ref in enumerate(step_refs, 1):
        group_ref[pl.ds((here ^ step) * rows, rows)] = ref[ref.shape[0] - rows :]
    group_ref[size * rows :] = step_refs[-1][: step_refs[-1].shape[0] - rows]


def features(planes):
    rows, _, width = planes.shape
    boxes = rows * 16 // 3
    planes = planes.astype(F32).reshape(3, boxes, width)
    at = lax.broadcasted_iota(jnp.int32, (boxes, 8, width), 1)
    pos = jnp.zeros((boxes, 8, width), F32)
    for axis in range(3):
        pos = jnp.where(at == axis, planes[axis][:, None, :], pos)
    scale = TURN * TURN
    norm = split3(scale * jnp.sum(pos * pos, axis=1, keepdims=True))
    first = jnp.where(at < 3, pos, 1.0)
    first = jnp.where(at == 3, norm[0], jnp.where(at == 4, norm[1], jnp.where(at == 5, norm[2], first)))
    second = jnp.where(at == 3, 1.0, pos + pltpu.roll(pos, 4, 1))
    source = jnp.concatenate([first, second], axis=1).astype(BF16)
    cross = split3((-2.0 * scale) * pos)
    first = jnp.where(at < 3, cross[0], 1.0)
    first = jnp.where(at == 6, norm[0], jnp.where(at == 7, norm[1], first))
    second = jnp.where(at == 3, norm[2], cross[1] + pltpu.roll(cross[2], 4, 1))
    return source, jnp.concatenate([first, second], axis=1).astype(BF16)


def turn_sources(source, src_ref, start):
    boxes, rows, width = source.shape
    eye = lax.broadcasted_iota(jnp.int32, (width, width), 0) == lax.broadcasted_iota(jnp.int32, (width, width), 1)
    twice = jnp.concatenate([source, source], axis=1).reshape(boxes * 2 * rows, width)
    turned = nt_dot(eye.astype(F32).astype(BF16), twice)
    for b in range(boxes):
        at = b * 2 * rows
        lanes = turned[:, at // 128 * 128 : at // 128 * 128 + 128]
        if at % 128:
            lanes = pltpu.roll(lanes, 128 - at % 128, 1)
        src_ref[start + b] = lanes.astype(BF16)


def take_currents(x_rows, win_ref, start):
    for k in range(x_rows.shape[0]):
        both = x_rows[k].astype(F32)
        win_ref[start + 2 * k] = both[:8]
        win_ref[start + 2 * k + 1] = both[8:]


def near_sum(entries, total, item_at, first_source, src_ref, win_ref, obs_ref, out_ref, scratch, ahead=0):
    u0_ref, u1_ref, t0_ref, t1_ref = scratch
    boxes, waves, width = out_ref.shape
    count_bits, box_bits, source_bits = code_bits(boxes, entries)
    pair_bits = count_bits + box_bits + source_bits
    t1_ref[...] = jnp.zeros(t1_ref.shape, F32)
    left = lax.broadcasted_iota(jnp.int32, (width, 128), 1) < 16
    empty = jnp.zeros((16, width), BF16)
    below = jnp.zeros((128 - 32, 2 * width), BF16)

    def pair_at(chunk, g, slot):
        code = item_at(chunk * ITEMS + g) >> (slot * pair_bits)
        source = (code >> (count_bits + box_bits)) & ((1 << source_bits) - 1)
        if first_source:
            source = jnp.maximum(source - first_source, 0)
        return source, (code >> count_bits) & ((1 << box_bits) - 1), code & ((1 << count_bits) - 1)

    def distances(chunk, g, u_ref):
        source0, box0, _ = pair_at(chunk, g, 0)
        source1, box1, _ = pair_at(chunk, g, 1)
        sources = jnp.where(left, src_ref[source0], src_ref[source1])
        observers = jnp.concatenate(
            [
                jnp.concatenate([obs_ref[box0], empty], axis=1),
                jnp.concatenate([empty, obs_ref[box1]], axis=1),
                below,
            ],
            axis=0,
        )
        u_ref[g] = nn_dot(sources, observers)

    def tile(g, u_ref, t_ref):
        for at in range(0, width, ROWS):
            v = jnp.maximum(u_ref[g, at : at + ROWS], 1e-12)
            q = v * lax.rsqrt(v)
            t = q - jnp.round(q)
            cosine = t * t + CHAIN[0]
            for constant in CHAIN[1:]:
                cosine = cosine * cosine + constant
            t_ref[g, at : at + ROWS] = cosine * pltpu.reciprocal(q + OFFSET * TURN, approx=True)

    def product(chunk, g, t_ref):
        source0, box0, count0 = pair_at(chunk, g, 0)
        source1, box1, count1 = pair_at(chunk, g, 1)
        currents = jnp.concatenate([win_ref[source0], win_ref[source1]], axis=0)
        got = nn_dot(currents, t_ref[g])
        out_ref[box0] += count0.astype(F32) * got[:waves, :width]
        out_ref[box1] += count1.astype(F32) * got[waves:, width:]

    u_refs = (u0_ref, u1_ref)
    t_refs = (t0_ref, t1_ref)

    def stage(chunk, turn):
        for g in range(ITEMS):
            distances(chunk + 1, g, u_refs[1 - turn])
            product(jnp.maximum(chunk - 1, 0), g, t_refs[1 - turn])
            tile(g, u_refs[turn], t_refs[turn])

    def body(k, carry):
        for j in range(STAGES):
            stage(ahead + k * STAGES + j, j & 1)
        return carry

    def finish(turn):
        for g in range(ITEMS):
            product(jnp.maximum(chunks - 1, 0), g, t_refs[turn])

    chunks = jnp.maximum((total + (ITEMS - 1)) // ITEMS, ahead)
    rounds = (chunks - ahead) // STAGES
    for g in range(ITEMS):
        distances(0, g, u0_ref)
    for j in range(ahead):
        stage(j, j & 1)
    lax.fori_loop(0, rounds, body, 0)
    last = ahead + rounds * STAGES
    for j in range(STAGES - 1):
        pl.when(last + j < chunks)(functools.partial(stage, last + j, j & 1))
    pl.when((chunks > 0) & ((chunks & 1) == 0))(functools.partial(finish, 1))
    pl.when((chunks & 1) == 1)(functools.partial(finish, 0))


def prepare_kernel(
    entries, own_ref, items_ref, src_hbm, id_hbm, count_hbm, table_hbm, out_ref, obs_ref, src_ref, win_ref, gain_ref,
    trans_src_ref, trans_id_ref, trans_count_ref, table_ref, list_ref, u0_ref, u1_ref, t0_ref, t1_ref, sems
):
    boxes = obs_ref.shape[0]
    length = list_ref.shape[1]
    parents, window = gain_ref.shape[:2]
    listed = src_hbm.shape[1]
    fetch, *trans_copies = start_all(
        (
            (items_ref, list_ref),
            (src_hbm, trans_src_ref),
            (id_hbm, trans_id_ref),
            (count_hbm, trans_count_ref),
            (table_hbm, table_ref),
        ),
        sems,
    )
    plane_rows = 3 * boxes // 16
    source, observer = features(own_ref[boxes // 2 : boxes // 2 + plane_rows])
    turn_sources(source, src_ref, 0)
    take_currents(own_ref[: boxes // 2], win_ref, 0)
    obs_ref[...] = observer
    out_ref[...] = jnp.zeros(out_ref.shape, F32)
    gain_ref[...] = jnp.zeros(gain_ref.shape, F32)
    fetch.wait()
    near_sum(
        entries,
        list_ref[0, length - 3],
        lambda k: list_ref[0, k],
        0,
        src_ref,
        win_ref,
        obs_ref,
        out_ref,
        (u0_ref, u1_ref, t0_ref, t1_ref),
    )
    wait_all(trans_copies)
    row0 = lax.axis_index("dir") * parents
    first = (lax.axis_index("box") - 1) * (window // 3)
    for q in range(parents):
        for e in range(listed):
            live = (e < trans_count_ref[row0 + q]).astype(F32)
            s = jnp.clip(trans_src_ref[row0 + q, e] - first, 0, window - 1)
            gain_ref[q, s] += table_ref[trans_id_ref[row0 + q, e]] * live


def near_kernel(entries, items_ref, *refs):
    *refs, sem = refs
    (
        *step_refs, obs_ref, first_ref, _, _, out_ref, src_ref, win_ref, list_ref, u0_ref, u1_ref, t0_ref, t1_ref
    ) = refs
    boxes, waves, width = out_ref.shape
    fetch = pltpu.make_async_copy(items_ref, list_ref, sem)
    fetch.start()
    length = list_ref.shape[1]
    here = lax.axis_index("dir")
    other_side = jnp.where((here & 1) == 0, here - 1, here + 1)
    x_rows = boxes // 2
    own_rows = x_rows + 3 * boxes // 16

    def take(packet, part):
        take_currents(packet[:x_rows], win_ref, part * boxes)
        source, _ = features(packet[x_rows:])
        turn_sources(source, src_ref, part * boxes)

    take(step_refs[0][:own_rows], 1)
    if len(step_refs) > 1:
        packet = step_refs[1][:own_rows]
        for k, ref in enumerate(step_refs[2:], 3):
            from_here = (here ^ ((1 << k) - 1)) == other_side
            packet = jnp.where(from_here, ref[:own_rows].astype(F32), packet.astype(F32)).astype(BF16)
        take(packet, 2)
    second_start = list_places(boxes, entries)[1]
    out_ref[...] = first_ref[...]
    fetch.wait()
    near_sum(
        entries,
        list_ref[0, length - 2],
        lambda k: list_ref[0, second_start + k],
        0,
        src_ref,
        win_ref,
        obs_ref,
        out_ref,
        (u0_ref, u1_ref, t0_ref, t1_ref),
    )


def incoming_kernel(entries, others, *refs):
    incoming(entries, *refs[others:], other_refs=refs[:others])


def incoming(
    entries, items_ref, even_ref, own_ref, odd_ref, gain_ref, cos_ref, sin_ref, imat_ref, rad_ref, obs_ref, near_ref, out_ref,
    sum_ref, win_ref, src_ref, down_re_ref, down_im_ref, list_ref, u0_ref, u1_ref, t0_ref, t1_ref, sem, other_refs=()
):
    parents, window, _, parent_dirs = gain_ref.shape
    boxes, waves, width = near_ref.shape
    chunks = parent_dirs // 128
    group = window // 3
    fetch = pltpu.make_async_copy(items_ref, list_ref, sem)
    fetch.start()
    length = list_ref.shape[1]
    odd_box = lax.axis_index("box") & 1
    sum_ref[...] = near_ref[...]
    x_rows = boxes // 2
    packet_rows = x_rows + 3 * boxes // 16
    here = lax.axis_index("dir")
    from_even = jnp.where(here == 0, 1, 0) == odd_box
    even_packet, odd_packet = (ref[ref.shape[0] - packet_rows :] for ref in (even_ref, odd_ref))
    packet = jnp.where(from_even, even_packet.astype(F32), odd_packet.astype(F32))
    other_side = jnp.where((here & 1) == 0, here - 1, here + 1)
    for k, ref in enumerate(other_refs, 2):
        from_group = (here ^ ((1 << k) - 1)) == other_side
        packet = jnp.where(from_group, ref[:packet_rows].astype(F32), packet)
    packet = packet.astype(BF16)
    take_currents(packet[:x_rows], win_ref, 0)
    source, _ = features(packet[x_rows:])
    turn_sources(source, src_ref, 0)
    fetch.wait()
    cos_phase = cos_ref[...]
    sin_phase = sin_ref[...]
    sums = tuple(jnp.zeros((waves, 128), F32) for _ in range(parents * chunks * 2))
    for part, ref in ((2 - 2 * odd_box, even_ref), (1, own_ref), (2 * odd_box, odd_ref)):

        def add_source(s, sums, part=part, ref=ref):
            sums = list(sums)
            gains = [gain_ref[q, part * group + s] for q in range(parents)]
            for k in range(chunks):
                spectrum = ref[s * chunks + k].astype(F32)
                sre, sim = spectrum[:waves], spectrum[waves:]
                for q in range(parents):
                    gre = gains[q][0:1, k * 128 : (k + 1) * 128]
                    gim = gains[q][1:2, k * 128 : (k + 1) * 128]
                    at = (q * chunks + k) * 2
                    sums[at] = sums[at] + (gre * sre - gim * sim)
                    sums[at + 1] = sums[at + 1] + (gre * sim + gim * sre)
            return tuple(sums)

        sums = lax.fori_loop(0, group, add_source, sums, unroll=8)
    for q in range(parents):
        for k in range(chunks):
            at = (q * chunks + k) * 2
            re = sums[at].astype(BF16).astype(F32)
            im = sums[at + 1].astype(BF16).astype(F32)
            lanes = slice(k * 128, (k + 1) * 128)
            for c in range(8):
                cos, sin = cos_phase[c : c + 1, lanes], sin_phase[c : c + 1, lanes]
                rows = slice((q * 8 + c) * waves, (q * 8 + c + 1) * waves)
                down_re_ref[rows, lanes] = cos * re + sin * im
                down_im_ref[rows, lanes] = cos * im - sin * re
    imat = imat_ref[...]
    in_re = nt_dot(down_re_ref[...].astype(BF16), imat)
    in_im = nt_dot(down_im_ref[...].astype(BF16), imat)
    incoming = jnp.concatenate([in_re, in_im], axis=1).astype(BF16)
    far = nt_dot(incoming, rad_ref[...])
    near_sum(
        entries,
        list_ref[0, length - 1],
        lambda k: list_ref[0, length - 4 - k],
        2 * boxes,
        src_ref,
        win_ref,
        obs_ref,
        sum_ref,
        (u0_ref, u1_ref, t0_ref, t1_ref),
        AHEAD,
    )
    factor = TURN * LEAD / math.sqrt(entries * width)
    out_ref[...] = sum_ref[...] * factor + far.reshape(near_ref.shape)


def per_device(
    currents, positions, radiation, interp_index, interp_weight, child_phase, near_src, trans_src, trans_id,
    trans_count, trans_table
):
    boxes, waves, width = currents.shape
    entries = near_src.shape[1]
    leaf_dirs = radiation.shape[1] // 2
    parent_dirs = child_phase.shape[1]
    parents = boxes // 8
    spectra_rows = parents * parent_dirs // 128
    size = lax.axis_size("dir")
    vmem = pl.BlockSpec(memory_space=pltpu.VMEM)
    hbm = pl.BlockSpec(memory_space=pltpu.HBM)
    params = pltpu.CompilerParams(vmem_limit_bytes=32 * 1024 * 1024)

    def in_hbm(x):
        return pltpu.with_memory_space_constraint(x, pltpu.HBM)

    def shaped(shape, dtype):
        return jax.ShapeDtypeStruct(shape, dtype)

    x_rows = boxes // 2
    own_rows = x_rows + 3 * boxes // 16
    operands = (currents.reshape(x_rows, 2 * waves, width), positions.transpose(1, 0, 2), radiation, interp_index.T, interp_weight.T, child_phase)
    operands = operands + (near_src,)
    length = list_places(boxes, entries)[2]
    packet, spectra, imat, cos_phase, sin_phase, rad, items = pl.pallas_call(
        outgoing_kernel,
        out_shape=(
            shaped((own_rows + spectra_rows, 16, width), BF16),
            shaped((spectra_rows, 2 * waves, 128), BF16),
            shaped((leaf_dirs, parent_dirs), BF16),
            shaped((8, parent_dirs), F32),
            shaped((8, parent_dirs), F32),
            shaped(radiation.shape, BF16),
            shaped((1, length), jnp.int32),
        ),
        in_specs=[hbm] * len(operands),
        out_specs=(vmem,) * 7,
        scratch_shapes=[pltpu.VMEM(x.shape, x.dtype) for x in operands if x is not radiation]
        + [pltpu.SemaphoreType.DMA((len(operands),))],
        compiler_params=params,
        name="outgoing",
    )(*[in_hbm(x) for x in operands])

    steps = []
    for step in range(1, size):
        pairs = [(i, i ^ step) for i in range(size) if i < i ^ step]
        steps.append(swapped(packet if carries_packet(step) else spectra, "dir", pairs))

    window = 3 * trans_src.shape[0]
    near_scratch = [
        pltpu.VMEM((ITEMS, width, 2 * width), F32),
        pltpu.VMEM((ITEMS, width, 2 * width), F32),
        pltpu.VMEM((ITEMS, width, 2 * width), F32),
        pltpu.VMEM((ITEMS, width, 2 * width), F32),
    ]
    first_sum, observers, sources, ordered, gains = pl.pallas_call(
        functools.partial(prepare_kernel, entries),
        out_shape=(
            shaped((boxes, waves, width), F32),
            shaped((boxes, 16, width), BF16),
            shaped((3 * boxes, width, 128), BF16),
            shaped((3 * boxes, waves, width), F32),
            shaped((parents, window, 2, parent_dirs), F32),
        ),
        in_specs=[vmem] * 2 + [hbm] * 4,
        out_specs=(vmem,) * 5,
        scratch_shapes=[
            pltpu.SMEM(trans_src.shape, jnp.int32),
            pltpu.SMEM(trans_id.shape, jnp.int32),
            pltpu.SMEM(trans_count.shape, jnp.int32),
            pltpu.VMEM(trans_table.shape, F32),
            pltpu.SMEM((1, length), jnp.int32),
        ]
        + near_scratch
        + [pltpu.SemaphoreType.DMA((5,))],
        compiler_params=params,
        name="prepare",
    )(packet, items, *[in_hbm(x) for x in (trans_src, trans_id, trans_count, trans_table)])

    group = pl.pallas_call(
        group_kernel,
        out_shape=shaped((size * spectra_rows + own_rows, 2 * waves, 128), BF16),
        in_specs=[vmem] * (2 + len(steps)),
        out_specs=vmem,
        compiler_params=params,
        name="group",
    )(spectra, *steps, first_sum)
    groups = lax.axis_size("box")
    group_odd = swapped(group, "box", [(i, i + 1) for i in range(1, groups - 1, 2)])
    group_even = swapped(group, "box", [(i, i + 1) for i in range(0, groups - 1, 2)])

    packets = [x for step, x in enumerate(steps, 1) if carries_packet(step)]
    near, _, _ = pl.pallas_call(
        functools.partial(near_kernel, entries),
        out_shape=(
            shaped((boxes, waves, width), F32),
            shaped(sources.shape, BF16),
            shaped(ordered.shape, F32),
        ),
        in_specs=[vmem] * (5 + len(packets)),
        out_specs=(vmem,) * 3,
        input_output_aliases={3 + len(packets): 1, 4 + len(packets): 2},
        scratch_shapes=[pltpu.SMEM((1, length), jnp.int32)] + near_scratch + [pltpu.SemaphoreType.DMA],
        compiler_params=params,
        name="near",
    )(items, *packets, observers, first_sum, sources, ordered)

    return pl.pallas_call(
        functools.partial(incoming_kernel, entries, len(packets) - 1),
        out_shape=shaped((boxes, waves, width), F32),
        in_specs=[vmem] * (10 + len(packets)),
        out_specs=vmem,
        scratch_shapes=[
            pltpu.VMEM((boxes, waves, width), F32),
            pltpu.VMEM((boxes, waves, width), F32),
            pltpu.VMEM((boxes, width, 128), BF16),
            pltpu.VMEM((boxes * waves, parent_dirs), F32),
            pltpu.VMEM((boxes * waves, parent_dirs), F32),
            pltpu.SMEM((1, length), jnp.int32),
        ]
        + near_scratch
        + [pltpu.SemaphoreType.DMA],
        compiler_params=params,
        name="incoming",
    )(*packets[1:], items, group_even, group, group_odd, gains, cos_phase, sin_phase, imat, rad, observers, near)


def solution(mesh):
    placed = (
        P(("box", "dir"), None, None),
        P(("box", "dir"), None, None),
        P(),
        P(),
        P(),
        P(),
        P(("box", "dir"), None),
        P("box", None),
        P("box", None),
        P("box"),
        P(),
    )
    return jax.shard_map(
        per_device,
        mesh=mesh,
        in_specs=placed,
        out_specs=P(("box", "dir"), None, None),
        check_vma=False,
    )
```

```python
import functools
import math

import jax
import jax.numpy as jnp
from jax import lax
from jax.experimental import pallas as pl
from jax.experimental.pallas import tpu as pltpu
from jax.sharding import PartitionSpec as P

F32 = jnp.float32
BF16 = jnp.bfloat16

WAVENUMBER = 4.0
OFFSET = 0.5
TURN = WAVENUMBER / (2.0 * math.pi)
CHAIN = (-2.2803148655023415, -1.415255674611144, -7.327656729815578, -24.467745134801202)
LEAD = 0.04087004462557604
COSINE = (
    0.9999999999990674, -0.49999999998466105, 0.04166666662512991, -0.0013888888455587084, 2.480156463978284e-05,
    -2.7556652559151664e-07, 2.08652097543821e-09, -1.135363495216746e-11, 4.13155312368983e-14,
)
SINE = (
    0.9999999999999502, -0.16666666666584865, 0.008333333331120085, -0.00019841269610529892, 2.755730716252212e-06,
    -2.5051753759896685e-08, 1.6052905945426492e-10, -7.584986682610132e-13, 2.4682378516637708e-15,
)
ITEMS = 4
ROWS = 32
STAGES = 2
FIRST_ITEMS = 6
AHEAD = 2
LEFT_OVER = 2


def round_up(value, step):
    return -(-value // step) * step


def swapped(x, axis, pairs):
    return lax.ppermute(x, axis, [way for i, j in pairs for way in ((i, j), (j, i))])


def polynomial(coefficients, z):
    value = jnp.full_like(z, coefficients[-1])
    for coefficient in coefficients[-2::-1]:
        value = value * z + coefficient
    return value


def split3(x):
    high = x.astype(BF16).astype(F32)
    rest = x - high
    mid = rest.astype(BF16).astype(F32)
    return high, mid, rest - mid


def nt_dot(a, b):
    return lax.dot_general(a, b, (((1,), (1,)), ((), ())), preferred_element_type=F32)


def nn_dot(a, b):
    return jnp.dot(a, b, preferred_element_type=F32)


def code_bits(boxes, entries):
    return entries.bit_length(), (boxes - 1).bit_length(), (3 * boxes - 1).bit_length()


def list_places(boxes, entries):
    gap = 2 * ITEMS
    most = FIRST_ITEMS * boxes // 2
    return most, most + gap, round_up(most + gap + boxes * entries // 2 + 2 * gap + 6, 128)


def list_items(near_src, block, here, size):
    boxes, entries = near_src.shape
    most, second_start, length = list_places(boxes, entries)
    count_bits, box_bits, source_bits = code_bits(boxes, entries)
    pair_bits = count_bits + box_bits + source_bits
    lanes = round_up(3 * boxes, 128)
    odd = (here & 1) == 1
    edge = (here == 0) | (here == size - 1)
    local = near_src - block * boxes
    below = local + jnp.where(odd, 2 * boxes, 3 * boxes)
    above = local + jnp.where(odd, boxes, 0)
    local = jnp.where(local < 0, below, jnp.where(local >= boxes, above, local))
    lane = lax.broadcasted_iota(jnp.int32, (boxes, lanes), 1)
    box = lax.broadcasted_iota(jnp.int32, (boxes, lanes), 0)
    count = jnp.zeros((boxes, lanes), jnp.int32)
    for e in range(entries):
        count = count + (local[:, e : e + 1] == lane).astype(jnp.int32)
    present = count > 0
    flags = present.astype(F32)
    box_row = lax.broadcasted_iota(jnp.int32, (boxes, boxes), 0)
    box_col = lax.broadcasted_iota(jnp.int32, (boxes, boxes), 1)
    rank = nn_dot((box_col < box_row).astype(F32).astype(BF16), flags.astype(BF16)).astype(jnp.int32)
    pairs = jnp.sum(flags, axis=0, keepdims=True)
    from_cross = lane >= jnp.where(edge, 2 * boxes, 3 * boxes - LEFT_OVER)
    cross_pairs = jnp.where(from_cross[:1], pairs, 0.0)
    group_pairs = jnp.where(from_cross[:1], 0.0, pairs)
    row = lax.broadcasted_iota(jnp.int32, (lanes, lanes), 0)
    col = lax.broadcasted_iota(jnp.int32, (lanes, lanes), 1)
    ahead = (row < col).astype(F32).astype(BF16)
    lists = jnp.concatenate([group_pairs, cross_pairs, jnp.zeros((6, lanes), F32)], axis=0)
    offset = nn_dot(lists.astype(BF16), ahead).astype(jnp.int32)
    own_pairs = jnp.where(lane[:1] < boxes, group_pairs, 0.0)

    def total(pairs):
        return jnp.sum(pairs, axis=1, keepdims=True).astype(jnp.int32)

    first_total = jnp.minimum(total(own_pairs), 2 * most)
    second_total = total(group_pairs) - first_total
    cross_total = total(cross_pairs)
    order = offset[0:1] + rank
    in_second = order >= first_total
    order = jnp.where(in_second, order - first_total, order)
    order = jnp.where(from_cross, offset[1:2] + rank, order)
    half = order >> 1
    place = jnp.where(from_cross, (length - 4) - half, jnp.where(in_second, second_start + half, half))
    place = jnp.where(present, place, -1)
    code = (lane << (count_bits + box_bits)) | (box << count_bits) | count
    code = jnp.where((order & 1) == 1, code << pair_bits, code)
    place_t = place.T
    code_t = code.T
    rows = 3 * boxes
    slot = lax.broadcasted_iota(jnp.int32, (rows, length), 1)
    found = jnp.zeros((rows, length), jnp.int32)
    for i in range(boxes):
        hit = place_t[:rows, i : i + 1] == slot
        found = found + jnp.where(hit, code_t[:rows, i : i + 1], 0)
    listed = jnp.sum(found, axis=0, keepdims=True)
    at = lax.broadcasted_iota(jnp.int32, (1, length), 1)
    for back, pairs in ((3, first_total), (2, second_total), (1, cross_total)):
        listed = jnp.where(at == length - back, (pairs + 1) >> 1, listed)
    return listed


def start_all(copies, sems):
    started = [pltpu.make_async_copy(src, dst, sems.at[k]) for k, (src, dst) in enumerate(copies)]
    for copy in started:
        copy.start()
    return started


def wait_all(started):
    for copy in started:
        copy.wait()


def outgoing_kernel(
    x_hbm, pos_hbm, rad_hbm, idx_hbm, wgt_hbm, phase_hbm, near_hbm, packet_ref, spectra_ref, imat_ref, cos_ref, sin_ref,
    rad_ref, items_ref, x_ref, pos_ref, idx_ref, wgt_ref, phase_ref, near_ref, sems
):
    wait_all(
        start_all(
            (
                (x_hbm, x_ref),
                (pos_hbm, pos_ref),
                (rad_hbm, rad_ref),
                (idx_hbm, idx_ref),
                (wgt_hbm, wgt_ref),
                (phase_hbm, phase_ref),
                (near_hbm, near_ref),
            ),
            sems,
        )
    )
    block = lax.axis_index(("box", "dir"))
    items_ref[...] = list_items(near_ref[...], block, lax.axis_index("dir"), lax.axis_size("dir"))
    leaf_dirs, parent_dirs = imat_ref.shape
    x_rows, _, width = x_ref.shape
    axes, boxes, _ = pos_ref.shape
    waves = x_rows * 16 // boxes
    chunks = parent_dirs // 128
    own_rows = x_rows + axes * boxes // 16
    packet_ref[:x_rows] = x_ref[...]
    packet_ref[x_rows:own_rows] = pos_ref[...].reshape(axes * boxes // 16, 16, width)
    column = lax.broadcasted_iota(jnp.int32, (leaf_dirs, parent_dirs), 0)
    imat = jnp.zeros((leaf_dirs, parent_dirs), F32)
    for s in range(idx_ref.shape[0]):
        imat = imat + jnp.where(idx_ref[s : s + 1, :] == column, wgt_ref[s : s + 1, :], 0.0)
    imat = imat.astype(BF16)
    imat_ref[...] = imat
    phase = phase_ref[...]
    cos_phase = polynomial(COSINE, phase * phase)
    sin_phase = phase * polynomial(SINE, phase * phase)
    cos_ref[...] = cos_phase
    sin_ref[...] = sin_phase
    leaf = nn_dot(x_ref[...].reshape(boxes * waves, width), rad_ref[...]).astype(BF16)
    up_re = nn_dot(leaf[:, :leaf_dirs], imat)
    up_im = nn_dot(leaf[:, leaf_dirs:], imat)
    for q in range(boxes // 8):
        re = jnp.zeros((waves, parent_dirs), F32)
        im = jnp.zeros((waves, parent_dirs), F32)
        for c in range(8):
            at = (q * 8 + c) * waves
            ure = up_re[at : at + waves]
            uim = up_im[at : at + waves]
            re = re + (cos_phase[c : c + 1] * ure - sin_phase[c : c + 1] * uim)
            im = im + (sin_phase[c : c + 1] * ure + cos_phase[c : c + 1] * uim)
        both = jnp.concatenate([re, im], axis=0).astype(BF16)
        for k in range(chunks):
            part = both[:, k * 128 : (k + 1) * 128]
            packet_ref[own_rows + q * chunks + k] = part
            spectra_ref[q * chunks + k] = part


def carries_packet(step):
    return step & (step + 1) == 0


def group_kernel(own_ref, *refs):
    *step_refs, _, group_ref = refs
    size = lax.axis_size("dir")
    rows = own_ref.shape[0]
    here = lax.axis_index("dir")
    group_ref[pl.ds(here * rows, rows)] = own_ref[...]
    for step, ref in enumerate(step_refs, 1):
        group_ref[pl.ds((here ^ step) * rows, rows)] = ref[ref.shape[0] - rows :]
    group_ref[size * rows :] = step_refs[-1][: step_refs[-1].shape[0] - rows]


def features(planes):
    rows, _, width = planes.shape
    boxes = rows * 16 // 3
    planes = planes.astype(F32).reshape(3, boxes, width)
    at = lax.broadcasted_iota(jnp.int32, (boxes, 8, width), 1)
    pos = jnp.zeros((boxes, 8, width), F32)
    for axis in range(3):
        pos = jnp.where(at == axis, planes[axis][:, None, :], pos)
    scale = TURN * TURN
    norm = split3(scale * jnp.sum(pos * pos, axis=1, keepdims=True))
    first = jnp.where(at < 3, pos, 1.0)
    first = jnp.where(at == 3, norm[0], jnp.where(at == 4, norm[1], jnp.where(at == 5, norm[2], first)))
    second = jnp.where(at == 3, 1.0, pos + pltpu.roll(pos, 4, 1))
    source = jnp.concatenate([first, second], axis=1).astype(BF16)
    cross = split3((-2.0 * scale) * pos)
    first = jnp.where(at < 3, cross[0], 1.0)
    first = jnp.where(at == 6, norm[0], jnp.where(at == 7, norm[1], first))
    second = jnp.where(at == 3, norm[2], cross[1] + pltpu.roll(cross[2], 4, 1))
    return source, jnp.concatenate([first, second], axis=1).astype(BF16)


def turn_sources(source, src_ref, start):
    boxes, rows, width = source.shape
    eye = lax.broadcasted_iota(jnp.int32, (width, width), 0) == lax.broadcasted_iota(jnp.int32, (width, width), 1)
    twice = jnp.concatenate([source, source], axis=1).reshape(boxes * 2 * rows, width)
    turned = nt_dot(eye.astype(F32).astype(BF16), twice)
    for b in range(boxes):
        at = b * 2 * rows
        lanes = turned[:, at // 128 * 128 : at // 128 * 128 + 128]
        if at % 128:
            lanes = pltpu.roll(lanes, 128 - at % 128, 1)
        src_ref[start + b] = lanes.astype(BF16)


def take_currents(x_rows, win_ref, start):
    for k in range(x_rows.shape[0]):
        both = x_rows[k].astype(F32)
        win_ref[start + 2 * k] = both[:8]
        win_ref[start + 2 * k + 1] = both[8:]


def near_sum(entries, total, item_at, first_source, src_ref, win_ref, obs_ref, out_ref, scratch, ahead=0):
    u0_ref, u1_ref, t0_ref, t1_ref = scratch
    boxes, waves, width = out_ref.shape
    count_bits, box_bits, source_bits = code_bits(boxes, entries)
    pair_bits = count_bits + box_bits + source_bits
    t1_ref[...] = jnp.zeros(t1_ref.shape, F32)
    left = lax.broadcasted_iota(jnp.int32, (width, 128), 1) < 16
    empty = jnp.zeros((16, width), BF16)

    def pair_at(chunk, g, slot):
        code = item_at(chunk * ITEMS + g) >> (slot * pair_bits)
        source = (code >> (count_bits + box_bits)) & ((1 << source_bits) - 1)
        if first_source:
            source = jnp.maximum(source - first_source, 0)
        return source, (code >> count_bits) & ((1 << box_bits) - 1), code & ((1 << count_bits) - 1)

    def distances(chunk, g, u_ref):
        source0, box0, _ = pair_at(chunk, g, 0)
        source1, box1, _ = pair_at(chunk, g, 1)
        sources = jnp.where(left, src_ref[source0], src_ref[source1])
        observers = jnp.concatenate(
            [
                jnp.concatenate([obs_ref[box0], empty], axis=1),
                jnp.concatenate([empty, obs_ref[box1]], axis=1),
            ],
            axis=0,
        )
        u_ref[g] = nn_dot(sources[:, :32], observers)

    def tile(g, u_ref, t_ref):
        for at in range(0, width, ROWS):
            v = jnp.maximum(u_ref[g, at : at + ROWS], 1e-12)
            q = v * lax.rsqrt(v)
            t = q - jnp.round(q)
            cosine = t * t + CHAIN[0]
            for constant in CHAIN[1:]:
                cosine = cosine * cosine + constant
            t_ref[g, at : at + ROWS] = cosine * pltpu.reciprocal(q + OFFSET * TURN, approx=True)

    def product(chunk, g, t_ref):
        source0, box0, count0 = pair_at(chunk, g, 0)
        source1, box1, count1 = pair_at(chunk, g, 1)
        currents = jnp.concatenate([win_ref[source0], win_ref[source1]], axis=0)
        got = nn_dot(currents, t_ref[g])
        out_ref[box0] += count0.astype(F32) * got[:waves, :width]
        out_ref[box1] += count1.astype(F32) * got[waves:, width:]

    u_refs = (u0_ref, u1_ref)
    t_refs = (t0_ref, t1_ref)

    def stage(chunk, turn):
        for g in range(ITEMS):
            distances(chunk + 1, g, u_refs[1 - turn])
            product(jnp.maximum(chunk - 1, 0), g, t_refs[1 - turn])
            tile(g, u_refs[turn], t_refs[turn])

    def body(k, carry):
        for j in range(STAGES):
            stage(ahead + k * STAGES + j, j & 1)
        return carry

    def finish(turn):
        for g in range(ITEMS):
            product(jnp.maximum(chunks - 1, 0), g, t_refs[turn])

    chunks = jnp.maximum((total + (ITEMS - 1)) // ITEMS, ahead)
    rounds = (chunks - ahead) // STAGES
    for g in range(ITEMS):
        distances(0, g, u0_ref)
    for j in range(ahead):
        stage(j, j & 1)
    lax.fori_loop(0, rounds, body, 0)
    last = ahead + rounds * STAGES
    for j in range(STAGES - 1):
        pl.when(last + j < chunks)(functools.partial(stage, last + j, j & 1))
    pl.when((chunks > 0) & ((chunks & 1) == 0))(functools.partial(finish, 1))
    pl.when((chunks & 1) == 1)(functools.partial(finish, 0))


def prepare_kernel(
    entries, own_ref, items_ref, src_hbm, id_hbm, count_hbm, table_hbm, out_ref, obs_ref, src_ref, win_ref, gain_ref,
    trans_src_ref, trans_id_ref, trans_count_ref, table_ref, list_ref, u0_ref, u1_ref, t0_ref, t1_ref, sems
):
    boxes = obs_ref.shape[0]
    length = list_ref.shape[1]
    parents, window = gain_ref.shape[:2]
    listed = src_hbm.shape[1]
    fetch, *trans_copies = start_all(
        (
            (items_ref, list_ref),
            (src_hbm, trans_src_ref),
            (id_hbm, trans_id_ref),
            (count_hbm, trans_count_ref),
            (table_hbm, table_ref),
        ),
        sems,
    )
    plane_rows = 3 * boxes // 16
    source, observer = features(own_ref[boxes // 2 : boxes // 2 + plane_rows])
    turn_sources(source, src_ref, 0)
    take_currents(own_ref[: boxes // 2], win_ref, 0)
    obs_ref[...] = observer
    out_ref[...] = jnp.zeros(out_ref.shape, F32)
    gain_ref[...] = jnp.zeros(gain_ref.shape, F32)
    fetch.wait()
    near_sum(
        entries,
        list_ref[0, length - 3],
        lambda k: list_ref[0, k],
        0,
        src_ref,
        win_ref,
        obs_ref,
        out_ref,
        (u0_ref, u1_ref, t0_ref, t1_ref),
    )
    wait_all(trans_copies)
    row0 = lax.axis_index("dir") * parents
    first = (lax.axis_index("box") - 1) * (window // 3)
    for q in range(parents):
        for e in range(listed):
            live = (e < trans_count_ref[row0 + q]).astype(F32)
            s = jnp.clip(trans_src_ref[row0 + q, e] - first, 0, window - 1)
            gain_ref[q, s] += table_ref[trans_id_ref[row0 + q, e]] * live


def near_kernel(entries, items_ref, *refs):
    *refs, sem = refs
    (
        *step_refs, obs_ref, first_ref, _, _, out_ref, src_ref, win_ref, list_ref, u0_ref, u1_ref, t0_ref, t1_ref
    ) = refs
    boxes, waves, width = out_ref.shape
    fetch = pltpu.make_async_copy(items_ref, list_ref, sem)
    fetch.start()
    length = list_ref.shape[1]
    here = lax.axis_index("dir")
    other_side = jnp.where((here & 1) == 0, here - 1, here + 1)
    x_rows = boxes // 2
    own_rows = x_rows + 3 * boxes // 16

    def take(packet, part):
        take_currents(packet[:x_rows], win_ref, part * boxes)
        source, _ = features(packet[x_rows:])
        turn_sources(source, src_ref, part * boxes)

    take(step_refs[0][:own_rows], 1)
    if len(step_refs) > 1:
        packet = step_refs[1][:own_rows]
        for k, ref in enumerate(step_refs[2:], 3):
            from_here = (here ^ ((1 << k) - 1)) == other_side
            packet = jnp.where(from_here, ref[:own_rows].astype(F32), packet.astype(F32)).astype(BF16)
        take(packet, 2)
    second_start = list_places(boxes, entries)[1]
    out_ref[...] = first_ref[...]
    fetch.wait()
    near_sum(
        entries,
        list_ref[0, length - 2],
        lambda k: list_ref[0, second_start + k],
        0,
        src_ref,
        win_ref,
        obs_ref,
        out_ref,
        (u0_ref, u1_ref, t0_ref, t1_ref),
    )


def incoming_kernel(entries, others, *refs):
    incoming(entries, *refs[others:], other_refs=refs[:others])


def incoming(
    entries, items_ref, even_ref, own_ref, odd_ref, gain_ref, cos_ref, sin_ref, imat_ref, rad_ref, obs_ref, near_ref, out_ref,
    sum_ref, win_ref, src_ref, down_ref, list_ref, u0_ref, u1_ref, t0_ref, t1_ref, sem, other_refs=()
):
    parents, window, _, parent_dirs = gain_ref.shape
    boxes, waves, width = near_ref.shape
    chunks = parent_dirs // 128
    group = window // 3
    fetch = pltpu.make_async_copy(items_ref, list_ref, sem)
    fetch.start()
    length = list_ref.shape[1]
    odd_box = lax.axis_index("box") & 1
    sum_ref[...] = near_ref[...]
    x_rows = boxes // 2
    packet_rows = x_rows + 3 * boxes // 16
    here = lax.axis_index("dir")
    from_even = jnp.where(here == 0, 1, 0) == odd_box
    even_packet, odd_packet = (ref[ref.shape[0] - packet_rows :] for ref in (even_ref, odd_ref))
    packet = jnp.where(from_even, even_packet.astype(F32), odd_packet.astype(F32))
    other_side = jnp.where((here & 1) == 0, here - 1, here + 1)
    for k, ref in enumerate(other_refs, 2):
        from_group = (here ^ ((1 << k) - 1)) == other_side
        packet = jnp.where(from_group, ref[:packet_rows].astype(F32), packet)
    packet = packet.astype(BF16)
    take_currents(packet[:x_rows], win_ref, 0)
    source, _ = features(packet[x_rows:])
    turn_sources(source, src_ref, 0)
    fetch.wait()
    cos_phase = cos_ref[...]
    sin_phase = sin_ref[...]
    sums = tuple(jnp.zeros((waves, 128), F32) for _ in range(parents * chunks * 2))
    for part, ref in ((2 - 2 * odd_box, even_ref), (1, own_ref), (2 * odd_box, odd_ref)):

        def add_source(s, sums, part=part, ref=ref):
            sums = list(sums)
            gains = [gain_ref[q, part * group + s] for q in range(parents)]
            for k in range(chunks):
                spectrum = ref[s * chunks + k].astype(F32)
                sre, sim = spectrum[:waves], spectrum[waves:]
                for q in range(parents):
                    gre = gains[q][0:1, k * 128 : (k + 1) * 128]
                    gim = gains[q][1:2, k * 128 : (k + 1) * 128]
                    at = (q * chunks + k) * 2
                    sums[at] = sums[at] + (gre * sre - gim * sim)
                    sums[at + 1] = sums[at + 1] + (gre * sim + gim * sre)
            return tuple(sums)

        sums = lax.fori_loop(0, group, add_source, sums, unroll=8)
    for q in range(parents):
        for k in range(chunks):
            at = (q * chunks + k) * 2
            re = sums[at].astype(BF16).astype(F32)
            im = sums[at + 1].astype(BF16).astype(F32)
            lanes = slice(k * 128, (k + 1) * 128)
            for c in range(8):
                cos, sin = cos_phase[c : c + 1, lanes], sin_phase[c : c + 1, lanes]
                rows = slice((q * 8 + c) * waves, (q * 8 + c + 1) * waves)
                down_ref[0, rows, lanes] = cos * re + sin * im
                down_ref[1, rows, lanes] = cos * im - sin * re
    imat = imat_ref[...]
    rows = boxes * waves
    both = nt_dot(down_ref[...].reshape(2 * rows, parent_dirs).astype(BF16), imat)
    incoming = jnp.concatenate([both[:rows], both[rows:]], axis=1).astype(BF16)
    far = nt_dot(incoming, rad_ref[...])
    near_sum(
        entries,
        list_ref[0, length - 1],
        lambda k: list_ref[0, length - 4 - k],
        2 * boxes,
        src_ref,
        win_ref,
        obs_ref,
        sum_ref,
        (u0_ref, u1_ref, t0_ref, t1_ref),
        AHEAD,
    )
    factor = TURN * LEAD / math.sqrt(entries * width)
    out_ref[...] = sum_ref[...] * factor + far.reshape(near_ref.shape)


def per_device(
    currents, positions, radiation, interp_index, interp_weight, child_phase, near_src, trans_src, trans_id,
    trans_count, trans_table
):
    boxes, waves, width = currents.shape
    entries = near_src.shape[1]
    leaf_dirs = radiation.shape[1] // 2
    parent_dirs = child_phase.shape[1]
    parents = boxes // 8
    spectra_rows = parents * parent_dirs // 128
    size = lax.axis_size("dir")
    vmem = pl.BlockSpec(memory_space=pltpu.VMEM)
    hbm = pl.BlockSpec(memory_space=pltpu.HBM)
    params = pltpu.CompilerParams(vmem_limit_bytes=32 * 1024 * 1024)

    def in_hbm(x):
        return pltpu.with_memory_space_constraint(x, pltpu.HBM)

    def shaped(shape, dtype):
        return jax.ShapeDtypeStruct(shape, dtype)

    x_rows = boxes // 2
    own_rows = x_rows + 3 * boxes // 16
    operands = (currents.reshape(x_rows, 2 * waves, width), positions.transpose(1, 0, 2), radiation, interp_index.T, interp_weight.T, child_phase)
    operands = operands + (near_src,)
    length = list_places(boxes, entries)[2]
    packet, spectra, imat, cos_phase, sin_phase, rad, items = pl.pallas_call(
        outgoing_kernel,
        out_shape=(
            shaped((own_rows + spectra_rows, 16, width), BF16),
            shaped((spectra_rows, 2 * waves, 128), BF16),
            shaped((leaf_dirs, parent_dirs), BF16),
            shaped((8, parent_dirs), F32),
            shaped((8, parent_dirs), F32),
            shaped(radiation.shape, BF16),
            shaped((1, length), jnp.int32),
        ),
        in_specs=[hbm] * len(operands),
        out_specs=(vmem,) * 7,
        scratch_shapes=[pltpu.VMEM(x.shape, x.dtype) for x in operands if x is not radiation]
        + [pltpu.SemaphoreType.DMA((len(operands),))],
        compiler_params=params,
        name="outgoing",
    )(*[in_hbm(x) for x in operands])

    steps = []
    for step in range(1, size):
        pairs = [(i, i ^ step) for i in range(size) if i < i ^ step]
        steps.append(swapped(packet if carries_packet(step) else spectra, "dir", pairs))

    window = 3 * trans_src.shape[0]
    near_scratch = [
        pltpu.VMEM((ITEMS, width, 2 * width), F32),
        pltpu.VMEM((ITEMS, width, 2 * width), F32),
        pltpu.VMEM((ITEMS, width, 2 * width), F32),
        pltpu.VMEM((ITEMS, width, 2 * width), F32),
    ]
    first_sum, observers, sources, ordered, gains = pl.pallas_call(
        functools.partial(prepare_kernel, entries),
        out_shape=(
            shaped((boxes, waves, width), F32),
            shaped((boxes, 16, width), BF16),
            shaped((3 * boxes, width, 128), BF16),
            shaped((3 * boxes, waves, width), F32),
            shaped((parents, window, 2, parent_dirs), F32),
        ),
        in_specs=[vmem] * 2 + [hbm] * 4,
        out_specs=(vmem,) * 5,
        scratch_shapes=[
            pltpu.SMEM(trans_src.shape, jnp.int32),
            pltpu.SMEM(trans_id.shape, jnp.int32),
            pltpu.SMEM(trans_count.shape, jnp.int32),
            pltpu.VMEM(trans_table.shape, F32),
            pltpu.SMEM((1, length), jnp.int32),
        ]
        + near_scratch
        + [pltpu.SemaphoreType.DMA((5,))],
        compiler_params=params,
        name="prepare",
    )(packet, items, *[in_hbm(x) for x in (trans_src, trans_id, trans_count, trans_table)])

    group = pl.pallas_call(
        group_kernel,
        out_shape=shaped((size * spectra_rows + own_rows, 2 * waves, 128), BF16),
        in_specs=[vmem] * (2 + len(steps)),
        out_specs=vmem,
        compiler_params=params,
        name="group",
    )(spectra, *steps, first_sum)
    groups = lax.axis_size("box")
    group_odd = swapped(group, "box", [(i, i + 1) for i in range(1, groups - 1, 2)])
    group_even = swapped(group, "box", [(i, i + 1) for i in range(0, groups - 1, 2)])

    packets = [x for step, x in enumerate(steps, 1) if carries_packet(step)]
    near, _, _ = pl.pallas_call(
        functools.partial(near_kernel, entries),
        out_shape=(
            shaped((boxes, waves, width), F32),
            shaped(sources.shape, BF16),
            shaped(ordered.shape, F32),
        ),
        in_specs=[vmem] * (5 + len(packets)),
        out_specs=(vmem,) * 3,
        input_output_aliases={3 + len(packets): 1, 4 + len(packets): 2},
        scratch_shapes=[pltpu.SMEM((1, length), jnp.int32)] + near_scratch + [pltpu.SemaphoreType.DMA],
        compiler_params=params,
        name="near",
    )(items, *packets, observers, first_sum, sources, ordered)

    return pl.pallas_call(
        functools.partial(incoming_kernel, entries, len(packets) - 1),
        out_shape=shaped((boxes, waves, width), F32),
        in_specs=[vmem] * (10 + len(packets)),
        out_specs=vmem,
        scratch_shapes=[
            pltpu.VMEM((boxes, waves, width), F32),
            pltpu.VMEM((boxes, waves, width), F32),
            pltpu.VMEM((boxes, width, 128), BF16),
            pltpu.VMEM((2, boxes * waves, parent_dirs), F32),
            pltpu.SMEM((1, length), jnp.int32),
        ]
        + near_scratch
        + [pltpu.SemaphoreType.DMA],
        compiler_params=params,
        name="incoming",
    )(*packets[1:], items, group_even, group, group_odd, gains, cos_phase, sin_phase, imat, rad, observers, near)


def solution(mesh):
    placed = (
        P(("box", "dir"), None, None),
        P(("box", "dir"), None, None),
        P(),
        P(),
        P(),
        P(),
        P(("box", "dir"), None),
        P("box", None),
        P("box", None),
        P("box"),
        P(),
    )
    return jax.shard_map(
        per_device,
        mesh=mesh,
        in_specs=placed,
        out_specs=P(("box", "dir"), None, None),
        check_vma=False,
    )
```

```python
import functools
import math

import jax
import jax.numpy as jnp
from jax import lax
from jax.experimental import pallas as pl
from jax.experimental.pallas import tpu as pltpu
from jax.sharding import PartitionSpec as P

F32 = jnp.float32
BF16 = jnp.bfloat16

WAVENUMBER = 4.0
OFFSET = 0.5
TURN = WAVENUMBER / (2.0 * math.pi)
CHAIN = (-2.2803148655023415, -1.415255674611144, -7.327656729815578, -24.467745134801202)
LEAD = 0.04087004462557604
COSINE = (
    0.9999999999990674, -0.49999999998466105, 0.04166666662512991, -0.0013888888455587084, 2.480156463978284e-05,
    -2.7556652559151664e-07, 2.08652097543821e-09, -1.135363495216746e-11, 4.13155312368983e-14,
)
SINE = (
    0.9999999999999502, -0.16666666666584865, 0.008333333331120085, -0.00019841269610529892, 2.755730716252212e-06,
    -2.5051753759896685e-08, 1.6052905945426492e-10, -7.584986682610132e-13, 2.4682378516637708e-15,
)
ITEMS = 4
ROWS = 64
STAGES = 2
FIRST_ITEMS = 6
AHEAD = 2
LEFT_OVER = 2


def round_up(value, step):
    return -(-value // step) * step


def swapped(x, axis, pairs):
    return lax.ppermute(x, axis, [way for i, j in pairs for way in ((i, j), (j, i))])


def polynomial(coefficients, z):
    value = jnp.full_like(z, coefficients[-1])
    for coefficient in coefficients[-2::-1]:
        value = value * z + coefficient
    return value


def split3(x):
    high = x.astype(BF16).astype(F32)
    rest = x - high
    mid = rest.astype(BF16).astype(F32)
    return high, mid, rest - mid


def nt_dot(a, b):
    return lax.dot_general(a, b, (((1,), (1,)), ((), ())), preferred_element_type=F32)


def nn_dot(a, b):
    return jnp.dot(a, b, preferred_element_type=F32)


def code_bits(boxes, entries):
    return entries.bit_length(), (boxes - 1).bit_length(), (3 * boxes - 1).bit_length()


def list_places(boxes, entries):
    gap = 2 * ITEMS
    most = FIRST_ITEMS * boxes // 2
    return most, most + gap, round_up(most + gap + boxes * entries // 2 + 2 * gap + 6, 128)


def list_items(near_src, block, here, size):
    boxes, entries = near_src.shape
    most, second_start, length = list_places(boxes, entries)
    count_bits, box_bits, source_bits = code_bits(boxes, entries)
    pair_bits = count_bits + box_bits + source_bits
    lanes = round_up(3 * boxes, 128)
    odd = (here & 1) == 1
    edge = (here == 0) | (here == size - 1)
    local = near_src - block * boxes
    below = local + jnp.where(odd, 2 * boxes, 3 * boxes)
    above = local + jnp.where(odd, boxes, 0)
    local = jnp.where(local < 0, below, jnp.where(local >= boxes, above, local))
    lane = lax.broadcasted_iota(jnp.int32, (boxes, lanes), 1)
    box = lax.broadcasted_iota(jnp.int32, (boxes, lanes), 0)
    count = jnp.zeros((boxes, lanes), jnp.int32)
    for e in range(entries):
        count = count + (local[:, e : e + 1] == lane).astype(jnp.int32)
    present = count > 0
    flags = present.astype(F32)
    box_row = lax.broadcasted_iota(jnp.int32, (boxes, boxes), 0)
    box_col = lax.broadcasted_iota(jnp.int32, (boxes, boxes), 1)
    rank = nn_dot((box_col < box_row).astype(F32).astype(BF16), flags.astype(BF16)).astype(jnp.int32)
    pairs = jnp.sum(flags, axis=0, keepdims=True)
    from_cross = lane >= jnp.where(edge, 2 * boxes, 3 * boxes - LEFT_OVER)
    cross_pairs = jnp.where(from_cross[:1], pairs, 0.0)
    group_pairs = jnp.where(from_cross[:1], 0.0, pairs)
    row = lax.broadcasted_iota(jnp.int32, (lanes, lanes), 0)
    col = lax.broadcasted_iota(jnp.int32, (lanes, lanes), 1)
    ahead = (row < col).astype(F32).astype(BF16)
    lists = jnp.concatenate([group_pairs, cross_pairs, jnp.zeros((6, lanes), F32)], axis=0)
    offset = nn_dot(lists.astype(BF16), ahead).astype(jnp.int32)
    own_pairs = jnp.where(lane[:1] < boxes, group_pairs, 0.0)

    def total(pairs):
        return jnp.sum(pairs, axis=1, keepdims=True).astype(jnp.int32)

    first_total = jnp.minimum(total(own_pairs), 2 * most)
    second_total = total(group_pairs) - first_total
    cross_total = total(cross_pairs)
    order = offset[0:1] + rank
    in_second = order >= first_total
    order = jnp.where(in_second, order - first_total, order)
    order = jnp.where(from_cross, offset[1:2] + rank, order)
    half = order >> 1
    place = jnp.where(from_cross, (length - 4) - half, jnp.where(in_second, second_start + half, half))
    place = jnp.where(present, place, -1)
    code = (lane << (count_bits + box_bits)) | (box << count_bits) | count
    code = jnp.where((order & 1) == 1, code << pair_bits, code)
    place_t = place.T
    code_t = code.T
    rows = 3 * boxes
    slot = lax.broadcasted_iota(jnp.int32, (rows, length), 1)
    found = jnp.zeros((rows, length), jnp.int32)
    for i in range(boxes):
        hit = place_t[:rows, i : i + 1] == slot
        found = found + jnp.where(hit, code_t[:rows, i : i + 1], 0)
    listed = jnp.sum(found, axis=0, keepdims=True)
    at = lax.broadcasted_iota(jnp.int32, (1, length), 1)
    for back, pairs in ((3, first_total), (2, second_total), (1, cross_total)):
        listed = jnp.where(at == length - back, (pairs + 1) >> 1, listed)
    return listed


def start_all(copies, sems):
    started = [pltpu.make_async_copy(src, dst, sems.at[k]) for k, (src, dst) in enumerate(copies)]
    for copy in started:
        copy.start()
    return started


def wait_all(started):
    for copy in started:
        copy.wait()


def outgoing_kernel(
    x_hbm, pos_hbm, rad_hbm, idx_hbm, wgt_hbm, phase_hbm, near_hbm, packet_ref, spectra_ref, imat_ref, cos_ref, sin_ref,
    rad_ref, items_ref, x_ref, pos_ref, idx_ref, wgt_ref, phase_ref, near_ref, sems
):
    wait_all(
        start_all(
            (
                (x_hbm, x_ref),
                (pos_hbm, pos_ref),
                (rad_hbm, rad_ref),
                (idx_hbm, idx_ref),
                (wgt_hbm, wgt_ref),
                (phase_hbm, phase_ref),
                (near_hbm, near_ref),
            ),
            sems,
        )
    )
    block = lax.axis_index(("box", "dir"))
    items_ref[...] = list_items(near_ref[...], block, lax.axis_index("dir"), lax.axis_size("dir"))
    leaf_dirs, parent_dirs = imat_ref.shape
    x_rows, _, width = x_ref.shape
    axes, boxes, _ = pos_ref.shape
    waves = x_rows * 16 // boxes
    chunks = parent_dirs // 128
    own_rows = x_rows + axes * boxes // 16
    packet_ref[:x_rows] = x_ref[...]
    packet_ref[x_rows:own_rows] = pos_ref[...].reshape(axes * boxes // 16, 16, width)
    column = lax.broadcasted_iota(jnp.int32, (leaf_dirs, parent_dirs), 0)
    imat = jnp.zeros((leaf_dirs, parent_dirs), F32)
    for s in range(idx_ref.shape[0]):
        imat = imat + jnp.where(idx_ref[s : s + 1, :] == column, wgt_ref[s : s + 1, :], 0.0)
    imat = imat.astype(BF16)
    imat_ref[...] = imat
    phase = phase_ref[...]
    cos_phase = polynomial(COSINE, phase * phase)
    sin_phase = phase * polynomial(SINE, phase * phase)
    cos_ref[...] = cos_phase
    sin_ref[...] = sin_phase
    leaf = nn_dot(x_ref[...].reshape(boxes * waves, width), rad_ref[...]).astype(BF16)
    up_re = nn_dot(leaf[:, :leaf_dirs], imat)
    up_im = nn_dot(leaf[:, leaf_dirs:], imat)
    for q in range(boxes // 8):
        re = jnp.zeros((waves, parent_dirs), F32)
        im = jnp.zeros((waves, parent_dirs), F32)
        for c in range(8):
            at = (q * 8 + c) * waves
            ure = up_re[at : at + waves]
            uim = up_im[at : at + waves]
            re = re + (cos_phase[c : c + 1] * ure - sin_phase[c : c + 1] * uim)
            im = im + (sin_phase[c : c + 1] * ure + cos_phase[c : c + 1] * uim)
        both = jnp.concatenate([re, im], axis=0).astype(BF16)
        for k in range(chunks):
            part = both[:, k * 128 : (k + 1) * 128]
            packet_ref[own_rows + q * chunks + k] = part
            spectra_ref[q * chunks + k] = part


def carries_packet(step):
    return step & (step + 1) == 0


def group_kernel(own_ref, *refs):
    *step_refs, _, group_ref = refs
    size = lax.axis_size("dir")
    rows = own_ref.shape[0]
    here = lax.axis_index("dir")
    group_ref[pl.ds(here * rows, rows)] = own_ref[...]
    for step, ref in enumerate(step_refs, 1):
        group_ref[pl.ds((here ^ step) * rows, rows)] = ref[ref.shape[0] - rows :]
    group_ref[size * rows :] = step_refs[-1][: step_refs[-1].shape[0] - rows]


def features(planes):
    rows, _, width = planes.shape
    boxes = rows * 16 // 3
    planes = planes.astype(F32).reshape(3, boxes, width)
    at = lax.broadcasted_iota(jnp.int32, (boxes, 8, width), 1)
    pos = jnp.zeros((boxes, 8, width), F32)
    for axis in range(3):
        pos = jnp.where(at == axis, planes[axis][:, None, :], pos)
    scale = TURN * TURN
    norm = split3(scale * jnp.sum(pos * pos, axis=1, keepdims=True))
    first = jnp.where(at < 3, pos, 1.0)
    first = jnp.where(at == 3, norm[0], jnp.where(at == 4, norm[1], jnp.where(at == 5, norm[2], first)))
    second = jnp.where(at == 3, 1.0, pos + pltpu.roll(pos, 4, 1))
    source = jnp.concatenate([first, second], axis=1).astype(BF16)
    cross = split3((-2.0 * scale) * pos)
    first = jnp.where(at < 3, cross[0], 1.0)
    first = jnp.where(at == 6, norm[0], jnp.where(at == 7, norm[1], first))
    second = jnp.where(at == 3, norm[2], cross[1] + pltpu.roll(cross[2], 4, 1))
    return source, jnp.concatenate([first, second], axis=1).astype(BF16)


def turn_sources(source, src_ref, start):
    boxes, rows, width = source.shape
    eye = lax.broadcasted_iota(jnp.int32, (width, width), 0) == lax.broadcasted_iota(jnp.int32, (width, width), 1)
    twice = jnp.concatenate([source, source], axis=1).reshape(boxes * 2 * rows, width)
    turned = nt_dot(eye.astype(F32).astype(BF16), twice)
    for b in range(boxes):
        at = b * 2 * rows
        lanes = turned[:, at // 128 * 128 : at // 128 * 128 + 128]
        if at % 128:
            lanes = pltpu.roll(lanes, 128 - at % 128, 1)
        src_ref[start + b] = lanes.astype(BF16)


def take_currents(x_rows, win_ref, start):
    for k in range(x_rows.shape[0]):
        both = x_rows[k].astype(F32)
        win_ref[start + 2 * k] = both[:8]
        win_ref[start + 2 * k + 1] = both[8:]


def near_sum(entries, total, item_at, first_source, src_ref, win_ref, obs_ref, out_ref, scratch, ahead=0):
    u0_ref, u1_ref, t0_ref, t1_ref = scratch
    boxes, waves, width = out_ref.shape
    count_bits, box_bits, source_bits = code_bits(boxes, entries)
    pair_bits = count_bits + box_bits + source_bits
    t1_ref[...] = jnp.zeros(t1_ref.shape, F32)
    left = lax.broadcasted_iota(jnp.int32, (width, 128), 1) < 16
    empty = jnp.zeros((16, width), BF16)

    def pair_at(chunk, g, slot):
        code = item_at(chunk * ITEMS + g) >> (slot * pair_bits)
        source = (code >> (count_bits + box_bits)) & ((1 << source_bits) - 1)
        if first_source:
            source = jnp.maximum(source - first_source, 0)
        return source, (code >> count_bits) & ((1 << box_bits) - 1), code & ((1 << count_bits) - 1)

    def distances(chunk, g, u_ref):
        source0, box0, _ = pair_at(chunk, g, 0)
        source1, box1, _ = pair_at(chunk, g, 1)
        sources = jnp.where(left, src_ref[source0], src_ref[source1])
        observers = jnp.concatenate(
            [
                jnp.concatenate([obs_ref[box0], empty], axis=1),
                jnp.concatenate([empty, obs_ref[box1]], axis=1),
            ],
            axis=0,
        )
        u_ref[g] = nn_dot(sources[:, :32], observers)

    def tile(g, u_ref, t_ref):
        for at in range(0, width, ROWS):
            v = jnp.maximum(u_ref[g, at : at + ROWS], 1e-12)
            q = v * lax.rsqrt(v)
            t = q - jnp.round(q)
            cosine = t * t + CHAIN[0]
            for constant in CHAIN[1:]:
                cosine = cosine * cosine + constant
            t_ref[g, at : at + ROWS] = cosine * pltpu.reciprocal(q + OFFSET * TURN, approx=True)

    def product(chunk, g, t_ref):
        source0, box0, count0 = pair_at(chunk, g, 0)
        source1, box1, count1 = pair_at(chunk, g, 1)
        currents = jnp.concatenate([win_ref[source0], win_ref[source1]], axis=0)
        got = nn_dot(currents, t_ref[g])
        out_ref[box0] += count0.astype(F32) * got[:waves, :width]
        out_ref[box1] += count1.astype(F32) * got[waves:, width:]

    u_refs = (u0_ref, u1_ref)
    t_refs = (t0_ref, t1_ref)

    def stage(chunk, turn):
        for g in range(ITEMS):
            distances(chunk + 1, g, u_refs[1 - turn])
            product(jnp.maximum(chunk - 1, 0), g, t_refs[1 - turn])
            tile(g, u_refs[turn], t_refs[turn])

    def body(k, carry):
        for j in range(STAGES):
            stage(ahead + k * STAGES + j, j & 1)
        return carry

    def finish(turn):
        for g in range(ITEMS):
            product(jnp.maximum(chunks - 1, 0), g, t_refs[turn])

    chunks = jnp.maximum((total + (ITEMS - 1)) // ITEMS, ahead)
    rounds = (chunks - ahead) // STAGES
    for g in range(ITEMS):
        distances(0, g, u0_ref)
    for j in range(ahead):
        stage(j, j & 1)
    lax.fori_loop(0, rounds, body, 0)
    last = ahead + rounds * STAGES
    for j in range(STAGES - 1):
        pl.when(last + j < chunks)(functools.partial(stage, last + j, j & 1))
    pl.when((chunks > 0) & ((chunks & 1) == 0))(functools.partial(finish, 1))
    pl.when((chunks & 1) == 1)(functools.partial(finish, 0))


def prepare_kernel(
    entries, own_ref, items_ref, src_hbm, id_hbm, count_hbm, table_hbm, out_ref, obs_ref, src_ref, win_ref, gain_ref,
    trans_src_ref, trans_id_ref, trans_count_ref, table_ref, list_ref, u0_ref, u1_ref, t0_ref, t1_ref, sems
):
    boxes = obs_ref.shape[0]
    length = list_ref.shape[1]
    parents, window = gain_ref.shape[:2]
    listed = src_hbm.shape[1]
    fetch, *trans_copies = start_all(
        (
            (items_ref, list_ref),
            (src_hbm, trans_src_ref),
            (id_hbm, trans_id_ref),
            (count_hbm, trans_count_ref),
            (table_hbm, table_ref),
        ),
        sems,
    )
    plane_rows = 3 * boxes // 16
    source, observer = features(own_ref[boxes // 2 : boxes // 2 + plane_rows])
    turn_sources(source, src_ref, 0)
    take_currents(own_ref[: boxes // 2], win_ref, 0)
    obs_ref[...] = observer
    out_ref[...] = jnp.zeros(out_ref.shape, F32)
    gain_ref[...] = jnp.zeros(gain_ref.shape, F32)
    fetch.wait()
    near_sum(
        entries,
        list_ref[0, length - 3],
        lambda k: list_ref[0, k],
        0,
        src_ref,
        win_ref,
        obs_ref,
        out_ref,
        (u0_ref, u1_ref, t0_ref, t1_ref),
    )
    wait_all(trans_copies)
    row0 = lax.axis_index("dir") * parents
    first = (lax.axis_index("box") - 1) * (window // 3)
    for q in range(parents):
        for e in range(listed):
            live = (e < trans_count_ref[row0 + q]).astype(F32)
            s = jnp.clip(trans_src_ref[row0 + q, e] - first, 0, window - 1)
            gain_ref[q, s] += table_ref[trans_id_ref[row0 + q, e]] * live


def near_kernel(entries, items_ref, *refs):
    *refs, sem = refs
    (
        *step_refs, obs_ref, first_ref, _, _, out_ref, src_ref, win_ref, list_ref, u0_ref, u1_ref, t0_ref, t1_ref
    ) = refs
    boxes, waves, width = out_ref.shape
    fetch = pltpu.make_async_copy(items_ref, list_ref, sem)
    fetch.start()
    length = list_ref.shape[1]
    here = lax.axis_index("dir")
    other_side = jnp.where((here & 1) == 0, here - 1, here + 1)
    x_rows = boxes // 2
    own_rows = x_rows + 3 * boxes // 16

    def take(packet, part):
        take_currents(packet[:x_rows], win_ref, part * boxes)
        source, _ = features(packet[x_rows:])
        turn_sources(source, src_ref, part * boxes)

    take(step_refs[0][:own_rows], 1)
    if len(step_refs) > 1:
        packet = step_refs[1][:own_rows]
        for k, ref in enumerate(step_refs[2:], 3):
            from_here = (here ^ ((1 << k) - 1)) == other_side
            packet = jnp.where(from_here, ref[:own_rows].astype(F32), packet.astype(F32)).astype(BF16)
        take(packet, 2)
    second_start = list_places(boxes, entries)[1]
    out_ref[...] = first_ref[...]
    fetch.wait()
    near_sum(
        entries,
        list_ref[0, length - 2],
        lambda k: list_ref[0, second_start + k],
        0,
        src_ref,
        win_ref,
        obs_ref,
        out_ref,
        (u0_ref, u1_ref, t0_ref, t1_ref),
    )


def incoming_kernel(entries, others, *refs):
    incoming(entries, *refs[others:], other_refs=refs[:others])


def incoming(
    entries, items_ref, even_ref, own_ref, odd_ref, gain_ref, cos_ref, sin_ref, imat_ref, rad_ref, obs_ref, near_ref, out_ref,
    sum_ref, win_ref, src_ref, down_ref, list_ref, u0_ref, u1_ref, t0_ref, t1_ref, sem, other_refs=()
):
    parents, window, _, parent_dirs = gain_ref.shape
    boxes, waves, width = near_ref.shape
    chunks = parent_dirs // 128
    group = window // 3
    fetch = pltpu.make_async_copy(items_ref, list_ref, sem)
    fetch.start()
    length = list_ref.shape[1]
    odd_box = lax.axis_index("box") & 1
    sum_ref[...] = near_ref[...]
    x_rows = boxes // 2
    packet_rows = x_rows + 3 * boxes // 16
    here = lax.axis_index("dir")
    from_even = jnp.where(here == 0, 1, 0) == odd_box
    even_packet, odd_packet = (ref[ref.shape[0] - packet_rows :] for ref in (even_ref, odd_ref))
    packet = jnp.where(from_even, even_packet.astype(F32), odd_packet.astype(F32))
    other_side = jnp.where((here & 1) == 0, here - 1, here + 1)
    for k, ref in enumerate(other_refs, 2):
        from_group = (here ^ ((1 << k) - 1)) == other_side
        packet = jnp.where(from_group, ref[:packet_rows].astype(F32), packet)
    packet = packet.astype(BF16)
    take_currents(packet[:x_rows], win_ref, 0)
    source, _ = features(packet[x_rows:])
    turn_sources(source, src_ref, 0)
    fetch.wait()
    cos_phase = cos_ref[...]
    sin_phase = sin_ref[...]
    sums = tuple(jnp.zeros((waves, 128), F32) for _ in range(parents * chunks * 2))
    for part, ref in ((2 - 2 * odd_box, even_ref), (1, own_ref), (2 * odd_box, odd_ref)):

        def add_source(s, sums, part=part, ref=ref):
            sums = list(sums)
            gains = [gain_ref[q, part * group + s] for q in range(parents)]
            for k in range(chunks):
                spectrum = ref[s * chunks + k].astype(F32)
                sre, sim = spectrum[:waves], spectrum[waves:]
                for q in range(parents):
                    gre = gains[q][0:1, k * 128 : (k + 1) * 128]
                    gim = gains[q][1:2, k * 128 : (k + 1) * 128]
                    at = (q * chunks + k) * 2
                    sums[at] = sums[at] + (gre * sre - gim * sim)
                    sums[at + 1] = sums[at + 1] + (gre * sim + gim * sre)
            return tuple(sums)

        sums = lax.fori_loop(0, group, add_source, sums, unroll=8)
    for q in range(parents):
        for k in range(chunks):
            at = (q * chunks + k) * 2
            re = sums[at].astype(BF16).astype(F32)
            im = sums[at + 1].astype(BF16).astype(F32)
            lanes = slice(k * 128, (k + 1) * 128)
            for c in range(8):
                cos, sin = cos_phase[c : c + 1, lanes], sin_phase[c : c + 1, lanes]
                rows = slice((q * 8 + c) * waves, (q * 8 + c + 1) * waves)
                down_ref[0, rows, lanes] = cos * re + sin * im
                down_ref[1, rows, lanes] = cos * im - sin * re
    imat = imat_ref[...]
    rows = boxes * waves
    both = nt_dot(down_ref[...].reshape(2 * rows, parent_dirs).astype(BF16), imat)
    incoming = jnp.concatenate([both[:rows], both[rows:]], axis=1).astype(BF16)
    far = nt_dot(incoming, rad_ref[...])
    near_sum(
        entries,
        list_ref[0, length - 1],
        lambda k: list_ref[0, length - 4 - k],
        2 * boxes,
        src_ref,
        win_ref,
        obs_ref,
        sum_ref,
        (u0_ref, u1_ref, t0_ref, t1_ref),
        AHEAD,
    )
    factor = TURN * LEAD / math.sqrt(entries * width)
    out_ref[...] = sum_ref[...] * factor + far.reshape(near_ref.shape)


def per_device(
    currents, positions, radiation, interp_index, interp_weight, child_phase, near_src, trans_src, trans_id,
    trans_count, trans_table
):
    boxes, waves, width = currents.shape
    entries = near_src.shape[1]
    leaf_dirs = radiation.shape[1] // 2
    parent_dirs = child_phase.shape[1]
    parents = boxes // 8
    spectra_rows = parents * parent_dirs // 128
    size = lax.axis_size("dir")
    vmem = pl.BlockSpec(memory_space=pltpu.VMEM)
    hbm = pl.BlockSpec(memory_space=pltpu.HBM)
    params = pltpu.CompilerParams(vmem_limit_bytes=32 * 1024 * 1024)

    def in_hbm(x):
        return pltpu.with_memory_space_constraint(x, pltpu.HBM)

    def shaped(shape, dtype):
        return jax.ShapeDtypeStruct(shape, dtype)

    x_rows = boxes // 2
    own_rows = x_rows + 3 * boxes // 16
    operands = (currents.reshape(x_rows, 2 * waves, width), positions.transpose(1, 0, 2), radiation, interp_index.T, interp_weight.T, child_phase)
    operands = operands + (near_src,)
    length = list_places(boxes, entries)[2]
    packet, spectra, imat, cos_phase, sin_phase, rad, items = pl.pallas_call(
        outgoing_kernel,
        out_shape=(
            shaped((own_rows + spectra_rows, 16, width), BF16),
            shaped((spectra_rows, 2 * waves, 128), BF16),
            shaped((leaf_dirs, parent_dirs), BF16),
            shaped((8, parent_dirs), F32),
            shaped((8, parent_dirs), F32),
            shaped(radiation.shape, BF16),
            shaped((1, length), jnp.int32),
        ),
        in_specs=[hbm] * len(operands),
        out_specs=(vmem,) * 7,
        scratch_shapes=[pltpu.VMEM(x.shape, x.dtype) for x in operands if x is not radiation]
        + [pltpu.SemaphoreType.DMA((len(operands),))],
        compiler_params=params,
        name="outgoing",
    )(*[in_hbm(x) for x in operands])

    steps = []
    for step in range(1, size):
        pairs = [(i, i ^ step) for i in range(size) if i < i ^ step]
        steps.append(swapped(packet if carries_packet(step) else spectra, "dir", pairs))

    window = 3 * trans_src.shape[0]
    near_scratch = [
        pltpu.VMEM((ITEMS, width, 2 * width), F32),
        pltpu.VMEM((ITEMS, width, 2 * width), F32),
        pltpu.VMEM((ITEMS, width, 2 * width), F32),
        pltpu.VMEM((ITEMS, width, 2 * width), F32),
    ]
    first_sum, observers, sources, ordered, gains = pl.pallas_call(
        functools.partial(prepare_kernel, entries),
        out_shape=(
            shaped((boxes, waves, width), F32),
            shaped((boxes, 16, width), BF16),
            shaped((3 * boxes, width, 128), BF16),
            shaped((3 * boxes, waves, width), F32),
            shaped((parents, window, 2, parent_dirs), F32),
        ),
        in_specs=[vmem] * 2 + [hbm] * 4,
        out_specs=(vmem,) * 5,
        scratch_shapes=[
            pltpu.SMEM(trans_src.shape, jnp.int32),
            pltpu.SMEM(trans_id.shape, jnp.int32),
            pltpu.SMEM(trans_count.shape, jnp.int32),
            pltpu.VMEM(trans_table.shape, F32),
            pltpu.SMEM((1, length), jnp.int32),
        ]
        + near_scratch
        + [pltpu.SemaphoreType.DMA((5,))],
        compiler_params=params,
        name="prepare",
    )(packet, items, *[in_hbm(x) for x in (trans_src, trans_id, trans_count, trans_table)])

    group = pl.pallas_call(
        group_kernel,
        out_shape=shaped((size * spectra_rows + own_rows, 2 * waves, 128), BF16),
        in_specs=[vmem] * (2 + len(steps)),
        out_specs=vmem,
        compiler_params=params,
        name="group",
    )(spectra, *steps, first_sum)
    groups = lax.axis_size("box")
    group_odd = swapped(group, "box", [(i, i + 1) for i in range(1, groups - 1, 2)])
    group_even = swapped(group, "box", [(i, i + 1) for i in range(0, groups - 1, 2)])

    packets = [x for step, x in enumerate(steps, 1) if carries_packet(step)]
    near, _, _ = pl.pallas_call(
        functools.partial(near_kernel, entries),
        out_shape=(
            shaped((boxes, waves, width), F32),
            shaped(sources.shape, BF16),
            shaped(ordered.shape, F32),
        ),
        in_specs=[vmem] * (5 + len(packets)),
        out_specs=(vmem,) * 3,
        input_output_aliases={3 + len(packets): 1, 4 + len(packets): 2},
        scratch_shapes=[pltpu.SMEM((1, length), jnp.int32)] + near_scratch + [pltpu.SemaphoreType.DMA],
        compiler_params=params,
        name="near",
    )(items, *packets, observers, first_sum, sources, ordered)

    return pl.pallas_call(
        functools.partial(incoming_kernel, entries, len(packets) - 1),
        out_shape=shaped((boxes, waves, width), F32),
        in_specs=[vmem] * (10 + len(packets)),
        out_specs=vmem,
        scratch_shapes=[
            pltpu.VMEM((boxes, waves, width), F32),
            pltpu.VMEM((boxes, waves, width), F32),
            pltpu.VMEM((boxes, width, 128), BF16),
            pltpu.VMEM((2, boxes * waves, parent_dirs), F32),
            pltpu.SMEM((1, length), jnp.int32),
        ]
        + near_scratch
        + [pltpu.SemaphoreType.DMA],
        compiler_params=params,
        name="incoming",
    )(*packets[1:], items, group_even, group, group_odd, gains, cos_phase, sin_phase, imat, rad, observers, near)


def solution(mesh):
    placed = (
        P(("box", "dir"), None, None),
        P(("box", "dir"), None, None),
        P(),
        P(),
        P(),
        P(),
        P(("box", "dir"), None),
        P("box", None),
        P("box", None),
        P("box"),
        P(),
    )
    return jax.shard_map(
        per_device,
        mesh=mesh,
        in_specs=placed,
        out_specs=P(("box", "dir"), None, None),
        check_vma=False,
    )
```

```python
import functools
import math

import jax
import jax.numpy as jnp
from jax import lax
from jax.experimental import pallas as pl
from jax.experimental.pallas import tpu as pltpu
from jax.sharding import PartitionSpec as P

F32 = jnp.float32
BF16 = jnp.bfloat16

WAVENUMBER = 4.0
OFFSET = 0.5
TURN = WAVENUMBER / (2.0 * math.pi)
CHAIN = (-2.2803148655023415, -1.415255674611144, -7.327656729815578, -24.467745134801202)
LEAD = 0.04087004462557604
COSINE = (
    0.9999999999990674, -0.49999999998466105, 0.04166666662512991, -0.0013888888455587084, 2.480156463978284e-05,
    -2.7556652559151664e-07, 2.08652097543821e-09, -1.135363495216746e-11, 4.13155312368983e-14,
)
SINE = (
    0.9999999999999502, -0.16666666666584865, 0.008333333331120085, -0.00019841269610529892, 2.755730716252212e-06,
    -2.5051753759896685e-08, 1.6052905945426492e-10, -7.584986682610132e-13, 2.4682378516637708e-15,
)
ITEMS = 4
ROWS = 64
STAGES = 2
FIRST_ITEMS = 6
AHEAD = 2
LEFT_OVER = 2


def round_up(value, step):
    return -(-value // step) * step


def swapped(x, axis, pairs):
    return lax.ppermute(x, axis, [way for i, j in pairs for way in ((i, j), (j, i))])


def polynomial(coefficients, z):
    value = jnp.full_like(z, coefficients[-1])
    for coefficient in coefficients[-2::-1]:
        value = value * z + coefficient
    return value


def split3(x):
    high = x.astype(BF16).astype(F32)
    rest = x - high
    mid = rest.astype(BF16).astype(F32)
    return high, mid, rest - mid


def nt_dot(a, b):
    return lax.dot_general(a, b, (((1,), (1,)), ((), ())), preferred_element_type=F32)


def nn_dot(a, b):
    return jnp.dot(a, b, preferred_element_type=F32)


def code_bits(boxes, entries):
    return entries.bit_length(), (boxes - 1).bit_length(), (3 * boxes - 1).bit_length()


def list_places(boxes, entries):
    gap = 2 * ITEMS
    most = FIRST_ITEMS * boxes // 2
    return most, most + gap, round_up(most + gap + boxes * entries // 2 + 2 * gap + 6, 128)


def list_items(near_src, block, here, size):
    boxes, entries = near_src.shape
    most, second_start, length = list_places(boxes, entries)
    count_bits, box_bits, source_bits = code_bits(boxes, entries)
    pair_bits = count_bits + box_bits + source_bits
    lanes = round_up(3 * boxes, 128)
    odd = (here & 1) == 1
    edge = (here == 0) | (here == size - 1)
    local = near_src - block * boxes
    below = local + jnp.where(odd, 2 * boxes, 3 * boxes)
    above = local + jnp.where(odd, boxes, 0)
    local = jnp.where(local < 0, below, jnp.where(local >= boxes, above, local))
    lane = lax.broadcasted_iota(jnp.int32, (boxes, lanes), 1)
    box = lax.broadcasted_iota(jnp.int32, (boxes, lanes), 0)
    count = jnp.zeros((boxes, lanes), jnp.int32)
    for e in range(entries):
        count = count + (local[:, e : e + 1] == lane).astype(jnp.int32)
    present = count > 0
    flags = present.astype(F32)
    box_row = lax.broadcasted_iota(jnp.int32, (boxes, boxes), 0)
    box_col = lax.broadcasted_iota(jnp.int32, (boxes, boxes), 1)
    rank = nn_dot((box_col < box_row).astype(F32).astype(BF16), flags.astype(BF16)).astype(jnp.int32)
    pairs = jnp.sum(flags, axis=0, keepdims=True)
    from_cross = lane >= jnp.where(edge, 2 * boxes, 3 * boxes - LEFT_OVER)
    cross_pairs = jnp.where(from_cross[:1], pairs, 0.0)
    group_pairs = jnp.where(from_cross[:1], 0.0, pairs)
    row = lax.broadcasted_iota(jnp.int32, (lanes, lanes), 0)
    col = lax.broadcasted_iota(jnp.int32, (lanes, lanes), 1)
    ahead = (row < col).astype(F32).astype(BF16)
    lists = jnp.concatenate([group_pairs, cross_pairs, jnp.zeros((6, lanes), F32)], axis=0)
    offset = nn_dot(lists.astype(BF16), ahead).astype(jnp.int32)
    own_pairs = jnp.where(lane[:1] < boxes, group_pairs, 0.0)

    def total(pairs):
        return jnp.sum(pairs, axis=1, keepdims=True).astype(jnp.int32)

    first_total = jnp.minimum(total(own_pairs), 2 * most)
    second_total = total(group_pairs) - first_total
    cross_total = total(cross_pairs)
    order = offset[0:1] + rank
    in_second = order >= first_total
    order = jnp.where(in_second, order - first_total, order)
    order = jnp.where(from_cross, offset[1:2] + rank, order)
    half = order >> 1
    place = jnp.where(from_cross, (length - 4) - half, jnp.where(in_second, second_start + half, half))
    place = jnp.where(present, place, -1)
    code = (lane << (count_bits + box_bits)) | (box << count_bits) | count
    code = jnp.where((order & 1) == 1, code << pair_bits, code)
    place_t = place.T
    code_t = code.T
    rows = 3 * boxes
    slot = lax.broadcasted_iota(jnp.int32, (rows, length), 1)
    found = jnp.zeros((rows, length), jnp.int32)
    for i in range(boxes):
        hit = place_t[:rows, i : i + 1] == slot
        found = found + jnp.where(hit, code_t[:rows, i : i + 1], 0)
    listed = jnp.sum(found, axis=0, keepdims=True)
    at = lax.broadcasted_iota(jnp.int32, (1, length), 1)
    for back, pairs in ((3, first_total), (2, second_total), (1, cross_total)):
        listed = jnp.where(at == length - back, (pairs + 1) >> 1, listed)
    return listed


def start_all(copies, sems):
    started = [pltpu.make_async_copy(src, dst, sems.at[k]) for k, (src, dst) in enumerate(copies)]
    for copy in started:
        copy.start()
    return started


def wait_all(started):
    for copy in started:
        copy.wait()


def outgoing_kernel(
    x_hbm, pos_hbm, rad_hbm, idx_hbm, wgt_hbm, phase_hbm, near_hbm, packet_ref, spectra_ref, imat_ref, cos_ref, sin_ref,
    rad_ref, items_ref, x_ref, pos_ref, idx_ref, wgt_ref, phase_ref, near_ref, sems
):
    wait_all(
        start_all(
            (
                (x_hbm, x_ref),
                (pos_hbm, pos_ref),
                (rad_hbm, rad_ref),
                (idx_hbm, idx_ref),
                (wgt_hbm, wgt_ref),
                (phase_hbm, phase_ref),
                (near_hbm, near_ref),
            ),
            sems,
        )
    )
    block = lax.axis_index(("box", "dir"))
    items_ref[...] = list_items(near_ref[...], block, lax.axis_index("dir"), lax.axis_size("dir"))
    leaf_dirs, parent_dirs = imat_ref.shape
    x_rows, _, width = x_ref.shape
    axes, boxes, _ = pos_ref.shape
    waves = x_rows * 16 // boxes
    chunks = parent_dirs // 128
    own_rows = x_rows + axes * boxes // 16
    packet_ref[:x_rows] = x_ref[...]
    packet_ref[x_rows:own_rows] = pos_ref[...].reshape(axes * boxes // 16, 16, width)
    column = lax.broadcasted_iota(jnp.int32, (leaf_dirs, parent_dirs), 0)
    imat = jnp.zeros((leaf_dirs, parent_dirs), F32)
    for s in range(idx_ref.shape[0]):
        imat = imat + jnp.where(idx_ref[s : s + 1, :] == column, wgt_ref[s : s + 1, :], 0.0)
    imat = imat.astype(BF16)
    imat_ref[...] = imat
    phase = phase_ref[...]
    cos_phase = polynomial(COSINE, phase * phase)
    sin_phase = phase * polynomial(SINE, phase * phase)
    cos_ref[...] = cos_phase
    sin_ref[...] = sin_phase
    leaf = nn_dot(x_ref[...].reshape(boxes * waves, width), rad_ref[...]).astype(BF16)
    up_re = nn_dot(leaf[:, :leaf_dirs], imat)
    up_im = nn_dot(leaf[:, leaf_dirs:], imat)
    for q in range(boxes // 8):
        re = jnp.zeros((waves, parent_dirs), F32)
        im = jnp.zeros((waves, parent_dirs), F32)
        for c in range(8):
            at = (q * 8 + c) * waves
            ure = up_re[at : at + waves]
            uim = up_im[at : at + waves]
            re = re + (cos_phase[c : c + 1] * ure - sin_phase[c : c + 1] * uim)
            im = im + (sin_phase[c : c + 1] * ure + cos_phase[c : c + 1] * uim)
        both = jnp.concatenate([re, im], axis=0).astype(BF16)
        for k in range(chunks):
            part = both[:, k * 128 : (k + 1) * 128]
            packet_ref[own_rows + q * chunks + k] = part
            spectra_ref[q * chunks + k] = part


def carries_packet(step):
    return step & (step + 1) == 0


def group_kernel(own_ref, *refs):
    *step_refs, _, group_ref = refs
    size = lax.axis_size("dir")
    rows = own_ref.shape[0]
    here = lax.axis_index("dir")
    group_ref[pl.ds(here * rows, rows)] = own_ref[...]
    for step, ref in enumerate(step_refs, 1):
        group_ref[pl.ds((here ^ step) * rows, rows)] = ref[ref.shape[0] - rows :]
    group_ref[size * rows :] = step_refs[-1][: step_refs[-1].shape[0] - rows]


def features(planes):
    rows, _, width = planes.shape
    boxes = rows * 16 // 3
    planes = planes.astype(F32).reshape(3, boxes, width)
    at = lax.broadcasted_iota(jnp.int32, (boxes, 8, width), 1)
    pos = jnp.zeros((boxes, 8, width), F32)
    for axis in range(3):
        pos = jnp.where(at == axis, planes[axis][:, None, :], pos)
    scale = TURN * TURN
    norm = split3(scale * jnp.sum(pos * pos, axis=1, keepdims=True))
    first = jnp.where(at < 3, pos, 1.0)
    first = jnp.where(at == 3, norm[0], jnp.where(at == 4, norm[1], jnp.where(at == 5, norm[2], first)))
    second = jnp.where(at == 3, 1.0, pos + pltpu.roll(pos, 4, 1))
    source = jnp.concatenate([first, second], axis=1).astype(BF16)
    cross = split3((-2.0 * scale) * pos)
    first = jnp.where(at < 3, cross[0], 1.0)
    first = jnp.where(at == 6, norm[0], jnp.where(at == 7, norm[1], first))
    second = jnp.where(at == 3, norm[2], cross[1] + pltpu.roll(cross[2], 4, 1))
    return source, jnp.concatenate([first, second], axis=1).astype(BF16)


def turn_sources(source, src_ref, start):
    boxes, rows, width = source.shape
    eye = lax.broadcasted_iota(jnp.int32, (width, width), 0) == lax.broadcasted_iota(jnp.int32, (width, width), 1)
    twice = jnp.concatenate([source, source], axis=1).reshape(boxes * 2 * rows, width)
    turned = nt_dot(eye.astype(F32).astype(BF16), twice)
    for b in range(boxes):
        at = b * 2 * rows
        lanes = turned[:, at // 128 * 128 : at // 128 * 128 + 128]
        if at % 128:
            lanes = pltpu.roll(lanes, 128 - at % 128, 1)
        src_ref[start + b] = lanes.astype(BF16)


def take_currents(x_rows, win_ref, start):
    for k in range(x_rows.shape[0]):
        both = x_rows[k].astype(F32)
        win_ref[start + 2 * k] = both[:8]
        win_ref[start + 2 * k + 1] = both[8:]


def near_sum(entries, total, item_at, first_source, src_ref, win_ref, obs_ref, out_ref, scratch, ahead=0):
    u0_ref, u1_ref, t0_ref, t1_ref = scratch
    boxes, waves, width = out_ref.shape
    count_bits, box_bits, source_bits = code_bits(boxes, entries)
    pair_bits = count_bits + box_bits + source_bits
    t1_ref[...] = jnp.zeros(t1_ref.shape, F32)
    left = lax.broadcasted_iota(jnp.int32, (width, 128), 1) < 16
    empty = jnp.zeros((16, width), BF16)

    def pair_at(chunk, g, slot):
        code = item_at(chunk * ITEMS + g) >> (slot * pair_bits)
        source = (code >> (count_bits + box_bits)) & ((1 << source_bits) - 1)
        if first_source:
            source = jnp.maximum(source - first_source, 0)
        return source, (code >> count_bits) & ((1 << box_bits) - 1), code & ((1 << count_bits) - 1)

    def distances(chunk, g, u_ref):
        source0, box0, _ = pair_at(chunk, g, 0)
        source1, box1, _ = pair_at(chunk, g, 1)
        sources = jnp.where(left, src_ref[source0], src_ref[source1])
        observers = jnp.concatenate(
            [
                jnp.concatenate([obs_ref[box0], empty], axis=1),
                jnp.concatenate([empty, obs_ref[box1]], axis=1),
            ],
            axis=0,
        )
        u_ref[g] = nn_dot(sources[:, :32], observers)

    def tile(g, u_ref, t_ref):
        for at in range(0, width, ROWS):
            v = jnp.maximum(u_ref[g, at : at + ROWS], 1e-12)
            q = v * lax.rsqrt(v)
            t = q - jnp.round(q)
            cosine = t * t + CHAIN[0]
            for constant in CHAIN[1:]:
                cosine = cosine * cosine + constant
            t_ref[g, at : at + ROWS] = cosine * pltpu.reciprocal(q + OFFSET * TURN, approx=True)

    def product(chunk, g, t_ref):
        source0, box0, count0 = pair_at(chunk, g, 0)
        source1, box1, count1 = pair_at(chunk, g, 1)
        currents = jnp.concatenate([win_ref[source0], win_ref[source1]], axis=0)
        got = nn_dot(currents, t_ref[g])
        out_ref[box0] += count0.astype(F32) * got[:waves, :width]
        out_ref[box1] += count1.astype(F32) * got[waves:, width:]

    u_refs = (u0_ref, u1_ref)
    t_refs = (t0_ref, t1_ref)

    def stage(chunk, turn):
        for g in range(ITEMS):
            distances(chunk + 1, g, u_refs[1 - turn])
            product(jnp.maximum(chunk - 1, 0), g, t_refs[1 - turn])
            tile(g, u_refs[turn], t_refs[turn])

    def body(k, carry):
        for j in range(STAGES):
            stage(ahead + k * STAGES + j, j & 1)
        return carry

    def finish(turn):
        for g in range(ITEMS):
            product(jnp.maximum(chunks - 1, 0), g, t_refs[turn])

    chunks = jnp.maximum((total + (ITEMS - 1)) // ITEMS, ahead)
    rounds = (chunks - ahead) // STAGES
    for g in range(ITEMS):
        distances(0, g, u0_ref)
    for j in range(ahead):
        stage(j, j & 1)
    lax.fori_loop(0, rounds, body, 0)
    last = ahead + rounds * STAGES
    for j in range(STAGES - 1):
        pl.when(last + j < chunks)(functools.partial(stage, last + j, j & 1))
    pl.when((chunks > 0) & ((chunks & 1) == 0))(functools.partial(finish, 1))
    pl.when((chunks & 1) == 1)(functools.partial(finish, 0))


def prepare_kernel(
    entries, parents, own_ref, items_ref, src_hbm, id_hbm, count_hbm, table_hbm, out_ref, obs_ref, src_ref, win_ref, *refs
):
    gain_refs, refs = refs[:parents], refs[parents:]
    trans_src_ref, trans_id_ref, trans_count_ref, table_ref, list_ref, u0_ref, u1_ref, t0_ref, t1_ref, sems = refs
    boxes = obs_ref.shape[0]
    length = list_ref.shape[1]
    window = gain_refs[0].shape[0]
    listed = src_hbm.shape[1]
    fetch, *trans_copies = start_all(
        (
            (items_ref, list_ref),
            (src_hbm, trans_src_ref),
            (id_hbm, trans_id_ref),
            (count_hbm, trans_count_ref),
            (table_hbm, table_ref),
        ),
        sems,
    )
    plane_rows = 3 * boxes // 16
    source, observer = features(own_ref[boxes // 2 : boxes // 2 + plane_rows])
    turn_sources(source, src_ref, 0)
    take_currents(own_ref[: boxes // 2], win_ref, 0)
    obs_ref[...] = observer
    out_ref[...] = jnp.zeros(out_ref.shape, F32)
    for gain_ref in gain_refs:
        gain_ref[...] = jnp.zeros(gain_ref.shape, F32)
    fetch.wait()
    near_sum(
        entries,
        list_ref[0, length - 3],
        lambda k: list_ref[0, k],
        0,
        src_ref,
        win_ref,
        obs_ref,
        out_ref,
        (u0_ref, u1_ref, t0_ref, t1_ref),
    )
    wait_all(trans_copies)
    row0 = lax.axis_index("dir") * parents
    first = (lax.axis_index("box") - 1) * (window // 3)
    for e in range(listed):
        for q, gain_ref in enumerate(gain_refs):
            live = (e < trans_count_ref[row0 + q]).astype(F32)
            s = jnp.clip(trans_src_ref[row0 + q, e] - first, 0, window - 1)
            gain_ref[s] += table_ref[trans_id_ref[row0 + q, e]] * live


def near_kernel(entries, items_ref, *refs):
    *refs, sem = refs
    (
        *step_refs, obs_ref, first_ref, _, _, out_ref, src_ref, win_ref, list_ref, u0_ref, u1_ref, t0_ref, t1_ref
    ) = refs
    boxes, waves, width = out_ref.shape
    fetch = pltpu.make_async_copy(items_ref, list_ref, sem)
    fetch.start()
    length = list_ref.shape[1]
    here = lax.axis_index("dir")
    other_side = jnp.where((here & 1) == 0, here - 1, here + 1)
    x_rows = boxes // 2
    own_rows = x_rows + 3 * boxes // 16

    def take(packet, part):
        take_currents(packet[:x_rows], win_ref, part * boxes)
        source, _ = features(packet[x_rows:])
        turn_sources(source, src_ref, part * boxes)

    take(step_refs[0][:own_rows], 1)
    if len(step_refs) > 1:
        packet = step_refs[1][:own_rows]
        for k, ref in enumerate(step_refs[2:], 3):
            from_here = (here ^ ((1 << k) - 1)) == other_side
            packet = jnp.where(from_here, ref[:own_rows].astype(F32), packet.astype(F32)).astype(BF16)
        take(packet, 2)
    second_start = list_places(boxes, entries)[1]
    out_ref[...] = first_ref[...]
    fetch.wait()
    near_sum(
        entries,
        list_ref[0, length - 2],
        lambda k: list_ref[0, second_start + k],
        0,
        src_ref,
        win_ref,
        obs_ref,
        out_ref,
        (u0_ref, u1_ref, t0_ref, t1_ref),
    )


def incoming_kernel(entries, others, parents, *refs):
    incoming(entries, *refs[others + parents :], other_refs=refs[:others], gain_refs=refs[others : others + parents])


def incoming(
    entries, items_ref, even_ref, own_ref, odd_ref, cos_ref, sin_ref, imat_ref, rad_ref, obs_ref, near_ref, out_ref,
    sum_ref, win_ref, src_ref, down_ref, list_ref, u0_ref, u1_ref, t0_ref, t1_ref, sem, other_refs=(),
    gain_refs=()
):
    parents = len(gain_refs)
    window, _, parent_dirs = gain_refs[0].shape
    boxes, waves, width = near_ref.shape
    chunks = parent_dirs // 128
    group = window // 3
    fetch = pltpu.make_async_copy(items_ref, list_ref, sem)
    fetch.start()
    length = list_ref.shape[1]
    odd_box = lax.axis_index("box") & 1
    sum_ref[...] = near_ref[...]
    x_rows = boxes // 2
    packet_rows = x_rows + 3 * boxes // 16
    here = lax.axis_index("dir")
    from_even = jnp.where(here == 0, 1, 0) == odd_box
    even_packet, odd_packet = (ref[ref.shape[0] - packet_rows :] for ref in (even_ref, odd_ref))
    packet = jnp.where(from_even, even_packet.astype(F32), odd_packet.astype(F32))
    other_side = jnp.where((here & 1) == 0, here - 1, here + 1)
    for k, ref in enumerate(other_refs, 2):
        from_group = (here ^ ((1 << k) - 1)) == other_side
        packet = jnp.where(from_group, ref[:packet_rows].astype(F32), packet)
    packet = packet.astype(BF16)
    take_currents(packet[:x_rows], win_ref, 0)
    source, _ = features(packet[x_rows:])
    turn_sources(source, src_ref, 0)
    fetch.wait()
    cos_phase = cos_ref[...]
    sin_phase = sin_ref[...]
    sums = tuple(jnp.zeros((waves, 128), F32) for _ in range(parents * chunks * 2))
    for part, ref in ((2 - 2 * odd_box, even_ref), (1, own_ref), (2 * odd_box, odd_ref)):

        def add_source(s, sums, part=part, ref=ref):
            sums = list(sums)
            gains = [gain_ref[part * group + s] for gain_ref in gain_refs]
            for k in range(chunks):
                spectrum = ref[s * chunks + k].astype(F32)
                sre, sim = spectrum[:waves], spectrum[waves:]
                for q in range(parents):
                    gre = gains[q][0:1, k * 128 : (k + 1) * 128]
                    gim = gains[q][1:2, k * 128 : (k + 1) * 128]
                    at = (q * chunks + k) * 2
                    sums[at] = sums[at] + (gre * sre - gim * sim)
                    sums[at + 1] = sums[at + 1] + (gre * sim + gim * sre)
            return tuple(sums)

        sums = lax.fori_loop(0, group, add_source, sums, unroll=8)
    for q in range(parents):
        for k in range(chunks):
            at = (q * chunks + k) * 2
            re = sums[at].astype(BF16).astype(F32)
            im = sums[at + 1].astype(BF16).astype(F32)
            lanes = slice(k * 128, (k + 1) * 128)
            for c in range(8):
                cos, sin = cos_phase[c : c + 1, lanes], sin_phase[c : c + 1, lanes]
                rows = slice((q * 8 + c) * waves, (q * 8 + c + 1) * waves)
                down_ref[0, rows, lanes] = cos * re + sin * im
                down_ref[1, rows, lanes] = cos * im - sin * re
    imat = imat_ref[...]
    rows = boxes * waves
    both = nt_dot(down_ref[...].reshape(2 * rows, parent_dirs).astype(BF16), imat)
    incoming = jnp.concatenate([both[:rows], both[rows:]], axis=1).astype(BF16)
    far = nt_dot(incoming, rad_ref[...])
    near_sum(
        entries,
        list_ref[0, length - 1],
        lambda k: list_ref[0, length - 4 - k],
        2 * boxes,
        src_ref,
        win_ref,
        obs_ref,
        sum_ref,
        (u0_ref, u1_ref, t0_ref, t1_ref),
        AHEAD,
    )
    factor = TURN * LEAD / math.sqrt(entries * width)
    out_ref[...] = sum_ref[...] * factor + far.reshape(near_ref.shape)


def per_device(
    currents, positions, radiation, interp_index, interp_weight, child_phase, near_src, trans_src, trans_id,
    trans_count, trans_table
):
    boxes, waves, width = currents.shape
    entries = near_src.shape[1]
    leaf_dirs = radiation.shape[1] // 2
    parent_dirs = child_phase.shape[1]
    parents = boxes // 8
    spectra_rows = parents * parent_dirs // 128
    size = lax.axis_size("dir")
    vmem = pl.BlockSpec(memory_space=pltpu.VMEM)
    hbm = pl.BlockSpec(memory_space=pltpu.HBM)
    params = pltpu.CompilerParams(vmem_limit_bytes=32 * 1024 * 1024)

    def in_hbm(x):
        return pltpu.with_memory_space_constraint(x, pltpu.HBM)

    def shaped(shape, dtype):
        return jax.ShapeDtypeStruct(shape, dtype)

    x_rows = boxes // 2
    own_rows = x_rows + 3 * boxes // 16
    operands = (currents.reshape(x_rows, 2 * waves, width), positions.transpose(1, 0, 2), radiation, interp_index.T, interp_weight.T, child_phase)
    operands = operands + (near_src,)
    length = list_places(boxes, entries)[2]
    packet, spectra, imat, cos_phase, sin_phase, rad, items = pl.pallas_call(
        outgoing_kernel,
        out_shape=(
            shaped((own_rows + spectra_rows, 16, width), BF16),
            shaped((spectra_rows, 2 * waves, 128), BF16),
            shaped((leaf_dirs, parent_dirs), BF16),
            shaped((8, parent_dirs), F32),
            shaped((8, parent_dirs), F32),
            shaped(radiation.shape, BF16),
            shaped((1, length), jnp.int32),
        ),
        in_specs=[hbm] * len(operands),
        out_specs=(vmem,) * 7,
        scratch_shapes=[pltpu.VMEM(x.shape, x.dtype) for x in operands if x is not radiation]
        + [pltpu.SemaphoreType.DMA((len(operands),))],
        compiler_params=params,
        name="outgoing",
    )(*[in_hbm(x) for x in operands])

    steps = []
    for step in range(1, size):
        pairs = [(i, i ^ step) for i in range(size) if i < i ^ step]
        steps.append(swapped(packet if carries_packet(step) else spectra, "dir", pairs))

    window = 3 * trans_src.shape[0]
    near_scratch = [
        pltpu.VMEM((ITEMS, width, 2 * width), F32),
        pltpu.VMEM((ITEMS, width, 2 * width), F32),
        pltpu.VMEM((ITEMS, width, 2 * width), F32),
        pltpu.VMEM((ITEMS, width, 2 * width), F32),
    ]
    first_sum, observers, sources, ordered, *gains = pl.pallas_call(
        functools.partial(prepare_kernel, entries, parents),
        out_shape=(
            shaped((boxes, waves, width), F32),
            shaped((boxes, 16, width), BF16),
            shaped((3 * boxes, width, 128), BF16),
            shaped((3 * boxes, waves, width), F32),
        )
        + (shaped((window, 2, parent_dirs), F32),) * parents,
        in_specs=[vmem] * 2 + [hbm] * 4,
        out_specs=(vmem,) * (4 + parents),
        scratch_shapes=[
            pltpu.SMEM(trans_src.shape, jnp.int32),
            pltpu.SMEM(trans_id.shape, jnp.int32),
            pltpu.SMEM(trans_count.shape, jnp.int32),
            pltpu.VMEM(trans_table.shape, F32),
            pltpu.SMEM((1, length), jnp.int32),
        ]
        + near_scratch
        + [pltpu.SemaphoreType.DMA((5,))],
        compiler_params=params,
        name="prepare",
    )(packet, items, *[in_hbm(x) for x in (trans_src, trans_id, trans_count, trans_table)])

    group = pl.pallas_call(
        group_kernel,
        out_shape=shaped((size * spectra_rows + own_rows, 2 * waves, 128), BF16),
        in_specs=[vmem] * (2 + len(steps)),
        out_specs=vmem,
        compiler_params=params,
        name="group",
    )(spectra, *steps, first_sum)
    groups = lax.axis_size("box")
    group_odd = swapped(group, "box", [(i, i + 1) for i in range(1, groups - 1, 2)])
    group_even = swapped(group, "box", [(i, i + 1) for i in range(0, groups - 1, 2)])

    packets = [x for step, x in enumerate(steps, 1) if carries_packet(step)]
    near, _, _ = pl.pallas_call(
        functools.partial(near_kernel, entries),
        out_shape=(
            shaped((boxes, waves, width), F32),
            shaped(sources.shape, BF16),
            shaped(ordered.shape, F32),
        ),
        in_specs=[vmem] * (5 + len(packets)),
        out_specs=(vmem,) * 3,
        input_output_aliases={3 + len(packets): 1, 4 + len(packets): 2},
        scratch_shapes=[pltpu.SMEM((1, length), jnp.int32)] + near_scratch + [pltpu.SemaphoreType.DMA],
        compiler_params=params,
        name="near",
    )(items, *packets, observers, first_sum, sources, ordered)

    return pl.pallas_call(
        functools.partial(incoming_kernel, entries, len(packets) - 1, parents),
        out_shape=shaped((boxes, waves, width), F32),
        in_specs=[vmem] * (9 + parents + len(packets)),
        out_specs=vmem,
        scratch_shapes=[
            pltpu.VMEM((boxes, waves, width), F32),
            pltpu.VMEM((boxes, waves, width), F32),
            pltpu.VMEM((boxes, width, 128), BF16),
            pltpu.VMEM((2, boxes * waves, parent_dirs), F32),
            pltpu.SMEM((1, length), jnp.int32),
        ]
        + near_scratch
        + [pltpu.SemaphoreType.DMA],
        compiler_params=params,
        name="incoming",
    )(*packets[1:], *gains, items, group_even, group, group_odd, cos_phase, sin_phase, imat, rad, observers, near)


def solution(mesh):
    placed = (
        P(("box", "dir"), None, None),
        P(("box", "dir"), None, None),
        P(),
        P(),
        P(),
        P(),
        P(("box", "dir"), None),
        P("box", None),
        P("box", None),
        P("box"),
        P(),
    )
    return jax.shard_map(
        per_device,
        mesh=mesh,
        in_specs=placed,
        out_specs=P(("box", "dir"), None, None),
        check_vma=False,
    )
```

```python
import functools
import math

import jax
import jax.numpy as jnp
from jax import lax
from jax.experimental import pallas as pl
from jax.experimental.pallas import tpu as pltpu
from jax.sharding import PartitionSpec as P

F32 = jnp.float32
BF16 = jnp.bfloat16

WAVENUMBER = 4.0
OFFSET = 0.5
TURN = WAVENUMBER / (2.0 * math.pi)
CHAIN = (-2.2803148655023415, -1.415255674611144, -7.327656729815578, -24.467745134801202)
LEAD = 0.04087004462557604
COSINE = (
    0.9999999999990674, -0.49999999998466105, 0.04166666662512991, -0.0013888888455587084, 2.480156463978284e-05,
    -2.7556652559151664e-07, 2.08652097543821e-09, -1.135363495216746e-11, 4.13155312368983e-14,
)
SINE = (
    0.9999999999999502, -0.16666666666584865, 0.008333333331120085, -0.00019841269610529892, 2.755730716252212e-06,
    -2.5051753759896685e-08, 1.6052905945426492e-10, -7.584986682610132e-13, 2.4682378516637708e-15,
)
ITEMS = 4
ROWS = 64
STAGES = 2
FIRST_ITEMS = 6
AHEAD = 2
LEFT_OVER = 2


def round_up(value, step):
    return -(-value // step) * step


def swapped(x, axis, pairs):
    return lax.ppermute(x, axis, [way for i, j in pairs for way in ((i, j), (j, i))])


def polynomial(coefficients, z):
    value = jnp.full_like(z, coefficients[-1])
    for coefficient in coefficients[-2::-1]:
        value = value * z + coefficient
    return value


def split3(x):
    high = x.astype(BF16).astype(F32)
    rest = x - high
    mid = rest.astype(BF16).astype(F32)
    return high, mid, rest - mid


def nt_dot(a, b):
    return lax.dot_general(a, b, (((1,), (1,)), ((), ())), preferred_element_type=F32)


def nn_dot(a, b):
    return jnp.dot(a, b, preferred_element_type=F32)


def code_bits(boxes, entries):
    return entries.bit_length(), (boxes - 1).bit_length(), (3 * boxes - 1).bit_length()


def list_places(boxes, entries):
    gap = 2 * ITEMS
    most = FIRST_ITEMS * boxes // 2
    return most, most + gap, round_up(most + gap + boxes * entries // 2 + 2 * gap + 6, 128)


def list_items(near_src, block, here, size):
    boxes, entries = near_src.shape
    most, second_start, length = list_places(boxes, entries)
    count_bits, box_bits, source_bits = code_bits(boxes, entries)
    pair_bits = count_bits + box_bits + source_bits
    lanes = round_up(3 * boxes, 128)
    odd = (here & 1) == 1
    edge = (here == 0) | (here == size - 1)
    local = near_src - block * boxes
    below = local + jnp.where(odd, 2 * boxes, 3 * boxes)
    above = local + jnp.where(odd, boxes, 0)
    local = jnp.where(local < 0, below, jnp.where(local >= boxes, above, local))
    lane = lax.broadcasted_iota(jnp.int32, (boxes, lanes), 1)
    box = lax.broadcasted_iota(jnp.int32, (boxes, lanes), 0)
    count = jnp.zeros((boxes, lanes), jnp.int32)
    for e in range(entries):
        count = count + (local[:, e : e + 1] == lane).astype(jnp.int32)
    present = count > 0
    flags = present.astype(F32)
    box_row = lax.broadcasted_iota(jnp.int32, (boxes, boxes), 0)
    box_col = lax.broadcasted_iota(jnp.int32, (boxes, boxes), 1)
    rank = nn_dot((box_col < box_row).astype(F32).astype(BF16), flags.astype(BF16)).astype(jnp.int32)
    pairs = jnp.sum(flags, axis=0, keepdims=True)
    from_cross = lane >= jnp.where(edge, 2 * boxes, 3 * boxes - LEFT_OVER)
    cross_pairs = jnp.where(from_cross[:1], pairs, 0.0)
    group_pairs = jnp.where(from_cross[:1], 0.0, pairs)
    row = lax.broadcasted_iota(jnp.int32, (lanes, lanes), 0)
    col = lax.broadcasted_iota(jnp.int32, (lanes, lanes), 1)
    ahead = (row < col).astype(F32).astype(BF16)
    lists = jnp.concatenate([group_pairs, cross_pairs, jnp.zeros((6, lanes), F32)], axis=0)
    offset = nn_dot(lists.astype(BF16), ahead).astype(jnp.int32)
    own_pairs = jnp.where(lane[:1] < boxes, group_pairs, 0.0)

    def total(pairs):
        return jnp.sum(pairs, axis=1, keepdims=True).astype(jnp.int32)

    first_total = jnp.minimum(total(own_pairs), 2 * most)
    second_total = total(group_pairs) - first_total
    cross_total = total(cross_pairs)
    order = offset[0:1] + rank
    in_second = order >= first_total
    order = jnp.where(in_second, order - first_total, order)
    order = jnp.where(from_cross, offset[1:2] + rank, order)
    half = order >> 1
    place = jnp.where(from_cross, (length - 4) - half, jnp.where(in_second, second_start + half, half))
    place = jnp.where(present, place, -1)
    code = (lane << (count_bits + box_bits)) | (box << count_bits) | count
    code = jnp.where((order & 1) == 1, code << pair_bits, code)
    place_t = place.T
    code_t = code.T
    rows = 3 * boxes
    slot = lax.broadcasted_iota(jnp.int32, (rows, length), 1)
    found = jnp.zeros((rows, length), jnp.int32)
    for i in range(boxes):
        hit = place_t[:rows, i : i + 1] == slot
        found = found + jnp.where(hit, code_t[:rows, i : i + 1], 0)
    listed = jnp.sum(found, axis=0, keepdims=True)
    at = lax.broadcasted_iota(jnp.int32, (1, length), 1)
    for back, pairs in ((3, first_total), (2, second_total), (1, cross_total)):
        listed = jnp.where(at == length - back, (pairs + 1) >> 1, listed)
    return listed


def start_all(copies, sems):
    started = [pltpu.make_async_copy(src, dst, sems.at[k]) for k, (src, dst) in enumerate(copies)]
    for copy in started:
        copy.start()
    return started


def wait_all(started):
    for copy in started:
        copy.wait()


def outgoing_kernel(
    x_hbm, pos_hbm, rad_hbm, idx_hbm, wgt_hbm, phase_hbm, near_hbm, packet_ref, spectra_ref, imat_ref, cos_ref, sin_ref,
    rad_ref, items_ref, x_ref, pos_ref, idx_ref, wgt_ref, phase_ref, near_ref, sems
):
    wait_all(
        start_all(
            (
                (x_hbm, x_ref),
                (pos_hbm, pos_ref),
                (rad_hbm, rad_ref),
                (idx_hbm, idx_ref),
                (wgt_hbm, wgt_ref),
                (phase_hbm, phase_ref),
                (near_hbm, near_ref),
            ),
            sems,
        )
    )
    block = lax.axis_index(("box", "dir"))
    items_ref[...] = list_items(near_ref[...], block, lax.axis_index("dir"), lax.axis_size("dir"))
    leaf_dirs, parent_dirs = imat_ref.shape
    x_rows, _, width = x_ref.shape
    axes, boxes, _ = pos_ref.shape
    waves = x_rows * 16 // boxes
    chunks = parent_dirs // 128
    own_rows = x_rows + axes * boxes // 16
    packet_ref[:x_rows] = x_ref[...]
    packet_ref[x_rows:own_rows] = pos_ref[...].reshape(axes * boxes // 16, 16, width)
    column = lax.broadcasted_iota(jnp.int32, (leaf_dirs, parent_dirs), 0)
    imat = jnp.zeros((leaf_dirs, parent_dirs), F32)
    for s in range(idx_ref.shape[0]):
        imat = imat + jnp.where(idx_ref[s : s + 1, :] == column, wgt_ref[s : s + 1, :], 0.0)
    imat = imat.astype(BF16)
    imat_ref[...] = imat
    phase = phase_ref[...]
    cos_phase = polynomial(COSINE, phase * phase)
    sin_phase = phase * polynomial(SINE, phase * phase)
    cos_ref[...] = cos_phase
    sin_ref[...] = sin_phase
    leaf = nn_dot(x_ref[...].reshape(boxes * waves, width), rad_ref[...]).astype(BF16)
    up_re = nn_dot(leaf[:, :leaf_dirs], imat)
    up_im = nn_dot(leaf[:, leaf_dirs:], imat)
    for q in range(boxes // 8):
        re = jnp.zeros((waves, parent_dirs), F32)
        im = jnp.zeros((waves, parent_dirs), F32)
        for c in range(8):
            at = (q * 8 + c) * waves
            ure = up_re[at : at + waves]
            uim = up_im[at : at + waves]
            re = re + (cos_phase[c : c + 1] * ure - sin_phase[c : c + 1] * uim)
            im = im + (sin_phase[c : c + 1] * ure + cos_phase[c : c + 1] * uim)
        both = jnp.concatenate([re, im], axis=0).astype(BF16)
        for k in range(chunks):
            part = both[:, k * 128 : (k + 1) * 128]
            packet_ref[own_rows + q * chunks + k] = part
            spectra_ref[q * chunks + k] = part


def carries_packet(step):
    return step & (step + 1) == 0


def group_kernel(own_ref, *refs):
    *step_refs, _, group_ref = refs
    size = lax.axis_size("dir")
    rows = own_ref.shape[0]
    here = lax.axis_index("dir")
    group_ref[pl.ds(here * rows, rows)] = own_ref[...]
    for step, ref in enumerate(step_refs, 1):
        group_ref[pl.ds((here ^ step) * rows, rows)] = ref[ref.shape[0] - rows :]
    group_ref[size * rows :] = step_refs[-1][: step_refs[-1].shape[0] - rows]


def features(planes):
    rows, _, width = planes.shape
    boxes = rows * 16 // 3
    planes = planes.astype(F32).reshape(3, boxes, width)
    at = lax.broadcasted_iota(jnp.int32, (boxes, 8, width), 1)
    pos = jnp.zeros((boxes, 8, width), F32)
    for axis in range(3):
        pos = jnp.where(at == axis, planes[axis][:, None, :], pos)
    scale = TURN * TURN
    norm = split3(scale * jnp.sum(pos * pos, axis=1, keepdims=True))
    first = jnp.where(at < 3, pos, 1.0)
    first = jnp.where(at == 3, norm[0], jnp.where(at == 4, norm[1], jnp.where(at == 5, norm[2], first)))
    second = jnp.where(at == 3, 1.0, pos + pltpu.roll(pos, 4, 1))
    source = jnp.concatenate([first, second], axis=1).astype(BF16)
    cross = split3((-2.0 * scale) * pos)
    first = jnp.where(at < 3, cross[0], 1.0)
    first = jnp.where(at == 6, norm[0], jnp.where(at == 7, norm[1], first))
    second = jnp.where(at == 3, norm[2], cross[1] + pltpu.roll(cross[2], 4, 1))
    return source, jnp.concatenate([first, second], axis=1).astype(BF16)


def turn_sources(source, src_ref, start):
    boxes, rows, width = source.shape
    eye = lax.broadcasted_iota(jnp.int32, (width, width), 0) == lax.broadcasted_iota(jnp.int32, (width, width), 1)
    twice = jnp.concatenate([source, source], axis=1).reshape(boxes * 2 * rows, width)
    turned = nt_dot(eye.astype(F32).astype(BF16), twice)
    for b in range(boxes):
        at = b * 2 * rows
        lanes = turned[:, at // 128 * 128 : at // 128 * 128 + 128]
        if at % 128:
            lanes = pltpu.roll(lanes, 128 - at % 128, 1)
        src_ref[start + b] = lanes.astype(BF16)


def take_currents(x_rows, win_ref, start):
    for k in range(x_rows.shape[0]):
        both = x_rows[k].astype(F32)
        win_ref[start + 2 * k] = both[:8]
        win_ref[start + 2 * k + 1] = both[8:]


def near_sum(entries, total, item_at, first_source, src_ref, win_ref, obs_ref, out_ref, scratch, ahead=0):
    u0_ref, u1_ref, t0_ref, t1_ref = scratch
    boxes, waves, width = out_ref.shape
    count_bits, box_bits, source_bits = code_bits(boxes, entries)
    pair_bits = count_bits + box_bits + source_bits
    t1_ref[...] = jnp.zeros(t1_ref.shape, F32)
    left = lax.broadcasted_iota(jnp.int32, (width, 128), 1) < 16
    empty = jnp.zeros((16, width), BF16)

    def pair_at(chunk, g, slot):
        code = item_at(chunk * ITEMS + g) >> (slot * pair_bits)
        source = (code >> (count_bits + box_bits)) & ((1 << source_bits) - 1)
        if first_source:
            source = jnp.maximum(source - first_source, 0)
        return source, (code >> count_bits) & ((1 << box_bits) - 1), code & ((1 << count_bits) - 1)

    def distances(chunk, g, u_ref):
        source0, box0, _ = pair_at(chunk, g, 0)
        source1, box1, _ = pair_at(chunk, g, 1)
        sources = jnp.where(left, src_ref[source0], src_ref[source1])
        observers = jnp.concatenate(
            [
                jnp.concatenate([obs_ref[box0], empty], axis=1),
                jnp.concatenate([empty, obs_ref[box1]], axis=1),
            ],
            axis=0,
        )
        u_ref[g] = nn_dot(sources[:, :32], observers)

    def tile(g, u_ref, t_ref):
        for at in range(0, width, ROWS):
            v = jnp.maximum(u_ref[g, at : at + ROWS], 1e-12)
            q = v * lax.rsqrt(v)
            t = q - jnp.round(q)
            cosine = t * t + CHAIN[0]
            for constant in CHAIN[1:]:
                cosine = cosine * cosine + constant
            t_ref[g, at : at + ROWS] = cosine * pltpu.reciprocal(q + OFFSET * TURN, approx=True)

    def product(chunk, g, t_ref):
        source0, box0, count0 = pair_at(chunk, g, 0)
        source1, box1, count1 = pair_at(chunk, g, 1)
        currents = jnp.concatenate([win_ref[source0], win_ref[source1]], axis=0)
        got = nn_dot(currents, t_ref[g])
        out_ref[box0] += count0.astype(F32) * got[:waves, :width]
        out_ref[box1] += count1.astype(F32) * got[waves:, width:]

    u_refs = (u0_ref, u1_ref)
    t_refs = (t0_ref, t1_ref)

    def stage(chunk, turn):
        for g in range(ITEMS):
            distances(chunk + 1, g, u_refs[1 - turn])
            product(jnp.maximum(chunk - 1, 0), g, t_refs[1 - turn])
            tile(g, u_refs[turn], t_refs[turn])

    def body(k, carry):
        for j in range(STAGES):
            stage(ahead + k * STAGES + j, j & 1)
        return carry

    def finish(turn):
        for g in range(ITEMS):
            product(jnp.maximum(chunks - 1, 0), g, t_refs[turn])

    chunks = jnp.maximum((total + (ITEMS - 1)) // ITEMS, ahead)
    rounds = (chunks - ahead) // STAGES
    for g in range(ITEMS):
        distances(0, g, u0_ref)
    for j in range(ahead):
        stage(j, j & 1)
    lax.fori_loop(0, rounds, body, 0)
    last = ahead + rounds * STAGES
    for j in range(STAGES - 1):
        pl.when(last + j < chunks)(functools.partial(stage, last + j, j & 1))
    pl.when((chunks > 0) & ((chunks & 1) == 0))(functools.partial(finish, 1))
    pl.when((chunks & 1) == 1)(functools.partial(finish, 0))


def prepare_kernel(
    entries, parents, own_ref, items_ref, src_hbm, id_hbm, count_hbm, table_hbm, out_ref, obs_ref, src_ref, win_ref, *refs
):
    gain_refs, refs = refs[:parents], refs[parents:]
    trans_src_ref, trans_id_ref, trans_count_ref, table_ref, list_ref, u0_ref, u1_ref, t0_ref, t1_ref, sems = refs
    boxes = obs_ref.shape[0]
    length = list_ref.shape[1]
    window = gain_refs[0].shape[0]
    listed = src_hbm.shape[1]
    fetch, *trans_copies = start_all(
        (
            (items_ref, list_ref),
            (src_hbm, trans_src_ref),
            (id_hbm, trans_id_ref),
            (count_hbm, trans_count_ref),
            (table_hbm, table_ref),
        ),
        sems,
    )
    plane_rows = 3 * boxes // 16
    source, observer = features(own_ref[boxes // 2 : boxes // 2 + plane_rows])
    turn_sources(source, src_ref, 0)
    take_currents(own_ref[: boxes // 2], win_ref, 0)
    obs_ref[...] = observer
    out_ref[...] = jnp.zeros(out_ref.shape, F32)
    for gain_ref in gain_refs:
        gain_ref[...] = jnp.zeros(gain_ref.shape, F32)
    fetch.wait()
    near_sum(
        entries,
        list_ref[0, length - 3],
        lambda k: list_ref[0, k],
        0,
        src_ref,
        win_ref,
        obs_ref,
        out_ref,
        (u0_ref, u1_ref, t0_ref, t1_ref),
    )
    wait_all(trans_copies)
    row0 = lax.axis_index("dir") * parents
    first = (lax.axis_index("box") - 1) * (window // 3)
    for e in range(listed):
        for q, gain_ref in enumerate(gain_refs):
            live = (e < trans_count_ref[row0 + q]).astype(F32)
            s = jnp.clip(trans_src_ref[row0 + q, e] - first, 0, window - 1)
            gain_ref[s] += table_ref[trans_id_ref[row0 + q, e]] * live


def near_kernel(entries, items_ref, *refs):
    *refs, sem = refs
    (
        *step_refs, obs_ref, first_ref, _, _, out_ref, src_ref, win_ref, list_ref, u0_ref, u1_ref, t0_ref, t1_ref
    ) = refs
    boxes, waves, width = out_ref.shape
    fetch = pltpu.make_async_copy(items_ref, list_ref, sem)
    fetch.start()
    length = list_ref.shape[1]
    here = lax.axis_index("dir")
    other_side = jnp.where((here & 1) == 0, here - 1, here + 1)
    x_rows = boxes // 2
    own_rows = x_rows + 3 * boxes // 16

    def take(packet, part):
        take_currents(packet[:x_rows], win_ref, part * boxes)
        source, _ = features(packet[x_rows:])
        turn_sources(source, src_ref, part * boxes)

    take(step_refs[0][:own_rows], 1)
    if len(step_refs) > 1:

        @pl.when((here != 0) & (here != lax.axis_size("dir") - 1))
        def _():
            packet = step_refs[1][:own_rows]
            for k, ref in enumerate(step_refs[2:], 3):
                from_here = (here ^ ((1 << k) - 1)) == other_side
                packet = jnp.where(from_here, ref[:own_rows].astype(F32), packet.astype(F32)).astype(BF16)
            take(packet, 2)

    second_start = list_places(boxes, entries)[1]
    out_ref[...] = first_ref[...]
    fetch.wait()
    near_sum(
        entries,
        list_ref[0, length - 2],
        lambda k: list_ref[0, second_start + k],
        0,
        src_ref,
        win_ref,
        obs_ref,
        out_ref,
        (u0_ref, u1_ref, t0_ref, t1_ref),
    )


def incoming_kernel(entries, others, parents, *refs):
    incoming(entries, *refs[others + parents :], other_refs=refs[:others], gain_refs=refs[others : others + parents])


def incoming(
    entries, items_ref, even_ref, own_ref, odd_ref, cos_ref, sin_ref, imat_ref, rad_ref, obs_ref, near_ref, out_ref,
    sum_ref, win_ref, src_ref, down_ref, list_ref, u0_ref, u1_ref, t0_ref, t1_ref, sem, other_refs=(),
    gain_refs=()
):
    parents = len(gain_refs)
    window, _, parent_dirs = gain_refs[0].shape
    boxes, waves, width = near_ref.shape
    chunks = parent_dirs // 128
    group = window // 3
    fetch = pltpu.make_async_copy(items_ref, list_ref, sem)
    fetch.start()
    length = list_ref.shape[1]
    odd_box = lax.axis_index("box") & 1
    sum_ref[...] = near_ref[...]
    x_rows = boxes // 2
    packet_rows = x_rows + 3 * boxes // 16
    here = lax.axis_index("dir")
    from_even = jnp.where(here == 0, 1, 0) == odd_box
    even_packet, odd_packet = (ref[ref.shape[0] - packet_rows :] for ref in (even_ref, odd_ref))
    packet = jnp.where(from_even, even_packet.astype(F32), odd_packet.astype(F32))
    other_side = jnp.where((here & 1) == 0, here - 1, here + 1)
    for k, ref in enumerate(other_refs, 2):
        from_group = (here ^ ((1 << k) - 1)) == other_side
        packet = jnp.where(from_group, ref[:packet_rows].astype(F32), packet)
    packet = packet.astype(BF16)
    take_currents(packet[:x_rows], win_ref, 0)
    source, _ = features(packet[x_rows:])
    turn_sources(source, src_ref, 0)
    fetch.wait()
    cos_phase = cos_ref[...]
    sin_phase = sin_ref[...]
    sums = tuple(jnp.zeros((waves, 128), F32) for _ in range(parents * chunks * 2))
    for part, ref in ((2 - 2 * odd_box, even_ref), (1, own_ref), (2 * odd_box, odd_ref)):

        def add_source(s, sums, part=part, ref=ref):
            sums = list(sums)
            gains = [gain_ref[part * group + s] for gain_ref in gain_refs]
            for k in range(chunks):
                spectrum = ref[s * chunks + k].astype(F32)
                sre, sim = spectrum[:waves], spectrum[waves:]
                for q in range(parents):
                    gre = gains[q][0:1, k * 128 : (k + 1) * 128]
                    gim = gains[q][1:2, k * 128 : (k + 1) * 128]
                    at = (q * chunks + k) * 2
                    sums[at] = sums[at] + (gre * sre - gim * sim)
                    sums[at + 1] = sums[at + 1] + (gre * sim + gim * sre)
            return tuple(sums)

        sums = lax.fori_loop(0, group, add_source, sums, unroll=8)
    for q in range(parents):
        for k in range(chunks):
            at = (q * chunks + k) * 2
            re = sums[at].astype(BF16).astype(F32)
            im = sums[at + 1].astype(BF16).astype(F32)
            lanes = slice(k * 128, (k + 1) * 128)
            for c in range(8):
                cos, sin = cos_phase[c : c + 1, lanes], sin_phase[c : c + 1, lanes]
                rows = slice((q * 8 + c) * waves, (q * 8 + c + 1) * waves)
                down_ref[0, rows, lanes] = cos * re + sin * im
                down_ref[1, rows, lanes] = cos * im - sin * re
    imat = imat_ref[...]
    rows = boxes * waves
    both = nt_dot(down_ref[...].reshape(2 * rows, parent_dirs).astype(BF16), imat)
    incoming = jnp.concatenate([both[:rows], both[rows:]], axis=1).astype(BF16)
    far = nt_dot(incoming, rad_ref[...])
    near_sum(
        entries,
        list_ref[0, length - 1],
        lambda k: list_ref[0, length - 4 - k],
        2 * boxes,
        src_ref,
        win_ref,
        obs_ref,
        sum_ref,
        (u0_ref, u1_ref, t0_ref, t1_ref),
        AHEAD,
    )
    factor = TURN * LEAD / math.sqrt(entries * width)
    out_ref[...] = sum_ref[...] * factor + far.reshape(near_ref.shape)


def per_device(
    currents, positions, radiation, interp_index, interp_weight, child_phase, near_src, trans_src, trans_id,
    trans_count, trans_table
):
    boxes, waves, width = currents.shape
    entries = near_src.shape[1]
    leaf_dirs = radiation.shape[1] // 2
    parent_dirs = child_phase.shape[1]
    parents = boxes // 8
    spectra_rows = parents * parent_dirs // 128
    size = lax.axis_size("dir")
    vmem = pl.BlockSpec(memory_space=pltpu.VMEM)
    hbm = pl.BlockSpec(memory_space=pltpu.HBM)
    params = pltpu.CompilerParams(vmem_limit_bytes=32 * 1024 * 1024)

    def in_hbm(x):
        return pltpu.with_memory_space_constraint(x, pltpu.HBM)

    def shaped(shape, dtype):
        return jax.ShapeDtypeStruct(shape, dtype)

    x_rows = boxes // 2
    own_rows = x_rows + 3 * boxes // 16
    operands = (currents.reshape(x_rows, 2 * waves, width), positions.transpose(1, 0, 2), radiation, interp_index.T, interp_weight.T, child_phase)
    operands = operands + (near_src,)
    length = list_places(boxes, entries)[2]
    packet, spectra, imat, cos_phase, sin_phase, rad, items = pl.pallas_call(
        outgoing_kernel,
        out_shape=(
            shaped((own_rows + spectra_rows, 16, width), BF16),
            shaped((spectra_rows, 2 * waves, 128), BF16),
            shaped((leaf_dirs, parent_dirs), BF16),
            shaped((8, parent_dirs), F32),
            shaped((8, parent_dirs), F32),
            shaped(radiation.shape, BF16),
            shaped((1, length), jnp.int32),
        ),
        in_specs=[hbm] * len(operands),
        out_specs=(vmem,) * 7,
        scratch_shapes=[pltpu.VMEM(x.shape, x.dtype) for x in operands if x is not radiation]
        + [pltpu.SemaphoreType.DMA((len(operands),))],
        compiler_params=params,
        name="outgoing",
    )(*[in_hbm(x) for x in operands])

    steps = []
    for step in range(1, size):
        pairs = [(i, i ^ step) for i in range(size) if i < i ^ step]
        steps.append(swapped(packet if carries_packet(step) else spectra, "dir", pairs))

    window = 3 * trans_src.shape[0]
    near_scratch = [
        pltpu.VMEM((ITEMS, width, 2 * width), F32),
        pltpu.VMEM((ITEMS, width, 2 * width), F32),
        pltpu.VMEM((ITEMS, width, 2 * width), F32),
        pltpu.VMEM((ITEMS, width, 2 * width), F32),
    ]
    first_sum, observers, sources, ordered, *gains = pl.pallas_call(
        functools.partial(prepare_kernel, entries, parents),
        out_shape=(
            shaped((boxes, waves, width), F32),
            shaped((boxes, 16, width), BF16),
            shaped((3 * boxes, width, 128), BF16),
            shaped((3 * boxes, waves, width), F32),
        )
        + (shaped((window, 2, parent_dirs), F32),) * parents,
        in_specs=[vmem] * 2 + [hbm] * 4,
        out_specs=(vmem,) * (4 + parents),
        scratch_shapes=[
            pltpu.SMEM(trans_src.shape, jnp.int32),
            pltpu.SMEM(trans_id.shape, jnp.int32),
            pltpu.SMEM(trans_count.shape, jnp.int32),
            pltpu.VMEM(trans_table.shape, F32),
            pltpu.SMEM((1, length), jnp.int32),
        ]
        + near_scratch
        + [pltpu.SemaphoreType.DMA((5,))],
        compiler_params=params,
        name="prepare",
    )(packet, items, *[in_hbm(x) for x in (trans_src, trans_id, trans_count, trans_table)])

    group = pl.pallas_call(
        group_kernel,
        out_shape=shaped((size * spectra_rows + own_rows, 2 * waves, 128), BF16),
        in_specs=[vmem] * (2 + len(steps)),
        out_specs=vmem,
        compiler_params=params,
        name="group",
    )(spectra, *steps, first_sum)
    groups = lax.axis_size("box")
    group_odd = swapped(group, "box", [(i, i + 1) for i in range(1, groups - 1, 2)])
    group_even = swapped(group, "box", [(i, i + 1) for i in range(0, groups - 1, 2)])

    packets = [x for step, x in enumerate(steps, 1) if carries_packet(step)]
    near, _, _ = pl.pallas_call(
        functools.partial(near_kernel, entries),
        out_shape=(
            shaped((boxes, waves, width), F32),
            shaped(sources.shape, BF16),
            shaped(ordered.shape, F32),
        ),
        in_specs=[vmem] * (5 + len(packets)),
        out_specs=(vmem,) * 3,
        input_output_aliases={3 + len(packets): 1, 4 + len(packets): 2},
        scratch_shapes=[pltpu.SMEM((1, length), jnp.int32)] + near_scratch + [pltpu.SemaphoreType.DMA],
        compiler_params=params,
        name="near",
    )(items, *packets, observers, first_sum, sources, ordered)

    return pl.pallas_call(
        functools.partial(incoming_kernel, entries, len(packets) - 1, parents),
        out_shape=shaped((boxes, waves, width), F32),
        in_specs=[vmem] * (9 + parents + len(packets)),
        out_specs=vmem,
        scratch_shapes=[
            pltpu.VMEM((boxes, waves, width), F32),
            pltpu.VMEM((boxes, waves, width), F32),
            pltpu.VMEM((boxes, width, 128), BF16),
            pltpu.VMEM((2, boxes * waves, parent_dirs), F32),
            pltpu.SMEM((1, length), jnp.int32),
        ]
        + near_scratch
        + [pltpu.SemaphoreType.DMA],
        compiler_params=params,
        name="incoming",
    )(*packets[1:], *gains, items, group_even, group, group_odd, cos_phase, sin_phase, imat, rad, observers, near)


def solution(mesh):
    placed = (
        P(("box", "dir"), None, None),
        P(("box", "dir"), None, None),
        P(),
        P(),
        P(),
        P(),
        P(("box", "dir"), None),
        P("box", None),
        P("box", None),
        P("box"),
        P(),
    )
    return jax.shard_map(
        per_device,
        mesh=mesh,
        in_specs=placed,
        out_specs=P(("box", "dir"), None, None),
        check_vma=False,
    )
```
